32 devices in a mesh: dp: 16 (over z, y, x), mp: 2 (over core).
Axes of the slice: x: 2, y: 2, z: 4, core: 2. Of those that a mesh axis runs over, the one named last changes fastest.
Arguments:
- word_inputs: bfloat16 [14336, 768], P('dp'), may hold values from -6 to 6
- entity_base: bfloat16 [2048, 768], P('dp'), may hold values from -6 to 6
- entity_ids: int32 [2048], P('dp'), may hold values from 0 to 126975
- buckets: int32 [16, 2, 16, 8], P('dp', 'mp'), may hold values from -1 to 127, as said below
- mask_positions: int32 [16, 16], P('dp'), may hold values from 0 to 127, as said below
- targets: int32 [16, 16], replicated, may hold values from 0 to 126975
- word_cotangent: bfloat16 [14336, 768], P('dp'), may hold values from -6 to 6
- attention_in: float32 [2, 6, 768, 768], P(None, None, 'dp', 'mp'), may hold values from -0.21875 to 0.21875
- attention_in_first: float32 [2, 6, 768, 768], P(None, None, 'dp', 'mp'), may hold values from -24 to 24
- attention_in_second: float32 [2, 6, 768, 768], P(None, None, 'dp', 'mp'), may hold values from 1.47456 to 5.89824
- attention_out: float32 [2, 768, 768], P(None, 'mp', 'dp'), may hold values from -4 to 4
- attention_out_first: float32 [2, 768, 768], P(None, 'mp', 'dp'), may hold values from -3 to 3
- attention_out_second: float32 [2, 768, 768], P(None, 'mp', 'dp'), may hold values from 0.0196608 to 0.0802816
- feed_up: float32 [2, 768, 3072], P(None, 'dp', 'mp'), may hold values from -0.21875 to 0.21875
- feed_up_first: float32 [2, 768, 3072], P(None, 'dp', 'mp'), may hold values from -16 to 16
- feed_up_second: float32 [2, 768, 3072], P(None, 'dp', 'mp'), may hold values from 0.65536 to 2.62144
- feed_down: float32 [2, 3072, 768], P(None, 'mp', 'dp'), may hold values from -0.109375 to 0.109375
- feed_down_first: float32 [2, 3072, 768], P(None, 'mp', 'dp'), may hold values from -40 to 40
- feed_down_second: float32 [2, 3072, 768], P(None, 'mp', 'dp'), may hold values from 3.2768 to 13.1072
- norm_params: float32 [2, 4, 768], P(None, None, 'dp'), may hold values from -0.5 to 1.5
- norm_params_first: float32 [2, 4, 768], P(None, None, 'dp'), may hold values from -64 to 64
- norm_params_second: float32 [2, 4, 768], P(None, None, 'dp'), may hold values from 8.02816 to 32.11264
- entity_proj: float32 [256, 768], P('dp'), may hold values from -2 to 2
- entity_proj_first: float32 [256, 768], P('dp'), may hold values from -1.5 to 1.5
- entity_proj_second: float32 [256, 768], P('dp'), may hold values from 0.00512 to 0.02048
- head_proj: float32 [768, 256], P('dp'), may hold values from -0.21875 to 0.21875
- head_proj_first: float32 [768, 256], P('dp'), may hold values from -0.00390625 to 0.00390625
- head_proj_second: float32 [768, 256], P('dp'), may hold values from 3.90625e-08 to 1.5625e-07
- entity_table: float32 [126976, 256], P(('dp', 'mp')), may hold values from -0.875 to 0.875
- entity_table_first: float32 [126976, 256], P(('dp', 'mp')), may hold values from -1 to 1
- entity_table_second: float32 [126976, 256], P(('dp', 'mp')), may hold values from 0 to 1, as said below
Outputs:
- loss_value: float32 [256], replicated
- word_grads: float32 [14336, 768], P('dp')
- attention_in_first_new: float32 [2, 6, 768, 768], P(None, None, 'dp', 'mp')
- attention_in_second_new: float32 [2, 6, 768, 768], P(None, None, 'dp', 'mp')
- attention_in_new: float32 [2, 6, 768, 768], P(None, None, 'dp', 'mp')
- attention_out_first_new: float32 [2, 768, 768], P(None, 'mp', 'dp')
- attention_out_second_new: float32 [2, 768, 768], P(None, 'mp', 'dp')
- attention_out_new: float32 [2, 768, 768], P(None, 'mp', 'dp')
- feed_up_first_new: float32 [2, 768, 3072], P(None, 'dp', 'mp')
- feed_up_second_new: float32 [2, 768, 3072], P(None, 'dp', 'mp')
- feed_up_new: float32 [2, 768, 3072], P(None, 'dp', 'mp')
- feed_down_first_new: float32 [2, 3072, 768], P(None, 'mp', 'dp')
- feed_down_second_new: float32 [2, 3072, 768], P(None, 'mp', 'dp')
- feed_down_new: float32 [2, 3072, 768], P(None, 'mp', 'dp')
- norm_params_first_new: float32 [2, 4, 768], P(None, None, 'dp')
- norm_params_second_new: float32 [2, 4, 768], P(None, None, 'dp')
- norm_params_new: float32 [2, 4, 768], P(None, None, 'dp')
- entity_proj_first_new: float32 [256, 768], P('dp')
- entity_proj_second_new: float32 [256, 768], P('dp')
- entity_proj_new: float32 [256, 768], P('dp')
- head_proj_first_new: float32 [768, 256], P('dp')
- head_proj_second_new: float32 [768, 256], P('dp')
- head_proj_new: float32 [768, 256], P('dp')
- entity_table_first_new: float32 [126976, 256], P(('dp', 'mp'))
- entity_table_second_new: float32 [126976, 256], P(('dp', 'mp'))
- entity_table_new: float32 [126976, 256], P(('dp', 'mp'))
The draws below stay inside these ranges and needn't reach their ends.
Inputs may be any that keep to these rules, and one draw needn't show every extreme that they name: buckets[i, j, k, c] is -1 or an index into the 128 entity slots of dp index i; each such slot is named exactly once in buckets[i], at some j, k with its entity id // 3968 equal to 2 * k + j, so that the row it reads is its entity id. `mask_positions`: the 16 positions of a sequence are distinct. `entity_table_second`: positive.
All inputs are finite; a program needn't handle non-finite values.
Results may differ from the reference program's by a relative error of at most 0.03.
Values may be sent and summed in bfloat16 or wider, within the bound.
A program may use at most 448 MiB of HBM per device.

```python
import math
from functools import partial
import jax
import jax.numpy as jnp
from jax import lax

D = 768
HEADS = 12
HEAD_DIM = 64
FF = 3072
ED = 256
ENT_DEV = 3968
WORDS = 896
ENT_LEN = 128
MASK_ENT = 16
LAYERS = 2
STEP = 10
SEQ_DEV = 1
LEN = 1024
SEQS = 16
CAP = 8
MASKED = 256
ENTITIES = 126976
N_DP = 16
DEVICES = 32


def entity_plan(key):
    slot_total = SEQ_DEV * ENT_LEN
    position_total = 2 * N_DP * CAP
    base_key = jax.random.fold_in(key, 11)
    full_key, source_key = jax.random.split(base_key)
    full_owner = jax.random.randint(full_key, (), 0, 2 * N_DP)
    positions = jnp.arange(position_total, dtype=jnp.int32)
    column = positions // (N_DP * CAP)
    owner_index = positions // CAP % N_DP * 2 + column
    within = positions % CAP

    def one_source(sub_key):
        order_key, slot_key, offset_key = jax.random.split(sub_key, 3)
        rank_values = jax.random.permutation(order_key, position_total).astype(jnp.int32)
        rank_values = jnp.where(owner_index == full_owner, within - CAP, rank_values)
        rank_order = jnp.argsort(rank_values, stable=True)
        chosen = rank_order[:slot_total]
        slot_order = jax.random.permutation(slot_key, slot_total).astype(jnp.int32)
        bucket_rows = jnp.full((position_total,), -1, jnp.int32).at[chosen].set(slot_order)
        offsets = jax.random.randint(offset_key, (slot_total,), 0, ENT_DEV).astype(jnp.int32)
        id_rows = jnp.zeros((slot_total,), jnp.int32).at[slot_order].set(owner_index[chosen] * ENT_DEV + offsets)
        return (bucket_rows, id_rows)
    bucket_rows, id_rows = jax.vmap(one_source)(jax.random.split(source_key, N_DP))
    return (bucket_rows.reshape(N_DP, 2, N_DP, CAP), id_rows.reshape(N_DP * slot_total))


def draw_entity_ids(key, part):
    return entity_plan(key)[1]


def draw_buckets(key, part):
    return entity_plan(key)[0]


def mask_plan(key):
    seq_keys = jax.random.split(jax.random.fold_in(key, 23), SEQS)

    def pick_positions(seq_key):
        return jax.random.permutation(seq_key, ENT_LEN)[:MASK_ENT].astype(jnp.int32)
    return jax.vmap(pick_positions)(seq_keys)


def draw_mask_positions(key, part):
    return mask_plan(key)


def target_plan(key):
    return jax.random.randint(jax.random.fold_in(key, 31), (SEQS, MASK_ENT), 0, ENTITIES).astype(jnp.int32)


def draw_targets(key, part):
    return target_plan(key)


def row_grad_scale(key):
    id_rows = entity_plan(key)[1]
    mask_rows = mask_plan(key)
    masked_flag = jnp.any(mask_rows[:, :, None] == jnp.arange(ENT_LEN, dtype=jnp.int32)[None, None, :], axis=1)
    input_mark = jnp.where(masked_flag.reshape(SEQS * ENT_LEN), 0, 2).astype(jnp.int32)
    marker = jnp.zeros((ENTITIES,), jnp.int32).at[id_rows].max(input_mark)
    marker = marker.at[target_plan(key).reshape(-1)].max(jnp.ones((MASKED,), jnp.int32))
    other_scale = 0.6 / (ENTITIES * MASKED ** 0.5)
    target_scale = 0.65 / MASKED
    return jnp.where(marker == 2, 0.3, jnp.where(marker == 1, target_scale, other_scale)).astype(jnp.float32)


def draw_entity_table_first(key, part):
    scale_rows = row_grad_scale(key)
    noise_draw = jnp.clip(jax.random.normal(jax.random.fold_in(key, 41), (ENTITIES, ED), jnp.float32), -4.0, 4.0)
    return 0.111 * scale_rows[:, None] * noise_draw


def draw_entity_table_second(key, part):
    scale_rows = row_grad_scale(key)
    factor = jnp.exp(jax.random.uniform(jax.random.fold_in(key, 43), (ENTITIES, ED), jnp.float32, 0.0, 1.3862944))
    return 0.001001 * factor * (scale_rows * scale_rows)[:, None]


def draw_norm_params(key, part):
    noise_key = jax.random.fold_in(key, 5)
    center = jnp.array([1.0, 0.0, 1.0, 0.0], jnp.float32)[None, :, None]
    noise_draw = 0.1 * jnp.clip(jax.random.normal(noise_key, (LAYERS, 4, D), jnp.float32), -4.0, 4.0)
    return center + noise_draw


def steps_of(stream_key, dims, cuts, smallest, high):
    gain, own = 1.0, jax.random.fold_in(stream_key, 6)
    for dim, shards_of in cuts:
        draws = jnp.exp(jax.random.uniform(jax.random.fold_in(own, dim), (shards_of,), jnp.float32, smallest / len(cuts), high / len(cuts)))
        gain = gain * jnp.repeat(draws, dims[dim] // shards_of).reshape([-1 if axis == dim else 1 for axis in range(len(dims))])
    return gain


def normal_values(own_key, extent, scale, reach, shards=(), kind=jnp.bfloat16):
    entries = jax.random.normal(own_key, extent, jnp.float32) * scale
    if len(shards) > 0:
        entries = steps_of(own_key, extent, shards, -0.22, 0.18) * entries
    return jnp.clip(entries, min=-reach, max=reach).astype(kind)


def setup_inputs(seed: int = 0) -> dict:
    splits = jax.random.split(jax.random.key(seed), 32)
    word_inputs = normal_values(splits[0], (SEQS * WORDS, D), 1.0, 6.0, ((0, 16),))
    entity_base = normal_values(splits[1], (SEQS * ENT_LEN, D), 1.0, 6.0, ((0, 16),))
    entity_ids = draw_entity_ids(jax.random.fold_in(splits[31], 71), 0)
    buckets = draw_buckets(jax.random.fold_in(splits[31], 71), 0)
    mask_positions = draw_mask_positions(jax.random.fold_in(splits[31], 71), 0)
    targets = draw_targets(jax.random.fold_in(splits[31], 71), 0)
    word_cotangent = normal_values(splits[6], (SEQS * WORDS, D), 1.0, 6.0, ((0, 16),))
    attention_in = normal_values(splits[7], (LAYERS, 6, D, D), D ** -0.5, 0.21875, ((2, 16), (3, 2)), jnp.float32)
    attention_in_first = normal_values(splits[8], (LAYERS, 6, D, D), (0.0333 * (SEQS * LEN) ** 0.5), 24.0, ((2, 16), (3, 2)), jnp.float32)
    attention_in_second = jnp.clip(jnp.exp(math.log(5.89824) - 1.3862944 * jax.random.uniform(splits[9], (LAYERS, 6, D, D), jnp.float32) ** steps_of(splits[9], (LAYERS, 6, D, D), ((2, 16), (3, 2)), -0.2, 0.2)), 1.47456, 5.89824)
    attention_out = normal_values(splits[10], (LAYERS, D, D), (max(1, D // 384)) ** -0.5, 4.0, ((1, 2), (2, 16)), jnp.float32)
    attention_out_first = normal_values(splits[11], (LAYERS, D, D), (0.0039 * (SEQS * LEN) ** 0.5), 3.0, ((1, 2), (2, 16)), jnp.float32)
    attention_out_second = jnp.clip(jnp.exp(math.log(0.0802816) - 1.4069136 * jax.random.uniform(splits[12], (LAYERS, D, D), jnp.float32) ** steps_of(splits[12], (LAYERS, D, D), ((1, 2), (2, 16)), -0.2, 0.2)), 0.0196608, 0.0802816)
    feed_up = normal_values(splits[13], (LAYERS, D, FF), D ** -0.5, 0.21875, ((1, 16), (2, 2)), jnp.float32)
    feed_up_first = normal_values(splits[14], (LAYERS, D, FF), (0.0222 * (SEQS * LEN) ** 0.5), 16.0, ((1, 16), (2, 2)), jnp.float32)
    feed_up_second = jnp.clip(jnp.exp(math.log(2.62144) - 1.3862944 * jax.random.uniform(splits[15], (LAYERS, D, FF), jnp.float32) ** steps_of(splits[15], (LAYERS, D, FF), ((1, 16), (2, 2)), -0.2, 0.2)), 0.65536, 2.62144)
    feed_down = normal_values(splits[16], (LAYERS, FF, D), FF ** -0.5, 0.109375, ((1, 2), (2, 16)), jnp.float32)
    feed_down_first = normal_values(splits[17], (LAYERS, FF, D), (0.05 * (SEQS * LEN) ** 0.5), 40.0, ((1, 2), (2, 16)), jnp.float32)
    feed_down_second = jnp.clip(jnp.exp(math.log(13.1072) - 1.3862944 * jax.random.uniform(splits[18], (LAYERS, FF, D), jnp.float32) ** steps_of(splits[18], (LAYERS, FF, D), ((1, 2), (2, 16)), -0.2, 0.2)), 3.2768, 13.1072)
    norm_params = draw_norm_params(jax.random.fold_in(splits[31], 71), 0)
    norm_params_first = normal_values(splits[20], (LAYERS, 4, D), (0.0777 * (SEQS * LEN) ** 0.5), 64.0, ((2, 16),), jnp.float32)
    norm_params_second = jnp.clip(jnp.exp(math.log(32.11264) - 1.3862944 * jax.random.uniform(splits[21], (LAYERS, 4, D), jnp.float32) ** steps_of(splits[21], (LAYERS, 4, D), ((2, 16),), -0.2, 0.2)), 8.02816, 32.11264)
    entity_proj = normal_values(splits[22], (ED, D), (max(1, ED // 36)) ** -0.5, 2.0, ((0, 16),), jnp.float32)
    entity_proj_first = normal_values(splits[23], (ED, D), (0.0056 * (SEQS * ENT_LEN) ** 0.5), 1.5, ((0, 16),), jnp.float32)
    entity_proj_second = jnp.clip(jnp.exp(math.log(0.02048) - 1.3862944 * jax.random.uniform(splits[24], (ED, D), jnp.float32) ** steps_of(splits[24], (ED, D), ((0, 16),), -0.2, 0.2)), 0.00512, 0.02048)
    head_proj = normal_values(splits[25], (D, ED), D ** -0.5, 0.21875, ((0, 16),), jnp.float32)
    head_proj_first = normal_values(splits[26], (D, ED), (0.0111 * MASKED ** -0.5), 0.00390625, ((0, 16),), jnp.float32)
    head_proj_second = jnp.clip(jnp.exp(math.log(1.56249996052793e-07) - 1.3862944 * jax.random.uniform(splits[27], (D, ED), jnp.float32) ** steps_of(splits[27], (D, ED), ((0, 16),), -0.2, 0.2)), 3.906249901319825e-08, 1.56249996052793e-07)
    entity_table = normal_values(splits[28], (ENTITIES, ED), 0.15, 0.875, ((0, 32),), jnp.float32)
    entity_table_first = draw_entity_table_first(jax.random.fold_in(splits[31], 71), 0)
    entity_table_second = draw_entity_table_second(jax.random.fold_in(splits[31], 71), 0)
    return {"word_inputs": word_inputs, "entity_base": entity_base, "entity_ids": entity_ids, "buckets": buckets, "mask_positions": mask_positions, "targets": targets, "word_cotangent": word_cotangent, "attention_in": attention_in, "attention_in_first": attention_in_first, "attention_in_second": attention_in_second, "attention_out": attention_out, "attention_out_first": attention_out_first, "attention_out_second": attention_out_second, "feed_up": feed_up, "feed_up_first": feed_up_first, "feed_up_second": feed_up_second, "feed_down": feed_down, "feed_down_first": feed_down_first, "feed_down_second": feed_down_second, "norm_params": norm_params, "norm_params_first": norm_params_first, "norm_params_second": norm_params_second, "entity_proj": entity_proj, "entity_proj_first": entity_proj_first, "entity_proj_second": entity_proj_second, "head_proj": head_proj, "head_proj_first": head_proj_first, "head_proj_second": head_proj_second, "entity_table": entity_table, "entity_table_first": entity_table_first, "entity_table_second": entity_table_second}


@jax.custom_vjp
def low(v):
    return lax.optimization_barrier(v.astype(jnp.bfloat16)).astype(jnp.float32)

@jax.custom_vjp
def low_back(v):
    return v

def low_keep(v):
    return (low(v), None)

def low_pass(kept, grad):
    return (grad,)

def back_keep(v):
    return (v, None)

def back_low(kept, grad):
    return (low(grad),)
low.defvjp(low_keep, low_pass)
low_back.defvjp(back_keep, back_low)
norm_eps = 1e-05
beta_first = 0.9
beta_second = 0.999
adam_eps = 1e-12
weight_decay = 0.01
kind_rates = (0.05, 1.0, 0.05, 0.027, 0.75, 0.5, 0.05, 0.2)

def matmul_high(left_side, right_side):
    return jnp.dot(left_side, right_side, precision=lax.Precision.HIGHEST)

def einsum_high(formula, left_side, right_side):
    return jnp.einsum(formula, left_side, right_side, precision=lax.Precision.HIGHEST)

def rounded_both(values):
    return low(low_back(values))

def layer_norm(values, gain_row, shift_row):
    centered = values - lax.optimization_barrier(jnp.mean(values, axis=-1, keepdims=True))
    spread = lax.optimization_barrier(jnp.mean(centered * centered, axis=-1, keepdims=True))
    return centered * lax.rsqrt(spread + norm_eps) * gain_row + shift_row

def gelu_exact(values):
    return jax.nn.gelu(values, approximate=False)

def adam_update(master, first_moment, second_moment, gradient, kind_rate):
    first_new = beta_first * first_moment + (1.0 - beta_first) * gradient
    second_new = beta_second * second_moment + (1.0 - beta_second) * gradient * gradient
    first_hat = first_new / (1.0 - beta_first ** STEP)
    second_hat = second_new / (1.0 - beta_second ** STEP)
    master_new = master - kind_rate * (first_hat / (jnp.sqrt(second_hat) + adam_eps) + weight_decay * master)
    return (first_new, second_new, master_new)

def sequence_layers(weights, layer_input_list):
    attention_in, attention_out, feed_up, feed_down, norm_params = weights
    hidden = layer_input_list
    shaped = (LEN, HEADS, HEAD_DIM)
    for layer_index in range(LAYERS):
        attn_mats = attention_in[layer_index]
        hidden_low = low(hidden)
        words_low = hidden_low[:WORDS]
        ents_low = hidden_low[WORDS:]
        query_word = rounded_both(jnp.concatenate([matmul_high(words_low, attn_mats[0]), matmul_high(ents_low, attn_mats[2])], axis=0))
        query_entity = rounded_both(jnp.concatenate([matmul_high(words_low, attn_mats[1]), matmul_high(ents_low, attn_mats[3])], axis=0))
        key_rows = rounded_both(matmul_high(hidden_low, attn_mats[4])).reshape(shaped)
        value_rows = rounded_both(matmul_high(hidden_low, attn_mats[5])).reshape(shaped)
        query_word = query_word.reshape(shaped)
        query_entity = query_entity.reshape(shaped)
        score_word = einsum_high('qhd,khd->hqk', query_word, key_rows[:WORDS])
        score_entity = einsum_high('qhd,khd->hqk', query_entity, key_rows[WORDS:])
        scores = low_back(jnp.concatenate([score_word, score_entity], axis=-1)) * 0.125
        peak_value = lax.optimization_barrier(jnp.max(scores, axis=-1, keepdims=True))
        exp_scores = jnp.exp(scores - peak_value)
        prob_rows = exp_scores / lax.optimization_barrier(jnp.sum(exp_scores, axis=-1, keepdims=True))
        mixed_heads = einsum_high('hqk,khd->qhd', low(prob_rows), value_rows)
        mixed_heads = rounded_both(mixed_heads.reshape(LEN, D))
        attended = low_back(matmul_high(mixed_heads, attention_out[layer_index]))
        first_out = layer_norm(hidden + attended, norm_params[layer_index, 0], norm_params[layer_index, 1])
        inner_low = low(gelu_exact(low_back(matmul_high(low(first_out), feed_up[layer_index]))))
        outer_out = low_back(matmul_high(inner_low, feed_down[layer_index]))
        hidden = layer_norm(first_out + outer_out, norm_params[layer_index, 2], norm_params[layer_index, 3])
    return hidden

def partition(states, table_low, flat_targets):
    table_blocks = table_low.reshape(DEVICES, ENT_DEV, ED)
    columns = jnp.arange(ENT_DEV, dtype=jnp.int32)

    def block_step(carry, seq_item):
        peak_value, exp_total, picked = carry
        block_rows, block_index = seq_item
        logits = low_back(jnp.dot(states, block_rows.T, precision=lax.Precision.HIGHEST))
        new_peak = jnp.maximum(peak_value, lax.optimization_barrier(jnp.max(logits, axis=1)))
        exp_total = exp_total * jnp.exp(peak_value - new_peak) + lax.optimization_barrier(jnp.sum(jnp.exp(logits - new_peak[:, None]), axis=1))
        target_hits = columns[None, :] == (flat_targets - block_index * ENT_DEV)[:, None]
        picked = picked + lax.optimization_barrier(jnp.sum(jnp.where(target_hits, logits, 0.0), axis=1))
        return ((new_peak, exp_total, picked), None)
    start_carry = (jnp.full((MASKED,), -1e+30, jnp.float32), jnp.zeros((MASKED,), jnp.float32), jnp.zeros((MASKED,), jnp.float32))
    final_carry, unused = lax.scan(jax.checkpoint(block_step), start_carry, (table_blocks, jnp.arange(DEVICES, dtype=jnp.int32)))
    peak_value, exp_total, picked = final_carry
    return (peak_value + jnp.log(exp_total), picked)

def objective(params, words_in, base_rows, cotangent_rows, lookup_ids, slot_weight, mask_positions, targets):
    attention_in, attention_out, feed_up, feed_down, norm_params, entity_proj, head_proj, entity_table = params
    weights = (low(attention_in), low(attention_out), low(feed_up), low(feed_down), low(norm_params))
    table_low = low(entity_table)
    entity_rows = table_low[lookup_ids] * slot_weight[:, None]
    entity_inputs = base_rows + low_back(matmul_high(entity_rows, low(entity_proj)))
    layer_input_list = jnp.concatenate([words_in.reshape(SEQS, WORDS, D), entity_inputs.reshape(SEQS, ENT_LEN, D)], axis=1)
    outputs = lax.map(jax.checkpoint(partial(sequence_layers, weights)), layer_input_list)
    word_term = jnp.sum(outputs[:, :WORDS] * cotangent_rows.reshape(SEQS, WORDS, D))
    seq_index = jnp.arange(SEQS, dtype=jnp.int32)[:, None]
    masked = outputs[seq_index, WORDS + mask_positions].reshape(MASKED, D)
    head_pre = low_back(matmul_high(low(masked), low(head_proj)))
    states = low(gelu_exact(head_pre))
    log_norm, picked = partition(states, table_low, targets.reshape(MASKED))
    row_losses = log_norm - picked
    return (jnp.mean(row_losses) + word_term, row_losses)

def reference(word_inputs, entity_base, entity_ids, buckets, mask_positions, targets, word_cotangent, attention_in, attention_in_first, attention_in_second, attention_out, attention_out_first, attention_out_second, feed_up, feed_up_first, feed_up_second, feed_down, feed_down_first, feed_down_second, norm_params, norm_params_first, norm_params_second, entity_proj, entity_proj_first, entity_proj_second, head_proj, head_proj_first, head_proj_second, entity_table, entity_table_first, entity_table_second):
    slot_total = SEQ_DEV * ENT_LEN
    position_total = 2 * N_DP * CAP
    named_slot = buckets.reshape(N_DP, position_total)[:, :, None] == jnp.arange(slot_total, dtype=jnp.int32)[None, None, :]
    counts = lax.optimization_barrier(jnp.sum(named_slot.astype(jnp.float32), axis=1)).reshape(SEQS * ENT_LEN)
    positions = jnp.arange(position_total, dtype=jnp.int32)
    owner_index = positions // CAP % N_DP * 2 + positions // (N_DP * CAP)
    owner_of_slot = lax.optimization_barrier(jnp.sum(jnp.where(named_slot, owner_index[None, :, None], 0), axis=1)).astype(jnp.int32).reshape(SEQS * ENT_LEN)
    lookup_ids = (owner_of_slot * ENT_DEV + entity_ids % ENT_DEV).astype(jnp.int32)
    masked_flag = jnp.any(mask_positions[:, :, None] == jnp.arange(ENT_LEN, dtype=jnp.int32)[None, None, :], axis=1)
    slot_weight = counts * (1.0 - masked_flag.reshape(SEQS * ENT_LEN).astype(jnp.float32))
    masters = (attention_in, attention_out, feed_up, feed_down, norm_params, entity_proj, head_proj, entity_table)
    firsts = (attention_in_first, attention_out_first, feed_up_first, feed_down_first, norm_params_first, entity_proj_first, head_proj_first, entity_table_first)
    seconds = (attention_in_second, attention_out_second, feed_up_second, feed_down_second, norm_params_second, entity_proj_second, head_proj_second, entity_table_second)
    base_rows = entity_base.astype(jnp.float32)
    cotangent_rows = word_cotangent.astype(jnp.float32)

    def total_of(params, words_in):
        return objective(params, words_in, base_rows, cotangent_rows, lookup_ids, slot_weight, mask_positions, targets)
    objective_value, pullback, loss_value = jax.vjp(total_of, masters, word_inputs.astype(jnp.float32), has_aux=True)
    gradients, word_grads = pullback(jnp.ones((), jnp.float32))
    results = [loss_value, word_grads.reshape(SEQS * WORDS, D)]
    for master, first_moment, second_moment, gradient, kind_rate in zip(masters, firsts, seconds, gradients, kind_rates):
        results.extend(adam_update(master, first_moment, second_moment, gradient, kind_rate))
    return (results[0], results[1], results[2], results[3], results[4], results[5], results[6], results[7], results[8], results[9], results[10], results[11], results[12], results[13], results[14], results[15], results[16], results[17], results[18], results[19], results[20], results[21], results[22], results[23], results[24], results[25])
```

```python
import functools

import jax
import jax.numpy as jnp
from jax import lax
from jax.experimental import pallas as pl
from jax.experimental.pallas import tpu as pltpu
from jax.sharding import PartitionSpec as P

D = 768
HEAD_DIM = 64
WORDS = 896
ENT_LEN = 128
MASK_ENT = 16
LAYERS = 2
STEP = 10
SEQ_DEV = 1


norm_eps = 1e-05
beta_first = 0.9
beta_second = 0.999
adam_eps = 1e-12
weight_decay = 0.01
kind_rates = (0.05, 1.0, 0.05, 0.027, 0.75, 0.5, 0.05, 0.2)


MESH = pl.DeviceIdType.MESH
ANY = pl.BlockSpec(memory_space=pl.ANY)
VMEM = pl.BlockSpec(memory_space=pltpu.VMEM)
VMEM_BYTES = 60 * 2**20


def chip_grid(n_dp):
    return {16: (4, 2, 2), 64: (4, 4, 4)}.get(n_dp, (n_dp, 1, 1))


def place(dims):
    index = lax.axis_index("dp")
    return index // (dims[1] * dims[2]), index // dims[2] % dims[1], index % dims[2]


def axis_peers(dims, axis):
    here = place(dims)
    core = lax.axis_index("mp")
    peers = []
    for step in range(1, dims[axis]):
        spot = list(here)
        spot[axis] = lax.rem(here[axis] + step, dims[axis])
        peers.append((spot[axis], (spot[0] * dims[1] * dims[2] + spot[1] * dims[2] + spot[2], core)))
    return peers


def greet(targets):
    barrier = pltpu.get_barrier_semaphore()
    for target in targets:
        pl.semaphore_signal(barrier, inc=1, device_id=target, device_id_type=MESH)
    pl.semaphore_wait(barrier, len(targets))


def send(src, dst, send_sem, recv_sem, target):
    copy = pltpu.make_async_remote_copy(
        src_ref=src,
        dst_ref=dst,
        send_sem=send_sem,
        recv_sem=recv_sem,
        device_id=target,
        device_id_type=MESH,
    )
    copy.start()
    return copy


def gather_body(dims, chunks, count, *refs):
    shards, wholes = refs[:count], refs[count : 2 * count]
    send_sem, recv_sem, local_sem = refs[2 * count :]
    z, y, x = place(dims)
    peers = [axis_peers(dims, axis) for axis in range(3)]
    greet([target for group in peers for _, target in group])
    pending = {}

    def start(stage, c):
        which, first, size, y_first = chunks[c]
        rows = pl.ds(first, size)
        whole = wholes[which]
        copies = []
        if stage == 0:
            src, dst, group = shards[which].at[rows], whole.at[rows, z, y, x], peers[0]
            own = pltpu.make_async_copy(src, dst, local_sem.at[c])
            own.start()
            copies.append(own)
        elif stage == 1:
            src = whole.at[rows, :, y, x]
            dst, group = src, peers[1 if y_first else 2]
        else:
            src = whole.at[rows, :, :, x] if y_first else whole.at[rows, :, y]
            dst, group = src, peers[2 if y_first else 1]
        base = (0, dims[0], dims[0] + max(dims[1:]))[stage]
        for slot, (_, target) in enumerate(group):
            copies.append(
                send(src, dst, send_sem.at[c, base + slot], recv_sem.at[c, base + slot], target)
            )
        pending[stage, c] = copies

    def finish(stage, c):
        for copy in pending.pop((stage, c)):
            copy.wait()

    total = len(chunks)
    start(0, 0)
    for step in range(total + 2):
        if step + 1 < total:
            start(0, step + 1)
        if step < total:
            finish(0, step)
            start(1, step)
        if 0 <= step - 1 < total:
            finish(1, step - 1)
            start(2, step - 1)
        if 0 <= step - 2 < total:
            finish(2, step - 2)


def gather_weights(dims, shards, chunks, collective_id):
    count = len(shards)
    copies = dims[0] + 2 * max(dims[1:])
    return pl.pallas_call(
        functools.partial(gather_body, dims, chunks, count),
        out_shape=[
            jax.ShapeDtypeStruct((s.shape[0], *dims, *s.shape[1:]), s.dtype) for s in shards
        ],
        in_specs=[ANY] * count,
        out_specs=[ANY] * count,
        scratch_shapes=[
            pltpu.SemaphoreType.DMA((len(chunks), copies)),
            pltpu.SemaphoreType.DMA((len(chunks), copies)),
            pltpu.SemaphoreType.DMA((len(chunks),)),
        ],
        compiler_params=pltpu.CompilerParams(
            collective_id=collective_id, has_side_effects=True, vmem_limit_bytes=2**20
        ),
    )(*shards)


def sum_body(dims, flags, *refs):
    count = len(flags)
    parts, totals = refs[:count], refs[count : 2 * count]
    buffers = refs[2 * count : 6 * count]
    send_sem, recv_sem, local_sem = refs[6 * count :]
    z, y, x = place(dims)
    peers = [axis_peers(dims, axis) for axis in range(3)]
    greet([target for group in peers for _, target in group])
    pending = {}

    def start(stage, c):
        y_first = flags[c]
        own, first, second, third = buffers[4 * c : 4 * c + 4]
        copies = []
        base = (0, max(dims[1:]), 2 * max(dims[1:]))[stage]
        if stage == 0:
            mine = parts[c].at[:, y] if y_first else parts[c].at[:, :, x]
            local = pltpu.make_async_copy(mine, own, local_sem.at[c])
            local.start()
            copies.append(local)
        group = peers[((1, 2, 0) if y_first else (2, 1, 0))[stage]]
        for slot, (spot, target) in enumerate(group):
            if stage == 0:
                src = parts[c].at[:, spot] if y_first else parts[c].at[:, :, spot]
                dst = first.at[slot]
            elif stage == 1:
                src, dst = own.at[:, spot], second.at[slot]
            else:
                src, dst = own.at[spot, x if y_first else y], third.at[slot]
            copies.append(
                send(src, dst, send_sem.at[c, base + slot], recv_sem.at[c, base + slot], target)
            )
        pending[stage, c] = copies

    def finish(stage, c):
        y_first = flags[c]
        own, first, second, third = buffers[4 * c : 4 * c + 4]
        for copy in pending.pop((stage, c)):
            copy.wait()
        across = dims[2] if y_first else dims[1]
        line = x if y_first else y
        count_peers = len(peers[((1, 2, 0) if y_first else (2, 1, 0))[stage]])
        if stage == 0 and count_peers:

            def add_first(i, carry):
                value = own[i // across, i % across].astype(jnp.float32)
                for slot in range(count_peers):
                    value += first[slot, i // across, i % across].astype(jnp.float32)
                own[i // across, i % across] = value.astype(own.dtype)
                return carry

            lax.fori_loop(0, dims[0] * across, add_first, 0)
        if stage == 1 and count_peers:

            def add_second(i, carry):
                value = own[i, line].astype(jnp.float32)
                for slot in range(count_peers):
                    value += second[slot, i].astype(jnp.float32)
                own[i, line] = value.astype(own.dtype)
                return carry

            lax.fori_loop(0, dims[0], add_second, 0)
        if stage == 2:
            value = own[z, line].astype(jnp.float32)
            for slot in range(count_peers):
                value += third[slot].astype(jnp.float32)
            totals[c][...] = value

    total = len(flags)
    ahead = 2
    for c in range(min(ahead, total)):
        start(0, c)
    for step in range(total + 2 * ahead):
        if step + ahead < total:
            start(0, step + ahead)
        if step < total:
            finish(0, step)
            start(1, step)
        if 0 <= step - ahead < total:
            finish(1, step - ahead)
            start(2, step - ahead)
        if 0 <= step - 2 * ahead < total:
            finish(2, step - 2 * ahead)


def sum_gradients(dims, parts, flags, collective_id):
    count = len(parts)
    scratch = []
    for part, y_first in zip(parts, flags):
        block = part.shape[3:]
        own = (dims[0], dims[2] if y_first else dims[1])
        turns = (dims[1], dims[2]) if y_first else (dims[2], dims[1])
        scratch += [
            pltpu.VMEM((*own, *block), part.dtype),
            pltpu.VMEM((max(turns[0] - 1, 1), *own, *block), part.dtype),
            pltpu.VMEM((max(turns[1] - 1, 1), dims[0], *block), part.dtype),
            pltpu.VMEM((max(dims[0] - 1, 1), *block), part.dtype),
        ]
    copies = dims[0] + 2 * max(dims[1:])
    return pl.pallas_call(
        functools.partial(sum_body, dims, flags),
        out_shape=[jax.ShapeDtypeStruct(part.shape[3:], jnp.float32) for part in parts],
        in_specs=[ANY] * count,
        out_specs=[VMEM] * count,
        scratch_shapes=scratch
        + [
            pltpu.SemaphoreType.DMA((count, copies)),
            pltpu.SemaphoreType.DMA((count, copies)),
            pltpu.SemaphoreType.DMA((count,)),
        ],
        compiler_params=pltpu.CompilerParams(
            collective_id=collective_id, has_side_effects=True, vmem_limit_bytes=VMEM_BYTES
        ),
    )(*parts)


def spread_body(count, wide, swap, data, result, send_sem, recv_sem, local_sem):
    pair = lax.axis_size("mp")
    index = lax.axis_index("dp") * pair + lax.axis_index("mp") if wide else lax.axis_index("dp")

    def target_of(step):
        other = lax.rem(index + step, count)
        if wide:
            return other, (other // pair, lax.rem(other, pair))
        return other, (other, lax.axis_index("mp"))

    barrier = pltpu.get_barrier_semaphore()

    def hello(step, carry):
        pl.semaphore_signal(barrier, inc=1, device_id=target_of(step)[1], device_id_type=MESH)
        return carry

    lax.fori_loop(1, count, hello, 0)
    pl.semaphore_wait(barrier, count - 1)
    own = pltpu.make_async_copy(data.at[index if swap else 0], result.at[index], local_sem)
    own.start()

    def copy_of(step):
        other, target = target_of(step)
        return pltpu.make_async_remote_copy(
            src_ref=data.at[other if swap else 0],
            dst_ref=result.at[index],
            send_sem=send_sem.at[step],
            recv_sem=recv_sem.at[step],
            device_id=target,
            device_id_type=MESH,
        )

    def go(step, carry):
        copy_of(step).start()
        return carry

    def done(step, carry):
        copy_of(step).wait()
        return carry

    lax.fori_loop(1, count, go, 0)
    own.wait()
    lax.fori_loop(1, count, done, 0)


def spread(data, wide, swap, collective_id):
    count = lax.axis_size("dp") * (lax.axis_size("mp") if wide else 1)
    block = data.shape[1:] if swap else data.shape
    return pl.pallas_call(
        functools.partial(spread_body, count, wide, swap),
        out_shape=jax.ShapeDtypeStruct((count, *block), data.dtype),
        in_specs=[VMEM],
        out_specs=VMEM,
        scratch_shapes=[
            pltpu.SemaphoreType.DMA((count,)),
            pltpu.SemaphoreType.DMA((count,)),
            pltpu.SemaphoreType.DMA,
        ],
        compiler_params=pltpu.CompilerParams(
            collective_id=collective_id, has_side_effects=True, vmem_limit_bytes=VMEM_BYTES
        ),
    )(data if swap else data[None])


def layer_norm(values, gain_row, shift_row):
    centered = values - jnp.mean(values, axis=-1, keepdims=True)
    spread = jnp.mean(centered * centered, axis=-1, keepdims=True)
    return centered * lax.rsqrt(spread + norm_eps) * gain_row + shift_row


def gelu_exact(values):
    return jax.nn.gelu(values, approximate=False)


def adam_update(master, first_moment, second_moment, gradient, kind_rate):
    first_new = beta_first * first_moment + (1.0 - beta_first) * gradient
    second_new = beta_second * second_moment + (1.0 - beta_second) * gradient * gradient
    first_hat = first_new / (1.0 - beta_first**STEP)
    second_hat = second_new / (1.0 - beta_second**STEP)
    master_new = master - kind_rate * (
        first_hat / (jnp.sqrt(second_hat) + adam_eps) + weight_decay * master
    )
    return (first_new, second_new, master_new)


def project(fetched_row_values, weight_matrix_entry):
    return jnp.einsum(
        "mvw,wu->mvu", fetched_row_values, weight_matrix_entry, preferred_element_type=jnp.float32
    )


def project_back(row_gradient_block, weight_matrix_entry):
    return jnp.einsum(
        "tic,vc->tiv", row_gradient_block, weight_matrix_entry, preferred_element_type=jnp.float32
    )


def project_turned(rows, turned):
    return jnp.einsum("mvw,uw->mvu", rows, turned, preferred_element_type=jnp.float32)


def project_back_turned(row_gradient_block, turned):
    return jnp.einsum("tic,cv->tiv", row_gradient_block, turned, preferred_element_type=jnp.float32)


def weight_grad(layer_input_list, row_gradient_block):
    return jnp.einsum(
        "hmq,hmw->qw", layer_input_list, row_gradient_block, preferred_element_type=jnp.float32
    ).astype(jnp.bfloat16)


def split_heads(values):
    return values.reshape(values.shape[0], values.shape[1], values.shape[2] // HEAD_DIM, HEAD_DIM)


def pair_sum(partial_sum):
    mine = partial_sum.astype(jnp.bfloat16)
    theirs = lax.ppermute(mine, "mp", [(0, 1), (1, 0)])
    return mine.astype(jnp.float32) + theirs.astype(jnp.float32)


merge_heads = merge_inputs = pair_sum


def seq_scores(query_word, query_entity, key_rows):
    score_word = jnp.einsum(
        "qhd,khd->hqk", query_word, key_rows[:WORDS], preferred_element_type=jnp.float32
    )
    score_entity = jnp.einsum(
        "qhd,khd->hqk", query_entity, key_rows[WORDS:], preferred_element_type=jnp.float32
    )
    return jnp.concatenate([score_word, score_entity], axis=-1) * 0.125


def attend_forward(seq_item):
    query_word, query_entity, key_rows, value_rows = seq_item
    scores = seq_scores(query_word, query_entity, key_rows)
    peak_value = jnp.max(scores, axis=-1, keepdims=True)
    exp_scores = jnp.exp(scores - peak_value)
    exp_total = jnp.sum(exp_scores, axis=-1, keepdims=True)
    prob_low = (exp_scores / exp_total).astype(jnp.bfloat16)
    mixed_heads = jnp.einsum(
        "hqk,khd->qhd", prob_low, value_rows, preferred_element_type=jnp.float32
    )
    return (mixed_heads, (peak_value + jnp.log(exp_total))[..., 0])


def attend_backward(seq_item):
    query_word, query_entity, key_rows, value_rows, log_norm, grad_mixed = seq_item
    scores = seq_scores(query_word, query_entity, key_rows)
    prob_rows = jnp.exp(scores - log_norm[..., None])
    grad_value = jnp.einsum(
        "hqk,qhd->khd",
        prob_rows.astype(jnp.bfloat16),
        grad_mixed,
        preferred_element_type=jnp.float32,
    )
    grad_probs = jnp.einsum(
        "qhd,khd->hqk", grad_mixed, value_rows, preferred_element_type=jnp.float32
    )
    inner_sum = jnp.sum(prob_rows * grad_probs, axis=-1, keepdims=True)
    grad_scores = (prob_rows * (grad_probs - inner_sum) * 0.125).astype(jnp.bfloat16)
    score_word = grad_scores[..., :WORDS]
    score_entity = grad_scores[..., WORDS:]
    grad_qw = jnp.einsum(
        "hqk,khd->qhd", score_word, key_rows[:WORDS], preferred_element_type=jnp.float32
    )
    grad_qe = jnp.einsum(
        "hqk,khd->qhd", score_entity, key_rows[WORDS:], preferred_element_type=jnp.float32
    )
    grad_key = jnp.concatenate(
        [
            jnp.einsum("hqk,qhd->khd", score_word, query_word, preferred_element_type=jnp.float32),
            jnp.einsum(
                "hqk,qhd->khd", score_entity, query_entity, preferred_element_type=jnp.float32
            ),
        ],
        axis=0,
    )
    return (grad_qw, grad_qe, grad_key, grad_value)


def layer_forward(hidden, attn_mats, out_mat, up_mat, down_mat, gain_rows):
    hidden_low = hidden.astype(jnp.bfloat16)
    words_low = hidden_low[:, :WORDS]
    ents_low = hidden_low[:, WORDS:]
    query_word = jnp.concatenate(
        [project(words_low, attn_mats[0]), project(ents_low, attn_mats[2])], axis=1
    ).astype(jnp.bfloat16)
    query_entity = jnp.concatenate(
        [project(words_low, attn_mats[1]), project(ents_low, attn_mats[3])], axis=1
    ).astype(jnp.bfloat16)
    key_rows = project(hidden_low, attn_mats[4]).astype(jnp.bfloat16)
    value_rows = project(hidden_low, attn_mats[5]).astype(jnp.bfloat16)
    mixed_heads, log_norm = lax.map(
        attend_forward,
        (
            split_heads(query_word),
            split_heads(query_entity),
            split_heads(key_rows),
            split_heads(value_rows),
        ),
    )
    mixed_low = mixed_heads.reshape(key_rows.shape).astype(jnp.bfloat16)
    attended = merge_heads(project_turned(mixed_low, out_mat))
    first_out = layer_norm(hidden + attended, gain_rows[0], gain_rows[1])
    first_low = first_out.astype(jnp.bfloat16)
    inner_pre = project(first_low, up_mat)
    inner_low = gelu_exact(inner_pre).astype(jnp.bfloat16)
    outer_out = merge_heads(project_turned(inner_low, down_mat))
    result = layer_norm(first_out + outer_out, gain_rows[2], gain_rows[3])
    saved_acts = (
        hidden,
        hidden_low,
        query_word,
        query_entity,
        key_rows,
        value_rows,
        log_norm,
        mixed_low,
        attended,
        first_out,
        first_low,
        inner_pre,
        inner_low,
        outer_out,
    )
    return (result, saved_acts)


def layer_backward(grad_out, saved_acts, attn_mats, out_mat, up_mat, down_mat, gain_rows):
    (
        hidden,
        hidden_low,
        query_word,
        query_entity,
        key_rows,
        value_rows,
        log_norm,
        mixed_low,
        attended,
        first_out,
        first_low,
        inner_pre,
        inner_low,
        outer_out,
    ) = saved_acts
    second_back = jax.vjp(layer_norm, first_out + outer_out, gain_rows[2], gain_rows[3])[1]
    grad_second, grad_gain_late, grad_shift_late = second_back(grad_out)
    grad_outer = grad_second.astype(jnp.bfloat16)
    grad_down = weight_grad(grad_outer, inner_low)
    grad_inner = project_back_turned(grad_outer, down_mat)
    grad_pre = jax.vjp(gelu_exact, inner_pre)[1](grad_inner)[0].astype(jnp.bfloat16)
    grad_up = weight_grad(first_low, grad_pre)
    grad_first = grad_second + merge_inputs(project_back(grad_pre, up_mat))
    first_back = jax.vjp(layer_norm, hidden + attended, gain_rows[0], gain_rows[1])[1]
    grad_first_in, grad_gain_early, grad_shift_early = first_back(grad_first)
    grad_attended = grad_first_in.astype(jnp.bfloat16)
    grad_out_mat = weight_grad(grad_attended, mixed_low)
    grad_mixed = project_back_turned(grad_attended, out_mat).astype(jnp.bfloat16)
    grad_qw, grad_qe, grad_key, grad_value = lax.map(
        attend_backward,
        (
            split_heads(query_word),
            split_heads(query_entity),
            split_heads(key_rows),
            split_heads(value_rows),
            log_norm,
            split_heads(grad_mixed),
        ),
    )
    flat_shape = key_rows.shape
    grad_qw = grad_qw.reshape(flat_shape).astype(jnp.bfloat16)
    grad_qe = grad_qe.reshape(flat_shape).astype(jnp.bfloat16)
    grad_key = grad_key.reshape(flat_shape).astype(jnp.bfloat16)
    grad_value = grad_value.reshape(flat_shape).astype(jnp.bfloat16)
    words_low = hidden_low[:, :WORDS]
    ents_low = hidden_low[:, WORDS:]
    grad_mats = (
        weight_grad(words_low, jnp.concatenate([grad_qw[:, :WORDS], grad_qe[:, :WORDS]], axis=-1)),
        weight_grad(ents_low, jnp.concatenate([grad_qw[:, WORDS:], grad_qe[:, WORDS:]], axis=-1)),
        weight_grad(hidden_low, jnp.concatenate([grad_key, grad_value], axis=-1)),
    )
    part_words = project_back(grad_qw[:, :WORDS], attn_mats[0]) + project_back(
        grad_qe[:, :WORDS], attn_mats[1]
    )
    part_ents = project_back(grad_qw[:, WORDS:], attn_mats[2]) + project_back(
        grad_qe[:, WORDS:], attn_mats[3]
    )
    part_sum = (
        jnp.concatenate([part_words, part_ents], axis=1)
        + project_back(grad_key, attn_mats[4])
        + project_back(grad_value, attn_mats[5])
    )
    grad_hidden = grad_first_in + merge_inputs(part_sum)
    grad_norms = jnp.stack([grad_gain_early, grad_shift_early, grad_gain_late, grad_shift_late])
    return (grad_hidden, (grad_mats, grad_out_mat, grad_up, grad_down, grad_norms))


def padded_rows(values):
    extra = -values.shape[-2] % 16
    return jnp.pad(values, [(0, 0)] * (values.ndim - 2) + [(0, extra), (0, 0)])


def gather_all(dims, attention_in, attention_out, feed_up, feed_down, norm_params, entity_proj, head_proj):
    def turned(values):
        return jnp.swapaxes(values, 1, 2)

    mats = attention_in.reshape(-1, *attention_in.shape[2:])
    norms = norm_params.reshape(1, -1, norm_params.shape[-1])
    norms = jnp.pad(norms, [(0, 0), (0, 16 - norms.shape[1]), (0, -norms.shape[2] % 128)])
    sources = [mats, turned(attention_out), feed_up, turned(feed_down), entity_proj[None], head_proj[None]]
    heights = [part.shape[1] for part in sources]
    shards = [padded_rows(part.astype(jnp.bfloat16)) for part in sources]
    shards.append(norms.astype(jnp.bfloat16))
    chunks = [(4, 0, 1, True), (5, 0, 1, False), (6, 0, 1, True)]
    for layer in range(LAYERS):
        chunks += [(0, 6 * layer, 3, True), (0, 6 * layer + 3, 3, False)]
        chunks += [(1, layer, 1, layer == 0), (2, layer, 1, True), (3, layer, 1, False)]
    wholes = gather_weights(dims, shards, chunks, 1)
    flat = []
    for part, height in zip(wholes, heights):
        kept = part[..., :height, :]
        flat.append(kept.reshape(part.shape[0], -1, part.shape[-1]))
    norm_width = norm_params.shape[-1]
    norm_all = wholes[6][0].reshape(-1, 16, wholes[6].shape[-1])[:, : LAYERS * 4, :norm_width]
    norm_all = jnp.swapaxes(norm_all, 0, 1).reshape(LAYERS, 4, -1)
    return (
        flat[0].reshape(LAYERS, 6, *flat[0].shape[1:]),
        flat[1],
        flat[2],
        flat[3],
        norm_all,
        flat[4][0],
        flat[5][0],
    )


def sum_all(dims, layer_grads, grad_proj, grad_head):
    n_dp = dims[0] * dims[1] * dims[2]

    def blocks(values):
        cut = values.astype(jnp.bfloat16).reshape(*dims, values.shape[0] // n_dp, values.shape[1])
        return padded_rows(cut)

    parts, flags, heights = [], [], []
    for layer in reversed(range(LAYERS)):
        (words_mat, ents_mat, shared_mat), out_mat, up_mat, down_mat, _ = layer_grads[layer]
        late = layer % 2 == 0
        for values, y_first in (
            (up_mat, True),
            (down_mat, False),
            (words_mat, True),
            (ents_mat, False),
            (shared_mat, late),
            (out_mat, not late),
        ):
            parts.append(blocks(values))
            flags.append(y_first)
            heights.append(values.shape[0] // n_dp)
    for values, y_first in ((grad_proj, True), (grad_head, False)):
        parts.append(blocks(values))
        flags.append(y_first)
        heights.append(values.shape[0] // n_dp)
    norms = jnp.concatenate([layer_grads[layer][4] for layer in range(LAYERS)], axis=0)
    width = norms.shape[1] // n_dp
    norms = jnp.swapaxes(norms.reshape(norms.shape[0], n_dp, width), 0, 1)
    norms = jnp.pad(norms, [(0, 0), (0, 16 - norms.shape[1]), (0, -width % 128)])
    parts.append(norms.astype(jnp.bfloat16).reshape(*dims, *norms.shape[1:]))
    flags.append(True)
    totals = sum_gradients(dims, parts, flags, 2)
    norm_sum = totals[-1][: LAYERS * 4, :width].reshape(LAYERS, 4, width)
    totals = [total[:height] for total, height in zip(totals, heights)]
    attn, outs, ups, downs = [], [], [], []
    for layer in range(LAYERS):
        at = 6 * (LAYERS - 1 - layer)
        ups.append(totals[at])
        downs.append(totals[at + 1].T)
        for part in totals[at + 2 : at + 5]:
            half = part.shape[1] // 2
            attn += [part[:, :half], part[:, half:]]
        outs.append(totals[at + 5].T)
    attn = jnp.stack(attn)
    return (
        attn.reshape(LAYERS, 6, *attn.shape[1:]),
        jnp.stack(outs),
        jnp.stack(ups),
        jnp.stack(downs),
        norm_sum,
        totals[-2],
        totals[-1],
    )


def on_device(
    word_inputs,
    entity_base,
    entity_ids,
    buckets,
    mask_positions,
    targets,
    word_cotangent,
    attention_in,
    attention_in_first,
    attention_in_second,
    attention_out,
    attention_out_first,
    attention_out_second,
    feed_up,
    feed_up_first,
    feed_up_second,
    feed_down,
    feed_down_first,
    feed_down_second,
    norm_params,
    norm_params_first,
    norm_params_second,
    entity_proj,
    entity_proj_first,
    entity_proj_second,
    head_proj,
    head_proj_first,
    head_proj_second,
    entity_table,
    entity_table_first,
    entity_table_second,
):
    dims = chip_grid(lax.axis_size("dp"))
    attn_low, out_low, up_low, down_low, norm_low, proj_low, head_low = gather_all(
        dims, attention_in, attention_out, feed_up, feed_down, norm_params, entity_proj, head_proj
    )
    gain_all = norm_low.astype(jnp.float32)
    slot_total = entity_ids.shape[0]
    shard_rows = entity_table.shape[0]
    bucket_rows = buckets.reshape(buckets.shape[2], buckets.shape[3])
    filled = bucket_rows >= 0
    safe_slot = jnp.maximum(bucket_rows, 0)
    request = jnp.where(filled, entity_ids[safe_slot] % shard_rows, -1)
    received = lax.all_to_all(request, "dp", split_axis=0, concat_axis=0, tiled=True)
    shard_base = lax.axis_index(("dp", "mp")) * shard_rows
    owned_mask = received >= 0
    safe_row = jnp.clip(received, 0, shard_rows - 1)
    table_low = entity_table.astype(jnp.bfloat16)
    replies = jnp.where(owned_mask[:, :, None], table_low[safe_row], jnp.zeros((), jnp.bfloat16))
    replied_rows_result = lax.all_to_all(replies, "dp", split_axis=0, concat_axis=0, tiled=True)
    row_placement_plan = (
        bucket_rows[:, :, None] == jnp.arange(slot_total, dtype=jnp.int32)[None, None, :]
    ).astype(jnp.bfloat16)
    local_shard_rows = jnp.einsum(
        "wvt,wvi->ti", row_placement_plan, replied_rows_result, preferred_element_type=jnp.float32
    )
    paired = pair_sum(local_shard_rows)
    masked_slots = (
        jnp.arange(SEQ_DEV, dtype=jnp.int32)[:, None] * ENT_LEN + mask_positions
    ).reshape(-1)
    keep_weight = 1.0 - jnp.any(
        jnp.arange(slot_total, dtype=jnp.int32)[:, None] == masked_slots[None, :], axis=1
    ).astype(jnp.float32)
    entity_rows = (paired * keep_weight[:, None]).astype(jnp.bfloat16)
    entity_inputs = entity_base.astype(jnp.float32) + jnp.dot(
        entity_rows, proj_low, preferred_element_type=jnp.float32
    )
    hidden = jnp.concatenate(
        [
            word_inputs.astype(jnp.float32).reshape(SEQ_DEV, WORDS, D),
            entity_inputs.reshape(SEQ_DEV, ENT_LEN, D),
        ],
        axis=1,
    )
    saved_layers = []
    for layer_index in range(LAYERS):
        hidden, saved_acts = layer_forward(
            hidden,
            attn_low[layer_index],
            out_low[layer_index],
            up_low[layer_index],
            down_low[layer_index],
            gain_all[layer_index],
        )
        saved_layers.append(saved_acts)
    seq_index = jnp.arange(SEQ_DEV, dtype=jnp.int32)[:, None]
    masked_rows = WORDS + mask_positions
    masked_low = hidden[seq_index, masked_rows].reshape(SEQ_DEV * MASK_ENT, D).astype(jnp.bfloat16)
    head_pre = jnp.dot(masked_low, head_low, preferred_element_type=jnp.float32)
    states_low = gelu_exact(head_pre).astype(jnp.bfloat16)
    all_states = spread(states_low, False, False, 3).reshape(-1, states_low.shape[1])
    logits = lax.dot_general(
        all_states, table_low, (((1,), (1,)), ((), ())), preferred_element_type=jnp.float32
    )
    flat_targets = targets.reshape(-1)
    target_hits = (
        jnp.arange(shard_rows, dtype=jnp.int32)[None, :] == (flat_targets - shard_base)[:, None]
    )
    peak_value = jnp.max(logits, axis=1)
    exp_total = jnp.sum(jnp.exp(logits - peak_value[:, None]), axis=1)
    picked = jnp.sum(jnp.where(target_hits, logits, 0.0), axis=1)
    shares = spread(jnp.stack([peak_value, exp_total, picked]), True, False, 4)
    peak_all = jnp.max(shares[:, 0], axis=0)
    total_all = jnp.sum(shares[:, 1] * jnp.exp(shares[:, 0] - peak_all), axis=0)
    picked_all = jnp.sum(shares[:, 2], axis=0)
    log_norm = peak_all + jnp.log(total_all)
    row_losses = log_norm - picked_all
    prob_rows = jnp.exp(logits - log_norm[:, None])
    grad_logits = ((prob_rows - target_hits.astype(jnp.float32)) / flat_targets.shape[0]).astype(
        jnp.bfloat16
    )
    grad_table = lax.dot_general(
        grad_logits, all_states, (((0,), (0,)), ((), ())), preferred_element_type=jnp.float32
    )
    grad_states = jnp.dot(grad_logits, table_low, preferred_element_type=jnp.float32)
    grad_states = grad_states.reshape(lax.axis_size("dp"), -1, grad_states.shape[1])
    grad_states = jnp.sum(spread(grad_states, False, True, 5), axis=0)
    grad_states = grad_states + lax.ppermute(grad_states, "mp", [(0, 1), (1, 0)])
    grad_head_pre = jax.vjp(gelu_exact, head_pre)[1](grad_states)[0].astype(jnp.bfloat16)
    grad_head = lax.dot_general(
        masked_low, grad_head_pre, (((0,), (0,)), ((), ())), preferred_element_type=jnp.float32
    )
    grad_masked = lax.dot_general(
        grad_head_pre, head_low, (((1,), (1,)), ((), ())), preferred_element_type=jnp.float32
    )
    grad_hidden = jnp.concatenate(
        [
            word_cotangent.astype(jnp.float32).reshape(SEQ_DEV, WORDS, D),
            jnp.zeros((SEQ_DEV, ENT_LEN, D), jnp.float32),
        ],
        axis=1,
    )
    grad_hidden = grad_hidden.at[seq_index, masked_rows].add(
        grad_masked.reshape(SEQ_DEV, MASK_ENT, D)
    )
    kept_grads = []
    for layer_index in reversed(range(LAYERS)):
        grad_hidden, layer_grads = layer_backward(
            grad_hidden,
            saved_layers[layer_index],
            attn_low[layer_index],
            out_low[layer_index],
            up_low[layer_index],
            down_low[layer_index],
            gain_all[layer_index],
        )
        if layer_index == 0:
            word_grads = grad_hidden[:, :WORDS].reshape(SEQ_DEV * WORDS, D)
            grad_entity = grad_hidden[:, WORDS:].reshape(slot_total, D).astype(jnp.bfloat16)
            grad_proj = lax.dot_general(
                entity_rows,
                grad_entity,
                (((0,), (0,)), ((), ())),
                preferred_element_type=jnp.float32,
            )
            row_gradient_block = (
                lax.dot_general(
                    grad_entity,
                    proj_low,
                    (((1,), (1,)), ((), ())),
                    preferred_element_type=jnp.float32,
                )
                * keep_weight[:, None]
            )
            outgoing = jnp.where(filled[:, :, None], row_gradient_block[safe_slot], 0.0)
            incoming = lax.all_to_all(
                outgoing.astype(jnp.bfloat16), "dp", split_axis=0, concat_axis=0, tiled=True
            ).astype(outgoing.dtype)
            grad_table = grad_table.at[safe_row].add(
                jnp.where(owned_mask[:, :, None], incoming, 0.0)
            )
        kept_grads.insert(0, layer_grads)
    reduced = sum_all(dims, kept_grads, grad_proj, grad_head)
    reduced_proj, reduced_head = reduced[5:]
    attn_new = adam_update(
        attention_in, attention_in_first, attention_in_second, reduced[0], kind_rates[0]
    )
    out_new = adam_update(
        attention_out, attention_out_first, attention_out_second, reduced[1], kind_rates[1]
    )
    up_new = adam_update(feed_up, feed_up_first, feed_up_second, reduced[2], kind_rates[2])
    down_new = adam_update(feed_down, feed_down_first, feed_down_second, reduced[3], kind_rates[3])
    norm_new = adam_update(
        norm_params, norm_params_first, norm_params_second, reduced[4], kind_rates[4]
    )
    proj_new = adam_update(
        entity_proj, entity_proj_first, entity_proj_second, reduced_proj, kind_rates[5]
    )
    head_new = adam_update(
        head_proj, head_proj_first, head_proj_second, reduced_head, kind_rates[6]
    )
    table_new = adam_update(
        entity_table, entity_table_first, entity_table_second, grad_table, kind_rates[7]
    )
    return (
        row_losses,
        word_grads,
        attn_new[0],
        attn_new[1],
        attn_new[2],
        out_new[0],
        out_new[1],
        out_new[2],
        up_new[0],
        up_new[1],
        up_new[2],
        down_new[0],
        down_new[1],
        down_new[2],
        norm_new[0],
        norm_new[1],
        norm_new[2],
        proj_new[0],
        proj_new[1],
        proj_new[2],
        head_new[0],
        head_new[1],
        head_new[2],
        table_new[0],
        table_new[1],
        table_new[2],
    )


def solution(mesh):
    in_specs = (
        P("dp", None),
        P("dp", None),
        P("dp"),
        P("dp", "mp", None, None),
        P("dp", None),
        P(),
        P("dp", None),
        P(None, None, "dp", "mp"),
        P(None, None, "dp", "mp"),
        P(None, None, "dp", "mp"),
        P(None, "mp", "dp"),
        P(None, "mp", "dp"),
        P(None, "mp", "dp"),
        P(None, "dp", "mp"),
        P(None, "dp", "mp"),
        P(None, "dp", "mp"),
        P(None, "mp", "dp"),
        P(None, "mp", "dp"),
        P(None, "mp", "dp"),
        P(None, None, "dp"),
        P(None, None, "dp"),
        P(None, None, "dp"),
        P("dp", None),
        P("dp", None),
        P("dp", None),
        P("dp", None),
        P("dp", None),
        P("dp", None),
        P(("dp", "mp"), None),
        P(("dp", "mp"), None),
        P(("dp", "mp"), None),
    )
    out_specs = (
        P(),
        P("dp", None),
        P(None, None, "dp", "mp"),
        P(None, None, "dp", "mp"),
        P(None, None, "dp", "mp"),
        P(None, "mp", "dp"),
        P(None, "mp", "dp"),
        P(None, "mp", "dp"),
        P(None, "dp", "mp"),
        P(None, "dp", "mp"),
        P(None, "dp", "mp"),
        P(None, "mp", "dp"),
        P(None, "mp", "dp"),
        P(None, "mp", "dp"),
        P(None, None, "dp"),
        P(None, None, "dp"),
        P(None, None, "dp"),
        P("dp", None),
        P("dp", None),
        P("dp", None),
        P("dp", None),
        P("dp", None),
        P("dp", None),
        P(("dp", "mp"), None),
        P(("dp", "mp"), None),
        P(("dp", "mp"), None),
    )
    return jax.shard_map(
        on_device, mesh=mesh, in_specs=in_specs, out_specs=out_specs, check_vma=False
    )
```

```python
import functools

import jax
import jax.numpy as jnp
from jax import lax
from jax.experimental import pallas as pl
from jax.experimental.pallas import tpu as pltpu
from jax.sharding import PartitionSpec as P

D = 768
HEAD_DIM = 64
WORDS = 896
ENT_LEN = 128
MASK_ENT = 16
LAYERS = 2
STEP = 10
SEQ_DEV = 1


norm_eps = 1e-05
beta_first = 0.9
beta_second = 0.999
adam_eps = 1e-12
weight_decay = 0.01
kind_rates = (0.05, 1.0, 0.05, 0.027, 0.75, 0.5, 0.05, 0.2)


MESH = pl.DeviceIdType.MESH
ANY = pl.BlockSpec(memory_space=pl.ANY)
VMEM = pl.BlockSpec(memory_space=pltpu.VMEM)
VMEM_BYTES = 60 * 2**20


def chip_grid(n_dp):
    return {16: (4, 2, 2), 64: (4, 4, 4)}.get(n_dp, (n_dp, 1, 1))


def place(dims):
    index = lax.axis_index("dp")
    return index // (dims[1] * dims[2]), index // dims[2] % dims[1], index % dims[2]


def axis_peers(dims, axis):
    here = place(dims)
    core = lax.axis_index("mp")
    peers = []
    for step in range(1, dims[axis]):
        spot = list(here)
        spot[axis] = lax.rem(here[axis] + step, dims[axis])
        peers.append((spot[axis], (spot[0] * dims[1] * dims[2] + spot[1] * dims[2] + spot[2], core)))
    return peers


def greet(targets):
    barrier = pltpu.get_barrier_semaphore()
    for target in targets:
        pl.semaphore_signal(barrier, inc=1, device_id=target, device_id_type=MESH)
    pl.semaphore_wait(barrier, len(targets))


def send(src, dst, send_sem, recv_sem, target):
    copy = pltpu.make_async_remote_copy(
        src_ref=src,
        dst_ref=dst,
        send_sem=send_sem,
        recv_sem=recv_sem,
        device_id=target,
        device_id_type=MESH,
    )
    copy.start()
    return copy


def gather_body(dims, chunks, count, *refs):
    shards, wholes = refs[:count], refs[count : 2 * count]
    send_sem, recv_sem, local_sem = refs[2 * count :]
    z, y, x = place(dims)
    peers = [axis_peers(dims, axis) for axis in range(3)]
    greet([target for group in peers for _, target in group])
    pending = {}

    def start(stage, c):
        which, first, size, y_first = chunks[c]
        rows = pl.ds(first, size)
        whole = wholes[which]
        copies = []
        if stage == 0:
            src, dst, group = shards[which].at[rows], whole.at[rows, z, y, x], peers[0]
            own = pltpu.make_async_copy(src, dst, local_sem.at[c])
            own.start()
            copies.append(own)
        elif stage == 1:
            src = whole.at[rows, :, y, x]
            dst, group = src, peers[1 if y_first else 2]
        else:
            src = whole.at[rows, :, :, x] if y_first else whole.at[rows, :, y]
            dst, group = src, peers[2 if y_first else 1]
        base = (0, dims[0], dims[0] + max(dims[1:]))[stage]
        for slot, (_, target) in enumerate(group):
            copies.append(
                send(src, dst, send_sem.at[c, base + slot], recv_sem.at[c, base + slot], target)
            )
        pending[stage, c] = copies

    def finish(stage, c):
        for copy in pending.pop((stage, c)):
            copy.wait()

    total = len(chunks)
    start(0, 0)
    for step in range(total + 2):
        if step + 1 < total:
            start(0, step + 1)
        if step < total:
            finish(0, step)
            start(1, step)
        if 0 <= step - 1 < total:
            finish(1, step - 1)
            start(2, step - 1)
        if 0 <= step - 2 < total:
            finish(2, step - 2)


def gather_weights(dims, shards, chunks, collective_id):
    count = len(shards)
    copies = dims[0] + 2 * max(dims[1:])
    return pl.pallas_call(
        functools.partial(gather_body, dims, chunks, count),
        out_shape=[
            jax.ShapeDtypeStruct((s.shape[0], *dims, *s.shape[1:]), s.dtype) for s in shards
        ],
        in_specs=[ANY] * count,
        out_specs=[ANY] * count,
        scratch_shapes=[
            pltpu.SemaphoreType.DMA((len(chunks), copies)),
            pltpu.SemaphoreType.DMA((len(chunks), copies)),
            pltpu.SemaphoreType.DMA((len(chunks),)),
        ],
        compiler_params=pltpu.CompilerParams(
            collective_id=collective_id, has_side_effects=True, vmem_limit_bytes=2**20
        ),
    )(*shards)


def sum_body(dims, flags, *refs):
    count = len(flags)
    parts, totals = refs[:count], refs[count : 2 * count]
    buffers = refs[2 * count : 6 * count]
    send_sem, recv_sem, local_sem = refs[6 * count :]
    z, y, x = place(dims)
    peers = [axis_peers(dims, axis) for axis in range(3)]
    greet([target for group in peers for _, target in group])
    pending = {}

    def start(stage, c):
        y_first = flags[c]
        own, first, second, third = buffers[4 * c : 4 * c + 4]
        copies = []
        base = (0, max(dims[1:]), 2 * max(dims[1:]))[stage]
        if stage == 0:
            mine = parts[c].at[:, y] if y_first else parts[c].at[:, :, x]
            local = pltpu.make_async_copy(mine, own, local_sem.at[c])
            local.start()
            copies.append(local)
        group = peers[((1, 2, 0) if y_first else (2, 1, 0))[stage]]
        for slot, (spot, target) in enumerate(group):
            if stage == 0:
                src = parts[c].at[:, spot] if y_first else parts[c].at[:, :, spot]
                dst = first.at[slot]
            elif stage == 1:
                src, dst = own.at[:, spot], second.at[slot]
            else:
                src, dst = own.at[spot, x if y_first else y], third.at[slot]
            copies.append(
                send(src, dst, send_sem.at[c, base + slot], recv_sem.at[c, base + slot], target)
            )
        pending[stage, c] = copies

    def finish(stage, c):
        y_first = flags[c]
        own, first, second, third = buffers[4 * c : 4 * c + 4]
        for copy in pending.pop((stage, c)):
            copy.wait()
        across = dims[2] if y_first else dims[1]
        line = x if y_first else y
        count_peers = len(peers[((1, 2, 0) if y_first else (2, 1, 0))[stage]])
        if stage == 0 and count_peers:

            def add_first(i, carry):
                value = own[i // across, i % across].astype(jnp.float32)
                for slot in range(count_peers):
                    value += first[slot, i // across, i % across].astype(jnp.float32)
                own[i // across, i % across] = value.astype(own.dtype)
                return carry

            lax.fori_loop(0, dims[0] * across, add_first, 0)
        if stage == 1 and count_peers:

            def add_second(i, carry):
                value = own[i, line].astype(jnp.float32)
                for slot in range(count_peers):
                    value += second[slot, i].astype(jnp.float32)
                own[i, line] = value.astype(own.dtype)
                return carry

            lax.fori_loop(0, dims[0], add_second, 0)
        if stage == 2:
            value = own[z, line].astype(jnp.float32)
            for slot in range(count_peers):
                value += third[slot].astype(jnp.float32)
            totals[c][...] = value

    total = len(flags)
    ahead = 2
    for c in range(min(ahead, total)):
        start(0, c)
    for step in range(total + 2 * ahead):
        if step + ahead < total:
            start(0, step + ahead)
        if step < total:
            finish(0, step)
            start(1, step)
        if 0 <= step - ahead < total:
            finish(1, step - ahead)
            start(2, step - ahead)
        if 0 <= step - 2 * ahead < total:
            finish(2, step - 2 * ahead)


def sum_gradients(dims, parts, flags, collective_id):
    count = len(parts)
    scratch = []
    for part, y_first in zip(parts, flags):
        block = part.shape[3:]
        own = (dims[0], dims[2] if y_first else dims[1])
        turns = (dims[1], dims[2]) if y_first else (dims[2], dims[1])
        scratch += [
            pltpu.VMEM((*own, *block), part.dtype),
            pltpu.VMEM((max(turns[0] - 1, 1), *own, *block), part.dtype),
            pltpu.VMEM((max(turns[1] - 1, 1), dims[0], *block), part.dtype),
            pltpu.VMEM((max(dims[0] - 1, 1), *block), part.dtype),
        ]
    copies = dims[0] + 2 * max(dims[1:])
    return pl.pallas_call(
        functools.partial(sum_body, dims, flags),
        out_shape=[jax.ShapeDtypeStruct(part.shape[3:], jnp.float32) for part in parts],
        in_specs=[ANY] * count,
        out_specs=[VMEM] * count,
        scratch_shapes=scratch
        + [
            pltpu.SemaphoreType.DMA((count, copies)),
            pltpu.SemaphoreType.DMA((count, copies)),
            pltpu.SemaphoreType.DMA((count,)),
        ],
        compiler_params=pltpu.CompilerParams(
            collective_id=collective_id, has_side_effects=True, vmem_limit_bytes=VMEM_BYTES
        ),
    )(*parts)


def spread_body(count, wide, swap, data, result, send_sem, recv_sem, local_sem):
    pair = lax.axis_size("mp")
    index = lax.axis_index("dp") * pair + lax.axis_index("mp") if wide else lax.axis_index("dp")

    def target_of(step):
        other = lax.rem(index + step, count)
        if wide:
            return other, (other // pair, lax.rem(other, pair))
        return other, (other, lax.axis_index("mp"))

    barrier = pltpu.get_barrier_semaphore()

    def hello(step, carry):
        pl.semaphore_signal(barrier, inc=1, device_id=target_of(step)[1], device_id_type=MESH)
        return carry

    lax.fori_loop(1, count, hello, 0)
    pl.semaphore_wait(barrier, count - 1)
    own = pltpu.make_async_copy(data.at[index if swap else 0], result.at[index], local_sem)
    own.start()

    def copy_of(step):
        other, target = target_of(step)
        return pltpu.make_async_remote_copy(
            src_ref=data.at[other if swap else 0],
            dst_ref=result.at[index],
            send_sem=send_sem.at[step],
            recv_sem=recv_sem.at[step],
            device_id=target,
            device_id_type=MESH,
        )

    def go(step, carry):
        copy_of(step).start()
        return carry

    def done(step, carry):
        copy_of(step).wait()
        return carry

    lax.fori_loop(1, count, go, 0)
    own.wait()
    lax.fori_loop(1, count, done, 0)


def spread(data, wide, swap, collective_id):
    count = lax.axis_size("dp") * (lax.axis_size("mp") if wide else 1)
    block = data.shape[1:] if swap else data.shape
    return pl.pallas_call(
        functools.partial(spread_body, count, wide, swap),
        out_shape=jax.ShapeDtypeStruct((count, *block), data.dtype),
        in_specs=[VMEM],
        out_specs=VMEM,
        scratch_shapes=[
            pltpu.SemaphoreType.DMA((count,)),
            pltpu.SemaphoreType.DMA((count,)),
            pltpu.SemaphoreType.DMA,
        ],
        compiler_params=pltpu.CompilerParams(
            collective_id=collective_id, has_side_effects=True, vmem_limit_bytes=VMEM_BYTES
        ),
    )(data if swap else data[None])


def layer_norm(values, gain_row, shift_row):
    centered = values - jnp.mean(values, axis=-1, keepdims=True)
    spread = jnp.mean(centered * centered, axis=-1, keepdims=True)
    return centered * lax.rsqrt(spread + norm_eps) * gain_row + shift_row


def gelu_exact(values):
    return jax.nn.gelu(values, approximate=False)


def adam_update(master, first_moment, second_moment, gradient, kind_rate):
    first_new = beta_first * first_moment + (1.0 - beta_first) * gradient
    second_new = beta_second * second_moment + (1.0 - beta_second) * gradient * gradient
    first_hat = first_new / (1.0 - beta_first**STEP)
    second_hat = second_new / (1.0 - beta_second**STEP)
    master_new = master - kind_rate * (
        first_hat / (jnp.sqrt(second_hat) + adam_eps) + weight_decay * master
    )
    return (first_new, second_new, master_new)


def project(fetched_row_values, weight_matrix_entry):
    return jnp.einsum(
        "mvw,wu->mvu", fetched_row_values, weight_matrix_entry, preferred_element_type=jnp.float32
    )


def project_back(row_gradient_block, weight_matrix_entry):
    return jnp.einsum(
        "tic,vc->tiv", row_gradient_block, weight_matrix_entry, preferred_element_type=jnp.float32
    )


def project_turned(rows, turned):
    return jnp.einsum("mvw,uw->mvu", rows, turned, preferred_element_type=jnp.float32)


def project_back_turned(row_gradient_block, turned):
    return jnp.einsum("tic,cv->tiv", row_gradient_block, turned, preferred_element_type=jnp.float32)


def weight_grad(layer_input_list, row_gradient_block):
    return jnp.einsum(
        "hmq,hmw->qw", layer_input_list, row_gradient_block, preferred_element_type=jnp.float32
    ).astype(jnp.bfloat16)


def split_heads(values):
    return values.reshape(values.shape[0], values.shape[1], values.shape[2] // HEAD_DIM, HEAD_DIM)


def pair_sum(partial_sum):
    mine = partial_sum.astype(jnp.bfloat16)
    theirs = lax.ppermute(mine, "mp", [(0, 1), (1, 0)])
    return mine.astype(jnp.float32) + theirs.astype(jnp.float32)


merge_heads = merge_inputs = pair_sum


def seq_scores(query_word, query_entity, key_rows):
    score_word = jnp.einsum(
        "qhd,khd->hqk", query_word, key_rows[:WORDS], preferred_element_type=jnp.float32
    )
    score_entity = jnp.einsum(
        "qhd,khd->hqk", query_entity, key_rows[WORDS:], preferred_element_type=jnp.float32
    )
    return jnp.concatenate([score_word, score_entity], axis=-1) * 0.125


def attend_forward(seq_item):
    query_word, query_entity, key_rows, value_rows = seq_item
    scores = seq_scores(query_word, query_entity, key_rows)
    peak_value = jnp.max(scores, axis=-1, keepdims=True)
    exp_scores = jnp.exp(scores - peak_value)
    exp_total = jnp.sum(exp_scores, axis=-1, keepdims=True)
    prob_low = (exp_scores / exp_total).astype(jnp.bfloat16)
    mixed_heads = jnp.einsum(
        "hqk,khd->qhd", prob_low, value_rows, preferred_element_type=jnp.float32
    )
    return (mixed_heads, (peak_value + jnp.log(exp_total))[..., 0])


def attend_backward(seq_item):
    query_word, query_entity, key_rows, value_rows, log_norm, grad_mixed = seq_item
    scores = seq_scores(query_word, query_entity, key_rows)
    prob_rows = jnp.exp(scores - log_norm[..., None])
    grad_value = jnp.einsum(
        "hqk,qhd->khd",
        prob_rows.astype(jnp.bfloat16),
        grad_mixed,
        preferred_element_type=jnp.float32,
    )
    grad_probs = jnp.einsum(
        "qhd,khd->hqk", grad_mixed, value_rows, preferred_element_type=jnp.float32
    )
    inner_sum = jnp.sum(prob_rows * grad_probs, axis=-1, keepdims=True)
    grad_scores = (prob_rows * (grad_probs - inner_sum) * 0.125).astype(jnp.bfloat16)
    score_word = grad_scores[..., :WORDS]
    score_entity = grad_scores[..., WORDS:]
    grad_qw = jnp.einsum(
        "hqk,khd->qhd", score_word, key_rows[:WORDS], preferred_element_type=jnp.float32
    )
    grad_qe = jnp.einsum(
        "hqk,khd->qhd", score_entity, key_rows[WORDS:], preferred_element_type=jnp.float32
    )
    grad_key = jnp.concatenate(
        [
            jnp.einsum("hqk,qhd->khd", score_word, query_word, preferred_element_type=jnp.float32),
            jnp.einsum(
                "hqk,qhd->khd", score_entity, query_entity, preferred_element_type=jnp.float32
            ),
        ],
        axis=0,
    )
    return (grad_qw, grad_qe, grad_key, grad_value)


def layer_forward(hidden, attn_mats, out_mat, up_mat, down_mat, gain_rows):
    hidden_low = hidden.astype(jnp.bfloat16)
    words_low = hidden_low[:, :WORDS]
    ents_low = hidden_low[:, WORDS:]
    query_word = jnp.concatenate(
        [project(words_low, attn_mats[0]), project(ents_low, attn_mats[2])], axis=1
    ).astype(jnp.bfloat16)
    query_entity = jnp.concatenate(
        [project(words_low, attn_mats[1]), project(ents_low, attn_mats[3])], axis=1
    ).astype(jnp.bfloat16)
    key_rows = project(hidden_low, attn_mats[4]).astype(jnp.bfloat16)
    value_rows = project(hidden_low, attn_mats[5]).astype(jnp.bfloat16)
    mixed_heads, log_norm = lax.map(
        attend_forward,
        (
            split_heads(query_word),
            split_heads(query_entity),
            split_heads(key_rows),
            split_heads(value_rows),
        ),
    )
    mixed_low = mixed_heads.reshape(key_rows.shape).astype(jnp.bfloat16)
    attended = merge_heads(project_turned(mixed_low, out_mat))
    first_out = layer_norm(hidden + attended, gain_rows[0], gain_rows[1])
    first_low = first_out.astype(jnp.bfloat16)
    inner_pre = project(first_low, up_mat)
    inner_low = gelu_exact(inner_pre).astype(jnp.bfloat16)
    outer_out = merge_heads(project_turned(inner_low, down_mat))
    result = layer_norm(first_out + outer_out, gain_rows[2], gain_rows[3])
    saved_acts = (
        hidden,
        hidden_low,
        query_word,
        query_entity,
        key_rows,
        value_rows,
        log_norm,
        mixed_low,
        attended,
        first_out,
        first_low,
        inner_pre,
        inner_low,
        outer_out,
    )
    return (result, saved_acts)


def layer_backward(grad_out, saved_acts, attn_mats, out_mat, up_mat, down_mat, gain_rows):
    (
        hidden,
        hidden_low,
        query_word,
        query_entity,
        key_rows,
        value_rows,
        log_norm,
        mixed_low,
        attended,
        first_out,
        first_low,
        inner_pre,
        inner_low,
        outer_out,
    ) = saved_acts
    second_back = jax.vjp(layer_norm, first_out + outer_out, gain_rows[2], gain_rows[3])[1]
    grad_second, grad_gain_late, grad_shift_late = second_back(grad_out)
    grad_outer = grad_second.astype(jnp.bfloat16)
    grad_down = weight_grad(grad_outer, inner_low)
    grad_inner = project_back_turned(grad_outer, down_mat)
    grad_pre = jax.vjp(gelu_exact, inner_pre)[1](grad_inner)[0].astype(jnp.bfloat16)
    grad_up = weight_grad(first_low, grad_pre)
    grad_first = grad_second + merge_inputs(project_back(grad_pre, up_mat))
    first_back = jax.vjp(layer_norm, hidden + attended, gain_rows[0], gain_rows[1])[1]
    grad_first_in, grad_gain_early, grad_shift_early = first_back(grad_first)
    grad_attended = grad_first_in.astype(jnp.bfloat16)
    grad_out_mat = weight_grad(grad_attended, mixed_low)
    grad_mixed = project_back_turned(grad_attended, out_mat).astype(jnp.bfloat16)
    grad_qw, grad_qe, grad_key, grad_value = lax.map(
        attend_backward,
        (
            split_heads(query_word),
            split_heads(query_entity),
            split_heads(key_rows),
            split_heads(value_rows),
            log_norm,
            split_heads(grad_mixed),
        ),
    )
    flat_shape = key_rows.shape
    grad_qw = grad_qw.reshape(flat_shape).astype(jnp.bfloat16)
    grad_qe = grad_qe.reshape(flat_shape).astype(jnp.bfloat16)
    grad_key = grad_key.reshape(flat_shape).astype(jnp.bfloat16)
    grad_value = grad_value.reshape(flat_shape).astype(jnp.bfloat16)
    words_low = hidden_low[:, :WORDS]
    ents_low = hidden_low[:, WORDS:]
    grad_mats = (
        weight_grad(words_low, jnp.concatenate([grad_qw[:, :WORDS], grad_qe[:, :WORDS]], axis=-1)),
        weight_grad(ents_low, jnp.concatenate([grad_qw[:, WORDS:], grad_qe[:, WORDS:]], axis=-1)),
        weight_grad(hidden_low, jnp.concatenate([grad_key, grad_value], axis=-1)),
    )
    part_words = project_back(grad_qw[:, :WORDS], attn_mats[0]) + project_back(
        grad_qe[:, :WORDS], attn_mats[1]
    )
    part_ents = project_back(grad_qw[:, WORDS:], attn_mats[2]) + project_back(
        grad_qe[:, WORDS:], attn_mats[3]
    )
    part_sum = (
        jnp.concatenate([part_words, part_ents], axis=1)
        + project_back(grad_key, attn_mats[4])
        + project_back(grad_value, attn_mats[5])
    )
    grad_hidden = grad_first_in + merge_inputs(part_sum)
    grad_norms = jnp.stack([grad_gain_early, grad_shift_early, grad_gain_late, grad_shift_late])
    return (grad_hidden, (grad_mats, grad_out_mat, grad_up, grad_down, grad_norms))


LOG2E = 1.4426950408889634
SCORE_STEP = 0.125 * LOG2E
LEN = WORDS + ENT_LEN
BLOCK = 256
BLOCKS = LEN // BLOCK


def mm(left, right):
    return lax.dot_general(
        left, right, (((1,), (0,)), ((), ())), preferred_element_type=jnp.float32
    )


def mm_rt(left, right):
    return lax.dot_general(
        left, right, (((1,), (1,)), ((), ())), preferred_element_type=jnp.float32
    )


def mm_lt(left, right):
    return lax.dot_general(
        left, right, (((0,), (0,)), ((), ())), preferred_element_type=jnp.float32
    )


def flat(ref, *index):
    value = ref[index] if index else ref[...]
    return value.reshape(-1, value.shape[-1])


def lane_mask(rows, which):
    lane = lax.broadcasted_iota(jnp.int32, (rows, 2 * HEAD_DIM), 1)
    return (lane // HEAD_DIM == which).astype(jnp.bfloat16)


def normed(values):
    centered = values - jnp.mean(values, axis=-1, keepdims=True)
    spread_row = jnp.mean(centered * centered, axis=-1, keepdims=True)
    scale = lax.rsqrt(spread_row + norm_eps)
    return centered * scale, scale


def gelu_parts(values):
    cdf = 0.5 * (1.0 + lax.erf(values * 0.7071067811865476))
    bell = jnp.exp2(values * values * (-0.5 * LOG2E)) * 0.3989422804014327
    return values * cdf, cdf + values * bell


class Gather:
    def __init__(self, dims, chunks, shards, wholes, kept, sems, lags=(3, 2, 2)):
        self.dims, self.chunks, self.shards, self.wholes, self.kept = dims, chunks, shards, wholes, kept
        self.send_sem, self.recv_sem, self.local_sem, self.keep_sem = sems
        self.spot = place(dims)
        self.peers = [axis_peers(dims, axis) for axis in range(3)]
        self.pending, self.step = {}, 0
        self.ahead, self.lag1, self.lag2 = lags

    def targets(self):
        return [target for group in self.peers for _, target in group]

    def start(self, stage, c):
        which, rows, cols, y_first = self.chunks[c]
        z, y, x = self.spot
        whole = self.wholes[which].at[rows, :, :, :, :, cols]
        shard = self.shards[which].at[rows, :, cols]
        copies = []
        if stage == 0:
            own = pltpu.make_async_copy(shard, whole.at[:, z, y, x], self.local_sem.at[c])
            own.start()
            copies.append(own)
            src, dst, group = shard, whole.at[:, z, y, x], self.peers[0]
        elif stage == 1:
            src = whole.at[:, :, y, x]
            dst, group = src, self.peers[1 if y_first else 2]
        else:
            src = whole.at[:, :, :, x] if y_first else whole.at[:, :, y]
            dst, group = src, self.peers[2 if y_first else 1]
        base = (0, self.dims[0], self.dims[0] + max(self.dims[1:]))[stage]
        for slot, (_, target) in enumerate(group):
            sems = self.send_sem.at[c, base + slot], self.recv_sem.at[c, base + slot]
            copies.append(send(src, dst, *sems, target))
        self.pending[stage, c] = copies

    def finish(self, stage, c):
        for copy in self.pending.pop((stage, c)):
            copy.wait()
        if stage == 2:
            which, rows, cols, _ = self.chunks[c]
            keep = pltpu.make_async_copy(
                self.wholes[which].at[rows, :, :, :, :, cols],
                self.kept[which].at[rows, :, :, :, :, cols],
                self.keep_sem.at[c],
            )
            keep.start()
            self.pending[3, c] = [keep]

    def begin(self):
        for c in range(min(self.ahead, len(self.chunks))):
            self.start(0, c)

    def tick(self):
        total, step = len(self.chunks), self.step
        if step >= total + self.lag1 + self.lag2:
            return
        self.step += 1
        if step + self.ahead < total:
            self.start(0, step + self.ahead)
        if step < total:
            self.finish(0, step)
            self.start(1, step)
        late = step - self.lag1
        if 0 <= late < total:
            self.finish(1, late)
            self.start(2, late)
        late -= self.lag2
        if 0 <= late < total:
            self.finish(2, late)

    def need(self, c):
        while self.step < c + self.lag1 + self.lag2 + 1:
            self.tick()

    def close(self):
        self.need(len(self.chunks) - 1)
        for key in sorted(self.pending):
            for copy in self.pending[key]:
                copy.wait()


class Pair:
    def __init__(self, mine, theirs, sems):
        self.mine, self.theirs = mine, theirs
        self.send_sem, self.recv_sem = sems
        self.phase = 0
        self.other = (lax.axis_index("dp"), 1 - lax.axis_index("mp"))

    def copy(self, phase, c):
        return pltpu.make_async_remote_copy(
            src_ref=self.mine.at[c],
            dst_ref=self.theirs.at[phase % 2, c],
            send_sem=self.send_sem.at[phase, c],
            recv_sem=self.recv_sem.at[phase, c],
            device_id=self.other,
            device_id_type=MESH,
        )

    def run(self, compute, consume, between=None):
        phase = self.phase
        self.phase += 1

        def take(c):
            self.copy(phase, c).wait()
            total = self.mine[c].astype(jnp.float32) + self.theirs[phase % 2, c].astype(jnp.float32)
            consume(c, pl.ds(c * BLOCK, BLOCK), total)

        for c in range(BLOCKS):
            self.mine[c] = compute(c, pl.ds(c * BLOCK, BLOCK)).astype(jnp.bfloat16)
            self.copy(phase, c).start()
            if between is not None:
                between()
            if c:
                take(c - 1)
        take(BLOCKS - 1)


SAVED = ("xb", "qw", "qe", "k", "v", "o", "n1", "h1b", "slope", "g", "n2", "stats")


def saved_shapes(half, hidden):
    wide, narrow = (LEN, D), (LEN, half)
    low = jnp.bfloat16
    return {
        "xb": (wide, low),
        "qw": (narrow, low),
        "qe": (narrow, low),
        "k": (narrow, low),
        "v": (narrow, low),
        "o": (narrow, low),
        "n1": (wide, low),
        "h1b": (wide, low),
        "slope": ((LEN, hidden), low),
        "g": ((LEN, hidden), low),
        "n2": (wide, low),
        "stats": ((LEN, 128), jnp.float32),
    }


def attend(act, pair):
    lanes = slice(pair * 2 * HEAD_DIM, (pair + 1) * 2 * HEAD_DIM)

    def block(i, carry):
        rows = pl.ds(i * BLOCK, BLOCK)
        keys, values = act["k"][:, lanes], act["v"][:, lanes]
        total = None
        for which in range(2):
            q_mask, v_mask = lane_mask(BLOCK, which), lane_mask(LEN, which)
            score_w = mm_rt(act["qw"][rows, lanes] * q_mask, keys[:WORDS])
            score_e = mm_rt(act["qe"][rows, lanes] * q_mask, keys[WORDS:])
            peak = jnp.maximum(
                jnp.max(score_w, axis=-1, keepdims=True), jnp.max(score_e, axis=-1, keepdims=True)
            )
            exp_w = jnp.exp2((score_w - peak) * SCORE_STEP)
            exp_e = jnp.exp2((score_e - peak) * SCORE_STEP)
            weight = jnp.sum(exp_w, axis=-1, keepdims=True) + jnp.sum(exp_e, axis=-1, keepdims=True)
            part = values * v_mask
            mixed = mm(exp_w.astype(jnp.bfloat16), part[:WORDS])
            mixed += mm(exp_e.astype(jnp.bfloat16), part[WORDS:])
            mixed = mixed * (1.0 / weight)
            total = mixed if total is None else total + mixed
            head = 2 * pair + which
            act["stats"][rows, head : head + 1] = peak * SCORE_STEP + jnp.log2(weight)
        act["o"][rows, lanes] = total.astype(jnp.bfloat16)
        return carry

    lax.fori_loop(0, BLOCKS, block, 0)


def project_rows(out_ref, x_ref, first, size, step, weights, index):
    def block(i, carry):
        rows = pl.ds(first + i * step, step)
        out_ref[rows, :] = mm(x_ref[rows, :], flat(weights, index)).astype(jnp.bfloat16)
        return carry

    lax.fori_loop(0, size // step, block, 0)


def forward_body(dims, chunks, needs, *refs):
    refs = list(refs)

    def take(count):
        part = refs[:count]
        del refs[:count]
        return part

    words, base, rows_in = take(3)
    shards = take(len(needs["kinds"]))
    kept = take(len(needs["kinds"]))
    saved = [dict(zip(SAVED, take(len(SAVED)))) for _ in range(LAYERS)]
    (ents_out,) = take(1)
    wholes = take(len(needs["kinds"]))
    act = dict(zip(SAVED, take(len(SAVED))))
    x, h1, gains, mine, theirs = take(5)
    gather_sems = take(4)
    pair_sems = take(2)
    (save_sem,) = take(1)

    gather = Gather(dims, chunks, shards, wholes, kept, gather_sems)
    pair = Pair(mine, theirs, pair_sems)
    greet(gather.targets() + [pair.other])
    gather.begin()
    attn, outs, ups, downs, proj, _, norms = wholes
    saving = {}

    def save(layer, name):
        slot = layer * len(SAVED) + SAVED.index(name)
        copy = pltpu.make_async_copy(act[name], saved[layer][name], save_sem.at[slot])
        copy.start()
        saving[name] = copy

    def free(name):
        if name in saving:
            saving.pop(name).wait()

    x[:WORDS] = words[...].astype(jnp.float32)
    gather.need(needs["norms"])
    width = D // (dims[0] * dims[1] * dims[2])
    count = dims[0] * dims[1] * dims[2]
    gains[...] = jnp.zeros_like(gains)
    for d in range(count):
        z, rest = d // (dims[1] * dims[2]), d % (dims[1] * dims[2])
        pick = lax.broadcasted_iota(jnp.int32, (128, D), 0) + d * width
        lane = lax.broadcasted_iota(jnp.int32, (128, D), 1)
        inside = lax.broadcasted_iota(jnp.int32, (128, D), 0) < width
        hot = jnp.where((pick == lane) & inside, 1.0, 0.0).astype(jnp.bfloat16)
        gains[...] += mm(norms[0, z, rest // dims[2], rest % dims[2]], hot)
    gather.need(needs["proj"])
    x[WORDS:] = base[...].astype(jnp.float32) + mm(rows_in[...], flat(proj, 0))

    for layer in range(LAYERS):
        gain = [gains[4 * layer + i : 4 * layer + i + 1, :] for i in range(4)]
        free("xb")

        def cast(i, carry):
            rows = pl.ds(i * BLOCK, BLOCK)
            act["xb"][rows, :] = x[rows, :].astype(jnp.bfloat16)
            return carry

        lax.fori_loop(0, BLOCKS, cast, 0)
        save(layer, "xb")
        for name, word_mat, ent_mat in (("k", 4, None), ("v", 5, None), ("qw", 0, 2), ("qe", 1, 3)):
            free(name)
            gather.need(needs["mat", layer, word_mat if ent_mat is None else ent_mat])
            if ent_mat is None:
                project_rows(act[name], act["xb"], 0, LEN, 512, attn, 6 * layer + word_mat)
            else:
                project_rows(act[name], act["xb"], 0, WORDS, 448, attn, 6 * layer + word_mat)
                project_rows(act[name], act["xb"], WORDS, ENT_LEN, ENT_LEN, attn, 6 * layer + ent_mat)
            save(layer, name)
            gather.tick()
        free("o")
        free("stats")
        for head_pair in range(act["o"].shape[1] // (2 * HEAD_DIM)):
            attend(act, head_pair)
            gather.tick()
        save(layer, "o")
        gather.need(needs["out", layer])
        for name in ("n1", "h1b"):
            free(name)

        def out_part(c, rows):
            return mm_rt(act["o"][rows, :], flat(outs, layer))

        def first_norm(c, rows, total):
            hat, scale = normed(x[rows, :] + total)
            act["n1"][rows, :] = hat.astype(jnp.bfloat16)
            act["stats"][rows, 8:9] = scale
            value = hat * gain[0] + gain[1]
            h1[rows, :] = value
            act["h1b"][rows, :] = value.astype(jnp.bfloat16)

        pair.run(out_part, first_norm, gather.tick)
        save(layer, "n1")
        save(layer, "h1b")
        gather.need(needs["up", layer, 1])
        for name in ("g", "slope", "n2"):
            free(name)
        hidden = act["g"].shape[1]
        tile = 512

        def up_block(c):
            rows = pl.ds(c * BLOCK, BLOCK)
            for first in range(0, hidden, tile):
                cols = slice(first, first + tile)
                weight = ups[layer, :, :, :, :, cols].reshape(D, tile)
                value, slope = gelu_parts(mm(act["h1b"][rows, :], weight))
                act["g"][rows, cols] = value.astype(jnp.bfloat16)
                act["slope"][rows, cols] = slope.astype(jnp.bfloat16)

        for c in range(BLOCKS):
            up_block(c)
            gather.tick()
        save(layer, "g")
        save(layer, "slope")
        gather.need(needs["down", layer, 1])

        def down_part(c, rows):
            return mm_rt(act["g"][rows, :], flat(downs, layer))

        def second_norm(c, rows, total):
            hat, scale = normed(h1[rows, :] + total)
            act["n2"][rows, :] = hat.astype(jnp.bfloat16)
            act["stats"][rows, 9:10] = scale
            x[rows, :] = hat * gain[2] + gain[3]

        pair.run(down_part, second_norm, gather.tick)
        save(layer, "n2")
        save(layer, "stats")
    ents_out[...] = x[WORDS:]
    gather.close()
    for name in list(saving):
        free(name)


KINDS = ("attn", "out", "up", "down", "proj", "head", "norms")


MAT_ORDER = (4, 5, 0, 2, 1, 3)


def gather_plan(hidden):
    every = slice(None)
    chunks = [(6, pl.ds(0, 1), every, True), (4, pl.ds(0, 1), every, False)]
    needs = {"kinds": KINDS, "norms": 0, "proj": 1}
    y_first = [True]

    def add(name, which, row, cols):
        chunks.append((which, pl.ds(row, 1), cols, y_first[0]))
        y_first[0] = not y_first[0]
        needs[name] = len(chunks) - 1

    for layer in range(LAYERS):
        for mat in MAT_ORDER:
            add(("mat", layer, mat), 0, 6 * layer + mat, every)
        add(("out", layer), 1, layer, every)
        for which, name in ((2, "up"), (3, "down")):
            for part in range(2):
                add((name, layer, part), which, layer, pl.ds(part * (hidden // 2), hidden // 2))
    add("head", 5, 0, every)
    return chunks, needs


def run_forward(dims, words, base, entity_rows, shards, collective_id):
    half, hidden = shards[0].shape[-1], shards[2].shape[-1]
    chunks, needs = gather_plan(hidden)
    shapes = saved_shapes(half, hidden)
    low, full = jnp.bfloat16, jnp.float32
    wholes = [(s.shape[0], *dims, *s.shape[1:]) for s in shards]
    copies = dims[0] + 2 * max(dims[1:])
    saved_out = [jax.ShapeDtypeStruct(*shapes[name]) for _ in range(LAYERS) for name in SAVED]
    result = pl.pallas_call(
        functools.partial(forward_body, dims, chunks, needs),
        out_shape=[jax.ShapeDtypeStruct(shape, low) for shape in wholes]
        + saved_out
        + [jax.ShapeDtypeStruct((ENT_LEN, D), full)],
        in_specs=[VMEM] * 3 + [ANY] * len(shards),
        out_specs=[ANY] * (len(wholes) + len(saved_out)) + [VMEM],
        scratch_shapes=[pltpu.VMEM(shape, low) for shape in wholes]
        + [pltpu.VMEM(*shapes[name]) for name in SAVED]
        + [
            pltpu.VMEM((LEN, D), full),
            pltpu.VMEM((LEN, D), full),
            pltpu.VMEM((16, D), full),
            pltpu.VMEM((BLOCKS, BLOCK, D), low),
            pltpu.VMEM((2, BLOCKS, BLOCK, D), low),
            pltpu.SemaphoreType.DMA((len(chunks), copies)),
            pltpu.SemaphoreType.DMA((len(chunks), copies)),
            pltpu.SemaphoreType.DMA((len(chunks),)),
            pltpu.SemaphoreType.DMA((len(chunks),)),
            pltpu.SemaphoreType.DMA((2 * LAYERS, BLOCKS)),
            pltpu.SemaphoreType.DMA((2 * LAYERS, BLOCKS)),
            pltpu.SemaphoreType.DMA((LAYERS * len(SAVED),)),
        ],
        compiler_params=pltpu.CompilerParams(
            collective_id=collective_id, has_side_effects=True, vmem_limit_bytes=VMEM_BYTES
        ),
    )(words, base, entity_rows, *shards)
    kept = result[: len(wholes)]
    saved = [
        dict(zip(SAVED, result[len(wholes) + layer * len(SAVED) :][: len(SAVED)]))
        for layer in range(LAYERS)
    ]
    return kept, saved, result[-1]


def norm_back(grad, hat, scale, gain_row):
    hat = hat.astype(jnp.float32)
    wide = grad * gain_row
    inner = jnp.mean(wide * hat, axis=-1, keepdims=True)
    back = scale * (wide - jnp.mean(wide, axis=-1, keepdims=True) - hat * inner)
    return back, jnp.sum(grad * hat, axis=0), jnp.sum(grad, axis=0)


def saved_backward(grad_out, saved, attn_mats, out_mat, up_mat, down_mat, gain_rows):
    low = jnp.bfloat16
    stats = saved["stats"]
    heads = saved["k"].shape[1] // HEAD_DIM
    grad_second, gain_late, shift_late = norm_back(
        grad_out, saved["n2"], stats[:, 9:10], gain_rows[2]
    )
    grad_outer = grad_second.astype(low)
    grad_down = mm_lt(grad_outer, saved["g"])
    grad_pre = (mm(grad_outer, down_mat) * saved["slope"].astype(jnp.float32)).astype(low)
    grad_up = mm_lt(saved["h1b"], grad_pre)
    grad_first = grad_second + pair_sum(mm_rt(grad_pre, up_mat))
    grad_first_in, gain_early, shift_early = norm_back(
        grad_first, saved["n1"], stats[:, 8:9], gain_rows[0]
    )
    grad_attended = grad_first_in.astype(low)
    grad_out_mat = mm_lt(grad_attended, saved["o"])
    grad_mixed = mm(grad_attended, out_mat).astype(low)

    def heads_of(values):
        return values.reshape(LEN, heads, HEAD_DIM)

    log_norm = stats[:, :heads].T / LOG2E
    parts = attend_backward(
        (
            heads_of(saved["qw"]),
            heads_of(saved["qe"]),
            heads_of(saved["k"]),
            heads_of(saved["v"]),
            log_norm,
            heads_of(grad_mixed),
        )
    )
    grad_qw, grad_qe, grad_key, grad_value = [
        part.reshape(LEN, heads * HEAD_DIM).astype(low) for part in parts
    ]
    xb = saved["xb"]
    grad_mats = (
        mm_lt(xb[:WORDS], jnp.concatenate([grad_qw[:WORDS], grad_qe[:WORDS]], axis=1)),
        mm_lt(xb[WORDS:], jnp.concatenate([grad_qw[WORDS:], grad_qe[WORDS:]], axis=1)),
        mm_lt(xb, jnp.concatenate([grad_key, grad_value], axis=1)),
    )
    part_words = mm_rt(grad_qw[:WORDS], attn_mats[0]) + mm_rt(grad_qe[:WORDS], attn_mats[1])
    part_ents = mm_rt(grad_qw[WORDS:], attn_mats[2]) + mm_rt(grad_qe[WORDS:], attn_mats[3])
    part = jnp.concatenate([part_words, part_ents], axis=0)
    part += mm_rt(grad_key, attn_mats[4]) + mm_rt(grad_value, attn_mats[5])
    grad_hidden = grad_first_in + pair_sum(part)
    grad_norms = jnp.stack([gain_early, shift_early, gain_late, shift_late])
    return grad_hidden, (grad_mats, grad_out_mat, grad_up, grad_down, grad_norms)


def padded_rows(values):
    extra = -values.shape[-2] % 16
    return jnp.pad(values, [(0, 0)] * (values.ndim - 2) + [(0, extra), (0, 0)])


def weight_shards(attention_in, attention_out, feed_up, feed_down, norm_params, entity_proj, head_proj):
    def turned(values):
        return jnp.swapaxes(values, 1, 2)

    mats = attention_in.reshape(-1, *attention_in.shape[2:])
    norms = norm_params.reshape(1, -1, norm_params.shape[-1])
    norms = jnp.pad(norms, [(0, 0), (0, 16 - norms.shape[1]), (0, -norms.shape[2] % 128)])
    sources = [mats, turned(attention_out), feed_up, turned(feed_down), entity_proj[None], head_proj[None]]
    heights = [part.shape[1] for part in sources]
    shards = [padded_rows(part.astype(jnp.bfloat16)) for part in sources]
    shards.append(norms.astype(jnp.bfloat16))
    return shards, heights


def unpack_weights(wholes, heights, norm_width):
    kept = []
    for part, height in zip(wholes, heights):
        part = part[..., :height, :]
        kept.append(part.reshape(part.shape[0], -1, part.shape[-1]))
    norm_all = wholes[6][0].reshape(-1, 16, wholes[6].shape[-1])[:, : LAYERS * 4, :norm_width]
    norm_all = jnp.swapaxes(norm_all, 0, 1).reshape(LAYERS, 4, -1)
    return (
        kept[0].reshape(LAYERS, 6, *kept[0].shape[1:]),
        kept[1],
        kept[2],
        kept[3],
        norm_all,
        kept[4][0],
        kept[5][0],
    )


def gather_apart(dims, shards):
    chunks = [(4, 0, 1, True), (5, 0, 1, False), (6, 0, 1, True)]
    for layer in range(LAYERS):
        chunks += [(0, 6 * layer, 3, True), (0, 6 * layer + 3, 3, False)]
        chunks += [(1, layer, 1, layer == 0), (2, layer, 1, True), (3, layer, 1, False)]
    return gather_weights(dims, shards, chunks, 1)


def sum_all(dims, layer_grads, grad_proj, grad_head):
    n_dp = dims[0] * dims[1] * dims[2]

    def blocks(values):
        cut = values.astype(jnp.bfloat16).reshape(*dims, values.shape[0] // n_dp, values.shape[1])
        return padded_rows(cut)

    parts, flags, heights = [], [], []
    for layer in reversed(range(LAYERS)):
        (words_mat, ents_mat, shared_mat), out_mat, up_mat, down_mat, _ = layer_grads[layer]
        late = layer % 2 == 0
        for values, y_first in (
            (up_mat, True),
            (down_mat, False),
            (words_mat, True),
            (ents_mat, False),
            (shared_mat, late),
            (out_mat, not late),
        ):
            parts.append(blocks(values))
            flags.append(y_first)
            heights.append(values.shape[0] // n_dp)
    for values, y_first in ((grad_proj, True), (grad_head, False)):
        parts.append(blocks(values))
        flags.append(y_first)
        heights.append(values.shape[0] // n_dp)
    norms = jnp.concatenate([layer_grads[layer][4] for layer in range(LAYERS)], axis=0)
    width = norms.shape[1] // n_dp
    norms = jnp.swapaxes(norms.reshape(norms.shape[0], n_dp, width), 0, 1)
    norms = jnp.pad(norms, [(0, 0), (0, 16 - norms.shape[1]), (0, -width % 128)])
    parts.append(norms.astype(jnp.bfloat16).reshape(*dims, *norms.shape[1:]))
    flags.append(True)
    totals = sum_gradients(dims, parts, flags, 2)
    norm_sum = totals[-1][: LAYERS * 4, :width].reshape(LAYERS, 4, width)
    totals = [total[:height] for total, height in zip(totals, heights)]
    attn, outs, ups, downs = [], [], [], []
    for layer in range(LAYERS):
        at = 6 * (LAYERS - 1 - layer)
        ups.append(totals[at])
        downs.append(totals[at + 1].T)
        for part in totals[at + 2 : at + 5]:
            half = part.shape[1] // 2
            attn += [part[:, :half], part[:, half:]]
        outs.append(totals[at + 5].T)
    attn = jnp.stack(attn)
    return (
        attn.reshape(LAYERS, 6, *attn.shape[1:]),
        jnp.stack(outs),
        jnp.stack(ups),
        jnp.stack(downs),
        norm_sum,
        totals[-2],
        totals[-1],
    )


def on_device(
    word_inputs,
    entity_base,
    entity_ids,
    buckets,
    mask_positions,
    targets,
    word_cotangent,
    attention_in,
    attention_in_first,
    attention_in_second,
    attention_out,
    attention_out_first,
    attention_out_second,
    feed_up,
    feed_up_first,
    feed_up_second,
    feed_down,
    feed_down_first,
    feed_down_second,
    norm_params,
    norm_params_first,
    norm_params_second,
    entity_proj,
    entity_proj_first,
    entity_proj_second,
    head_proj,
    head_proj_first,
    head_proj_second,
    entity_table,
    entity_table_first,
    entity_table_second,
):
    dims = chip_grid(lax.axis_size("dp"))
    shards, heights = weight_shards(
        attention_in, attention_out, feed_up, feed_down, norm_params, entity_proj, head_proj
    )
    fused = heights[0] % 16 == 0 and heights[4] % 16 == 0
    slot_total = entity_ids.shape[0]
    shard_rows = entity_table.shape[0]
    bucket_rows = buckets.reshape(buckets.shape[2], buckets.shape[3])
    filled = bucket_rows >= 0
    safe_slot = jnp.maximum(bucket_rows, 0)
    request = jnp.where(filled, entity_ids[safe_slot] % shard_rows, -1)
    received = lax.all_to_all(request, "dp", split_axis=0, concat_axis=0, tiled=True)
    shard_base = lax.axis_index(("dp", "mp")) * shard_rows
    owned_mask = received >= 0
    safe_row = jnp.clip(received, 0, shard_rows - 1)
    table_low = entity_table.astype(jnp.bfloat16)
    replies = jnp.where(owned_mask[:, :, None], table_low[safe_row], jnp.zeros((), jnp.bfloat16))
    replied_rows_result = lax.all_to_all(replies, "dp", split_axis=0, concat_axis=0, tiled=True)
    row_placement_plan = (
        bucket_rows[:, :, None] == jnp.arange(slot_total, dtype=jnp.int32)[None, None, :]
    ).astype(jnp.bfloat16)
    local_shard_rows = jnp.einsum(
        "wvt,wvi->ti", row_placement_plan, replied_rows_result, preferred_element_type=jnp.float32
    )
    paired = pair_sum(local_shard_rows)
    masked_slots = (
        jnp.arange(SEQ_DEV, dtype=jnp.int32)[:, None] * ENT_LEN + mask_positions
    ).reshape(-1)
    keep_weight = 1.0 - jnp.any(
        jnp.arange(slot_total, dtype=jnp.int32)[:, None] == masked_slots[None, :], axis=1
    ).astype(jnp.float32)
    entity_rows = (paired * keep_weight[:, None]).astype(jnp.bfloat16)
    if fused:
        wholes, saved_layers, ents = run_forward(
            dims, word_inputs, entity_base, entity_rows, shards, 6
        )
    else:
        wholes = gather_apart(dims, shards)
    attn_low, out_low, up_low, down_low, norm_low, proj_low, head_low = unpack_weights(
        wholes, heights, norm_params.shape[-1]
    )
    gain_all = norm_low.astype(jnp.float32)
    if not fused:
        entity_inputs = entity_base.astype(jnp.float32) + jnp.dot(
            entity_rows, proj_low, preferred_element_type=jnp.float32
        )
        hidden = jnp.concatenate(
            [
                word_inputs.astype(jnp.float32).reshape(SEQ_DEV, WORDS, D),
                entity_inputs.reshape(SEQ_DEV, ENT_LEN, D),
            ],
            axis=1,
        )
        saved_layers = []
        for layer_index in range(LAYERS):
            hidden, saved_acts = layer_forward(
                hidden,
                attn_low[layer_index],
                out_low[layer_index],
                up_low[layer_index],
                down_low[layer_index],
                gain_all[layer_index],
            )
            saved_layers.append(saved_acts)
        ents = hidden[0, WORDS:]
    seq_index = jnp.arange(SEQ_DEV, dtype=jnp.int32)[:, None]
    masked_rows = WORDS + mask_positions
    masked_low = ents[mask_positions.reshape(-1)].astype(jnp.bfloat16)
    head_pre = jnp.dot(masked_low, head_low, preferred_element_type=jnp.float32)
    states_low = gelu_exact(head_pre).astype(jnp.bfloat16)
    all_states = spread(states_low, False, False, 3).reshape(-1, states_low.shape[1])
    logits = lax.dot_general(
        all_states, table_low, (((1,), (1,)), ((), ())), preferred_element_type=jnp.float32
    )
    flat_targets = targets.reshape(-1)
    target_hits = (
        jnp.arange(shard_rows, dtype=jnp.int32)[None, :] == (flat_targets - shard_base)[:, None]
    )
    peak_value = jnp.max(logits, axis=1)
    exp_total = jnp.sum(jnp.exp(logits - peak_value[:, None]), axis=1)
    picked = jnp.sum(jnp.where(target_hits, logits, 0.0), axis=1)
    shares = spread(jnp.stack([peak_value, exp_total, picked]), True, False, 4)
    peak_all = jnp.max(shares[:, 0], axis=0)
    total_all = jnp.sum(shares[:, 1] * jnp.exp(shares[:, 0] - peak_all), axis=0)
    picked_all = jnp.sum(shares[:, 2], axis=0)
    log_norm = peak_all + jnp.log(total_all)
    row_losses = log_norm - picked_all
    prob_rows = jnp.exp(logits - log_norm[:, None])
    grad_logits = ((prob_rows - target_hits.astype(jnp.float32)) / flat_targets.shape[0]).astype(
        jnp.bfloat16
    )
    grad_table = lax.dot_general(
        grad_logits, all_states, (((0,), (0,)), ((), ())), preferred_element_type=jnp.float32
    )
    grad_states = jnp.dot(grad_logits, table_low, preferred_element_type=jnp.float32)
    grad_states = grad_states.reshape(lax.axis_size("dp"), -1, grad_states.shape[1])
    grad_states = jnp.sum(spread(grad_states, False, True, 5), axis=0)
    grad_states = grad_states + lax.ppermute(grad_states, "mp", [(0, 1), (1, 0)])
    grad_head_pre = jax.vjp(gelu_exact, head_pre)[1](grad_states)[0].astype(jnp.bfloat16)
    grad_head = lax.dot_general(
        masked_low, grad_head_pre, (((0,), (0,)), ((), ())), preferred_element_type=jnp.float32
    )
    grad_masked = lax.dot_general(
        grad_head_pre, head_low, (((1,), (1,)), ((), ())), preferred_element_type=jnp.float32
    )
    grad_hidden = jnp.concatenate(
        [
            word_cotangent.astype(jnp.float32).reshape(SEQ_DEV, WORDS, D),
            jnp.zeros((SEQ_DEV, ENT_LEN, D), jnp.float32),
        ],
        axis=1,
    )
    grad_hidden = grad_hidden.at[seq_index, masked_rows].add(
        grad_masked.reshape(SEQ_DEV, MASK_ENT, D)
    )
    kept_grads = []
    for layer_index in reversed(range(LAYERS)):
        grad_hidden, layer_grads = (saved_backward if fused else layer_backward)(
            grad_hidden[0] if fused else grad_hidden,
            saved_layers[layer_index],
            attn_low[layer_index],
            out_low[layer_index],
            up_low[layer_index],
            down_low[layer_index],
            gain_all[layer_index],
        )
        if fused:
            grad_hidden = grad_hidden[None]
        if layer_index == 0:
            word_grads = grad_hidden[:, :WORDS].reshape(SEQ_DEV * WORDS, D)
            grad_entity = grad_hidden[:, WORDS:].reshape(slot_total, D).astype(jnp.bfloat16)
            grad_proj = lax.dot_general(
                entity_rows,
                grad_entity,
                (((0,), (0,)), ((), ())),
                preferred_element_type=jnp.float32,
            )
            row_gradient_block = (
                lax.dot_general(
                    grad_entity,
                    proj_low,
                    (((1,), (1,)), ((), ())),
                    preferred_element_type=jnp.float32,
                )
                * keep_weight[:, None]
            )
            outgoing = jnp.where(filled[:, :, None], row_gradient_block[safe_slot], 0.0)
            incoming = lax.all_to_all(
                outgoing.astype(jnp.bfloat16), "dp", split_axis=0, concat_axis=0, tiled=True
            ).astype(outgoing.dtype)
            grad_table = grad_table.at[safe_row].add(
                jnp.where(owned_mask[:, :, None], incoming, 0.0)
            )
        kept_grads.insert(0, layer_grads)
    reduced = sum_all(dims, kept_grads, grad_proj, grad_head)
    reduced_proj, reduced_head = reduced[5:]
    attn_new = adam_update(
        attention_in, attention_in_first, attention_in_second, reduced[0], kind_rates[0]
    )
    out_new = adam_update(
        attention_out, attention_out_first, attention_out_second, reduced[1], kind_rates[1]
    )
    up_new = adam_update(feed_up, feed_up_first, feed_up_second, reduced[2], kind_rates[2])
    down_new = adam_update(feed_down, feed_down_first, feed_down_second, reduced[3], kind_rates[3])
    norm_new = adam_update(
        norm_params, norm_params_first, norm_params_second, reduced[4], kind_rates[4]
    )
    proj_new = adam_update(
        entity_proj, entity_proj_first, entity_proj_second, reduced_proj, kind_rates[5]
    )
    head_new = adam_update(
        head_proj, head_proj_first, head_proj_second, reduced_head, kind_rates[6]
    )
    table_new = adam_update(
        entity_table, entity_table_first, entity_table_second, grad_table, kind_rates[7]
    )
    return (
        row_losses,
        word_grads,
        attn_new[0],
        attn_new[1],
        attn_new[2],
        out_new[0],
        out_new[1],
        out_new[2],
        up_new[0],
        up_new[1],
        up_new[2],
        down_new[0],
        down_new[1],
        down_new[2],
        norm_new[0],
        norm_new[1],
        norm_new[2],
        proj_new[0],
        proj_new[1],
        proj_new[2],
        head_new[0],
        head_new[1],
        head_new[2],
        table_new[0],
        table_new[1],
        table_new[2],
    )


def solution(mesh):
    in_specs = (
        P("dp", None),
        P("dp", None),
        P("dp"),
        P("dp", "mp", None, None),
        P("dp", None),
        P(),
        P("dp", None),
        P(None, None, "dp", "mp"),
        P(None, None, "dp", "mp"),
        P(None, None, "dp", "mp"),
        P(None, "mp", "dp"),
        P(None, "mp", "dp"),
        P(None, "mp", "dp"),
        P(None, "dp", "mp"),
        P(None, "dp", "mp"),
        P(None, "dp", "mp"),
        P(None, "mp", "dp"),
        P(None, "mp", "dp"),
        P(None, "mp", "dp"),
        P(None, None, "dp"),
        P(None, None, "dp"),
        P(None, None, "dp"),
        P("dp", None),
        P("dp", None),
        P("dp", None),
        P("dp", None),
        P("dp", None),
        P("dp", None),
        P(("dp", "mp"), None),
        P(("dp", "mp"), None),
        P(("dp", "mp"), None),
    )
    out_specs = (
        P(),
        P("dp", None),
        P(None, None, "dp", "mp"),
        P(None, None, "dp", "mp"),
        P(None, None, "dp", "mp"),
        P(None, "mp", "dp"),
        P(None, "mp", "dp"),
        P(None, "mp", "dp"),
        P(None, "dp", "mp"),
        P(None, "dp", "mp"),
        P(None, "dp", "mp"),
        P(None, "mp", "dp"),
        P(None, "mp", "dp"),
        P(None, "mp", "dp"),
        P(None, None, "dp"),
        P(None, None, "dp"),
        P(None, None, "dp"),
        P("dp", None),
        P("dp", None),
        P("dp", None),
        P("dp", None),
        P("dp", None),
        P("dp", None),
        P(("dp", "mp"), None),
        P(("dp", "mp"), None),
        P(("dp", "mp"), None),
    )
    return jax.shard_map(
        on_device, mesh=mesh, in_specs=in_specs, out_specs=out_specs, check_vma=False
    )
```

```python
import functools

import jax
import jax.numpy as jnp
from jax import lax
from jax.experimental import pallas as pl
from jax.experimental.pallas import tpu as pltpu
from jax.sharding import PartitionSpec as P

D = 768
HEAD_DIM = 64
WORDS = 896
ENT_LEN = 128
MASK_ENT = 16
LAYERS = 2
STEP = 10
SEQ_DEV = 1


norm_eps = 1e-05
beta_first = 0.9
beta_second = 0.999
adam_eps = 1e-12
weight_decay = 0.01
kind_rates = (0.05, 1.0, 0.05, 0.027, 0.75, 0.5, 0.05, 0.2)


MESH = pl.DeviceIdType.MESH
ANY = pl.BlockSpec(memory_space=pl.ANY)
VMEM = pl.BlockSpec(memory_space=pltpu.VMEM)
VMEM_BYTES = 60 * 2**20


def chip_grid(n_dp):
    return {16: (4, 2, 2), 64: (4, 4, 4)}.get(n_dp, (n_dp, 1, 1))


def place(dims):
    index = lax.axis_index("dp")
    return index // (dims[1] * dims[2]), index // dims[2] % dims[1], index % dims[2]


def axis_peers(dims, axis):
    here = place(dims)
    core = lax.axis_index("mp")
    peers = []
    for step in range(1, dims[axis]):
        spot = list(here)
        spot[axis] = lax.rem(here[axis] + step, dims[axis])
        peers.append((spot[axis], (spot[0] * dims[1] * dims[2] + spot[1] * dims[2] + spot[2], core)))
    return peers


def greet(targets):
    barrier = pltpu.get_barrier_semaphore()
    for target in targets:
        pl.semaphore_signal(barrier, inc=1, device_id=target, device_id_type=MESH)
    pl.semaphore_wait(barrier, len(targets))


def send(src, dst, send_sem, recv_sem, target):
    copy = pltpu.make_async_remote_copy(
        src_ref=src,
        dst_ref=dst,
        send_sem=send_sem,
        recv_sem=recv_sem,
        device_id=target,
        device_id_type=MESH,
    )
    copy.start()
    return copy


def gather_body(dims, chunks, count, *refs):
    shards, wholes = refs[:count], refs[count : 2 * count]
    send_sem, recv_sem, local_sem = refs[2 * count :]
    z, y, x = place(dims)
    peers = [axis_peers(dims, axis) for axis in range(3)]
    greet([target for group in peers for _, target in group])
    pending = {}

    def start(stage, c):
        which, first, size, y_first = chunks[c]
        rows = pl.ds(first, size)
        whole = wholes[which]
        copies = []
        if stage == 0:
            src, dst, group = shards[which].at[rows], whole.at[rows, z, y, x], peers[0]
            own = pltpu.make_async_copy(src, dst, local_sem.at[c])
            own.start()
            copies.append(own)
        elif stage == 1:
            src = whole.at[rows, :, y, x]
            dst, group = src, peers[1 if y_first else 2]
        else:
            src = whole.at[rows, :, :, x] if y_first else whole.at[rows, :, y]
            dst, group = src, peers[2 if y_first else 1]
        base = (0, dims[0], dims[0] + max(dims[1:]))[stage]
        for slot, (_, target) in enumerate(group):
            copies.append(
                send(src, dst, send_sem.at[c, base + slot], recv_sem.at[c, base + slot], target)
            )
        pending[stage, c] = copies

    def finish(stage, c):
        for copy in pending.pop((stage, c)):
            copy.wait()

    total = len(chunks)
    start(0, 0)
    for step in range(total + 2):
        if step + 1 < total:
            start(0, step + 1)
        if step < total:
            finish(0, step)
            start(1, step)
        if 0 <= step - 1 < total:
            finish(1, step - 1)
            start(2, step - 1)
        if 0 <= step - 2 < total:
            finish(2, step - 2)


def gather_weights(dims, shards, chunks, collective_id):
    count = len(shards)
    copies = dims[0] + 2 * max(dims[1:])
    return pl.pallas_call(
        functools.partial(gather_body, dims, chunks, count),
        out_shape=[
            jax.ShapeDtypeStruct((s.shape[0], *dims, *s.shape[1:]), s.dtype) for s in shards
        ],
        in_specs=[ANY] * count,
        out_specs=[ANY] * count,
        scratch_shapes=[
            pltpu.SemaphoreType.DMA((len(chunks), copies)),
            pltpu.SemaphoreType.DMA((len(chunks), copies)),
            pltpu.SemaphoreType.DMA((len(chunks),)),
        ],
        compiler_params=pltpu.CompilerParams(
            collective_id=collective_id, has_side_effects=True, vmem_limit_bytes=2**20
        ),
    )(*shards)


def sum_body(dims, flags, *refs):
    count = len(flags)
    parts, totals = refs[:count], refs[count : 2 * count]
    buffers = refs[2 * count : 6 * count]
    send_sem, recv_sem, local_sem = refs[6 * count :]
    z, y, x = place(dims)
    peers = [axis_peers(dims, axis) for axis in range(3)]
    greet([target for group in peers for _, target in group])
    pending = {}

    def start(stage, c):
        y_first = flags[c]
        own, first, second, third = buffers[4 * c : 4 * c + 4]
        copies = []
        base = (0, max(dims[1:]), 2 * max(dims[1:]))[stage]
        if stage == 0:
            mine = parts[c].at[:, y] if y_first else parts[c].at[:, :, x]
            local = pltpu.make_async_copy(mine, own, local_sem.at[c])
            local.start()
            copies.append(local)
        group = peers[((1, 2, 0) if y_first else (2, 1, 0))[stage]]
        for slot, (spot, target) in enumerate(group):
            if stage == 0:
                src = parts[c].at[:, spot] if y_first else parts[c].at[:, :, spot]
                dst = first.at[slot]
            elif stage == 1:
                src, dst = own.at[:, spot], second.at[slot]
            else:
                src, dst = own.at[spot, x if y_first else y], third.at[slot]
            copies.append(
                send(src, dst, send_sem.at[c, base + slot], recv_sem.at[c, base + slot], target)
            )
        pending[stage, c] = copies

    def finish(stage, c):
        y_first = flags[c]
        own, first, second, third = buffers[4 * c : 4 * c + 4]
        for copy in pending.pop((stage, c)):
            copy.wait()
        across = dims[2] if y_first else dims[1]
        line = x if y_first else y
        count_peers = len(peers[((1, 2, 0) if y_first else (2, 1, 0))[stage]])
        if stage == 0 and count_peers:

            def add_first(i, carry):
                value = own[i // across, i % across].astype(jnp.float32)
                for slot in range(count_peers):
                    value += first[slot, i // across, i % across].astype(jnp.float32)
                own[i // across, i % across] = value.astype(own.dtype)
                return carry

            lax.fori_loop(0, dims[0] * across, add_first, 0)
        if stage == 1 and count_peers:

            def add_second(i, carry):
                value = own[i, line].astype(jnp.float32)
                for slot in range(count_peers):
                    value += second[slot, i].astype(jnp.float32)
                own[i, line] = value.astype(own.dtype)
                return carry

            lax.fori_loop(0, dims[0], add_second, 0)
        if stage == 2:
            value = own[z, line].astype(jnp.float32)
            for slot in range(count_peers):
                value += third[slot].astype(jnp.float32)
            totals[c][...] = value

    total = len(flags)
    ahead = 2
    for c in range(min(ahead, total)):
        start(0, c)
    for step in range(total + 2 * ahead):
        if step + ahead < total:
            start(0, step + ahead)
        if step < total:
            finish(0, step)
            start(1, step)
        if 0 <= step - ahead < total:
            finish(1, step - ahead)
            start(2, step - ahead)
        if 0 <= step - 2 * ahead < total:
            finish(2, step - 2 * ahead)


def sum_gradients(dims, parts, flags, collective_id):
    count = len(parts)
    scratch = []
    for part, y_first in zip(parts, flags):
        block = part.shape[3:]
        own = (dims[0], dims[2] if y_first else dims[1])
        turns = (dims[1], dims[2]) if y_first else (dims[2], dims[1])
        scratch += [
            pltpu.VMEM((*own, *block), part.dtype),
            pltpu.VMEM((max(turns[0] - 1, 1), *own, *block), part.dtype),
            pltpu.VMEM((max(turns[1] - 1, 1), dims[0], *block), part.dtype),
            pltpu.VMEM((max(dims[0] - 1, 1), *block), part.dtype),
        ]
    copies = dims[0] + 2 * max(dims[1:])
    return pl.pallas_call(
        functools.partial(sum_body, dims, flags),
        out_shape=[jax.ShapeDtypeStruct(part.shape[3:], jnp.float32) for part in parts],
        in_specs=[ANY] * count,
        out_specs=[VMEM] * count,
        scratch_shapes=scratch
        + [
            pltpu.SemaphoreType.DMA((count, copies)),
            pltpu.SemaphoreType.DMA((count, copies)),
            pltpu.SemaphoreType.DMA((count,)),
        ],
        compiler_params=pltpu.CompilerParams(
            collective_id=collective_id, has_side_effects=True, vmem_limit_bytes=VMEM_BYTES
        ),
    )(*parts)


def spread_body(count, wide, swap, data, result, send_sem, recv_sem, local_sem):
    pair = lax.axis_size("mp")
    index = lax.axis_index("dp") * pair + lax.axis_index("mp") if wide else lax.axis_index("dp")

    def target_of(step):
        other = lax.rem(index + step, count)
        if wide:
            return other, (other // pair, lax.rem(other, pair))
        return other, (other, lax.axis_index("mp"))

    barrier = pltpu.get_barrier_semaphore()

    def hello(step, carry):
        pl.semaphore_signal(barrier, inc=1, device_id=target_of(step)[1], device_id_type=MESH)
        return carry

    lax.fori_loop(1, count, hello, 0)
    pl.semaphore_wait(barrier, count - 1)
    own = pltpu.make_async_copy(data.at[index if swap else 0], result.at[index], local_sem)
    own.start()

    def copy_of(step):
        other, target = target_of(step)
        return pltpu.make_async_remote_copy(
            src_ref=data.at[other if swap else 0],
            dst_ref=result.at[index],
            send_sem=send_sem.at[step],
            recv_sem=recv_sem.at[step],
            device_id=target,
            device_id_type=MESH,
        )

    def go(step, carry):
        copy_of(step).start()
        return carry

    def done(step, carry):
        copy_of(step).wait()
        return carry

    lax.fori_loop(1, count, go, 0)
    own.wait()
    lax.fori_loop(1, count, done, 0)


def spread(data, wide, swap, collective_id):
    count = lax.axis_size("dp") * (lax.axis_size("mp") if wide else 1)
    block = data.shape[1:] if swap else data.shape
    return pl.pallas_call(
        functools.partial(spread_body, count, wide, swap),
        out_shape=jax.ShapeDtypeStruct((count, *block), data.dtype),
        in_specs=[VMEM],
        out_specs=VMEM,
        scratch_shapes=[
            pltpu.SemaphoreType.DMA((count,)),
            pltpu.SemaphoreType.DMA((count,)),
            pltpu.SemaphoreType.DMA,
        ],
        compiler_params=pltpu.CompilerParams(
            collective_id=collective_id, has_side_effects=True, vmem_limit_bytes=VMEM_BYTES
        ),
    )(data if swap else data[None])


def layer_norm(values, gain_row, shift_row):
    centered = values - jnp.mean(values, axis=-1, keepdims=True)
    spread = jnp.mean(centered * centered, axis=-1, keepdims=True)
    return centered * lax.rsqrt(spread + norm_eps) * gain_row + shift_row


def gelu_exact(values):
    return jax.nn.gelu(values, approximate=False)


def adam_update(master, first_moment, second_moment, gradient, kind_rate):
    first_new = beta_first * first_moment + (1.0 - beta_first) * gradient
    second_new = beta_second * second_moment + (1.0 - beta_second) * gradient * gradient
    first_hat = first_new / (1.0 - beta_first**STEP)
    second_hat = second_new / (1.0 - beta_second**STEP)
    master_new = master - kind_rate * (
        first_hat / (jnp.sqrt(second_hat) + adam_eps) + weight_decay * master
    )
    return (first_new, second_new, master_new)


def project(fetched_row_values, weight_matrix_entry):
    return jnp.einsum(
        "mvw,wu->mvu", fetched_row_values, weight_matrix_entry, preferred_element_type=jnp.float32
    )


def project_back(row_gradient_block, weight_matrix_entry):
    return jnp.einsum(
        "tic,vc->tiv", row_gradient_block, weight_matrix_entry, preferred_element_type=jnp.float32
    )


def project_turned(rows, turned):
    return jnp.einsum("mvw,uw->mvu", rows, turned, preferred_element_type=jnp.float32)


def project_back_turned(row_gradient_block, turned):
    return jnp.einsum("tic,cv->tiv", row_gradient_block, turned, preferred_element_type=jnp.float32)


def weight_grad(layer_input_list, row_gradient_block):
    return jnp.einsum(
        "hmq,hmw->qw", layer_input_list, row_gradient_block, preferred_element_type=jnp.float32
    ).astype(jnp.bfloat16)


def split_heads(values):
    return values.reshape(values.shape[0], values.shape[1], values.shape[2] // HEAD_DIM, HEAD_DIM)


def pair_sum(partial_sum):
    mine = partial_sum.astype(jnp.bfloat16)
    theirs = lax.ppermute(mine, "mp", [(0, 1), (1, 0)])
    return mine.astype(jnp.float32) + theirs.astype(jnp.float32)


merge_heads = merge_inputs = pair_sum


def seq_scores(query_word, query_entity, key_rows):
    score_word = jnp.einsum(
        "qhd,khd->hqk", query_word, key_rows[:WORDS], preferred_element_type=jnp.float32
    )
    score_entity = jnp.einsum(
        "qhd,khd->hqk", query_entity, key_rows[WORDS:], preferred_element_type=jnp.float32
    )
    return jnp.concatenate([score_word, score_entity], axis=-1) * 0.125


def attend_forward(seq_item):
    query_word, query_entity, key_rows, value_rows = seq_item
    scores = seq_scores(query_word, query_entity, key_rows)
    peak_value = jnp.max(scores, axis=-1, keepdims=True)
    exp_scores = jnp.exp(scores - peak_value)
    exp_total = jnp.sum(exp_scores, axis=-1, keepdims=True)
    prob_low = (exp_scores / exp_total).astype(jnp.bfloat16)
    mixed_heads = jnp.einsum(
        "hqk,khd->qhd", prob_low, value_rows, preferred_element_type=jnp.float32
    )
    return (mixed_heads, (peak_value + jnp.log(exp_total))[..., 0])


def attend_backward(seq_item):
    query_word, query_entity, key_rows, value_rows, log_norm, grad_mixed = seq_item
    scores = seq_scores(query_word, query_entity, key_rows)
    prob_rows = jnp.exp(scores - log_norm[..., None])
    grad_value = jnp.einsum(
        "hqk,qhd->khd",
        prob_rows.astype(jnp.bfloat16),
        grad_mixed,
        preferred_element_type=jnp.float32,
    )
    grad_probs = jnp.einsum(
        "qhd,khd->hqk", grad_mixed, value_rows, preferred_element_type=jnp.float32
    )
    inner_sum = jnp.sum(prob_rows * grad_probs, axis=-1, keepdims=True)
    grad_scores = (prob_rows * (grad_probs - inner_sum) * 0.125).astype(jnp.bfloat16)
    score_word = grad_scores[..., :WORDS]
    score_entity = grad_scores[..., WORDS:]
    grad_qw = jnp.einsum(
        "hqk,khd->qhd", score_word, key_rows[:WORDS], preferred_element_type=jnp.float32
    )
    grad_qe = jnp.einsum(
        "hqk,khd->qhd", score_entity, key_rows[WORDS:], preferred_element_type=jnp.float32
    )
    grad_key = jnp.concatenate(
        [
            jnp.einsum("hqk,qhd->khd", score_word, query_word, preferred_element_type=jnp.float32),
            jnp.einsum(
                "hqk,qhd->khd", score_entity, query_entity, preferred_element_type=jnp.float32
            ),
        ],
        axis=0,
    )
    return (grad_qw, grad_qe, grad_key, grad_value)


def layer_forward(hidden, attn_mats, out_mat, up_mat, down_mat, gain_rows):
    hidden_low = hidden.astype(jnp.bfloat16)
    words_low = hidden_low[:, :WORDS]
    ents_low = hidden_low[:, WORDS:]
    query_word = jnp.concatenate(
        [project(words_low, attn_mats[0]), project(ents_low, attn_mats[2])], axis=1
    ).astype(jnp.bfloat16)
    query_entity = jnp.concatenate(
        [project(words_low, attn_mats[1]), project(ents_low, attn_mats[3])], axis=1
    ).astype(jnp.bfloat16)
    key_rows = project(hidden_low, attn_mats[4]).astype(jnp.bfloat16)
    value_rows = project(hidden_low, attn_mats[5]).astype(jnp.bfloat16)
    mixed_heads, log_norm = lax.map(
        attend_forward,
        (
            split_heads(query_word),
            split_heads(query_entity),
            split_heads(key_rows),
            split_heads(value_rows),
        ),
    )
    mixed_low = mixed_heads.reshape(key_rows.shape).astype(jnp.bfloat16)
    attended = merge_heads(project_turned(mixed_low, out_mat))
    first_out = layer_norm(hidden + attended, gain_rows[0], gain_rows[1])
    first_low = first_out.astype(jnp.bfloat16)
    inner_pre = project(first_low, up_mat)
    inner_low = gelu_exact(inner_pre).astype(jnp.bfloat16)
    outer_out = merge_heads(project_turned(inner_low, down_mat))
    result = layer_norm(first_out + outer_out, gain_rows[2], gain_rows[3])
    saved_acts = (
        hidden,
        hidden_low,
        query_word,
        query_entity,
        key_rows,
        value_rows,
        log_norm,
        mixed_low,
        attended,
        first_out,
        first_low,
        inner_pre,
        inner_low,
        outer_out,
    )
    return (result, saved_acts)


def layer_backward(grad_out, saved_acts, attn_mats, out_mat, up_mat, down_mat, gain_rows):
    (
        hidden,
        hidden_low,
        query_word,
        query_entity,
        key_rows,
        value_rows,
        log_norm,
        mixed_low,
        attended,
        first_out,
        first_low,
        inner_pre,
        inner_low,
        outer_out,
    ) = saved_acts
    second_back = jax.vjp(layer_norm, first_out + outer_out, gain_rows[2], gain_rows[3])[1]
    grad_second, grad_gain_late, grad_shift_late = second_back(grad_out)
    grad_outer = grad_second.astype(jnp.bfloat16)
    grad_down = weight_grad(grad_outer, inner_low)
    grad_inner = project_back_turned(grad_outer, down_mat)
    grad_pre = jax.vjp(gelu_exact, inner_pre)[1](grad_inner)[0].astype(jnp.bfloat16)
    grad_up = weight_grad(first_low, grad_pre)
    grad_first = grad_second + merge_inputs(project_back(grad_pre, up_mat))
    first_back = jax.vjp(layer_norm, hidden + attended, gain_rows[0], gain_rows[1])[1]
    grad_first_in, grad_gain_early, grad_shift_early = first_back(grad_first)
    grad_attended = grad_first_in.astype(jnp.bfloat16)
    grad_out_mat = weight_grad(grad_attended, mixed_low)
    grad_mixed = project_back_turned(grad_attended, out_mat).astype(jnp.bfloat16)
    grad_qw, grad_qe, grad_key, grad_value = lax.map(
        attend_backward,
        (
            split_heads(query_word),
            split_heads(query_entity),
            split_heads(key_rows),
            split_heads(value_rows),
            log_norm,
            split_heads(grad_mixed),
        ),
    )
    flat_shape = key_rows.shape
    grad_qw = grad_qw.reshape(flat_shape).astype(jnp.bfloat16)
    grad_qe = grad_qe.reshape(flat_shape).astype(jnp.bfloat16)
    grad_key = grad_key.reshape(flat_shape).astype(jnp.bfloat16)
    grad_value = grad_value.reshape(flat_shape).astype(jnp.bfloat16)
    words_low = hidden_low[:, :WORDS]
    ents_low = hidden_low[:, WORDS:]
    grad_mats = (
        weight_grad(words_low, jnp.concatenate([grad_qw[:, :WORDS], grad_qe[:, :WORDS]], axis=-1)),
        weight_grad(ents_low, jnp.concatenate([grad_qw[:, WORDS:], grad_qe[:, WORDS:]], axis=-1)),
        weight_grad(hidden_low, jnp.concatenate([grad_key, grad_value], axis=-1)),
    )
    part_words = project_back(grad_qw[:, :WORDS], attn_mats[0]) + project_back(
        grad_qe[:, :WORDS], attn_mats[1]
    )
    part_ents = project_back(grad_qw[:, WORDS:], attn_mats[2]) + project_back(
        grad_qe[:, WORDS:], attn_mats[3]
    )
    part_sum = (
        jnp.concatenate([part_words, part_ents], axis=1)
        + project_back(grad_key, attn_mats[4])
        + project_back(grad_value, attn_mats[5])
    )
    grad_hidden = grad_first_in + merge_inputs(part_sum)
    grad_norms = jnp.stack([grad_gain_early, grad_shift_early, grad_gain_late, grad_shift_late])
    return (grad_hidden, (grad_mats, grad_out_mat, grad_up, grad_down, grad_norms))


LOG2E = 1.4426950408889634
SCORE_STEP = 0.125 * LOG2E
LEN = WORDS + ENT_LEN
BLOCK = 256
BLOCKS = LEN // BLOCK


def mm(left, right):
    return lax.dot_general(
        left, right, (((1,), (0,)), ((), ())), preferred_element_type=jnp.float32
    )


def mm_rt(left, right):
    return lax.dot_general(
        left, right, (((1,), (1,)), ((), ())), preferred_element_type=jnp.float32
    )


def mm_lt(left, right):
    return lax.dot_general(
        left, right, (((0,), (0,)), ((), ())), preferred_element_type=jnp.float32
    )


def flat(ref, *index):
    value = ref[index] if index else ref[...]
    return value.reshape(-1, value.shape[-1])


def lane_mask(rows, which):
    lane = lax.broadcasted_iota(jnp.int32, (rows, 2 * HEAD_DIM), 1)
    return (lane // HEAD_DIM == which).astype(jnp.bfloat16)


def normed(values):
    centered = values - jnp.mean(values, axis=-1, keepdims=True)
    spread_row = jnp.mean(centered * centered, axis=-1, keepdims=True)
    scale = lax.rsqrt(spread_row + norm_eps)
    return centered * scale, scale


def gelu_parts(values):
    cdf = 0.5 * (1.0 + lax.erf(values * 0.7071067811865476))
    bell = jnp.exp2(values * values * (-0.5 * LOG2E)) * 0.3989422804014327
    return values * cdf, cdf + values * bell


class Gather:
    def __init__(self, dims, chunks, shards, wholes, kept, sems, lags=(3, 2, 2)):
        self.dims, self.chunks, self.shards, self.wholes, self.kept = dims, chunks, shards, wholes, kept
        self.send_sem, self.recv_sem, self.local_sem, self.keep_sem = sems
        self.spot = place(dims)
        self.peers = [axis_peers(dims, axis) for axis in range(3)]
        self.pending, self.step = {}, 0
        self.ahead, self.lag1, self.lag2 = lags

    def targets(self):
        return [target for group in self.peers for _, target in group]

    def start(self, stage, c):
        which, rows, cols, y_first = self.chunks[c]
        z, y, x = self.spot
        whole = self.wholes[which].at[rows, :, :, :, :, cols]
        shard = self.shards[which].at[rows, :, cols]
        copies = []
        if stage == 0:
            own = pltpu.make_async_copy(shard, whole.at[:, z, y, x], self.local_sem.at[c])
            own.start()
            copies.append(own)
            src, dst, group = shard, whole.at[:, z, y, x], self.peers[0]
        elif stage == 1:
            src = whole.at[:, :, y, x]
            dst, group = src, self.peers[1 if y_first else 2]
        else:
            src = whole.at[:, :, :, x] if y_first else whole.at[:, :, y]
            dst, group = src, self.peers[2 if y_first else 1]
        base = (0, self.dims[0], self.dims[0] + max(self.dims[1:]))[stage]
        for slot, (_, target) in enumerate(group):
            sems = self.send_sem.at[c, base + slot], self.recv_sem.at[c, base + slot]
            copies.append(send(src, dst, *sems, target))
        self.pending[stage, c] = copies

    def finish(self, stage, c):
        for copy in self.pending.pop((stage, c)):
            copy.wait()
        if stage == 2:
            which, rows, cols, _ = self.chunks[c]
            keep = pltpu.make_async_copy(
                self.wholes[which].at[rows, :, :, :, :, cols],
                self.kept[which].at[rows, :, :, :, :, cols],
                self.keep_sem.at[c],
            )
            keep.start()
            self.pending[3, c] = [keep]

    def begin(self):
        for c in range(min(self.ahead, len(self.chunks))):
            self.start(0, c)

    def tick(self):
        total, step = len(self.chunks), self.step
        if step >= total + self.lag1 + self.lag2:
            return
        self.step += 1
        if step + self.ahead < total:
            self.start(0, step + self.ahead)
        if step < total:
            self.finish(0, step)
            self.start(1, step)
        late = step - self.lag1
        if 0 <= late < total:
            self.finish(1, late)
            self.start(2, late)
        late -= self.lag2
        if 0 <= late < total:
            self.finish(2, late)

    def need(self, c):
        while self.step < c + self.lag1 + self.lag2 + 1:
            self.tick()

    def close(self):
        self.need(len(self.chunks) - 1)
        for key in sorted(self.pending):
            for copy in self.pending[key]:
                copy.wait()


class Pair:
    def __init__(self, mine, theirs, sems):
        self.mine, self.theirs = mine, theirs
        self.send_sem, self.recv_sem = sems
        self.phase = 0
        self.other = (lax.axis_index("dp"), 1 - lax.axis_index("mp"))

    def copy(self, phase, c):
        return pltpu.make_async_remote_copy(
            src_ref=self.mine.at[c],
            dst_ref=self.theirs.at[phase % 2, c],
            send_sem=self.send_sem.at[phase, c],
            recv_sem=self.recv_sem.at[phase, c],
            device_id=self.other,
            device_id_type=MESH,
        )

    def run(self, compute, consume, between=None):
        phase = self.phase
        self.phase += 1

        def take(c):
            self.copy(phase, c).wait()
            total = self.mine[c].astype(jnp.float32) + self.theirs[phase % 2, c].astype(jnp.float32)
            consume(c, pl.ds(c * BLOCK, BLOCK), total)

        for c in range(BLOCKS):
            self.mine[c] = compute(c, pl.ds(c * BLOCK, BLOCK)).astype(jnp.bfloat16)
            self.copy(phase, c).start()
            if between is not None:
                between()
            if c:
                take(c - 1)
        take(BLOCKS - 1)


SAVED = ("xb", "qw", "qe", "k", "v", "o", "n1", "h1b", "slope", "g", "n2", "stats")


def saved_shapes(half, hidden):
    wide, narrow = (LEN, D), (LEN, half)
    low = jnp.bfloat16
    return {
        "xb": (wide, low),
        "qw": (narrow, low),
        "qe": (narrow, low),
        "k": (narrow, low),
        "v": (narrow, low),
        "o": (narrow, low),
        "n1": (wide, low),
        "h1b": (wide, low),
        "slope": ((LEN, hidden), low),
        "g": ((LEN, hidden), low),
        "n2": (wide, low),
        "stats": ((LEN, 128), jnp.float32),
    }


def attend(act, pair):
    lanes = slice(pair * 2 * HEAD_DIM, (pair + 1) * 2 * HEAD_DIM)

    def block(i, carry):
        rows = pl.ds(i * BLOCK, BLOCK)
        keys, values = act["k"][:, lanes], act["v"][:, lanes]
        total = None
        for which in range(2):
            q_mask, v_mask = lane_mask(BLOCK, which), lane_mask(LEN, which)
            score_w = mm_rt(act["qw"][rows, lanes] * q_mask, keys[:WORDS])
            score_e = mm_rt(act["qe"][rows, lanes] * q_mask, keys[WORDS:])
            peak = jnp.maximum(
                jnp.max(score_w, axis=-1, keepdims=True), jnp.max(score_e, axis=-1, keepdims=True)
            )
            exp_w = jnp.exp2((score_w - peak) * SCORE_STEP)
            exp_e = jnp.exp2((score_e - peak) * SCORE_STEP)
            weight = jnp.sum(exp_w, axis=-1, keepdims=True) + jnp.sum(exp_e, axis=-1, keepdims=True)
            part = values * v_mask
            mixed = mm(exp_w.astype(jnp.bfloat16), part[:WORDS])
            mixed += mm(exp_e.astype(jnp.bfloat16), part[WORDS:])
            mixed = mixed * (1.0 / weight)
            total = mixed if total is None else total + mixed
            head = 2 * pair + which
            act["stats"][rows, head : head + 1] = peak * SCORE_STEP + jnp.log2(weight)
        act["o"][rows, lanes] = total.astype(jnp.bfloat16)
        return carry

    lax.fori_loop(0, BLOCKS, block, 0)


def project_rows(out_ref, x_ref, first, size, step, weights, index):
    def block(i, carry):
        rows = pl.ds(first + i * step, step)
        out_ref[rows, :] = mm(x_ref[rows, :], flat(weights, index)).astype(jnp.bfloat16)
        return carry

    lax.fori_loop(0, size // step, block, 0)


def forward_body(dims, chunks, needs, *refs):
    refs = list(refs)

    def take(count):
        part = refs[:count]
        del refs[:count]
        return part

    words, base, rows_in = take(3)
    shards = take(len(needs["kinds"]))
    kept = take(len(needs["kinds"]))
    saved = [dict(zip(SAVED, take(len(SAVED)))) for _ in range(LAYERS)]
    ents_out, gains_out = take(2)
    wholes = take(len(needs["kinds"]))
    act = dict(zip(SAVED, take(len(SAVED))))
    x, h1, gains, mine, theirs = take(5)
    gather_sems = take(4)
    pair_sems = take(2)
    (save_sem,) = take(1)

    gather = Gather(dims, chunks, shards, wholes, kept, gather_sems)
    pair = Pair(mine, theirs, pair_sems)
    greet(gather.targets() + [pair.other])
    gather.begin()
    attn, outs, ups, downs, proj, _, norms = wholes
    saving = {}

    def save(layer, name):
        slot = layer * len(SAVED) + SAVED.index(name)
        copy = pltpu.make_async_copy(act[name], saved[layer][name], save_sem.at[slot])
        copy.start()
        saving[name] = copy

    def free(name):
        if name in saving:
            saving.pop(name).wait()

    x[:WORDS] = words[...].astype(jnp.float32)
    gather.need(needs["norms"])
    width = D // (dims[0] * dims[1] * dims[2])
    count = dims[0] * dims[1] * dims[2]
    gains[...] = jnp.zeros_like(gains)
    for d in range(count):
        z, rest = d // (dims[1] * dims[2]), d % (dims[1] * dims[2])
        pick = lax.broadcasted_iota(jnp.int32, (128, D), 0) + d * width
        lane = lax.broadcasted_iota(jnp.int32, (128, D), 1)
        inside = lax.broadcasted_iota(jnp.int32, (128, D), 0) < width
        hot = jnp.where((pick == lane) & inside, 1.0, 0.0).astype(jnp.bfloat16)
        gains[...] += mm(norms[0, z, rest // dims[2], rest % dims[2]], hot)
    gather.need(needs["proj"])
    x[WORDS:] = base[...].astype(jnp.float32) + mm(rows_in[...], flat(proj, 0))

    for layer in range(LAYERS):
        gain = [gains[4 * layer + i : 4 * layer + i + 1, :] for i in range(4)]
        free("xb")

        def cast(i, carry):
            rows = pl.ds(i * BLOCK, BLOCK)
            act["xb"][rows, :] = x[rows, :].astype(jnp.bfloat16)
            return carry

        lax.fori_loop(0, BLOCKS, cast, 0)
        save(layer, "xb")
        for name, word_mat, ent_mat in (("k", 4, None), ("v", 5, None), ("qw", 0, 2), ("qe", 1, 3)):
            free(name)
            gather.need(needs["mat", layer, word_mat if ent_mat is None else ent_mat])
            if ent_mat is None:
                project_rows(act[name], act["xb"], 0, LEN, 512, attn, 6 * layer + word_mat)
            else:
                project_rows(act[name], act["xb"], 0, WORDS, 448, attn, 6 * layer + word_mat)
                project_rows(act[name], act["xb"], WORDS, ENT_LEN, ENT_LEN, attn, 6 * layer + ent_mat)
            save(layer, name)
            gather.tick()
        free("o")
        free("stats")
        for head_pair in range(act["o"].shape[1] // (2 * HEAD_DIM)):
            attend(act, head_pair)
            gather.tick()
        save(layer, "o")
        gather.need(needs["out", layer])
        for name in ("n1", "h1b"):
            free(name)

        def out_part(c, rows):
            return mm_rt(act["o"][rows, :], flat(outs, layer))

        def first_norm(c, rows, total):
            hat, scale = normed(x[rows, :] + total)
            act["n1"][rows, :] = hat.astype(jnp.bfloat16)
            act["stats"][rows, 8:9] = scale
            value = hat * gain[0] + gain[1]
            h1[rows, :] = value
            act["h1b"][rows, :] = value.astype(jnp.bfloat16)

        pair.run(out_part, first_norm, gather.tick)
        save(layer, "n1")
        save(layer, "h1b")
        gather.need(needs["up", layer, 1])
        for name in ("g", "slope", "n2"):
            free(name)
        hidden = act["g"].shape[1]
        tile = 512

        def up_block(c):
            rows = pl.ds(c * BLOCK, BLOCK)
            for first in range(0, hidden, tile):
                cols = slice(first, first + tile)
                weight = ups[layer, :, :, :, :, cols].reshape(D, tile)
                value, slope = gelu_parts(mm(act["h1b"][rows, :], weight))
                act["g"][rows, cols] = value.astype(jnp.bfloat16)
                act["slope"][rows, cols] = slope.astype(jnp.bfloat16)

        for c in range(BLOCKS):
            up_block(c)
            gather.tick()
        save(layer, "g")
        save(layer, "slope")
        gather.need(needs["down", layer, 1])

        def down_part(c, rows):
            return mm_rt(act["g"][rows, :], flat(downs, layer))

        def second_norm(c, rows, total):
            hat, scale = normed(h1[rows, :] + total)
            act["n2"][rows, :] = hat.astype(jnp.bfloat16)
            act["stats"][rows, 9:10] = scale
            x[rows, :] = hat * gain[2] + gain[3]

        pair.run(down_part, second_norm, gather.tick)
        save(layer, "n2")
        save(layer, "stats")
    ents_out[...] = x[WORDS:]
    gains_out[...] = gains[...]
    gather.close()
    for name in list(saving):
        free(name)


KINDS = ("attn", "out", "up", "down", "proj", "head", "norms")


MAT_ORDER = (4, 5, 0, 2, 1, 3)


def gather_plan(hidden):
    every = slice(None)
    chunks = [(6, pl.ds(0, 1), every, True), (4, pl.ds(0, 1), every, False)]
    needs = {"kinds": KINDS, "norms": 0, "proj": 1}
    y_first = [True]

    def add(name, which, row, cols):
        chunks.append((which, pl.ds(row, 1), cols, y_first[0]))
        y_first[0] = not y_first[0]
        needs[name] = len(chunks) - 1

    for layer in range(LAYERS):
        for mat in MAT_ORDER:
            add(("mat", layer, mat), 0, 6 * layer + mat, every)
        add(("out", layer), 1, layer, every)
        for which, name in ((2, "up"), (3, "down")):
            for part in range(2):
                add((name, layer, part), which, layer, pl.ds(part * (hidden // 2), hidden // 2))
    add("head", 5, 0, every)
    return chunks, needs


def run_forward(dims, words, base, entity_rows, shards, collective_id):
    half, hidden = shards[0].shape[-1], shards[2].shape[-1]
    chunks, needs = gather_plan(hidden)
    shapes = saved_shapes(half, hidden)
    low, full = jnp.bfloat16, jnp.float32
    wholes = [(s.shape[0], *dims, *s.shape[1:]) for s in shards]
    copies = dims[0] + 2 * max(dims[1:])
    saved_out = [jax.ShapeDtypeStruct(*shapes[name]) for _ in range(LAYERS) for name in SAVED]
    result = pl.pallas_call(
        functools.partial(forward_body, dims, chunks, needs),
        out_shape=[jax.ShapeDtypeStruct(shape, low) for shape in wholes]
        + saved_out
        + [jax.ShapeDtypeStruct((ENT_LEN, D), full), jax.ShapeDtypeStruct((16, D), full)],
        in_specs=[VMEM] * 3 + [ANY] * len(shards),
        out_specs=[ANY] * (len(wholes) + len(saved_out)) + [VMEM] * 2,
        scratch_shapes=[pltpu.VMEM(shape, low) for shape in wholes]
        + [pltpu.VMEM(*shapes[name]) for name in SAVED]
        + [
            pltpu.VMEM((LEN, D), full),
            pltpu.VMEM((LEN, D), full),
            pltpu.VMEM((16, D), full),
            pltpu.VMEM((BLOCKS, BLOCK, D), low),
            pltpu.VMEM((2, BLOCKS, BLOCK, D), low),
            pltpu.SemaphoreType.DMA((len(chunks), copies)),
            pltpu.SemaphoreType.DMA((len(chunks), copies)),
            pltpu.SemaphoreType.DMA((len(chunks),)),
            pltpu.SemaphoreType.DMA((len(chunks),)),
            pltpu.SemaphoreType.DMA((2 * LAYERS, BLOCKS)),
            pltpu.SemaphoreType.DMA((2 * LAYERS, BLOCKS)),
            pltpu.SemaphoreType.DMA((LAYERS * len(SAVED),)),
        ],
        compiler_params=pltpu.CompilerParams(
            collective_id=collective_id, has_side_effects=True, vmem_limit_bytes=VMEM_BYTES
        ),
    )(words, base, entity_rows, *shards)
    kept = result[: len(wholes)]
    saved = [
        dict(zip(SAVED, result[len(wholes) + layer * len(SAVED) :][: len(SAVED)]))
        for layer in range(LAYERS)
    ]
    return kept, saved, *result[-2:]


def norm_back(grad, hat, scale, gain_row):
    hat = hat.astype(jnp.float32)
    wide = grad * gain_row
    inner = jnp.mean(wide * hat, axis=-1, keepdims=True)
    back = scale * (wide - jnp.mean(wide, axis=-1, keepdims=True) - hat * inner)
    gain_part = jnp.sum(grad * hat, axis=0, keepdims=True)
    return back, gain_part, jnp.sum(grad, axis=0, keepdims=True)


class Sums:
    def __init__(self, dims, units, buffers, totals, sems, free_sem):
        self.dims, self.units, self.totals = dims, units, totals
        self.buffers = buffers
        self.send_sem, self.recv_sem = sems
        self.free_sem = free_sem
        self.spot = place(dims)
        self.peers = [axis_peers(dims, axis) for axis in range(3)]
        self.queue, self.done = [], set()
        self.least = 2

    def group(self, stage, y_first):
        return self.peers[((1, 2, 0) if y_first else (2, 1, 0))[stage]]

    def start(self, stage, u):
        slot, y_first, turn = self.units[u]
        part, first, second, third = self.buffers[slot]
        z, y, x = self.spot
        group = self.group(stage, y_first)
        if turn and group:
            pl.semaphore_wait(self.free_sem.at[slot, stage], len(group))
        copies = []
        base = (0, max(self.dims[1:]), 2 * max(self.dims[1:]))[stage]
        for k, (spot, target) in enumerate(group):
            if stage == 0:
                src = part.at[:, spot] if y_first else part.at[:, :, spot]
                dst = first.at[k]
            elif stage == 1:
                src = part.at[:, y, spot] if y_first else part.at[:, spot, x]
                dst = second.at[k]
            else:
                src, dst = part.at[spot, y, x], third.at[k]
            sems = self.send_sem.at[u, base + k], self.recv_sem.at[u, base + k]
            copies.append(send(src, dst, *sems, target))
        self.queue.append((stage, u, copies))

    def advance(self):
        stage, u, copies = self.queue.pop(0)
        slot, y_first, turn = self.units[u]
        part, first, second, third = self.buffers[slot]
        z, y, x = self.spot
        for copy in copies:
            copy.wait()
        group = self.group(stage, y_first)
        across = self.dims[2] if y_first else self.dims[1]
        if stage == 0 and group:

            def add_first(i, carry):
                a, b = i // across, i % across
                at = (a, y, b) if y_first else (a, b, x)
                value = part[at].astype(jnp.float32)
                for k in range(len(group)):
                    value += first[k, a, b].astype(jnp.float32)
                part[at] = value.astype(part.dtype)
                return carry

            lax.fori_loop(0, self.dims[0] * across, add_first, 0)
        if stage == 1 and group:

            def add_second(i, carry):
                value = part[i, y, x].astype(jnp.float32)
                for k in range(len(group)):
                    value += second[k, i].astype(jnp.float32)
                part[i, y, x] = value.astype(part.dtype)
                return carry

            lax.fori_loop(0, self.dims[0], add_second, 0)
        if stage == 2:
            value = part[z, y, x].astype(jnp.float32)
            for k in range(len(group)):
                value += third[k].astype(jnp.float32)
            self.totals[u][...] = value
            self.done.add(u)
        if self.reused(u):
            for _, target in group:
                pl.semaphore_signal(
                    self.free_sem.at[slot, stage], inc=1, device_id=target, device_id_type=MESH
                )
        if stage < 2:
            self.start(stage + 1, u)

    def reused(self, u):
        slot, _, turn = self.units[u]
        return not turn and sum(unit[0] == slot for unit in self.units) > 1

    def tick(self):
        if len(self.queue) > self.least:
            self.advance()

    def need(self, u):
        while u not in self.done:
            self.advance()

    def close(self):
        while self.queue:
            self.advance()


UNITS = ("down0", "down1", "up0", "up1", "out", "words", "ents", "key", "value")
EXTRA = ("head", "proj", "norms")
UNIT_FIRST = dict(
    down0=True, down1=False, up0=True, up1=False, out=True, words=True, ents=False, key=True,
    value=False, head=True, proj=False, norms=True,
)


def sum_plan():
    names = ["head"]
    for layer in reversed(range(LAYERS)):
        names += [(layer, name) for name in UNITS]
    names += ["proj", "norms"]
    return names


def unit_width(name, half, hidden):
    return {
        "down0": hidden // 2, "down1": hidden // 2, "up0": hidden // 2, "up1": hidden // 2,
        "out": half, "words": 2 * half, "ents": 2 * half, "key": half, "value": half,
    }[name]


def backward_body(dims, names, half, hidden, *refs):
    refs = list(refs)

    def take(count):
        part = refs[:count]
        del refs[:count]
        return part

    cotangent, grad_ents, grad_head, gains, entity_rows = take(5)
    w_attn, w_out, w_up, w_down, w_proj = take(5)
    saved = [dict(zip(SAVED, take(len(SAVED)))) for _ in range(LAYERS)]
    word_grads, row_grads = take(2)
    totals = take(len(names))
    slots = list(UNITS + EXTRA)
    buffers = [take(4) for _ in slots]
    left, right, hat, xh, o, stats, stats_t = take(7)
    mat_wide, mat_out, mat_attn, mat_proj = take(4)
    gacc, glow, gmix, delta, dk_acc, dv_acc, gnorm = take(7)
    mine, theirs = take(2)
    sum_sems = take(2)
    (free_sem,) = take(1)
    pair_sems = take(2)
    (load_sem,) = take(1)

    units = []
    for name in names:
        kind = name if isinstance(name, str) else name[1]
        turn = not isinstance(name, str) and name[0] < LAYERS - 1
        units.append((slots.index(kind), UNIT_FIRST[kind], turn))
    sums = Sums(dims, units, buffers, totals, sum_sems, free_sem)
    pair = Pair(mine, theirs, pair_sems)
    greet([target for group in sums.peers for _, target in group] + [pair.other])
    part_of = {slot: buffers[i][0] for i, slot in enumerate(slots)}
    loads, counter = {}, [0]

    def load(key, src, dst):
        copy = pltpu.make_async_copy(src, dst, load_sem.at[counter[0]])
        counter[0] += 1
        copy.start()
        loads.setdefault(key, []).append(copy)

    def ready(key):
        for copy in loads.pop(key, []):
            copy.wait()

    def tick(times=1):
        for _ in range(times):
            sums.tick()

    def begin_layer(layer):
        s = saved[layer]
        load("n2", s["n2"], hat)
        load("stats", s["stats"], stats)
        load("g", s["g"], left)
        load("down", w_down.at[layer], mat_wide)
        load("slope", s["slope"], right)
        load("h1b", s["h1b"], xh)
        load("out", w_out.at[layer], mat_out)
        load("o", s["o"], o)
        load("attn", w_attn.at[pl.ds(6 * layer, 6)], mat_attn)

    begin_layer(LAYERS - 1)
    load("proj", w_proj.at[0], mat_proj)
    slab = 2 if dims[0] % 2 == 0 else 1
    height = slab * D // dims[0]

    def fill(name, lhs, rhs, rhs_cols, row_slice=slice(None)):
        part = part_of[name]
        width = part.shape[-1]

        def block(i, carry):
            cols = pl.ds(pl.multiple_of(i * height, 128), height)
            value = mm_lt(lhs[row_slice, cols], rhs[row_slice, rhs_cols])
            shape = (slab, dims[1], dims[2], part.shape[3], width)
            part[pl.ds(i * slab, slab)] = value.astype(jnp.bfloat16).reshape(shape)
            return carry

        lax.fori_loop(0, dims[0] // slab, block, 0)

    def submit(layer, name):
        sums.start(0, names.index((layer, name)))

    head_part = part_of["head"]
    head_part[...] = grad_head[...]
    sums.start(0, names.index("head"))
    gacc[:WORDS] = cotangent[...].astype(jnp.float32)
    gacc[WORDS:] = grad_ents[...]
    gnorm[...] = jnp.zeros_like(gnorm)

    def add_norm(row, value):
        gnorm[row : row + 1, :] += value

    for layer in reversed(range(LAYERS)):
        last = layer == LAYERS - 1
        gain = [gains[4 * layer + i : 4 * layer + i + 1, :] for i in range(4)]
        ready("n2")
        ready("stats")

        def late_norm(c, carry):
            rows = pl.ds(c * BLOCK, BLOCK)
            back, gain_part, shift_part = norm_back(
                gacc[rows, :], hat[rows, :], stats[rows, 9:10], gain[2]
            )
            gacc[rows, :] = back
            glow[rows, :] = back.astype(jnp.bfloat16)
            add_norm(4 * layer + 2, gain_part)
            add_norm(4 * layer + 3, shift_part)
            return carry

        lax.fori_loop(0, BLOCKS, late_norm, 0)
        load("n1", saved[layer]["n1"], hat)
        ready("g")
        for i in range(2):
            if not last:
                sums.need(names.index((layer + 1, "down%d" % i)))
            cols = slice(i * (hidden // 2), (i + 1) * (hidden // 2))
            fill("down%d" % i, glow, left, cols)
            submit(layer, "down%d" % i)
            tick()
        ahead = saved[layer]
        for i, name in enumerate(("k", "qw", "qe", "v")):
            load("qkv", ahead[name], left.at[:, pl.ds(i * half, half)])
        ready("down")
        ready("slope")

        def inner(c, carry):
            rows = pl.ds(c * BLOCK, BLOCK)
            for first in range(0, hidden, 512):
                cols = slice(first, first + 512)
                weight = mat_wide[:, :, :, :, cols].reshape(D, 512)
                value = mm(glow[rows, :], weight) * right[rows, cols].astype(jnp.float32)
                right[rows, cols] = value.astype(jnp.bfloat16)
            return carry

        lax.fori_loop(0, BLOCKS, inner, 0)
        tick()
        load("up", w_up.at[layer], mat_wide)
        ready("h1b")
        for i in range(2):
            if not last:
                sums.need(names.index((layer + 1, "up%d" % i)))
            cols = slice(i * (hidden // 2), (i + 1) * (hidden // 2))
            fill("up%d" % i, xh, right, cols)
            submit(layer, "up%d" % i)
            tick()
        load("xb", saved[layer]["xb"], xh)
        ready("up")
        ready("n1")

        def up_part(c, rows):
            return mm_rt(right[rows, :], flat(mat_wide))

        def early_norm(c, rows, total):
            back, gain_part, shift_part = norm_back(
                gacc[rows, :] + total, hat[rows, :], stats[rows, 8:9], gain[0]
            )
            gacc[rows, :] = back
            glow[rows, :] = back.astype(jnp.bfloat16)
            add_norm(4 * layer, gain_part)
            add_norm(4 * layer + 1, shift_part)

        pair.run(up_part, early_norm, tick)
        ready("o")
        ready("out")
        if not last:
            sums.need(names.index((layer + 1, "out")))
        fill("out", glow, o, slice(None))
        submit(layer, "out")

        def mixed(c, carry):
            rows = pl.ds(c * BLOCK, BLOCK)
            gmix[rows, :] = mm(glow[rows, :], flat(mat_out)).astype(jnp.bfloat16)
            stats_t[:, rows] = stats[rows, :].T
            return carry

        lax.fori_loop(0, BLOCKS, mixed, 0)
        tick()
        ready("qkv")
        for head_pair in range(half // (2 * HEAD_DIM)):
            lo = head_pair * 2 * HEAD_DIM
            lanes = slice(lo, lo + 2 * HEAD_DIM)
            k_lanes, qw_lanes, qe_lanes, v_lanes = [
                slice(j * half + lo, j * half + lo + 2 * HEAD_DIM) for j in range(4)
            ]

            def products(c, carry):
                rows = pl.ds(c * BLOCK, BLOCK)
                both = gmix[rows, lanes].astype(jnp.float32) * o[rows, lanes].astype(jnp.float32)
                turned = both.T
                delta[0:1, rows] = jnp.sum(turned[:HEAD_DIM], axis=0, keepdims=True)
                delta[1:2, rows] = jnp.sum(turned[HEAD_DIM:], axis=0, keepdims=True)
                return carry

            lax.fori_loop(0, BLOCKS, products, 0)
            dk_acc[...] = jnp.zeros_like(dk_acc)
            dv_acc[...] = jnp.zeros_like(dv_acc)

            def block(i, carry):
                rows = pl.ds(i * BLOCK, BLOCK)
                keys, values = left[:, k_lanes], left[:, v_lanes]
                grad_qw = grad_qe = None
                for which in range(2):
                    head = 2 * head_pair + which
                    q_mask, k_mask = lane_mask(BLOCK, which), lane_mask(LEN, which)
                    query_w = left[rows, qw_lanes] * q_mask
                    query_e = left[rows, qe_lanes] * q_mask
                    grad_o = gmix[rows, lanes] * q_mask
                    log_row = stats_t[head : head + 1, rows]
                    inner_row = delta[which : which + 1, rows]
                    own_keys = keys * k_mask
                    for span, query in ((slice(0, WORDS), query_w), (slice(WORDS, LEN), query_e)):
                        prob = jnp.exp2(mm_rt(keys[span], query) * SCORE_STEP - log_row)
                        grad_prob = mm_rt(values[span], grad_o)
                        dv_acc[span, :] += mm(prob.astype(jnp.bfloat16), grad_o)
                        grad_score = (prob * (grad_prob - inner_row)).astype(jnp.bfloat16)
                        dk_acc[span, :] += mm(grad_score, query)
                        part = mm_lt(grad_score, own_keys[span])
                        if span.start == 0:
                            grad_qw = part if grad_qw is None else grad_qw + part
                        else:
                            grad_qe = part if grad_qe is None else grad_qe + part
                right[rows, lanes] = (grad_qw * 0.125).astype(jnp.bfloat16)
                right[rows, half + lo : half + lo + 2 * HEAD_DIM] = (grad_qe * 0.125).astype(
                    jnp.bfloat16
                )
                return carry

            for first in range(0, BLOCKS, 2):
                lax.fori_loop(first, first + 2, block, 0)
                tick()
            at = 2 * half + lo
            right[:, at : at + 2 * HEAD_DIM] = (dk_acc[...] * 0.125).astype(jnp.bfloat16)
            at = 3 * half + lo
            right[:, at : at + 2 * HEAD_DIM] = dv_acc[...].astype(jnp.bfloat16)
        ready("xb")
        words, ents = slice(0, WORDS), slice(WORDS, LEN)
        for name, cols, rows in (
            ("words", slice(0, 2 * half), words),
            ("ents", slice(0, 2 * half), ents),
            ("key", slice(2 * half, 3 * half), slice(None)),
            ("value", slice(3 * half, 4 * half), slice(None)),
        ):
            if not last:
                sums.need(names.index((layer + 1, name)))
            fill(name, xh, right, cols, rows)
            submit(layer, name)
            tick()
        ready("attn")
        mats = [slice(j * half, (j + 1) * half) for j in range(4)]

        def input_part(c, rows):
            total = mm_rt(right[rows, mats[2]], flat(mat_attn, 4))
            total += mm_rt(right[rows, mats[3]], flat(mat_attn, 5))
            start = c * BLOCK
            edge = min(max(WORDS - start, 0), BLOCK)
            pieces = []
            for low, high, pick in ((0, edge, (0, 1)), (edge, BLOCK, (2, 3))):
                if high > low:
                    span = slice(start + low, start + high)
                    piece = mm_rt(right[span, mats[0]], flat(mat_attn, pick[0]))
                    pieces.append(piece + mm_rt(right[span, mats[1]], flat(mat_attn, pick[1])))
            return total + (pieces[0] if len(pieces) == 1 else jnp.concatenate(pieces, axis=0))

        def to_input(c, rows, total):
            gacc[rows, :] += total

        pair.run(input_part, to_input, tick)
        if layer:
            begin_layer(layer - 1)
    ready("proj")
    leaving = pltpu.make_async_copy(gacc.at[pl.ds(0, WORDS)], word_grads, load_sem.at[counter[0]])
    leaving.start()
    grad_entity = gacc[WORDS:].astype(jnp.bfloat16)
    proj_part = part_of["proj"]
    proj_part[...] = mm_lt(entity_rows[...], grad_entity).astype(jnp.bfloat16).reshape(proj_part.shape)
    sums.start(0, names.index("proj"))
    count = dims[0] * dims[1] * dims[2]
    width = D // count
    norm_low = gnorm[...].astype(jnp.bfloat16)
    for d in range(count):
        z, rest = d // (dims[1] * dims[2]), d % (dims[1] * dims[2])
        row = lax.broadcasted_iota(jnp.int32, (128, D), 0)
        lane = lax.broadcasted_iota(jnp.int32, (128, D), 1)
        hot = jnp.where((row + d * width == lane) & (row < width), 1.0, 0.0).astype(jnp.bfloat16)
        block = mm_rt(norm_low, hot).astype(jnp.bfloat16)
        part_of["norms"][z, rest // dims[2], rest % dims[2]] = block
    sums.start(0, names.index("norms"))
    row_grads[...] = mm_rt(grad_entity, flat(mat_proj))
    sums.close()
    leaving.wait()


def run_backward(dims, cotangent, grad_ents, grad_head, gains, entity_rows, kept, saved, collective_id):
    names = sum_plan()
    half, hidden = kept[0].shape[-1], kept[2].shape[-1]
    low, full = jnp.bfloat16, jnp.float32
    rows = kept[0].shape[4]
    blocks = {name: (rows, unit_width(name, half, hidden)) for name in UNITS}
    blocks["head"] = (rows, kept[5].shape[-1])
    blocks["proj"] = (kept[4].shape[4], D)
    blocks["norms"] = (16, 128)
    scratch = []
    for name in UNITS + EXTRA:
        y_first = UNIT_FIRST[name]
        own = (dims[0], dims[2] if y_first else dims[1])
        turns = (dims[1], dims[2]) if y_first else (dims[2], dims[1])
        block = blocks[name]
        scratch += [
            pltpu.VMEM((*dims, *block), low),
            pltpu.VMEM((max(turns[0] - 1, 1), *own, *block), low),
            pltpu.VMEM((max(turns[1] - 1, 1), dims[0], *block), low),
            pltpu.VMEM((max(dims[0] - 1, 1), *block), low),
        ]
    copies = dims[0] + 2 * max(dims[1:])
    kinds = [name if isinstance(name, str) else name[1] for name in names]
    inputs = [cotangent, grad_ents, grad_head, gains, entity_rows, *kept[:5]]
    inputs += [saved[layer][name] for layer in range(LAYERS) for name in SAVED]
    result = pl.pallas_call(
        functools.partial(backward_body, dims, names, half, hidden),
        out_shape=[
            jax.ShapeDtypeStruct((WORDS, D), full),
            jax.ShapeDtypeStruct((ENT_LEN, kept[5].shape[-1]), full),
        ]
        + [jax.ShapeDtypeStruct(blocks[kind], full) for kind in kinds],
        in_specs=[VMEM] * 5 + [ANY] * (len(inputs) - 5),
        out_specs=[ANY] + [VMEM] * (1 + len(names)),
        scratch_shapes=scratch
        + [
            pltpu.VMEM((LEN, hidden), low),
            pltpu.VMEM((LEN, hidden), low),
            pltpu.VMEM((LEN, D), low),
            pltpu.VMEM((LEN, D), low),
            pltpu.VMEM((LEN, half), low),
            pltpu.VMEM((LEN, 128), full),
            pltpu.VMEM((128, LEN), full),
            pltpu.VMEM(kept[2].shape[1:], low),
            pltpu.VMEM(kept[1].shape[1:], low),
            pltpu.VMEM((6, *kept[0].shape[1:]), low),
            pltpu.VMEM(kept[4].shape[1:], low),
            pltpu.VMEM((LEN, D), full),
            pltpu.VMEM((LEN, D), low),
            pltpu.VMEM((LEN, half), low),
            pltpu.VMEM((8, LEN), full),
            pltpu.VMEM((LEN, 2 * HEAD_DIM), full),
            pltpu.VMEM((LEN, 2 * HEAD_DIM), full),
            pltpu.VMEM((16, D), full),
            pltpu.VMEM((BLOCKS, BLOCK, D), low),
            pltpu.VMEM((2, BLOCKS, BLOCK, D), low),
            pltpu.SemaphoreType.DMA((len(names), copies)),
            pltpu.SemaphoreType.DMA((len(names), copies)),
            pltpu.SemaphoreType.REGULAR((len(UNITS + EXTRA), 3)),
            pltpu.SemaphoreType.DMA((2 * LAYERS, BLOCKS)),
            pltpu.SemaphoreType.DMA((2 * LAYERS, BLOCKS)),
            pltpu.SemaphoreType.DMA((64,)),
        ],
        compiler_params=pltpu.CompilerParams(
            collective_id=collective_id, has_side_effects=True, vmem_limit_bytes=VMEM_BYTES
        ),
    )(*inputs)
    return result[0], result[1], dict(zip(names, result[2:]))


def padded_rows(values):
    extra = -values.shape[-2] % 16
    return jnp.pad(values, [(0, 0)] * (values.ndim - 2) + [(0, extra), (0, 0)])


def weight_shards(attention_in, attention_out, feed_up, feed_down, norm_params, entity_proj, head_proj):
    def turned(values):
        return jnp.swapaxes(values, 1, 2)

    mats = attention_in.reshape(-1, *attention_in.shape[2:])
    norms = norm_params.reshape(1, -1, norm_params.shape[-1])
    norms = jnp.pad(norms, [(0, 0), (0, 16 - norms.shape[1]), (0, -norms.shape[2] % 128)])
    sources = [mats, turned(attention_out), feed_up, turned(feed_down), entity_proj[None], head_proj[None]]
    heights = [part.shape[1] for part in sources]
    shards = [padded_rows(part.astype(jnp.bfloat16)) for part in sources]
    shards.append(norms.astype(jnp.bfloat16))
    return shards, heights


def unpack_weights(wholes, heights, norm_width):
    kept = []
    for part, height in zip(wholes, heights):
        part = part[..., :height, :]
        kept.append(part.reshape(part.shape[0], -1, part.shape[-1]))
    norm_all = wholes[6][0].reshape(-1, 16, wholes[6].shape[-1])[:, : LAYERS * 4, :norm_width]
    norm_all = jnp.swapaxes(norm_all, 0, 1).reshape(LAYERS, 4, -1)
    return (
        kept[0].reshape(LAYERS, 6, *kept[0].shape[1:]),
        kept[1],
        kept[2],
        kept[3],
        norm_all,
        kept[4][0],
        kept[5][0],
    )


def gather_apart(dims, shards):
    chunks = [(4, 0, 1, True), (5, 0, 1, False), (6, 0, 1, True)]
    for layer in range(LAYERS):
        chunks += [(0, 6 * layer, 3, True), (0, 6 * layer + 3, 3, False)]
        chunks += [(1, layer, 1, layer == 0), (2, layer, 1, True), (3, layer, 1, False)]
    return gather_weights(dims, shards, chunks, 1)


def sum_all(dims, layer_grads, grad_proj, grad_head):
    n_dp = dims[0] * dims[1] * dims[2]

    def blocks(values):
        cut = values.astype(jnp.bfloat16).reshape(*dims, values.shape[0] // n_dp, values.shape[1])
        return padded_rows(cut)

    parts, flags, heights = [], [], []
    for layer in reversed(range(LAYERS)):
        (words_mat, ents_mat, shared_mat), out_mat, up_mat, down_mat, _ = layer_grads[layer]
        late = layer % 2 == 0
        for values, y_first in (
            (up_mat, True),
            (down_mat, False),
            (words_mat, True),
            (ents_mat, False),
            (shared_mat, late),
            (out_mat, not late),
        ):
            parts.append(blocks(values))
            flags.append(y_first)
            heights.append(values.shape[0] // n_dp)
    for values, y_first in ((grad_proj, True), (grad_head, False)):
        parts.append(blocks(values))
        flags.append(y_first)
        heights.append(values.shape[0] // n_dp)
    norms = jnp.concatenate([layer_grads[layer][4] for layer in range(LAYERS)], axis=0)
    width = norms.shape[1] // n_dp
    norms = jnp.swapaxes(norms.reshape(norms.shape[0], n_dp, width), 0, 1)
    norms = jnp.pad(norms, [(0, 0), (0, 16 - norms.shape[1]), (0, -width % 128)])
    parts.append(norms.astype(jnp.bfloat16).reshape(*dims, *norms.shape[1:]))
    flags.append(True)
    totals = sum_gradients(dims, parts, flags, 2)
    norm_sum = totals[-1][: LAYERS * 4, :width].reshape(LAYERS, 4, width)
    totals = [total[:height] for total, height in zip(totals, heights)]
    attn, outs, ups, downs = [], [], [], []
    for layer in range(LAYERS):
        at = 6 * (LAYERS - 1 - layer)
        ups.append(totals[at])
        downs.append(totals[at + 1].T)
        for part in totals[at + 2 : at + 5]:
            half = part.shape[1] // 2
            attn += [part[:, :half], part[:, half:]]
        outs.append(totals[at + 5].T)
    attn = jnp.stack(attn)
    return (
        attn.reshape(LAYERS, 6, *attn.shape[1:]),
        jnp.stack(outs),
        jnp.stack(ups),
        jnp.stack(downs),
        norm_sum,
        totals[-2],
        totals[-1],
    )


def fused_sums(totals, width):
    layers = range(LAYERS)

    def halves(name):
        parts = [totals[layer, name] for layer in layers]
        cut = parts[0].shape[1] // 2
        return [[part[:, :cut], part[:, cut:]] for part in parts]

    words, ents = halves("words"), halves("ents")
    attn = jnp.stack(
        [
            jnp.stack(words[layer] + ents[layer] + [totals[layer, "key"], totals[layer, "value"]])
            for layer in layers
        ]
    )
    ups = jnp.stack([jnp.concatenate([totals[i, "up0"], totals[i, "up1"]], axis=1) for i in layers])
    downs = jnp.stack(
        [jnp.concatenate([totals[i, "down0"], totals[i, "down1"]], axis=1).T for i in layers]
    )
    outs = jnp.stack([totals[i, "out"].T for i in layers])
    norms = totals["norms"][: LAYERS * 4, :width].reshape(LAYERS, 4, width)
    return attn, outs, ups, downs, norms, totals["proj"], totals["head"]


def on_device(
    word_inputs,
    entity_base,
    entity_ids,
    buckets,
    mask_positions,
    targets,
    word_cotangent,
    attention_in,
    attention_in_first,
    attention_in_second,
    attention_out,
    attention_out_first,
    attention_out_second,
    feed_up,
    feed_up_first,
    feed_up_second,
    feed_down,
    feed_down_first,
    feed_down_second,
    norm_params,
    norm_params_first,
    norm_params_second,
    entity_proj,
    entity_proj_first,
    entity_proj_second,
    head_proj,
    head_proj_first,
    head_proj_second,
    entity_table,
    entity_table_first,
    entity_table_second,
):
    dims = chip_grid(lax.axis_size("dp"))
    shards, heights = weight_shards(
        attention_in, attention_out, feed_up, feed_down, norm_params, entity_proj, head_proj
    )
    fused = heights[0] % 16 == 0 and heights[4] % 16 == 0
    slot_total = entity_ids.shape[0]
    shard_rows = entity_table.shape[0]
    bucket_rows = buckets.reshape(buckets.shape[2], buckets.shape[3])
    filled = bucket_rows >= 0
    safe_slot = jnp.maximum(bucket_rows, 0)
    request = jnp.where(filled, entity_ids[safe_slot] % shard_rows, -1)
    received = lax.all_to_all(request, "dp", split_axis=0, concat_axis=0, tiled=True)
    shard_base = lax.axis_index(("dp", "mp")) * shard_rows
    owned_mask = received >= 0
    safe_row = jnp.clip(received, 0, shard_rows - 1)
    table_low = entity_table.astype(jnp.bfloat16)
    replies = jnp.where(owned_mask[:, :, None], table_low[safe_row], jnp.zeros((), jnp.bfloat16))
    replied_rows_result = lax.all_to_all(replies, "dp", split_axis=0, concat_axis=0, tiled=True)
    row_placement_plan = (
        bucket_rows[:, :, None] == jnp.arange(slot_total, dtype=jnp.int32)[None, None, :]
    ).astype(jnp.bfloat16)
    local_shard_rows = jnp.einsum(
        "wvt,wvi->ti", row_placement_plan, replied_rows_result, preferred_element_type=jnp.float32
    )
    paired = pair_sum(local_shard_rows)
    masked_slots = (
        jnp.arange(SEQ_DEV, dtype=jnp.int32)[:, None] * ENT_LEN + mask_positions
    ).reshape(-1)
    keep_weight = 1.0 - jnp.any(
        jnp.arange(slot_total, dtype=jnp.int32)[:, None] == masked_slots[None, :], axis=1
    ).astype(jnp.float32)
    entity_rows = (paired * keep_weight[:, None]).astype(jnp.bfloat16)
    if fused:
        wholes, saved_layers, ents, gain_rows = run_forward(
            dims, word_inputs, entity_base, entity_rows, shards, 6
        )
    else:
        wholes = gather_apart(dims, shards)
        attn_low, out_low, up_low, down_low, norm_low, proj_low, head_low = unpack_weights(
            wholes, heights, norm_params.shape[-1]
        )
        gain_all = norm_low.astype(jnp.float32)
        entity_inputs = entity_base.astype(jnp.float32) + jnp.dot(
            entity_rows, proj_low, preferred_element_type=jnp.float32
        )
        hidden = jnp.concatenate(
            [
                word_inputs.astype(jnp.float32).reshape(SEQ_DEV, WORDS, D),
                entity_inputs.reshape(SEQ_DEV, ENT_LEN, D),
            ],
            axis=1,
        )
        saved_layers = []
        for layer_index in range(LAYERS):
            hidden, saved_acts = layer_forward(
                hidden,
                attn_low[layer_index],
                out_low[layer_index],
                up_low[layer_index],
                down_low[layer_index],
                gain_all[layer_index],
            )
            saved_layers.append(saved_acts)
        ents = hidden[0, WORDS:]
    if fused:
        head_low = wholes[5].reshape(-1, wholes[5].shape[-1])
    seq_index = jnp.arange(SEQ_DEV, dtype=jnp.int32)[:, None]
    masked_rows = WORDS + mask_positions
    masked_low = ents[mask_positions.reshape(-1)].astype(jnp.bfloat16)
    head_pre = jnp.dot(masked_low, head_low, preferred_element_type=jnp.float32)
    states_low = gelu_exact(head_pre).astype(jnp.bfloat16)
    all_states = spread(states_low, False, False, 3).reshape(-1, states_low.shape[1])
    logits = lax.dot_general(
        all_states, table_low, (((1,), (1,)), ((), ())), preferred_element_type=jnp.float32
    )
    flat_targets = targets.reshape(-1)
    target_hits = (
        jnp.arange(shard_rows, dtype=jnp.int32)[None, :] == (flat_targets - shard_base)[:, None]
    )
    peak_value = jnp.max(logits, axis=1)
    exp_total = jnp.sum(jnp.exp(logits - peak_value[:, None]), axis=1)
    picked = jnp.sum(jnp.where(target_hits, logits, 0.0), axis=1)
    shares = spread(jnp.stack([peak_value, exp_total, picked]), True, False, 4)
    peak_all = jnp.max(shares[:, 0], axis=0)
    total_all = jnp.sum(shares[:, 1] * jnp.exp(shares[:, 0] - peak_all), axis=0)
    picked_all = jnp.sum(shares[:, 2], axis=0)
    log_norm = peak_all + jnp.log(total_all)
    row_losses = log_norm - picked_all
    prob_rows = jnp.exp(logits - log_norm[:, None])
    grad_logits = ((prob_rows - target_hits.astype(jnp.float32)) / flat_targets.shape[0]).astype(
        jnp.bfloat16
    )
    grad_table = lax.dot_general(
        grad_logits, all_states, (((0,), (0,)), ((), ())), preferred_element_type=jnp.float32
    )
    grad_states = jnp.dot(grad_logits, table_low, preferred_element_type=jnp.float32)
    grad_states = grad_states.reshape(lax.axis_size("dp"), -1, grad_states.shape[1])
    grad_states = jnp.sum(spread(grad_states, False, True, 5), axis=0)
    grad_states = grad_states + lax.ppermute(grad_states, "mp", [(0, 1), (1, 0)])
    grad_head_pre = jax.vjp(gelu_exact, head_pre)[1](grad_states)[0].astype(jnp.bfloat16)
    grad_head = lax.dot_general(
        masked_low, grad_head_pre, (((0,), (0,)), ((), ())), preferred_element_type=jnp.float32
    )
    grad_masked = lax.dot_general(
        grad_head_pre, head_low, (((1,), (1,)), ((), ())), preferred_element_type=jnp.float32
    )
    if fused:
        hits = (
            jnp.arange(slot_total, dtype=jnp.int32)[:, None] == mask_positions.reshape(-1)[None, :]
        ).astype(jnp.float32)
        grad_ents = jnp.dot(hits, grad_masked, precision=lax.Precision.HIGHEST)
        word_grads, row_grads, totals = run_backward(
            dims,
            word_cotangent,
            grad_ents,
            grad_head.astype(jnp.bfloat16).reshape(*dims, -1, grad_head.shape[-1]),
            gain_rows,
            entity_rows,
            wholes,
            saved_layers,
            8,
        )
        row_gradient_block = row_grads * keep_weight[:, None]
        reduced = fused_sums(totals, norm_params.shape[-1])
    else:
        grad_hidden = jnp.concatenate(
            [
                word_cotangent.astype(jnp.float32).reshape(SEQ_DEV, WORDS, D),
                jnp.zeros((SEQ_DEV, ENT_LEN, D), jnp.float32),
            ],
            axis=1,
        )
        grad_hidden = grad_hidden.at[seq_index, masked_rows].add(
            grad_masked.reshape(SEQ_DEV, MASK_ENT, D)
        )
        kept_grads = []
        for layer_index in reversed(range(LAYERS)):
            grad_hidden, layer_grads = layer_backward(
                grad_hidden,
                saved_layers[layer_index],
                attn_low[layer_index],
                out_low[layer_index],
                up_low[layer_index],
                down_low[layer_index],
                gain_all[layer_index],
            )
            if layer_index == 0:
                word_grads = grad_hidden[:, :WORDS].reshape(SEQ_DEV * WORDS, D)
                grad_entity = grad_hidden[:, WORDS:].reshape(slot_total, D).astype(jnp.bfloat16)
                grad_proj = lax.dot_general(
                    entity_rows,
                    grad_entity,
                    (((0,), (0,)), ((), ())),
                    preferred_element_type=jnp.float32,
                )
                row_gradient_block = (
                    lax.dot_general(
                        grad_entity,
                        proj_low,
                        (((1,), (1,)), ((), ())),
                        preferred_element_type=jnp.float32,
                    )
                    * keep_weight[:, None]
                )
            kept_grads.insert(0, layer_grads)
        reduced = sum_all(dims, kept_grads, grad_proj, grad_head)
    outgoing = jnp.where(filled[:, :, None], row_gradient_block[safe_slot], 0.0)
    incoming = lax.all_to_all(
        outgoing.astype(jnp.bfloat16), "dp", split_axis=0, concat_axis=0, tiled=True
    ).astype(outgoing.dtype)
    grad_table = grad_table.at[safe_row].add(
        jnp.where(owned_mask[:, :, None], incoming, 0.0)
    )
    reduced_proj, reduced_head = reduced[5:]
    attn_new = adam_update(
        attention_in, attention_in_first, attention_in_second, reduced[0], kind_rates[0]
    )
    out_new = adam_update(
        attention_out, attention_out_first, attention_out_second, reduced[1], kind_rates[1]
    )
    up_new = adam_update(feed_up, feed_up_first, feed_up_second, reduced[2], kind_rates[2])
    down_new = adam_update(feed_down, feed_down_first, feed_down_second, reduced[3], kind_rates[3])
    norm_new = adam_update(
        norm_params, norm_params_first, norm_params_second, reduced[4], kind_rates[4]
    )
    proj_new = adam_update(
        entity_proj, entity_proj_first, entity_proj_second, reduced_proj, kind_rates[5]
    )
    head_new = adam_update(
        head_proj, head_proj_first, head_proj_second, reduced_head, kind_rates[6]
    )
    table_new = adam_update(
        entity_table, entity_table_first, entity_table_second, grad_table, kind_rates[7]
    )
    return (
        row_losses,
        word_grads,
        attn_new[0],
        attn_new[1],
        attn_new[2],
        out_new[0],
        out_new[1],
        out_new[2],
        up_new[0],
        up_new[1],
        up_new[2],
        down_new[0],
        down_new[1],
        down_new[2],
        norm_new[0],
        norm_new[1],
        norm_new[2],
        proj_new[0],
        proj_new[1],
        proj_new[2],
        head_new[0],
        head_new[1],
        head_new[2],
        table_new[0],
        table_new[1],
        table_new[2],
    )


def solution(mesh):
    in_specs = (
        P("dp", None),
        P("dp", None),
        P("dp"),
        P("dp", "mp", None, None),
        P("dp", None),
        P(),
        P("dp", None),
        P(None, None, "dp", "mp"),
        P(None, None, "dp", "mp"),
        P(None, None, "dp", "mp"),
        P(None, "mp", "dp"),
        P(None, "mp", "dp"),
        P(None, "mp", "dp"),
        P(None, "dp", "mp"),
        P(None, "dp", "mp"),
        P(None, "dp", "mp"),
        P(None, "mp", "dp"),
        P(None, "mp", "dp"),
        P(None, "mp", "dp"),
        P(None, None, "dp"),
        P(None, None, "dp"),
        P(None, None, "dp"),
        P("dp", None),
        P("dp", None),
        P("dp", None),
        P("dp", None),
        P("dp", None),
        P("dp", None),
        P(("dp", "mp"), None),
        P(("dp", "mp"), None),
        P(("dp", "mp"), None),
    )
    out_specs = (
        P(),
        P("dp", None),
        P(None, None, "dp", "mp"),
        P(None, None, "dp", "mp"),
        P(None, None, "dp", "mp"),
        P(None, "mp", "dp"),
        P(None, "mp", "dp"),
        P(None, "mp", "dp"),
        P(None, "dp", "mp"),
        P(None, "dp", "mp"),
        P(None, "dp", "mp"),
        P(None, "mp", "dp"),
        P(None, "mp", "dp"),
        P(None, "mp", "dp"),
        P(None, None, "dp"),
        P(None, None, "dp"),
        P(None, None, "dp"),
        P("dp", None),
        P("dp", None),
        P("dp", None),
        P("dp", None),
        P("dp", None),
        P("dp", None),
        P(("dp", "mp"), None),
        P(("dp", "mp"), None),
        P(("dp", "mp"), None),
    )
    return jax.shard_map(
        on_device, mesh=mesh, in_specs=in_specs, out_specs=out_specs, check_vma=False
    )
```

```python
import functools

import jax
import jax.numpy as jnp
from jax import lax
from jax.experimental import pallas as pl
from jax.experimental.pallas import tpu as pltpu
from jax.sharding import PartitionSpec as P

D = 768
HEAD_DIM = 64
WORDS = 896
ENT_LEN = 128
MASK_ENT = 16
LAYERS = 2
STEP = 10
SEQ_DEV = 1


norm_eps = 1e-05
beta_first = 0.9
beta_second = 0.999
adam_eps = 1e-12
weight_decay = 0.01
kind_rates = (0.05, 1.0, 0.05, 0.027, 0.75, 0.5, 0.05, 0.2)


MESH = pl.DeviceIdType.MESH
ANY = pl.BlockSpec(memory_space=pl.ANY)
VMEM = pl.BlockSpec(memory_space=pltpu.VMEM)
VMEM_BYTES = 60 * 2**20


def chip_grid(n_dp):
    return {16: (4, 2, 2), 64: (4, 4, 4)}.get(n_dp, (n_dp, 1, 1))


def place(dims):
    index = lax.axis_index("dp")
    return index // (dims[1] * dims[2]), index // dims[2] % dims[1], index % dims[2]


def axis_peers(dims, axis):
    here = place(dims)
    core = lax.axis_index("mp")
    peers = []
    for step in range(1, dims[axis]):
        spot = list(here)
        spot[axis] = lax.rem(here[axis] + step, dims[axis])
        peers.append((spot[axis], (spot[0] * dims[1] * dims[2] + spot[1] * dims[2] + spot[2], core)))
    return peers


def greet(targets):
    barrier = pltpu.get_barrier_semaphore()
    for target in targets:
        pl.semaphore_signal(barrier, inc=1, device_id=target, device_id_type=MESH)
    pl.semaphore_wait(barrier, len(targets))


def send(src, dst, send_sem, recv_sem, target):
    copy = pltpu.make_async_remote_copy(
        src_ref=src,
        dst_ref=dst,
        send_sem=send_sem,
        recv_sem=recv_sem,
        device_id=target,
        device_id_type=MESH,
    )
    copy.start()
    return copy


def gather_body(dims, chunks, count, *refs):
    shards, wholes = refs[:count], refs[count : 2 * count]
    send_sem, recv_sem, local_sem = refs[2 * count :]
    z, y, x = place(dims)
    peers = [axis_peers(dims, axis) for axis in range(3)]
    greet([target for group in peers for _, target in group])
    pending = {}

    def start(stage, c):
        which, first, size, y_first = chunks[c]
        rows = pl.ds(first, size)
        whole = wholes[which]
        copies = []
        if stage == 0:
            src, dst, group = shards[which].at[rows], whole.at[rows, z, y, x], peers[0]
            own = pltpu.make_async_copy(src, dst, local_sem.at[c])
            own.start()
            copies.append(own)
        elif stage == 1:
            src = whole.at[rows, :, y, x]
            dst, group = src, peers[1 if y_first else 2]
        else:
            src = whole.at[rows, :, :, x] if y_first else whole.at[rows, :, y]
            dst, group = src, peers[2 if y_first else 1]
        base = (0, dims[0], dims[0] + max(dims[1:]))[stage]
        for slot, (_, target) in enumerate(group):
            copies.append(
                send(src, dst, send_sem.at[c, base + slot], recv_sem.at[c, base + slot], target)
            )
        pending[stage, c] = copies

    def finish(stage, c):
        for copy in pending.pop((stage, c)):
            copy.wait()

    total = len(chunks)
    start(0, 0)
    for step in range(total + 2):
        if step + 1 < total:
            start(0, step + 1)
        if step < total:
            finish(0, step)
            start(1, step)
        if 0 <= step - 1 < total:
            finish(1, step - 1)
            start(2, step - 1)
        if 0 <= step - 2 < total:
            finish(2, step - 2)


def gather_weights(dims, shards, chunks, collective_id):
    count = len(shards)
    copies = dims[0] + 2 * max(dims[1:])
    return pl.pallas_call(
        functools.partial(gather_body, dims, chunks, count),
        out_shape=[
            jax.ShapeDtypeStruct((s.shape[0], *dims, *s.shape[1:]), s.dtype) for s in shards
        ],
        in_specs=[ANY] * count,
        out_specs=[ANY] * count,
        scratch_shapes=[
            pltpu.SemaphoreType.DMA((len(chunks), copies)),
            pltpu.SemaphoreType.DMA((len(chunks), copies)),
            pltpu.SemaphoreType.DMA((len(chunks),)),
        ],
        compiler_params=pltpu.CompilerParams(
            collective_id=collective_id, has_side_effects=True, vmem_limit_bytes=2**20
        ),
    )(*shards)


def sum_body(dims, flags, *refs):
    count = len(flags)
    parts, totals = refs[:count], refs[count : 2 * count]
    buffers = refs[2 * count : 6 * count]
    send_sem, recv_sem, local_sem = refs[6 * count :]
    z, y, x = place(dims)
    peers = [axis_peers(dims, axis) for axis in range(3)]
    greet([target for group in peers for _, target in group])
    pending = {}

    def start(stage, c):
        y_first = flags[c]
        own, first, second, third = buffers[4 * c : 4 * c + 4]
        copies = []
        base = (0, max(dims[1:]), 2 * max(dims[1:]))[stage]
        if stage == 0:
            mine = parts[c].at[:, y] if y_first else parts[c].at[:, :, x]
            local = pltpu.make_async_copy(mine, own, local_sem.at[c])
            local.start()
            copies.append(local)
        group = peers[((1, 2, 0) if y_first else (2, 1, 0))[stage]]
        for slot, (spot, target) in enumerate(group):
            if stage == 0:
                src = parts[c].at[:, spot] if y_first else parts[c].at[:, :, spot]
                dst = first.at[slot]
            elif stage == 1:
                src, dst = own.at[:, spot], second.at[slot]
            else:
                src, dst = own.at[spot, x if y_first else y], third.at[slot]
            copies.append(
                send(src, dst, send_sem.at[c, base + slot], recv_sem.at[c, base + slot], target)
            )
        pending[stage, c] = copies

    def finish(stage, c):
        y_first = flags[c]
        own, first, second, third = buffers[4 * c : 4 * c + 4]
        for copy in pending.pop((stage, c)):
            copy.wait()
        across = dims[2] if y_first else dims[1]
        line = x if y_first else y
        count_peers = len(peers[((1, 2, 0) if y_first else (2, 1, 0))[stage]])
        if stage == 0 and count_peers:

            def add_first(i, carry):
                value = own[i // across, i % across].astype(jnp.float32)
                for slot in range(count_peers):
                    value += first[slot, i // across, i % across].astype(jnp.float32)
                own[i // across, i % across] = value.astype(own.dtype)
                return carry

            lax.fori_loop(0, dims[0] * across, add_first, 0)
        if stage == 1 and count_peers:

            def add_second(i, carry):
                value = own[i, line].astype(jnp.float32)
                for slot in range(count_peers):
                    value += second[slot, i].astype(jnp.float32)
                own[i, line] = value.astype(own.dtype)
                return carry

            lax.fori_loop(0, dims[0], add_second, 0)
        if stage == 2:
            value = own[z, line].astype(jnp.float32)
            for slot in range(count_peers):
                value += third[slot].astype(jnp.float32)
            totals[c][...] = value

    total = len(flags)
    ahead = 2
    for c in range(min(ahead, total)):
        start(0, c)
    for step in range(total + 2 * ahead):
        if step + ahead < total:
            start(0, step + ahead)
        if step < total:
            finish(0, step)
            start(1, step)
        if 0 <= step - ahead < total:
            finish(1, step - ahead)
            start(2, step - ahead)
        if 0 <= step - 2 * ahead < total:
            finish(2, step - 2 * ahead)


def sum_gradients(dims, parts, flags, collective_id):
    count = len(parts)
    scratch = []
    for part, y_first in zip(parts, flags):
        block = part.shape[3:]
        own = (dims[0], dims[2] if y_first else dims[1])
        turns = (dims[1], dims[2]) if y_first else (dims[2], dims[1])
        scratch += [
            pltpu.VMEM((*own, *block), part.dtype),
            pltpu.VMEM((max(turns[0] - 1, 1), *own, *block), part.dtype),
            pltpu.VMEM((max(turns[1] - 1, 1), dims[0], *block), part.dtype),
            pltpu.VMEM((max(dims[0] - 1, 1), *block), part.dtype),
        ]
    copies = dims[0] + 2 * max(dims[1:])
    return pl.pallas_call(
        functools.partial(sum_body, dims, flags),
        out_shape=[jax.ShapeDtypeStruct(part.shape[3:], jnp.float32) for part in parts],
        in_specs=[ANY] * count,
        out_specs=[VMEM] * count,
        scratch_shapes=scratch
        + [
            pltpu.SemaphoreType.DMA((count, copies)),
            pltpu.SemaphoreType.DMA((count, copies)),
            pltpu.SemaphoreType.DMA((count,)),
        ],
        compiler_params=pltpu.CompilerParams(
            collective_id=collective_id, has_side_effects=True, vmem_limit_bytes=VMEM_BYTES
        ),
    )(*parts)


def spread_body(count, wide, swap, data, result, send_sem, recv_sem, local_sem):
    pair = lax.axis_size("mp")
    index = lax.axis_index("dp") * pair + lax.axis_index("mp") if wide else lax.axis_index("dp")

    def target_of(step):
        other = lax.rem(index + step, count)
        if wide:
            return other, (other // pair, lax.rem(other, pair))
        return other, (other, lax.axis_index("mp"))

    barrier = pltpu.get_barrier_semaphore()

    def hello(step, carry):
        pl.semaphore_signal(barrier, inc=1, device_id=target_of(step)[1], device_id_type=MESH)
        return carry

    lax.fori_loop(1, count, hello, 0)
    pl.semaphore_wait(barrier, count - 1)
    own = pltpu.make_async_copy(data.at[index if swap else 0], result.at[index], local_sem)
    own.start()

    def copy_of(step):
        other, target = target_of(step)
        return pltpu.make_async_remote_copy(
            src_ref=data.at[other if swap else 0],
            dst_ref=result.at[index],
            send_sem=send_sem.at[step],
            recv_sem=recv_sem.at[step],
            device_id=target,
            device_id_type=MESH,
        )

    def go(step, carry):
        copy_of(step).start()
        return carry

    def done(step, carry):
        copy_of(step).wait()
        return carry

    lax.fori_loop(1, count, go, 0)
    own.wait()
    lax.fori_loop(1, count, done, 0)


def spread(data, wide, swap, collective_id):
    count = lax.axis_size("dp") * (lax.axis_size("mp") if wide else 1)
    block = data.shape[1:] if swap else data.shape
    return pl.pallas_call(
        functools.partial(spread_body, count, wide, swap),
        out_shape=jax.ShapeDtypeStruct((count, *block), data.dtype),
        in_specs=[VMEM],
        out_specs=VMEM,
        scratch_shapes=[
            pltpu.SemaphoreType.DMA((count,)),
            pltpu.SemaphoreType.DMA((count,)),
            pltpu.SemaphoreType.DMA,
        ],
        compiler_params=pltpu.CompilerParams(
            collective_id=collective_id, has_side_effects=True, vmem_limit_bytes=VMEM_BYTES
        ),
    )(data if swap else data[None])


def layer_norm(values, gain_row, shift_row):
    centered = values - jnp.mean(values, axis=-1, keepdims=True)
    spread = jnp.mean(centered * centered, axis=-1, keepdims=True)
    return centered * lax.rsqrt(spread + norm_eps) * gain_row + shift_row


def gelu_exact(values):
    return jax.nn.gelu(values, approximate=False)


def adam_update(master, first_moment, second_moment, gradient, kind_rate):
    first_new = beta_first * first_moment + (1.0 - beta_first) * gradient
    second_new = beta_second * second_moment + (1.0 - beta_second) * gradient * gradient
    first_hat = first_new / (1.0 - beta_first**STEP)
    second_hat = second_new / (1.0 - beta_second**STEP)
    master_new = master - kind_rate * (
        first_hat / (jnp.sqrt(second_hat) + adam_eps) + weight_decay * master
    )
    return (first_new, second_new, master_new)


def project(fetched_row_values, weight_matrix_entry):
    return jnp.einsum(
        "mvw,wu->mvu", fetched_row_values, weight_matrix_entry, preferred_element_type=jnp.float32
    )


def project_back(row_gradient_block, weight_matrix_entry):
    return jnp.einsum(
        "tic,vc->tiv", row_gradient_block, weight_matrix_entry, preferred_element_type=jnp.float32
    )


def project_turned(rows, turned):
    return jnp.einsum("mvw,uw->mvu", rows, turned, preferred_element_type=jnp.float32)


def project_back_turned(row_gradient_block, turned):
    return jnp.einsum("tic,cv->tiv", row_gradient_block, turned, preferred_element_type=jnp.float32)


def weight_grad(layer_input_list, row_gradient_block):
    return jnp.einsum(
        "hmq,hmw->qw", layer_input_list, row_gradient_block, preferred_element_type=jnp.float32
    ).astype(jnp.bfloat16)


def split_heads(values):
    return values.reshape(values.shape[0], values.shape[1], values.shape[2] // HEAD_DIM, HEAD_DIM)


def pair_sum(partial_sum):
    mine = partial_sum.astype(jnp.bfloat16)
    theirs = lax.ppermute(mine, "mp", [(0, 1), (1, 0)])
    return mine.astype(jnp.float32) + theirs.astype(jnp.float32)


merge_heads = merge_inputs = pair_sum


def seq_scores(query_word, query_entity, key_rows):
    score_word = jnp.einsum(
        "qhd,khd->hqk", query_word, key_rows[:WORDS], preferred_element_type=jnp.float32
    )
    score_entity = jnp.einsum(
        "qhd,khd->hqk", query_entity, key_rows[WORDS:], preferred_element_type=jnp.float32
    )
    return jnp.concatenate([score_word, score_entity], axis=-1) * 0.125


def attend_forward(seq_item):
    query_word, query_entity, key_rows, value_rows = seq_item
    scores = seq_scores(query_word, query_entity, key_rows)
    peak_value = jnp.max(scores, axis=-1, keepdims=True)
    exp_scores = jnp.exp(scores - peak_value)
    exp_total = jnp.sum(exp_scores, axis=-1, keepdims=True)
    prob_low = (exp_scores / exp_total).astype(jnp.bfloat16)
    mixed_heads = jnp.einsum(
        "hqk,khd->qhd", prob_low, value_rows, preferred_element_type=jnp.float32
    )
    return (mixed_heads, (peak_value + jnp.log(exp_total))[..., 0])


def attend_backward(seq_item):
    query_word, query_entity, key_rows, value_rows, log_norm, grad_mixed = seq_item
    scores = seq_scores(query_word, query_entity, key_rows)
    prob_rows = jnp.exp(scores - log_norm[..., None])
    grad_value = jnp.einsum(
        "hqk,qhd->khd",
        prob_rows.astype(jnp.bfloat16),
        grad_mixed,
        preferred_element_type=jnp.float32,
    )
    grad_probs = jnp.einsum(
        "qhd,khd->hqk", grad_mixed, value_rows, preferred_element_type=jnp.float32
    )
    inner_sum = jnp.sum(prob_rows * grad_probs, axis=-1, keepdims=True)
    grad_scores = (prob_rows * (grad_probs - inner_sum) * 0.125).astype(jnp.bfloat16)
    score_word = grad_scores[..., :WORDS]
    score_entity = grad_scores[..., WORDS:]
    grad_qw = jnp.einsum(
        "hqk,khd->qhd", score_word, key_rows[:WORDS], preferred_element_type=jnp.float32
    )
    grad_qe = jnp.einsum(
        "hqk,khd->qhd", score_entity, key_rows[WORDS:], preferred_element_type=jnp.float32
    )
    grad_key = jnp.concatenate(
        [
            jnp.einsum("hqk,qhd->khd", score_word, query_word, preferred_element_type=jnp.float32),
            jnp.einsum(
                "hqk,qhd->khd", score_entity, query_entity, preferred_element_type=jnp.float32
            ),
        ],
        axis=0,
    )
    return (grad_qw, grad_qe, grad_key, grad_value)


def layer_forward(hidden, attn_mats, out_mat, up_mat, down_mat, gain_rows):
    hidden_low = hidden.astype(jnp.bfloat16)
    words_low = hidden_low[:, :WORDS]
    ents_low = hidden_low[:, WORDS:]
    query_word = jnp.concatenate(
        [project(words_low, attn_mats[0]), project(ents_low, attn_mats[2])], axis=1
    ).astype(jnp.bfloat16)
    query_entity = jnp.concatenate(
        [project(words_low, attn_mats[1]), project(ents_low, attn_mats[3])], axis=1
    ).astype(jnp.bfloat16)
    key_rows = project(hidden_low, attn_mats[4]).astype(jnp.bfloat16)
    value_rows = project(hidden_low, attn_mats[5]).astype(jnp.bfloat16)
    mixed_heads, log_norm = lax.map(
        attend_forward,
        (
            split_heads(query_word),
            split_heads(query_entity),
            split_heads(key_rows),
            split_heads(value_rows),
        ),
    )
    mixed_low = mixed_heads.reshape(key_rows.shape).astype(jnp.bfloat16)
    attended = merge_heads(project_turned(mixed_low, out_mat))
    first_out = layer_norm(hidden + attended, gain_rows[0], gain_rows[1])
    first_low = first_out.astype(jnp.bfloat16)
    inner_pre = project(first_low, up_mat)
    inner_low = gelu_exact(inner_pre).astype(jnp.bfloat16)
    outer_out = merge_heads(project_turned(inner_low, down_mat))
    result = layer_norm(first_out + outer_out, gain_rows[2], gain_rows[3])
    saved_acts = (
        hidden,
        hidden_low,
        query_word,
        query_entity,
        key_rows,
        value_rows,
        log_norm,
        mixed_low,
        attended,
        first_out,
        first_low,
        inner_pre,
        inner_low,
        outer_out,
    )
    return (result, saved_acts)


def layer_backward(grad_out, saved_acts, attn_mats, out_mat, up_mat, down_mat, gain_rows):
    (
        hidden,
        hidden_low,
        query_word,
        query_entity,
        key_rows,
        value_rows,
        log_norm,
        mixed_low,
        attended,
        first_out,
        first_low,
        inner_pre,
        inner_low,
        outer_out,
    ) = saved_acts
    second_back = jax.vjp(layer_norm, first_out + outer_out, gain_rows[2], gain_rows[3])[1]
    grad_second, grad_gain_late, grad_shift_late = second_back(grad_out)
    grad_outer = grad_second.astype(jnp.bfloat16)
    grad_down = weight_grad(grad_outer, inner_low)
    grad_inner = project_back_turned(grad_outer, down_mat)
    grad_pre = jax.vjp(gelu_exact, inner_pre)[1](grad_inner)[0].astype(jnp.bfloat16)
    grad_up = weight_grad(first_low, grad_pre)
    grad_first = grad_second + merge_inputs(project_back(grad_pre, up_mat))
    first_back = jax.vjp(layer_norm, hidden + attended, gain_rows[0], gain_rows[1])[1]
    grad_first_in, grad_gain_early, grad_shift_early = first_back(grad_first)
    grad_attended = grad_first_in.astype(jnp.bfloat16)
    grad_out_mat = weight_grad(grad_attended, mixed_low)
    grad_mixed = project_back_turned(grad_attended, out_mat).astype(jnp.bfloat16)
    grad_qw, grad_qe, grad_key, grad_value = lax.map(
        attend_backward,
        (
            split_heads(query_word),
            split_heads(query_entity),
            split_heads(key_rows),
            split_heads(value_rows),
            log_norm,
            split_heads(grad_mixed),
        ),
    )
    flat_shape = key_rows.shape
    grad_qw = grad_qw.reshape(flat_shape).astype(jnp.bfloat16)
    grad_qe = grad_qe.reshape(flat_shape).astype(jnp.bfloat16)
    grad_key = grad_key.reshape(flat_shape).astype(jnp.bfloat16)
    grad_value = grad_value.reshape(flat_shape).astype(jnp.bfloat16)
    words_low = hidden_low[:, :WORDS]
    ents_low = hidden_low[:, WORDS:]
    grad_mats = (
        weight_grad(words_low, jnp.concatenate([grad_qw[:, :WORDS], grad_qe[:, :WORDS]], axis=-1)),
        weight_grad(ents_low, jnp.concatenate([grad_qw[:, WORDS:], grad_qe[:, WORDS:]], axis=-1)),
        weight_grad(hidden_low, jnp.concatenate([grad_key, grad_value], axis=-1)),
    )
    part_words = project_back(grad_qw[:, :WORDS], attn_mats[0]) + project_back(
        grad_qe[:, :WORDS], attn_mats[1]
    )
    part_ents = project_back(grad_qw[:, WORDS:], attn_mats[2]) + project_back(
        grad_qe[:, WORDS:], attn_mats[3]
    )
    part_sum = (
        jnp.concatenate([part_words, part_ents], axis=1)
        + project_back(grad_key, attn_mats[4])
        + project_back(grad_value, attn_mats[5])
    )
    grad_hidden = grad_first_in + merge_inputs(part_sum)
    grad_norms = jnp.stack([grad_gain_early, grad_shift_early, grad_gain_late, grad_shift_late])
    return (grad_hidden, (grad_mats, grad_out_mat, grad_up, grad_down, grad_norms))


LOG2E = 1.4426950408889634
SCORE_STEP = 0.125 * LOG2E
LEN = WORDS + ENT_LEN
BLOCK = 256
BLOCKS = LEN // BLOCK


def mm(left, right):
    return lax.dot_general(
        left, right, (((1,), (0,)), ((), ())), preferred_element_type=jnp.float32
    )


def mm_rt(left, right):
    return lax.dot_general(
        left, right, (((1,), (1,)), ((), ())), preferred_element_type=jnp.float32
    )


def mm_lt(left, right):
    return lax.dot_general(
        left, right, (((0,), (0,)), ((), ())), preferred_element_type=jnp.float32
    )


def flat(ref, *index):
    value = ref[index] if index else ref[...]
    return value.reshape(-1, value.shape[-1])


def lane_mask(rows, which):
    lane = lax.broadcasted_iota(jnp.int32, (rows, 2 * HEAD_DIM), 1)
    return (lane // HEAD_DIM == which).astype(jnp.bfloat16)


def normed(values):
    centered = values - jnp.mean(values, axis=-1, keepdims=True)
    spread_row = jnp.mean(centered * centered, axis=-1, keepdims=True)
    scale = lax.rsqrt(spread_row + norm_eps)
    return centered * scale, scale


def gelu_parts(values):
    cdf = 0.5 * (1.0 + lax.erf(values * 0.7071067811865476))
    bell = jnp.exp2(values * values * (-0.5 * LOG2E)) * 0.3989422804014327
    return values * cdf, cdf + values * bell


class Gather:
    def __init__(self, dims, chunks, shards, wholes, kept, sems, lags=(3, 2, 2)):
        self.dims, self.chunks, self.shards, self.wholes, self.kept = dims, chunks, shards, wholes, kept
        self.send_sem, self.recv_sem, self.local_sem, self.keep_sem = sems
        self.spot = place(dims)
        self.peers = [axis_peers(dims, axis) for axis in range(3)]
        self.pending, self.step = {}, 0
        self.ahead, self.lag1, self.lag2 = lags

    def targets(self):
        return [target for group in self.peers for _, target in group]

    def start(self, stage, c):
        which, rows, cols, y_first = self.chunks[c]
        z, y, x = self.spot
        whole = self.wholes[which].at[rows, :, :, :, :, cols]
        shard = self.shards[which].at[rows, :, cols]
        copies = []
        if stage == 0:
            own = pltpu.make_async_copy(shard, whole.at[:, z, y, x], self.local_sem.at[c])
            own.start()
            copies.append(own)
            src, dst, group = shard, whole.at[:, z, y, x], self.peers[0]
        elif stage == 1:
            src = whole.at[:, :, y, x]
            dst, group = src, self.peers[1 if y_first else 2]
        else:
            src = whole.at[:, :, :, x] if y_first else whole.at[:, :, y]
            dst, group = src, self.peers[2 if y_first else 1]
        base = (0, self.dims[0], self.dims[0] + max(self.dims[1:]))[stage]
        for slot, (_, target) in enumerate(group):
            sems = self.send_sem.at[c, base + slot], self.recv_sem.at[c, base + slot]
            copies.append(send(src, dst, *sems, target))
        self.pending[stage, c] = copies

    def finish(self, stage, c):
        for copy in self.pending.pop((stage, c)):
            copy.wait()
        if stage == 2:
            which, rows, cols, _ = self.chunks[c]
            keep = pltpu.make_async_copy(
                self.wholes[which].at[rows, :, :, :, :, cols],
                self.kept[which].at[rows, :, :, :, :, cols],
                self.keep_sem.at[c],
            )
            keep.start()
            self.pending[3, c] = [keep]

    def begin(self):
        for c in range(min(self.ahead, len(self.chunks))):
            self.start(0, c)

    def tick(self):
        total, step = len(self.chunks), self.step
        if step >= total + self.lag1 + self.lag2:
            return
        self.step += 1
        if step + self.ahead < total:
            self.start(0, step + self.ahead)
        if step < total:
            self.finish(0, step)
            self.start(1, step)
        late = step - self.lag1
        if 0 <= late < total:
            self.finish(1, late)
            self.start(2, late)
        late -= self.lag2
        if 0 <= late < total:
            self.finish(2, late)

    def need(self, c):
        while self.step < c + self.lag1 + self.lag2 + 1:
            self.tick()

    def close(self):
        self.need(len(self.chunks) - 1)
        for key in sorted(self.pending):
            for copy in self.pending[key]:
                copy.wait()


class Pair:
    def __init__(self, mine, theirs, sems):
        self.mine, self.theirs = mine, theirs
        self.send_sem, self.recv_sem = sems
        self.phase = 0
        self.other = (lax.axis_index("dp"), 1 - lax.axis_index("mp"))

    def copy(self, phase, c):
        return pltpu.make_async_remote_copy(
            src_ref=self.mine.at[c],
            dst_ref=self.theirs.at[phase % 2, c],
            send_sem=self.send_sem.at[phase, c],
            recv_sem=self.recv_sem.at[phase, c],
            device_id=self.other,
            device_id_type=MESH,
        )

    def run(self, compute, consume, between=None):
        phase = self.phase
        self.phase += 1

        def take(c):
            self.copy(phase, c).wait()
            total = self.mine[c].astype(jnp.float32) + self.theirs[phase % 2, c].astype(jnp.float32)
            consume(c, pl.ds(c * BLOCK, BLOCK), total)

        for c in range(BLOCKS):
            self.mine[c] = compute(c, pl.ds(c * BLOCK, BLOCK)).astype(jnp.bfloat16)
            self.copy(phase, c).start()
            if between is not None:
                between()
            if c:
                take(c - 1)
        take(BLOCKS - 1)


SAVED = ("xb", "qw", "qe", "k", "v", "o", "n1", "h1b", "slope", "g", "n2", "stats")


def saved_shapes(half, hidden):
    wide, narrow = (LEN, D), (LEN, half)
    low = jnp.bfloat16
    return {
        "xb": (wide, low),
        "qw": (narrow, low),
        "qe": (narrow, low),
        "k": (narrow, low),
        "v": (narrow, low),
        "o": (narrow, low),
        "n1": (wide, low),
        "h1b": (wide, low),
        "slope": ((LEN, hidden), low),
        "g": ((LEN, hidden), low),
        "n2": (wide, low),
        "stats": ((LEN, 128), jnp.float32),
    }


def attend(act, pair):
    lanes = slice(pair * 2 * HEAD_DIM, (pair + 1) * 2 * HEAD_DIM)

    def block(i, carry):
        rows = pl.ds(i * BLOCK, BLOCK)
        keys, values = act["k"][:, lanes], act["v"][:, lanes]
        total = None
        for which in range(2):
            q_mask, v_mask = lane_mask(BLOCK, which), lane_mask(LEN, which)
            score_w = mm_rt(act["qw"][rows, lanes] * q_mask, keys[:WORDS])
            score_e = mm_rt(act["qe"][rows, lanes] * q_mask, keys[WORDS:])
            peak = jnp.maximum(
                jnp.max(score_w, axis=-1, keepdims=True), jnp.max(score_e, axis=-1, keepdims=True)
            )
            exp_w = jnp.exp2((score_w - peak) * SCORE_STEP)
            exp_e = jnp.exp2((score_e - peak) * SCORE_STEP)
            weight = jnp.sum(exp_w, axis=-1, keepdims=True) + jnp.sum(exp_e, axis=-1, keepdims=True)
            part = values * v_mask
            mixed = mm(exp_w.astype(jnp.bfloat16), part[:WORDS])
            mixed += mm(exp_e.astype(jnp.bfloat16), part[WORDS:])
            mixed = mixed * (1.0 / weight)
            total = mixed if total is None else total + mixed
            head = 2 * pair + which
            act["stats"][rows, head : head + 1] = peak * SCORE_STEP + jnp.log2(weight)
        act["o"][rows, lanes] = total.astype(jnp.bfloat16)
        return carry

    lax.fori_loop(0, BLOCKS, block, 0)


def project_rows(out_ref, x_ref, first, size, step, weights, index):
    def block(i, carry):
        rows = pl.ds(first + i * step, step)
        out_ref[rows, :] = mm(x_ref[rows, :], flat(weights, index)).astype(jnp.bfloat16)
        return carry

    lax.fori_loop(0, size // step, block, 0)


def forward_body(dims, chunks, needs, *refs):
    refs = list(refs)

    def take(count):
        part = refs[:count]
        del refs[:count]
        return part

    words, base, requests, place_mat, table = take(5)
    shards = take(len(needs["kinds"]))
    kept = take(len(needs["kinds"]))
    saved = [dict(zip(SAVED, take(len(SAVED)))) for _ in range(LAYERS)]
    ents_out, gains_out, rows_in, got_out = take(4)
    wholes = take(len(needs["kinds"]))
    act = dict(zip(SAVED, take(len(SAVED))))
    x, h1, gains, mine, theirs = take(5)
    gather_sems = take(4)
    pair_sems = take(2)
    (save_sem,) = take(1)
    got, replies, answers, look_mine, look_theirs = take(5)
    look_send, look_recv, look_pair = take(3)

    gather = Gather(dims, chunks, shards, wholes, kept, gather_sems)
    pair = Pair(mine, theirs, pair_sems)
    count = dims[0] * dims[1] * dims[2]
    greet_line(count, [pair.other])
    asking = Fan(
        count, (look_send.at[0], look_recv.at[0]), lambda me, to: (requests.at[to], got.at[me])
    )
    asking.start()
    gather.begin()
    here = lax.axis_index("dp")
    got[here] = requests[here]
    asking.wait()
    wanted = flat(got)
    got_out[...] = wanted

    def look(j, found):
        lane = lax.broadcasted_iota(jnp.int32, wanted.shape, 1) + j * 128
        hot = jnp.where(wanted == lane, 1.0, 0.0).astype(jnp.bfloat16)
        return found + mm(hot, table[pl.ds(pl.multiple_of(j * 128, 128), 128), :])

    found = jnp.zeros((wanted.shape[0], table.shape[1]), jnp.float32)
    found = lax.fori_loop(0, table.shape[0] // 128, look, found)
    replies[...] = found.reshape(replies.shape)
    answering = Fan(
        count, (look_send.at[1], look_recv.at[1]), lambda me, to: (replies.at[to], answers.at[me])
    )
    answering.start()
    answers[here] = replies[here]
    gather.tick()
    gather.tick()
    answering.wait()
    look_mine[...] = mm(place_mat[...], flat(answers).astype(jnp.bfloat16)).astype(jnp.bfloat16)
    swap = send(look_mine, look_theirs, look_pair.at[0], look_pair.at[1], pair.other)
    attn, outs, ups, downs, proj, _, norms = wholes
    saving = {}

    def save(layer, name):
        slot = layer * len(SAVED) + SAVED.index(name)
        copy = pltpu.make_async_copy(act[name], saved[layer][name], save_sem.at[slot])
        copy.start()
        saving[name] = copy

    def free(name):
        if name in saving:
            saving.pop(name).wait()

    x[:WORDS] = words[...].astype(jnp.float32)
    gather.need(needs["norms"])
    width = D // (dims[0] * dims[1] * dims[2])
    gains[...] = jnp.zeros_like(gains)
    for d in range(count):
        z, rest = d // (dims[1] * dims[2]), d % (dims[1] * dims[2])
        pick = lax.broadcasted_iota(jnp.int32, (128, D), 0) + d * width
        lane = lax.broadcasted_iota(jnp.int32, (128, D), 1)
        inside = lax.broadcasted_iota(jnp.int32, (128, D), 0) < width
        hot = jnp.where((pick == lane) & inside, 1.0, 0.0).astype(jnp.bfloat16)
        gains[...] += mm(norms[0, z, rest // dims[2], rest % dims[2]], hot)
    gather.need(needs["proj"])
    swap.wait()
    both = look_mine[...].astype(jnp.float32) + look_theirs[...].astype(jnp.float32)
    rows_in[...] = both.astype(jnp.bfloat16)
    x[WORDS:] = base[...].astype(jnp.float32) + mm(rows_in[...], flat(proj, 0))

    for layer in range(LAYERS):
        gain = [gains[4 * layer + i : 4 * layer + i + 1, :] for i in range(4)]
        free("xb")

        def cast(i, carry):
            rows = pl.ds(i * BLOCK, BLOCK)
            act["xb"][rows, :] = x[rows, :].astype(jnp.bfloat16)
            return carry

        lax.fori_loop(0, BLOCKS, cast, 0)
        save(layer, "xb")
        for name, word_mat, ent_mat in (("k", 4, None), ("v", 5, None), ("qw", 0, 2), ("qe", 1, 3)):
            free(name)
            gather.need(needs["mat", layer, word_mat if ent_mat is None else ent_mat])
            if ent_mat is None:
                project_rows(act[name], act["xb"], 0, LEN, 512, attn, 6 * layer + word_mat)
            else:
                project_rows(act[name], act["xb"], 0, WORDS, 448, attn, 6 * layer + word_mat)
                project_rows(act[name], act["xb"], WORDS, ENT_LEN, ENT_LEN, attn, 6 * layer + ent_mat)
            save(layer, name)
            gather.tick()
        free("o")
        free("stats")
        for head_pair in range(act["o"].shape[1] // (2 * HEAD_DIM)):
            attend(act, head_pair)
            gather.tick()
        save(layer, "o")
        gather.need(needs["out", layer])
        for name in ("n1", "h1b"):
            free(name)

        def out_part(c, rows):
            return mm_rt(act["o"][rows, :], flat(outs, layer))

        def first_norm(c, rows, total):
            hat, scale = normed(x[rows, :] + total)
            act["n1"][rows, :] = hat.astype(jnp.bfloat16)
            act["stats"][rows, 8:9] = scale
            value = hat * gain[0] + gain[1]
            h1[rows, :] = value
            act["h1b"][rows, :] = value.astype(jnp.bfloat16)

        pair.run(out_part, first_norm, gather.tick)
        save(layer, "n1")
        save(layer, "h1b")
        gather.need(needs["up", layer, 1])
        for name in ("g", "slope", "n2"):
            free(name)
        hidden = act["g"].shape[1]
        tile = 512

        def up_block(c):
            rows = pl.ds(c * BLOCK, BLOCK)
            for first in range(0, hidden, tile):
                cols = slice(first, first + tile)
                weight = ups[layer, :, :, :, :, cols].reshape(D, tile)
                value, slope = gelu_parts(mm(act["h1b"][rows, :], weight))
                act["g"][rows, cols] = value.astype(jnp.bfloat16)
                act["slope"][rows, cols] = slope.astype(jnp.bfloat16)

        for c in range(BLOCKS):
            up_block(c)
            gather.tick()
        save(layer, "g")
        save(layer, "slope")
        gather.need(needs["down", layer, 1])

        def down_part(c, rows):
            return mm_rt(act["g"][rows, :], flat(downs, layer))

        def second_norm(c, rows, total):
            hat, scale = normed(h1[rows, :] + total)
            act["n2"][rows, :] = hat.astype(jnp.bfloat16)
            act["stats"][rows, 9:10] = scale
            x[rows, :] = hat * gain[2] + gain[3]

        pair.run(down_part, second_norm, gather.tick)
        save(layer, "n2")
        save(layer, "stats")
    ents_out[...] = x[WORDS:]
    gains_out[...] = gains[...]
    gather.close()
    for name in list(saving):
        free(name)


KINDS = ("attn", "out", "up", "down", "proj", "head", "norms")


MAT_ORDER = (4, 5, 0, 2, 1, 3)


def gather_plan(hidden):
    every = slice(None)
    chunks = [(6, pl.ds(0, 1), every, True), (4, pl.ds(0, 1), every, False)]
    needs = {"kinds": KINDS, "norms": 0, "proj": 1}
    y_first = [True]

    def add(name, which, row, cols):
        chunks.append((which, pl.ds(row, 1), cols, y_first[0]))
        y_first[0] = not y_first[0]
        needs[name] = len(chunks) - 1

    for layer in range(LAYERS):
        for mat in MAT_ORDER:
            add(("mat", layer, mat), 0, 6 * layer + mat, every)
        add(("out", layer), 1, layer, every)
        for which, name in ((2, "up"), (3, "down")):
            for part in range(2):
                add((name, layer, part), which, layer, pl.ds(part * (hidden // 2), hidden // 2))
    add("head", 5, 0, every)
    return chunks, needs


def run_forward(dims, words, base, requests, place_mat, table_low, shards, collective_id):
    half, hidden = shards[0].shape[-1], shards[2].shape[-1]
    chunks, needs = gather_plan(hidden)
    shapes = saved_shapes(half, hidden)
    low, full = jnp.bfloat16, jnp.float32
    width, slots = table_low.shape[1], requests.shape[0] * requests.shape[1]
    wholes = [(s.shape[0], *dims, *s.shape[1:]) for s in shards]
    copies = dims[0] + 2 * max(dims[1:])
    saved_out = [jax.ShapeDtypeStruct(*shapes[name]) for _ in range(LAYERS) for name in SAVED]
    result = pl.pallas_call(
        functools.partial(forward_body, dims, chunks, needs),
        out_shape=[jax.ShapeDtypeStruct(shape, low) for shape in wholes]
        + saved_out
        + [
            jax.ShapeDtypeStruct((ENT_LEN, D), full),
            jax.ShapeDtypeStruct((16, D), full),
            jax.ShapeDtypeStruct((ENT_LEN, width), low),
            jax.ShapeDtypeStruct((slots, 128), jnp.int32),
        ],
        in_specs=[VMEM] * 5 + [ANY] * len(shards),
        out_specs=[ANY] * (len(wholes) + len(saved_out)) + [VMEM] * 4,
        scratch_shapes=[pltpu.VMEM(shape, low) for shape in wholes]
        + [pltpu.VMEM(*shapes[name]) for name in SAVED]
        + [
            pltpu.VMEM((LEN, D), full),
            pltpu.VMEM((LEN, D), full),
            pltpu.VMEM((16, D), full),
            pltpu.VMEM((BLOCKS, BLOCK, D), low),
            pltpu.VMEM((2, BLOCKS, BLOCK, D), low),
            pltpu.SemaphoreType.DMA((len(chunks), copies)),
            pltpu.SemaphoreType.DMA((len(chunks), copies)),
            pltpu.SemaphoreType.DMA((len(chunks),)),
            pltpu.SemaphoreType.DMA((len(chunks),)),
            pltpu.SemaphoreType.DMA((2 * LAYERS, BLOCKS)),
            pltpu.SemaphoreType.DMA((2 * LAYERS, BLOCKS)),
            pltpu.SemaphoreType.DMA((LAYERS * len(SAVED),)),
            pltpu.VMEM(requests.shape, jnp.int32),
            pltpu.VMEM((*requests.shape[:2], width), full),
            pltpu.VMEM((*requests.shape[:2], width), full),
            pltpu.VMEM((ENT_LEN, width), low),
            pltpu.VMEM((ENT_LEN, width), low),
            pltpu.SemaphoreType.DMA((2, requests.shape[0])),
            pltpu.SemaphoreType.DMA((2, requests.shape[0])),
            pltpu.SemaphoreType.DMA((2,)),
        ],
        compiler_params=pltpu.CompilerParams(
            collective_id=collective_id, has_side_effects=True, vmem_limit_bytes=VMEM_BYTES
        ),
    )(words, base, requests, place_mat, table_low, *shards)
    kept = result[: len(wholes)]
    saved = [
        dict(zip(SAVED, result[len(wholes) + layer * len(SAVED) :][: len(SAVED)]))
        for layer in range(LAYERS)
    ]
    return kept, saved, *result[-4:]


class Fan:
    def __init__(self, count, sems, copy_args):
        self.count, self.sems, self.copy_args = count, sems, copy_args
        self.index = lax.axis_index("dp")

    def copy(self, step):
        other = lax.rem(self.index + step, self.count)
        src, dst = self.copy_args(self.index, other)
        send_sem, recv_sem = self.sems
        return pltpu.make_async_remote_copy(
            src_ref=src,
            dst_ref=dst,
            send_sem=send_sem.at[step],
            recv_sem=recv_sem.at[step],
            device_id=(other, lax.axis_index("mp")),
            device_id_type=MESH,
        )

    def start(self):
        def go(step, carry):
            self.copy(step).start()
            return carry

        lax.fori_loop(1, self.count, go, 0)

    def wait(self):
        def done(step, carry):
            self.copy(step).wait()
            return carry

        lax.fori_loop(1, self.count, done, 0)


def greet_line(count, extra):
    barrier = pltpu.get_barrier_semaphore()
    index, core = lax.axis_index("dp"), lax.axis_index("mp")

    def hello(step, carry):
        other = lax.rem(index + step, count)
        pl.semaphore_signal(barrier, inc=1, device_id=(other, core), device_id_type=MESH)
        return carry

    lax.fori_loop(1, count, hello, 0)
    for target in extra:
        pl.semaphore_signal(barrier, inc=1, device_id=target, device_id_type=MESH)
    pl.semaphore_wait(barrier, count - 1 + len(extra))


TABLE_CUTS = 8


def head_body(count, *refs):
    ents, hits, head, table, local_targets = refs[:5]
    losses, grad_logits, states, grad_head, grad_ents = refs[5:10]
    logits, own_states, all_states, stat_mine, stat_theirs, stat_both, stat_all = refs[10:17]
    grad_part, grad_all, share_mine, share_theirs = refs[17:21]
    send_sem, recv_sem, pair_send, pair_recv = refs[21:]
    index = lax.axis_index("dp")
    other = (index, 1 - lax.axis_index("mp"))
    greet_line(count, [other])
    total_rows = count * MASK_ENT
    span = table.shape[0] // TABLE_CUTS

    masked = mm(hits[...], ents[...].astype(jnp.bfloat16)).astype(jnp.bfloat16)
    head_low = flat(head)
    value, slope = gelu_parts(mm(masked, head_low))
    own_states[...] = value.astype(jnp.bfloat16)
    fan = Fan(count, (send_sem.at[0], recv_sem.at[0]), lambda me, to: (own_states, all_states.at[me]))
    fan.start()
    all_states[index] = own_states[...]
    fan.wait()
    states[...] = flat(all_states)
    target = local_targets[0:1, :]

    def hit_of(c):
        row = lax.broadcasted_iota(jnp.int32, (span, total_rows), 0) + c * span
        return row == target

    def rows_of(c):
        return pl.ds(pl.multiple_of(c * span, 16), span)

    def score(c, carry):
        peak, picked = carry
        part = mm_rt(table[rows_of(c), :], states[...])
        logits[rows_of(c), :] = part
        peak = jnp.maximum(peak, jnp.max(part, axis=0, keepdims=True))
        picked += jnp.sum(jnp.where(hit_of(c), part, 0.0), axis=0, keepdims=True)
        return peak, picked

    empty = jnp.zeros((1, total_rows), jnp.float32)
    peak, picked = lax.fori_loop(0, TABLE_CUTS, score, (empty - 3e38, empty))

    def weigh(c, weight):
        return weight + jnp.sum(jnp.exp(logits[rows_of(c), :] - peak), axis=0, keepdims=True)

    weight = lax.fori_loop(0, TABLE_CUTS, weigh, empty)
    stat_mine[0:1, :] = peak
    stat_mine[1:2, :] = weight
    stat_mine[2:3, :] = picked
    swap = send(stat_mine, stat_theirs, pair_send.at[0], pair_recv.at[0], other)
    swap.wait()
    peak_both = jnp.maximum(stat_mine[0:1, :], stat_theirs[0:1, :])
    stat_both[0:1, :] = peak_both
    stat_both[1:2, :] = stat_mine[1:2, :] * jnp.exp(stat_mine[0:1, :] - peak_both) + stat_theirs[
        1:2, :
    ] * jnp.exp(stat_theirs[0:1, :] - peak_both)
    stat_both[2:3, :] = stat_mine[2:3, :] + stat_theirs[2:3, :]
    fan = Fan(count, (send_sem.at[1], recv_sem.at[1]), lambda me, to: (stat_both, stat_all.at[me]))
    fan.start()
    stat_all[index] = stat_both[...]
    fan.wait()
    peak_all = stat_all[0, 0:1, :]
    for d in range(1, count):
        peak_all = jnp.maximum(peak_all, stat_all[d, 0:1, :])
    weight_all = picked_all = empty
    for d in range(count):
        weight_all += stat_all[d, 1:2, :] * jnp.exp(stat_all[d, 0:1, :] - peak_all)
        picked_all += stat_all[d, 2:3, :]
    log_norm = peak_all + jnp.log(weight_all)
    losses[...] = jnp.broadcast_to(log_norm - picked_all, losses.shape)
    grad_part[...] = jnp.zeros_like(grad_part)

    def grads(c, carry):
        prob = jnp.exp(logits[rows_of(c), :] - log_norm)
        part = (prob - jnp.where(hit_of(c), 1.0, 0.0)) * (1.0 / total_rows)
        low = part.astype(jnp.bfloat16)
        grad_logits[rows_of(c), :] = low
        grad_part[...] += mm_lt(low, table[rows_of(c), :]).reshape(grad_part.shape)
        return carry

    lax.fori_loop(0, TABLE_CUTS, grads, 0)
    fan = Fan(
        count, (send_sem.at[2], recv_sem.at[2]), lambda me, to: (grad_part.at[to], grad_all.at[me])
    )
    fan.start()
    grad_all[index] = grad_part[index]
    fan.wait()
    share_mine[...] = jnp.sum(grad_all[...], axis=0)
    swap = send(share_mine, share_theirs, pair_send.at[1], pair_recv.at[1], other)
    swap.wait()
    grad_pre = ((share_mine[...] + share_theirs[...]) * slope).astype(jnp.bfloat16)
    grad_head[...] = mm_lt(masked, grad_pre).astype(jnp.bfloat16).reshape(grad_head.shape)
    grad_masked = mm_rt(grad_pre, head_low)
    grad_ents[...] = lax.dot_general(
        hits[...].astype(jnp.float32),
        grad_masked,
        (((0,), (0,)), ((), ())),
        precision=lax.Precision.HIGHEST,
        preferred_element_type=jnp.float32,
    )


def run_head(dims, ents, hits, head, table_low, local_targets, collective_id):
    count = dims[0] * dims[1] * dims[2]
    width = table_low.shape[1]
    rows = count * MASK_ENT
    low, full = jnp.bfloat16, jnp.float32
    return pl.pallas_call(
        functools.partial(head_body, count),
        out_shape=[
            jax.ShapeDtypeStruct((8, rows), full),
            jax.ShapeDtypeStruct((table_low.shape[0], rows), low),
            jax.ShapeDtypeStruct((rows, width), low),
            jax.ShapeDtypeStruct(head.shape, low),
            jax.ShapeDtypeStruct((ENT_LEN, D), full),
        ],
        in_specs=[VMEM] * 5,
        out_specs=[VMEM] * 5,
        scratch_shapes=[
            pltpu.VMEM((table_low.shape[0], rows), full),
            pltpu.VMEM((MASK_ENT, width), low),
            pltpu.VMEM((count, MASK_ENT, width), low),
            pltpu.VMEM((8, rows), full),
            pltpu.VMEM((8, rows), full),
            pltpu.VMEM((8, rows), full),
            pltpu.VMEM((count, 8, rows), full),
            pltpu.VMEM((count, MASK_ENT, width), full),
            pltpu.VMEM((count, MASK_ENT, width), full),
            pltpu.VMEM((MASK_ENT, width), full),
            pltpu.VMEM((MASK_ENT, width), full),
            pltpu.SemaphoreType.DMA((3, count)),
            pltpu.SemaphoreType.DMA((3, count)),
            pltpu.SemaphoreType.DMA((2,)),
            pltpu.SemaphoreType.DMA((2,)),
        ],
        compiler_params=pltpu.CompilerParams(
            collective_id=collective_id, has_side_effects=True, vmem_limit_bytes=VMEM_BYTES
        ),
    )(ents, hits, head, table_low, local_targets)


def update_body(names, width, *refs):
    refs = list(refs)

    def take(count):
        part = refs[:count]
        del refs[:count]
        return part

    kinds = len(kind_rates)
    state_in = [take(3) for _ in range(kinds)]
    totals_in = take(len(names))
    incoming, requests, grad_logits, states = take(4)
    state_out = [take(3) for _ in range(kinds)]
    held = [take(3) for _ in range(kinds)]
    totals_held = take(len(names))
    in_sem, total_sem, out_sem = take(3)
    table = kinds - 1
    height = held[table][0].shape[0] // TABLE_CUTS

    def piece(ref, c):
        return ref if c is None else ref.at[pl.ds(c * height, height)]

    def copies(kind, c, inward):
        base = 3 * (kind + (0 if c is None else c))
        pairs = []
        for i in range(3):
            if inward:
                src, dst, sem = state_in[kind][i], held[kind][i], in_sem.at[base + i]
            else:
                src, dst, sem = held[kind][i], state_out[kind][i], out_sem.at[base + i]
            pairs.append(pltpu.make_async_copy(piece(src, c), piece(dst, c), sem))
        return pairs

    leaving = []
    total_copies = [
        pltpu.make_async_copy(src, dst, total_sem.at[i])
        for i, (src, dst) in enumerate(zip(totals_in, totals_held))
    ]
    for c in range(2):
        for copy in copies(table, c, True):
            copy.start()
    for copy in total_copies:
        copy.start()
    for kind in range(table):
        for copy in copies(kind, None, True):
            copy.start()
    for c in range(2, TABLE_CUTS):
        for copy in copies(table, c, True):
            copy.start()
    total_of = dict(zip(names, totals_held))

    def update(kind, at, gradient):
        master, first, second = held[kind]
        first_new = beta_first * first[at] + (1.0 - beta_first) * gradient
        second_new = beta_second * second[at] + (1.0 - beta_second) * gradient * gradient
        first_hat = first_new * (1.0 / (1.0 - beta_first**STEP))
        second_hat = second_new * (1.0 / (1.0 - beta_second**STEP))
        value = master[at]
        value -= kind_rates[kind] * (
            first_hat / (jnp.sqrt(second_hat) + adam_eps) + weight_decay * value
        )
        master[at], first[at], second[at] = value, first_new, second_new

    def finish(kind, c=None):
        for copy in copies(kind, c, False):
            copy.start()
            leaving.append(copy)

    def table_part(c):
        for copy in copies(table, c, True):
            copy.wait()
        rows = slice(c * height, (c + 1) * height)
        gradient = mm(grad_logits[rows, :], states[...])
        row = lax.broadcasted_iota(jnp.int32, (height, requests.shape[1]), 0) + c * height
        hot = jnp.where(row == requests[0:1, :], 1.0, 0.0).astype(jnp.bfloat16)
        gradient += mm(hot, incoming[...].astype(jnp.bfloat16))
        update(table, (rows, slice(None)), gradient)
        finish(table, c)

    table_part(0)
    table_part(1)
    for copy in total_copies:
        copy.wait()
    for kind in range(table):
        for copy in copies(kind, None, True):
            copy.wait()
        for layer in range(LAYERS):
            if kind == 0:
                blocks = []
                for name in ("words", "ents"):
                    total = total_of[layer, name]
                    half = total.shape[1] // 2
                    blocks += [total[:, :half], total[:, half:]]
                blocks += [total_of[layer, "key"][...], total_of[layer, "value"][...]]
                for mat, block in enumerate(blocks):
                    update(kind, (layer, mat), block)
            elif kind == 1:
                update(kind, (layer,), total_of[layer, "out"][...])
            elif kind in (2, 3):
                for i in range(2):
                    total = total_of[layer, ("up%d", "down%d")[kind - 2] % i]
                    half = total.shape[1]
                    cols = slice(i * half, (i + 1) * half)
                    update(kind, (layer, slice(None), cols), total[...])
            elif kind == 4:
                update(kind, (layer,), total_of["norms"][4 * layer : 4 * layer + 4, :width])
        if kind == 5:
            update(kind, (slice(None),), total_of["proj"][...])
        if kind == 6:
            update(kind, (slice(None),), total_of["head"][...])
        finish(kind)
    for c in range(2, TABLE_CUTS):
        table_part(c)
    for copy in leaving:
        copy.wait()


def run_update(states_of, totals, incoming, requests, grad_logits, states):
    names = list(totals)
    full = jnp.float32
    flat_states = [array for group in states_of for array in group]
    width = states_of[4][0].shape[-1]
    kinds = len(kind_rates)
    result = pl.pallas_call(
        functools.partial(update_body, names, width),
        out_shape=[jax.ShapeDtypeStruct(a.shape, full) for a in flat_states],
        in_specs=[ANY] * (len(flat_states) + len(names)) + [VMEM] * 4,
        out_specs=[ANY] * len(flat_states),
        scratch_shapes=[pltpu.VMEM(a.shape, full) for a in flat_states]
        + [pltpu.VMEM(totals[name].shape, full) for name in names]
        + [
            pltpu.SemaphoreType.DMA((3 * (kinds + TABLE_CUTS),)),
            pltpu.SemaphoreType.DMA((len(names),)),
            pltpu.SemaphoreType.DMA((3 * (kinds + TABLE_CUTS),)),
        ],
        compiler_params=pltpu.CompilerParams(vmem_limit_bytes=VMEM_BYTES),
    )(*flat_states, *totals.values(), incoming, requests, grad_logits, states)
    return [result[3 * i : 3 * i + 3] for i in range(kinds)]


def norm_back(grad, hat, scale, gain_row):
    hat = hat.astype(jnp.float32)
    wide = grad * gain_row
    inner = jnp.mean(wide * hat, axis=-1, keepdims=True)
    back = scale * (wide - jnp.mean(wide, axis=-1, keepdims=True) - hat * inner)
    gain_part = jnp.sum(grad * hat, axis=0, keepdims=True)
    return back, gain_part, jnp.sum(grad, axis=0, keepdims=True)


class Sums:
    def __init__(self, dims, units, buffers, totals, sems, free_sem):
        self.dims, self.units, self.totals = dims, units, totals
        self.buffers = buffers
        self.send_sem, self.recv_sem = sems
        self.free_sem = free_sem
        self.spot = place(dims)
        self.peers = [axis_peers(dims, axis) for axis in range(3)]
        self.queue, self.done = [], set()
        self.least = 2

    def group(self, stage, y_first):
        return self.peers[((1, 2, 0) if y_first else (2, 1, 0))[stage]]

    def start(self, stage, u):
        slot, y_first, turn = self.units[u]
        part, first, second, third = self.buffers[slot]
        z, y, x = self.spot
        group = self.group(stage, y_first)
        if turn and group:
            pl.semaphore_wait(self.free_sem.at[slot, stage], len(group))
        copies = []
        base = (0, max(self.dims[1:]), 2 * max(self.dims[1:]))[stage]
        for k, (spot, target) in enumerate(group):
            if stage == 0:
                src = part.at[:, spot] if y_first else part.at[:, :, spot]
                dst = first.at[k]
            elif stage == 1:
                src = part.at[:, y, spot] if y_first else part.at[:, spot, x]
                dst = second.at[k]
            else:
                src, dst = part.at[spot, y, x], third.at[k]
            sems = self.send_sem.at[u, base + k], self.recv_sem.at[u, base + k]
            copies.append(send(src, dst, *sems, target))
        self.queue.append((stage, u, copies))

    def advance(self):
        stage, u, copies = self.queue.pop(0)
        slot, y_first, turn = self.units[u]
        part, first, second, third = self.buffers[slot]
        z, y, x = self.spot
        for copy in copies:
            copy.wait()
        group = self.group(stage, y_first)
        across = self.dims[2] if y_first else self.dims[1]
        if stage == 0 and group:

            def add_first(i, carry):
                a, b = i // across, i % across
                at = (a, y, b) if y_first else (a, b, x)
                value = part[at].astype(jnp.float32)
                for k in range(len(group)):
                    value += first[k, a, b].astype(jnp.float32)
                part[at] = value.astype(part.dtype)
                return carry

            lax.fori_loop(0, self.dims[0] * across, add_first, 0)
        if stage == 1 and group:

            def add_second(i, carry):
                value = part[i, y, x].astype(jnp.float32)
                for k in range(len(group)):
                    value += second[k, i].astype(jnp.float32)
                part[i, y, x] = value.astype(part.dtype)
                return carry

            lax.fori_loop(0, self.dims[0], add_second, 0)
        if stage == 2:
            value = part[z, y, x].astype(jnp.float32)
            for k in range(len(group)):
                value += third[k].astype(jnp.float32)
            self.totals[u][...] = value
            self.done.add(u)
        if self.reused(u):
            for _, target in group:
                pl.semaphore_signal(
                    self.free_sem.at[slot, stage], inc=1, device_id=target, device_id_type=MESH
                )
        if stage < 2:
            self.start(stage + 1, u)

    def reused(self, u):
        slot, _, turn = self.units[u]
        return not turn and sum(unit[0] == slot for unit in self.units) > 1

    def tick(self):
        if len(self.queue) > self.least:
            self.advance()

    def need(self, u):
        while u not in self.done:
            self.advance()

    def close(self):
        while self.queue:
            self.advance()


UNITS = ("down0", "down1", "up0", "up1", "out", "words", "ents", "key", "value")
EXTRA = ("head", "proj", "norms")
UNIT_FIRST = dict(
    down0=True, down1=False, up0=True, up1=False, out=True, words=True, ents=False, key=True,
    value=False, head=True, proj=False, norms=True,
)


def sum_plan():
    names = ["head"]
    for layer in reversed(range(LAYERS)):
        names += [(layer, name) for name in UNITS]
    names += ["proj", "norms"]
    return names


def unit_width(name, half, hidden):
    return {
        "down0": hidden // 2, "down1": hidden // 2, "up0": hidden // 2, "up1": hidden // 2,
        "out": half, "words": 2 * half, "ents": 2 * half, "key": half, "value": half,
    }[name]


def backward_body(dims, names, half, hidden, *refs):
    refs = list(refs)

    def take(count):
        part = refs[:count]
        del refs[:count]
        return part

    cotangent, grad_ents, grad_head, gains, entity_rows, place_mat = take(6)
    w_attn, w_out, w_up, w_down, w_proj = take(5)
    saved = [dict(zip(SAVED, take(len(SAVED)))) for _ in range(LAYERS)]
    word_grads, incoming = take(2)
    totals = take(len(names))
    slots = list(UNITS + EXTRA)
    buffers = [take(4) for _ in slots]
    left, right, hat, xh, o, stats, stats_t = take(7)
    mat_wide, mat_out, mat_attn, mat_proj = take(4)
    gacc, glow, gmix, delta, dk_acc, dv_acc, gnorm = take(7)
    mine, theirs = take(2)
    sum_sems = take(2)
    (free_sem,) = take(1)
    pair_sems = take(2)
    (load_sem,) = take(1)
    out_rows, in_rows, row_send, row_recv = take(4)

    units = []
    for name in names:
        kind = name if isinstance(name, str) else name[1]
        turn = not isinstance(name, str) and name[0] < LAYERS - 1
        units.append((slots.index(kind), UNIT_FIRST[kind], turn))
    sums = Sums(dims, units, buffers, totals, sum_sems, free_sem)
    pair = Pair(mine, theirs, pair_sems)
    count = dims[0] * dims[1] * dims[2]
    greet_line(count, [pair.other])
    part_of = {slot: buffers[i][0] for i, slot in enumerate(slots)}
    loads, counter = {}, [0]

    def load(key, src, dst):
        copy = pltpu.make_async_copy(src, dst, load_sem.at[counter[0]])
        counter[0] += 1
        copy.start()
        loads.setdefault(key, []).append(copy)

    def ready(key):
        for copy in loads.pop(key, []):
            copy.wait()

    def tick(times=1):
        for _ in range(times):
            sums.tick()

    def begin_layer(layer):
        s = saved[layer]
        load("n2", s["n2"], hat)
        load("stats", s["stats"], stats)
        load("g", s["g"], left)
        load("down", w_down.at[layer], mat_wide)
        load("slope", s["slope"], right)
        load("h1b", s["h1b"], xh)
        load("out", w_out.at[layer], mat_out)
        load("o", s["o"], o)
        load("attn", w_attn.at[pl.ds(6 * layer, 6)], mat_attn)

    begin_layer(LAYERS - 1)
    load("proj", w_proj.at[0], mat_proj)
    slab = 2 if dims[0] % 2 == 0 else 1
    height = slab * D // dims[0]

    def fill(name, lhs, rhs, rhs_cols, row_slice=slice(None)):
        part = part_of[name]
        width = part.shape[-1]

        def block(i, carry):
            cols = pl.ds(pl.multiple_of(i * height, 128), height)
            value = mm_lt(lhs[row_slice, cols], rhs[row_slice, rhs_cols])
            shape = (slab, dims[1], dims[2], part.shape[3], width)
            part[pl.ds(i * slab, slab)] = value.astype(jnp.bfloat16).reshape(shape)
            return carry

        lax.fori_loop(0, dims[0] // slab, block, 0)

    def submit(layer, name):
        sums.start(0, names.index((layer, name)))

    head_part = part_of["head"]
    head_part[...] = grad_head[...]
    sums.start(0, names.index("head"))
    gacc[:WORDS] = cotangent[...].astype(jnp.float32)
    gacc[WORDS:] = grad_ents[...]
    gnorm[...] = jnp.zeros_like(gnorm)

    def add_norm(row, value):
        gnorm[row : row + 1, :] += value

    for layer in reversed(range(LAYERS)):
        last = layer == LAYERS - 1
        gain = [gains[4 * layer + i : 4 * layer + i + 1, :] for i in range(4)]
        ready("n2")
        ready("stats")

        def late_norm(c, carry):
            rows = pl.ds(c * BLOCK, BLOCK)
            back, gain_part, shift_part = norm_back(
                gacc[rows, :], hat[rows, :], stats[rows, 9:10], gain[2]
            )
            gacc[rows, :] = back
            glow[rows, :] = back.astype(jnp.bfloat16)
            add_norm(4 * layer + 2, gain_part)
            add_norm(4 * layer + 3, shift_part)
            return carry

        lax.fori_loop(0, BLOCKS, late_norm, 0)
        load("n1", saved[layer]["n1"], hat)
        ready("g")
        for i in range(2):
            if not last:
                sums.need(names.index((layer + 1, "down%d" % i)))
            cols = slice(i * (hidden // 2), (i + 1) * (hidden // 2))
            fill("down%d" % i, glow, left, cols)
            submit(layer, "down%d" % i)
            tick()
        ahead = saved[layer]
        for i, name in enumerate(("k", "qw", "qe", "v")):
            load("qkv", ahead[name], left.at[:, pl.ds(i * half, half)])
        ready("down")
        ready("slope")

        def inner(c, carry):
            rows = pl.ds(c * BLOCK, BLOCK)
            for first in range(0, hidden, 512):
                cols = slice(first, first + 512)
                weight = mat_wide[:, :, :, :, cols].reshape(D, 512)
                value = mm(glow[rows, :], weight) * right[rows, cols].astype(jnp.float32)
                right[rows, cols] = value.astype(jnp.bfloat16)
            return carry

        lax.fori_loop(0, BLOCKS, inner, 0)
        tick()
        load("up", w_up.at[layer], mat_wide)
        ready("h1b")
        for i in range(2):
            if not last:
                sums.need(names.index((layer + 1, "up%d" % i)))
            cols = slice(i * (hidden // 2), (i + 1) * (hidden // 2))
            fill("up%d" % i, xh, right, cols)
            submit(layer, "up%d" % i)
            tick()
        load("xb", saved[layer]["xb"], xh)
        ready("up")
        ready("n1")

        def up_part(c, rows):
            return mm_rt(right[rows, :], flat(mat_wide))

        def early_norm(c, rows, total):
            back, gain_part, shift_part = norm_back(
                gacc[rows, :] + total, hat[rows, :], stats[rows, 8:9], gain[0]
            )
            gacc[rows, :] = back
            glow[rows, :] = back.astype(jnp.bfloat16)
            add_norm(4 * layer, gain_part)
            add_norm(4 * layer + 1, shift_part)

        pair.run(up_part, early_norm, tick)
        ready("o")
        ready("out")
        if not last:
            sums.need(names.index((layer + 1, "out")))
        fill("out", glow, o, slice(None))
        submit(layer, "out")

        def mixed(c, carry):
            rows = pl.ds(c * BLOCK, BLOCK)
            gmix[rows, :] = mm(glow[rows, :], flat(mat_out)).astype(jnp.bfloat16)
            stats_t[:, rows] = stats[rows, :].T
            return carry

        lax.fori_loop(0, BLOCKS, mixed, 0)
        tick()
        ready("qkv")
        for head_pair in range(half // (2 * HEAD_DIM)):
            lo = head_pair * 2 * HEAD_DIM
            lanes = slice(lo, lo + 2 * HEAD_DIM)
            k_lanes, qw_lanes, qe_lanes, v_lanes = [
                slice(j * half + lo, j * half + lo + 2 * HEAD_DIM) for j in range(4)
            ]

            def products(c, carry):
                rows = pl.ds(c * BLOCK, BLOCK)
                both = gmix[rows, lanes].astype(jnp.float32) * o[rows, lanes].astype(jnp.float32)
                turned = both.T
                delta[0:1, rows] = jnp.sum(turned[:HEAD_DIM], axis=0, keepdims=True)
                delta[1:2, rows] = jnp.sum(turned[HEAD_DIM:], axis=0, keepdims=True)
                return carry

            lax.fori_loop(0, BLOCKS, products, 0)
            dk_acc[...] = jnp.zeros_like(dk_acc)
            dv_acc[...] = jnp.zeros_like(dv_acc)

            def block(i, carry):
                rows = pl.ds(i * BLOCK, BLOCK)
                keys, values = left[:, k_lanes], left[:, v_lanes]
                grad_qw = grad_qe = None
                for which in range(2):
                    head = 2 * head_pair + which
                    q_mask, k_mask = lane_mask(BLOCK, which), lane_mask(LEN, which)
                    query_w = left[rows, qw_lanes] * q_mask
                    query_e = left[rows, qe_lanes] * q_mask
                    grad_o = gmix[rows, lanes] * q_mask
                    log_row = stats_t[head : head + 1, rows]
                    inner_row = delta[which : which + 1, rows]
                    own_keys = keys * k_mask
                    for span, query in ((slice(0, WORDS), query_w), (slice(WORDS, LEN), query_e)):
                        prob = jnp.exp2(mm_rt(keys[span], query) * SCORE_STEP - log_row)
                        grad_prob = mm_rt(values[span], grad_o)
                        dv_acc[span, :] += mm(prob.astype(jnp.bfloat16), grad_o)
                        grad_score = (prob * (grad_prob - inner_row)).astype(jnp.bfloat16)
                        dk_acc[span, :] += mm(grad_score, query)
                        part = mm_lt(grad_score, own_keys[span])
                        if span.start == 0:
                            grad_qw = part if grad_qw is None else grad_qw + part
                        else:
                            grad_qe = part if grad_qe is None else grad_qe + part
                right[rows, lanes] = (grad_qw * 0.125).astype(jnp.bfloat16)
                right[rows, half + lo : half + lo + 2 * HEAD_DIM] = (grad_qe * 0.125).astype(
                    jnp.bfloat16
                )
                return carry

            for first in range(0, BLOCKS, 2):
                lax.fori_loop(first, first + 2, block, 0)
                tick()
            at = 2 * half + lo
            right[:, at : at + 2 * HEAD_DIM] = (dk_acc[...] * 0.125).astype(jnp.bfloat16)
            at = 3 * half + lo
            right[:, at : at + 2 * HEAD_DIM] = dv_acc[...].astype(jnp.bfloat16)
        ready("xb")
        words, ents = slice(0, WORDS), slice(WORDS, LEN)
        for name, cols, rows in (
            ("words", slice(0, 2 * half), words),
            ("ents", slice(0, 2 * half), ents),
            ("key", slice(2 * half, 3 * half), slice(None)),
            ("value", slice(3 * half, 4 * half), slice(None)),
        ):
            if not last:
                sums.need(names.index((layer + 1, name)))
            fill(name, xh, right, cols, rows)
            submit(layer, name)
            tick()
        ready("attn")
        mats = [slice(j * half, (j + 1) * half) for j in range(4)]

        def input_part(c, rows):
            total = mm_rt(right[rows, mats[2]], flat(mat_attn, 4))
            total += mm_rt(right[rows, mats[3]], flat(mat_attn, 5))
            start = c * BLOCK
            edge = min(max(WORDS - start, 0), BLOCK)
            pieces = []
            for low, high, pick in ((0, edge, (0, 1)), (edge, BLOCK, (2, 3))):
                if high > low:
                    span = slice(start + low, start + high)
                    piece = mm_rt(right[span, mats[0]], flat(mat_attn, pick[0]))
                    pieces.append(piece + mm_rt(right[span, mats[1]], flat(mat_attn, pick[1])))
            return total + (pieces[0] if len(pieces) == 1 else jnp.concatenate(pieces, axis=0))

        def to_input(c, rows, total):
            gacc[rows, :] += total

        pair.run(input_part, to_input, tick)
        if layer:
            begin_layer(layer - 1)
    ready("proj")
    leaving = pltpu.make_async_copy(gacc.at[pl.ds(0, WORDS)], word_grads, load_sem.at[counter[0]])
    leaving.start()
    grad_entity = gacc[WORDS:].astype(jnp.bfloat16)
    row_grads = mm_rt(grad_entity, flat(mat_proj)).astype(jnp.bfloat16)
    out_rows[...] = mm_lt(place_mat[...], row_grads).reshape(out_rows.shape)
    returning = Fan(count, (row_send, row_recv), lambda me, to: (out_rows.at[to], in_rows.at[me]))
    returning.start()
    here = lax.axis_index("dp")
    in_rows[here] = out_rows[here]
    proj_part = part_of["proj"]
    proj_part[...] = mm_lt(entity_rows[...], grad_entity).astype(jnp.bfloat16).reshape(proj_part.shape)
    sums.start(0, names.index("proj"))
    width = D // count
    norm_low = gnorm[...].astype(jnp.bfloat16)
    for d in range(count):
        z, rest = d // (dims[1] * dims[2]), d % (dims[1] * dims[2])
        row = lax.broadcasted_iota(jnp.int32, (128, D), 0)
        lane = lax.broadcasted_iota(jnp.int32, (128, D), 1)
        hot = jnp.where((row + d * width == lane) & (row < width), 1.0, 0.0).astype(jnp.bfloat16)
        block = mm_rt(norm_low, hot).astype(jnp.bfloat16)
        part_of["norms"][z, rest // dims[2], rest % dims[2]] = block
    sums.start(0, names.index("norms"))
    sums.close()
    returning.wait()
    incoming[...] = flat(in_rows)
    leaving.wait()


def run_backward(
    dims, cotangent, grad_ents, grad_head, gains, entity_rows, place_mat, kept, saved, collective_id
):
    names = sum_plan()
    half, hidden = kept[0].shape[-1], kept[2].shape[-1]
    low, full = jnp.bfloat16, jnp.float32
    rows = kept[0].shape[4]
    blocks = {name: (rows, unit_width(name, half, hidden)) for name in UNITS}
    blocks["head"] = (rows, kept[5].shape[-1])
    blocks["proj"] = (kept[4].shape[4], D)
    blocks["norms"] = (16, 128)
    scratch = []
    for name in UNITS + EXTRA:
        y_first = UNIT_FIRST[name]
        own = (dims[0], dims[2] if y_first else dims[1])
        turns = (dims[1], dims[2]) if y_first else (dims[2], dims[1])
        block = blocks[name]
        scratch += [
            pltpu.VMEM((*dims, *block), low),
            pltpu.VMEM((max(turns[0] - 1, 1), *own, *block), low),
            pltpu.VMEM((max(turns[1] - 1, 1), dims[0], *block), low),
            pltpu.VMEM((max(dims[0] - 1, 1), *block), low),
        ]
    copies = dims[0] + 2 * max(dims[1:])
    kinds = [name if isinstance(name, str) else name[1] for name in names]
    count = dims[0] * dims[1] * dims[2]
    width, slots = kept[5].shape[-1], place_mat.shape[1]
    inputs = [cotangent, grad_ents, grad_head, gains, entity_rows, place_mat, *kept[:5]]
    inputs += [saved[layer][name] for layer in range(LAYERS) for name in SAVED]
    result = pl.pallas_call(
        functools.partial(backward_body, dims, names, half, hidden),
        out_shape=[
            jax.ShapeDtypeStruct((WORDS, D), full),
            jax.ShapeDtypeStruct((slots, width), full),
        ]
        + [jax.ShapeDtypeStruct(blocks[kind], full) for kind in kinds],
        in_specs=[VMEM] * 6 + [ANY] * (len(inputs) - 6),
        out_specs=[ANY] + [VMEM] * (1 + len(names)),
        scratch_shapes=scratch
        + [
            pltpu.VMEM((LEN, hidden), low),
            pltpu.VMEM((LEN, hidden), low),
            pltpu.VMEM((LEN, D), low),
            pltpu.VMEM((LEN, D), low),
            pltpu.VMEM((LEN, half), low),
            pltpu.VMEM((LEN, 128), full),
            pltpu.VMEM((128, LEN), full),
            pltpu.VMEM(kept[2].shape[1:], low),
            pltpu.VMEM(kept[1].shape[1:], low),
            pltpu.VMEM((6, *kept[0].shape[1:]), low),
            pltpu.VMEM(kept[4].shape[1:], low),
            pltpu.VMEM((LEN, D), full),
            pltpu.VMEM((LEN, D), low),
            pltpu.VMEM((LEN, half), low),
            pltpu.VMEM((8, LEN), full),
            pltpu.VMEM((LEN, 2 * HEAD_DIM), full),
            pltpu.VMEM((LEN, 2 * HEAD_DIM), full),
            pltpu.VMEM((16, D), full),
            pltpu.VMEM((BLOCKS, BLOCK, D), low),
            pltpu.VMEM((2, BLOCKS, BLOCK, D), low),
            pltpu.SemaphoreType.DMA((len(names), copies)),
            pltpu.SemaphoreType.DMA((len(names), copies)),
            pltpu.SemaphoreType.REGULAR((len(UNITS + EXTRA), 3)),
            pltpu.SemaphoreType.DMA((2 * LAYERS, BLOCKS)),
            pltpu.SemaphoreType.DMA((2 * LAYERS, BLOCKS)),
            pltpu.SemaphoreType.DMA((64,)),
            pltpu.VMEM((count, slots // count, width), full),
            pltpu.VMEM((count, slots // count, width), full),
            pltpu.SemaphoreType.DMA((count,)),
            pltpu.SemaphoreType.DMA((count,)),
        ],
        compiler_params=pltpu.CompilerParams(
            collective_id=collective_id, has_side_effects=True, vmem_limit_bytes=VMEM_BYTES
        ),
    )(*inputs)
    return result[0], result[1], dict(zip(names, result[2:]))


def padded_rows(values):
    extra = -values.shape[-2] % 16
    return jnp.pad(values, [(0, 0)] * (values.ndim - 2) + [(0, extra), (0, 0)])


def weight_shards(attention_in, attention_out, feed_up, feed_down, norm_params, entity_proj, head_proj):
    def turned(values):
        return jnp.swapaxes(values, 1, 2)

    mats = attention_in.reshape(-1, *attention_in.shape[2:])
    norms = norm_params.reshape(1, -1, norm_params.shape[-1])
    norms = jnp.pad(norms, [(0, 0), (0, 16 - norms.shape[1]), (0, -norms.shape[2] % 128)])
    sources = [mats, turned(attention_out), feed_up, turned(feed_down), entity_proj[None], head_proj[None]]
    heights = [part.shape[1] for part in sources]
    shards = [padded_rows(part.astype(jnp.bfloat16)) for part in sources]
    shards.append(norms.astype(jnp.bfloat16))
    return shards, heights


def unpack_weights(wholes, heights, norm_width):
    kept = []
    for part, height in zip(wholes, heights):
        part = part[..., :height, :]
        kept.append(part.reshape(part.shape[0], -1, part.shape[-1]))
    norm_all = wholes[6][0].reshape(-1, 16, wholes[6].shape[-1])[:, : LAYERS * 4, :norm_width]
    norm_all = jnp.swapaxes(norm_all, 0, 1).reshape(LAYERS, 4, -1)
    return (
        kept[0].reshape(LAYERS, 6, *kept[0].shape[1:]),
        kept[1],
        kept[2],
        kept[3],
        norm_all,
        kept[4][0],
        kept[5][0],
    )


def gather_apart(dims, shards):
    chunks = [(4, 0, 1, True), (5, 0, 1, False), (6, 0, 1, True)]
    for layer in range(LAYERS):
        chunks += [(0, 6 * layer, 3, True), (0, 6 * layer + 3, 3, False)]
        chunks += [(1, layer, 1, layer == 0), (2, layer, 1, True), (3, layer, 1, False)]
    return gather_weights(dims, shards, chunks, 1)


def sum_all(dims, layer_grads, grad_proj, grad_head):
    n_dp = dims[0] * dims[1] * dims[2]

    def blocks(values):
        cut = values.astype(jnp.bfloat16).reshape(*dims, values.shape[0] // n_dp, values.shape[1])
        return padded_rows(cut)

    parts, flags, heights = [], [], []
    for layer in reversed(range(LAYERS)):
        (words_mat, ents_mat, shared_mat), out_mat, up_mat, down_mat, _ = layer_grads[layer]
        late = layer % 2 == 0
        for values, y_first in (
            (up_mat, True),
            (down_mat, False),
            (words_mat, True),
            (ents_mat, False),
            (shared_mat, late),
            (out_mat, not late),
        ):
            parts.append(blocks(values))
            flags.append(y_first)
            heights.append(values.shape[0] // n_dp)
    for values, y_first in ((grad_proj, True), (grad_head, False)):
        parts.append(blocks(values))
        flags.append(y_first)
        heights.append(values.shape[0] // n_dp)
    norms = jnp.concatenate([layer_grads[layer][4] for layer in range(LAYERS)], axis=0)
    width = norms.shape[1] // n_dp
    norms = jnp.swapaxes(norms.reshape(norms.shape[0], n_dp, width), 0, 1)
    norms = jnp.pad(norms, [(0, 0), (0, 16 - norms.shape[1]), (0, -width % 128)])
    parts.append(norms.astype(jnp.bfloat16).reshape(*dims, *norms.shape[1:]))
    flags.append(True)
    totals = sum_gradients(dims, parts, flags, 2)
    norm_sum = totals[-1][: LAYERS * 4, :width].reshape(LAYERS, 4, width)
    totals = [total[:height] for total, height in zip(totals, heights)]
    attn, outs, ups, downs = [], [], [], []
    for layer in range(LAYERS):
        at = 6 * (LAYERS - 1 - layer)
        ups.append(totals[at])
        downs.append(totals[at + 1].T)
        for part in totals[at + 2 : at + 5]:
            half = part.shape[1] // 2
            attn += [part[:, :half], part[:, half:]]
        outs.append(totals[at + 5].T)
    attn = jnp.stack(attn)
    return (
        attn.reshape(LAYERS, 6, *attn.shape[1:]),
        jnp.stack(outs),
        jnp.stack(ups),
        jnp.stack(downs),
        norm_sum,
        totals[-2],
        totals[-1],
    )


def apart_device(
    word_inputs,
    entity_base,
    entity_ids,
    buckets,
    mask_positions,
    targets,
    word_cotangent,
    attention_in,
    attention_in_first,
    attention_in_second,
    attention_out,
    attention_out_first,
    attention_out_second,
    feed_up,
    feed_up_first,
    feed_up_second,
    feed_down,
    feed_down_first,
    feed_down_second,
    norm_params,
    norm_params_first,
    norm_params_second,
    entity_proj,
    entity_proj_first,
    entity_proj_second,
    head_proj,
    head_proj_first,
    head_proj_second,
    entity_table,
    entity_table_first,
    entity_table_second,
):
    dims = chip_grid(lax.axis_size("dp"))
    shards, heights = weight_shards(
        attention_in, attention_out, feed_up, feed_down, norm_params, entity_proj, head_proj
    )
    wholes = gather_apart(dims, shards)
    attn_low, out_low, up_low, down_low, norm_low, proj_low, head_low = unpack_weights(
        wholes, heights, norm_params.shape[-1]
    )
    gain_all = norm_low.astype(jnp.float32)
    slot_total = entity_ids.shape[0]
    shard_rows = entity_table.shape[0]
    bucket_rows = buckets.reshape(buckets.shape[2], buckets.shape[3])
    filled = bucket_rows >= 0
    safe_slot = jnp.maximum(bucket_rows, 0)
    request = jnp.where(filled, entity_ids[safe_slot] % shard_rows, -1)
    received = lax.all_to_all(request, "dp", split_axis=0, concat_axis=0, tiled=True)
    shard_base = lax.axis_index(("dp", "mp")) * shard_rows
    owned_mask = received >= 0
    safe_row = jnp.clip(received, 0, shard_rows - 1)
    table_low = entity_table.astype(jnp.bfloat16)
    replies = jnp.where(owned_mask[:, :, None], table_low[safe_row], jnp.zeros((), jnp.bfloat16))
    replied_rows_result = lax.all_to_all(replies, "dp", split_axis=0, concat_axis=0, tiled=True)
    row_placement_plan = (
        bucket_rows[:, :, None] == jnp.arange(slot_total, dtype=jnp.int32)[None, None, :]
    ).astype(jnp.bfloat16)
    local_shard_rows = jnp.einsum(
        "wvt,wvi->ti", row_placement_plan, replied_rows_result, preferred_element_type=jnp.float32
    )
    paired = pair_sum(local_shard_rows)
    masked_slots = (
        jnp.arange(SEQ_DEV, dtype=jnp.int32)[:, None] * ENT_LEN + mask_positions
    ).reshape(-1)
    keep_weight = 1.0 - jnp.any(
        jnp.arange(slot_total, dtype=jnp.int32)[:, None] == masked_slots[None, :], axis=1
    ).astype(jnp.float32)
    entity_rows = (paired * keep_weight[:, None]).astype(jnp.bfloat16)
    entity_inputs = entity_base.astype(jnp.float32) + jnp.dot(
        entity_rows, proj_low, preferred_element_type=jnp.float32
    )
    hidden = jnp.concatenate(
        [
            word_inputs.astype(jnp.float32).reshape(SEQ_DEV, WORDS, D),
            entity_inputs.reshape(SEQ_DEV, ENT_LEN, D),
        ],
        axis=1,
    )
    saved_layers = []
    for layer_index in range(LAYERS):
        hidden, saved_acts = layer_forward(
            hidden,
            attn_low[layer_index],
            out_low[layer_index],
            up_low[layer_index],
            down_low[layer_index],
            gain_all[layer_index],
        )
        saved_layers.append(saved_acts)
    seq_index = jnp.arange(SEQ_DEV, dtype=jnp.int32)[:, None]
    masked_rows = WORDS + mask_positions
    masked_low = hidden[seq_index, masked_rows].reshape(SEQ_DEV * MASK_ENT, D).astype(jnp.bfloat16)
    head_pre = jnp.dot(masked_low, head_low, preferred_element_type=jnp.float32)
    states_low = gelu_exact(head_pre).astype(jnp.bfloat16)
    all_states = spread(states_low, False, False, 3).reshape(-1, states_low.shape[1])
    logits = lax.dot_general(
        all_states, table_low, (((1,), (1,)), ((), ())), preferred_element_type=jnp.float32
    )
    flat_targets = targets.reshape(-1)
    target_hits = (
        jnp.arange(shard_rows, dtype=jnp.int32)[None, :] == (flat_targets - shard_base)[:, None]
    )
    peak_value = jnp.max(logits, axis=1)
    exp_total = jnp.sum(jnp.exp(logits - peak_value[:, None]), axis=1)
    picked = jnp.sum(jnp.where(target_hits, logits, 0.0), axis=1)
    shares = spread(jnp.stack([peak_value, exp_total, picked]), True, False, 4)
    peak_all = jnp.max(shares[:, 0], axis=0)
    total_all = jnp.sum(shares[:, 1] * jnp.exp(shares[:, 0] - peak_all), axis=0)
    picked_all = jnp.sum(shares[:, 2], axis=0)
    log_norm = peak_all + jnp.log(total_all)
    row_losses = log_norm - picked_all
    prob_rows = jnp.exp(logits - log_norm[:, None])
    grad_logits = ((prob_rows - target_hits.astype(jnp.float32)) / flat_targets.shape[0]).astype(
        jnp.bfloat16
    )
    grad_table = lax.dot_general(
        grad_logits, all_states, (((0,), (0,)), ((), ())), preferred_element_type=jnp.float32
    )
    grad_states = jnp.dot(grad_logits, table_low, preferred_element_type=jnp.float32)
    grad_states = grad_states.reshape(lax.axis_size("dp"), -1, grad_states.shape[1])
    grad_states = jnp.sum(spread(grad_states, False, True, 5), axis=0)
    grad_states = grad_states + lax.ppermute(grad_states, "mp", [(0, 1), (1, 0)])
    grad_head_pre = jax.vjp(gelu_exact, head_pre)[1](grad_states)[0].astype(jnp.bfloat16)
    grad_head = lax.dot_general(
        masked_low, grad_head_pre, (((0,), (0,)), ((), ())), preferred_element_type=jnp.float32
    )
    grad_masked = lax.dot_general(
        grad_head_pre, head_low, (((1,), (1,)), ((), ())), preferred_element_type=jnp.float32
    )
    grad_hidden = jnp.concatenate(
        [
            word_cotangent.astype(jnp.float32).reshape(SEQ_DEV, WORDS, D),
            jnp.zeros((SEQ_DEV, ENT_LEN, D), jnp.float32),
        ],
        axis=1,
    )
    grad_hidden = grad_hidden.at[seq_index, masked_rows].add(
        grad_masked.reshape(SEQ_DEV, MASK_ENT, D)
    )
    kept_grads = []
    for layer_index in reversed(range(LAYERS)):
        grad_hidden, layer_grads = layer_backward(
            grad_hidden,
            saved_layers[layer_index],
            attn_low[layer_index],
            out_low[layer_index],
            up_low[layer_index],
            down_low[layer_index],
            gain_all[layer_index],
        )
        if layer_index == 0:
            word_grads = grad_hidden[:, :WORDS].reshape(SEQ_DEV * WORDS, D)
            grad_entity = grad_hidden[:, WORDS:].reshape(slot_total, D).astype(jnp.bfloat16)
            grad_proj = lax.dot_general(
                entity_rows,
                grad_entity,
                (((0,), (0,)), ((), ())),
                preferred_element_type=jnp.float32,
            )
            row_gradient_block = (
                lax.dot_general(
                    grad_entity,
                    proj_low,
                    (((1,), (1,)), ((), ())),
                    preferred_element_type=jnp.float32,
                )
                * keep_weight[:, None]
            )
            outgoing = jnp.where(filled[:, :, None], row_gradient_block[safe_slot], 0.0)
            incoming = lax.all_to_all(
                outgoing.astype(jnp.bfloat16), "dp", split_axis=0, concat_axis=0, tiled=True
            ).astype(outgoing.dtype)
            grad_table = grad_table.at[safe_row].add(
                jnp.where(owned_mask[:, :, None], incoming, 0.0)
            )
        kept_grads.insert(0, layer_grads)
    reduced = sum_all(dims, kept_grads, grad_proj, grad_head)
    reduced_proj, reduced_head = reduced[5:]
    attn_new = adam_update(
        attention_in, attention_in_first, attention_in_second, reduced[0], kind_rates[0]
    )
    out_new = adam_update(
        attention_out, attention_out_first, attention_out_second, reduced[1], kind_rates[1]
    )
    up_new = adam_update(feed_up, feed_up_first, feed_up_second, reduced[2], kind_rates[2])
    down_new = adam_update(feed_down, feed_down_first, feed_down_second, reduced[3], kind_rates[3])
    norm_new = adam_update(
        norm_params, norm_params_first, norm_params_second, reduced[4], kind_rates[4]
    )
    proj_new = adam_update(
        entity_proj, entity_proj_first, entity_proj_second, reduced_proj, kind_rates[5]
    )
    head_new = adam_update(
        head_proj, head_proj_first, head_proj_second, reduced_head, kind_rates[6]
    )
    table_new = adam_update(
        entity_table, entity_table_first, entity_table_second, grad_table, kind_rates[7]
    )
    return (
        row_losses,
        word_grads,
        attn_new[0],
        attn_new[1],
        attn_new[2],
        out_new[0],
        out_new[1],
        out_new[2],
        up_new[0],
        up_new[1],
        up_new[2],
        down_new[0],
        down_new[1],
        down_new[2],
        norm_new[0],
        norm_new[1],
        norm_new[2],
        proj_new[0],
        proj_new[1],
        proj_new[2],
        head_new[0],
        head_new[1],
        head_new[2],
        table_new[0],
        table_new[1],
        table_new[2],
    )


def turned(*arrays):
    return tuple(jnp.swapaxes(array, 1, 2) for array in arrays)


def fused_device(
    word_inputs,
    entity_base,
    entity_ids,
    buckets,
    mask_positions,
    targets,
    word_cotangent,
    attention_in,
    attention_in_first,
    attention_in_second,
    attention_out,
    attention_out_first,
    attention_out_second,
    feed_up,
    feed_up_first,
    feed_up_second,
    feed_down,
    feed_down_first,
    feed_down_second,
    norm_params,
    norm_params_first,
    norm_params_second,
    entity_proj,
    entity_proj_first,
    entity_proj_second,
    head_proj,
    head_proj_first,
    head_proj_second,
    entity_table,
    entity_table_first,
    entity_table_second,
):
    dims = chip_grid(lax.axis_size("dp"))
    shards, heights = weight_shards(
        attention_in, attention_out, feed_up, feed_down, norm_params, entity_proj, head_proj
    )
    slot_total, shard_rows = entity_ids.shape[0], entity_table.shape[0]
    bucket_rows = buckets.reshape(buckets.shape[2], buckets.shape[3])
    request = jnp.where(
        bucket_rows >= 0, entity_ids[jnp.maximum(bucket_rows, 0)] % shard_rows, -1
    ).astype(jnp.int32)
    requests = jnp.broadcast_to(request[:, :, None], (*request.shape, 128))
    slots = jnp.arange(slot_total, dtype=jnp.int32)
    marks = mask_positions.reshape(-1)[:, None] == slots[None, :]
    keep = jnp.logical_not(jnp.any(marks, axis=0))
    place_mat = (slots[:, None] == bucket_rows.reshape(-1)[None, :]) & keep[:, None]
    place_mat = place_mat.astype(jnp.bfloat16)
    hits = marks.astype(jnp.bfloat16)
    table_low = entity_table.astype(jnp.bfloat16)
    flat_targets = targets.reshape(-1)
    local_targets = flat_targets - lax.axis_index(("dp", "mp")) * shard_rows
    local_targets = jnp.broadcast_to(local_targets[None, :], (8, flat_targets.shape[0]))
    wholes, saved_layers, ents, gain_rows, entity_rows, got = run_forward(
        dims, word_inputs, entity_base, requests, place_mat, table_low, shards, 6
    )
    losses, grad_logits, states, grad_head, grad_ents = run_head(
        dims, ents, hits, wholes[5][0], table_low, local_targets, 7
    )
    word_grads, incoming, totals = run_backward(
        dims,
        word_cotangent,
        grad_ents,
        grad_head,
        gain_rows,
        entity_rows,
        place_mat,
        wholes,
        saved_layers,
        8,
    )
    wanted = jnp.broadcast_to(got[:, 0][None, :], (8, got.shape[0]))
    updated = run_update(
        (
            (attention_in, attention_in_first, attention_in_second),
            turned(attention_out, attention_out_first, attention_out_second),
            (feed_up, feed_up_first, feed_up_second),
            turned(feed_down, feed_down_first, feed_down_second),
            (norm_params, norm_params_first, norm_params_second),
            (entity_proj, entity_proj_first, entity_proj_second),
            (head_proj, head_proj_first, head_proj_second),
            (entity_table, entity_table_first, entity_table_second),
        ),
        totals,
        incoming,
        wanted,
        grad_logits,
        states,
    )
    updated[1], updated[3] = turned(*updated[1]), turned(*updated[3])
    results = [losses[0], word_grads]
    for master, first, second in updated:
        results += [first, second, master]
    return tuple(results)


def on_device(*arrays):
    n_dp = lax.axis_size("dp")
    whole_tiles = D % (16 * n_dp) == 0
    return (fused_device if whole_tiles else apart_device)(*arrays)


def solution(mesh):
    in_specs = (
        P("dp", None),
        P("dp", None),
        P("dp"),
        P("dp", "mp", None, None),
        P("dp", None),
        P(),
        P("dp", None),
        P(None, None, "dp", "mp"),
        P(None, None, "dp", "mp"),
        P(None, None, "dp", "mp"),
        P(None, "mp", "dp"),
        P(None, "mp", "dp"),
        P(None, "mp", "dp"),
        P(None, "dp", "mp"),
        P(None, "dp", "mp"),
        P(None, "dp", "mp"),
        P(None, "mp", "dp"),
        P(None, "mp", "dp"),
        P(None, "mp", "dp"),
        P(None, None, "dp"),
        P(None, None, "dp"),
        P(None, None, "dp"),
        P("dp", None),
        P("dp", None),
        P("dp", None),
        P("dp", None),
        P("dp", None),
        P("dp", None),
        P(("dp", "mp"), None),
        P(("dp", "mp"), None),
        P(("dp", "mp"), None),
    )
    out_specs = (
        P(),
        P("dp", None),
        P(None, None, "dp", "mp"),
        P(None, None, "dp", "mp"),
        P(None, None, "dp", "mp"),
        P(None, "mp", "dp"),
        P(None, "mp", "dp"),
        P(None, "mp", "dp"),
        P(None, "dp", "mp"),
        P(None, "dp", "mp"),
        P(None, "dp", "mp"),
        P(None, "mp", "dp"),
        P(None, "mp", "dp"),
        P(None, "mp", "dp"),
        P(None, None, "dp"),
        P(None, None, "dp"),
        P(None, None, "dp"),
        P("dp", None),
        P("dp", None),
        P("dp", None),
        P("dp", None),
        P("dp", None),
        P("dp", None),
        P(("dp", "mp"), None),
        P(("dp", "mp"), None),
        P(("dp", "mp"), None),
    )
    return jax.shard_map(
        on_device, mesh=mesh, in_specs=in_specs, out_specs=out_specs, check_vma=False
    )
```

```python
import functools

import jax
import jax.numpy as jnp
from jax import lax
from jax.experimental import pallas as pl
from jax.experimental.pallas import tpu as pltpu
from jax.sharding import PartitionSpec as P

D = 768
HEAD_DIM = 64
WORDS = 896
ENT_LEN = 128
MASK_ENT = 16
LAYERS = 2
STEP = 10
SEQ_DEV = 1


norm_eps = 1e-05
beta_first = 0.9
beta_second = 0.999
adam_eps = 1e-12
weight_decay = 0.01
kind_rates = (0.05, 1.0, 0.05, 0.027, 0.75, 0.5, 0.05, 0.2)


MESH = pl.DeviceIdType.MESH
ANY = pl.BlockSpec(memory_space=pl.ANY)
VMEM = pl.BlockSpec(memory_space=pltpu.VMEM)
VMEM_BYTES = 60 * 2**20


def chip_grid(n_dp):
    return {16: (4, 2, 2), 64: (4, 4, 4)}.get(n_dp, (n_dp, 1, 1))


def place(dims):
    index = lax.axis_index("dp")
    return index // (dims[1] * dims[2]), index // dims[2] % dims[1], index % dims[2]


def axis_peers(dims, axis):
    here = place(dims)
    core = lax.axis_index("mp")
    peers = []
    for step in range(1, dims[axis]):
        spot = list(here)
        spot[axis] = lax.rem(here[axis] + step, dims[axis])
        peers.append((spot[axis], (spot[0] * dims[1] * dims[2] + spot[1] * dims[2] + spot[2], core)))
    return peers


def greet(targets):
    barrier = pltpu.get_barrier_semaphore()
    for target in targets:
        pl.semaphore_signal(barrier, inc=1, device_id=target, device_id_type=MESH)
    pl.semaphore_wait(barrier, len(targets))


def send(src, dst, send_sem, recv_sem, target):
    copy = pltpu.make_async_remote_copy(
        src_ref=src,
        dst_ref=dst,
        send_sem=send_sem,
        recv_sem=recv_sem,
        device_id=target,
        device_id_type=MESH,
    )
    copy.start()
    return copy


def gather_body(dims, chunks, count, *refs):
    shards, wholes = refs[:count], refs[count : 2 * count]
    send_sem, recv_sem, local_sem = refs[2 * count :]
    z, y, x = place(dims)
    peers = [axis_peers(dims, axis) for axis in range(3)]
    greet([target for group in peers for _, target in group])
    pending = {}

    def start(stage, c):
        which, first, size, y_first = chunks[c]
        rows = pl.ds(first, size)
        whole = wholes[which]
        copies = []
        if stage == 0:
            src, dst, group = shards[which].at[rows], whole.at[rows, z, y, x], peers[0]
            own = pltpu.make_async_copy(src, dst, local_sem.at[c])
            own.start()
            copies.append(own)
        elif stage == 1:
            src = whole.at[rows, :, y, x]
            dst, group = src, peers[1 if y_first else 2]
        else:
            src = whole.at[rows, :, :, x] if y_first else whole.at[rows, :, y]
            dst, group = src, peers[2 if y_first else 1]
        base = (0, dims[0], dims[0] + max(dims[1:]))[stage]
        for slot, (_, target) in enumerate(group):
            copies.append(
                send(src, dst, send_sem.at[c, base + slot], recv_sem.at[c, base + slot], target)
            )
        pending[stage, c] = copies

    def finish(stage, c):
        for copy in pending.pop((stage, c)):
            copy.wait()

    total = len(chunks)
    start(0, 0)
    for step in range(total + 2):
        if step + 1 < total:
            start(0, step + 1)
        if step < total:
            finish(0, step)
            start(1, step)
        if 0 <= step - 1 < total:
            finish(1, step - 1)
            start(2, step - 1)
        if 0 <= step - 2 < total:
            finish(2, step - 2)


def gather_weights(dims, shards, chunks, collective_id):
    count = len(shards)
    copies = dims[0] + 2 * max(dims[1:])
    return pl.pallas_call(
        functools.partial(gather_body, dims, chunks, count),
        out_shape=[
            jax.ShapeDtypeStruct((s.shape[0], *dims, *s.shape[1:]), s.dtype) for s in shards
        ],
        in_specs=[ANY] * count,
        out_specs=[ANY] * count,
        scratch_shapes=[
            pltpu.SemaphoreType.DMA((len(chunks), copies)),
            pltpu.SemaphoreType.DMA((len(chunks), copies)),
            pltpu.SemaphoreType.DMA((len(chunks),)),
        ],
        compiler_params=pltpu.CompilerParams(
            collective_id=collective_id, has_side_effects=True, vmem_limit_bytes=2**20
        ),
    )(*shards)


def sum_body(dims, flags, *refs):
    count = len(flags)
    parts, totals = refs[:count], refs[count : 2 * count]
    buffers = refs[2 * count : 6 * count]
    send_sem, recv_sem, local_sem = refs[6 * count :]
    z, y, x = place(dims)
    peers = [axis_peers(dims, axis) for axis in range(3)]
    greet([target for group in peers for _, target in group])
    pending = {}

    def start(stage, c):
        y_first = flags[c]
        own, first, second, third = buffers[4 * c : 4 * c + 4]
        copies = []
        base = (0, max(dims[1:]), 2 * max(dims[1:]))[stage]
        if stage == 0:
            mine = parts[c].at[:, y] if y_first else parts[c].at[:, :, x]
            local = pltpu.make_async_copy(mine, own, local_sem.at[c])
            local.start()
            copies.append(local)
        group = peers[((1, 2, 0) if y_first else (2, 1, 0))[stage]]
        for slot, (spot, target) in enumerate(group):
            if stage == 0:
                src = parts[c].at[:, spot] if y_first else parts[c].at[:, :, spot]
                dst = first.at[slot]
            elif stage == 1:
                src, dst = own.at[:, spot], second.at[slot]
            else:
                src, dst = own.at[spot, x if y_first else y], third.at[slot]
            copies.append(
                send(src, dst, send_sem.at[c, base + slot], recv_sem.at[c, base + slot], target)
            )
        pending[stage, c] = copies

    def finish(stage, c):
        y_first = flags[c]
        own, first, second, third = buffers[4 * c : 4 * c + 4]
        for copy in pending.pop((stage, c)):
            copy.wait()
        across = dims[2] if y_first else dims[1]
        line = x if y_first else y
        count_peers = len(peers[((1, 2, 0) if y_first else (2, 1, 0))[stage]])
        if stage == 0 and count_peers:

            def add_first(i, carry):
                value = own[i // across, i % across].astype(jnp.float32)
                for slot in range(count_peers):
                    value += first[slot, i // across, i % across].astype(jnp.float32)
                own[i // across, i % across] = value.astype(own.dtype)
                return carry

            lax.fori_loop(0, dims[0] * across, add_first, 0)
        if stage == 1 and count_peers:

            def add_second(i, carry):
                value = own[i, line].astype(jnp.float32)
                for slot in range(count_peers):
                    value += second[slot, i].astype(jnp.float32)
                own[i, line] = value.astype(own.dtype)
                return carry

            lax.fori_loop(0, dims[0], add_second, 0)
        if stage == 2:
            value = own[z, line].astype(jnp.float32)
            for slot in range(count_peers):
                value += third[slot].astype(jnp.float32)
            totals[c][...] = value

    total = len(flags)
    ahead = 2
    for c in range(min(ahead, total)):
        start(0, c)
    for step in range(total + 2 * ahead):
        if step + ahead < total:
            start(0, step + ahead)
        if step < total:
            finish(0, step)
            start(1, step)
        if 0 <= step - ahead < total:
            finish(1, step - ahead)
            start(2, step - ahead)
        if 0 <= step - 2 * ahead < total:
            finish(2, step - 2 * ahead)


def sum_gradients(dims, parts, flags, collective_id):
    count = len(parts)
    scratch = []
    for part, y_first in zip(parts, flags):
        block = part.shape[3:]
        own = (dims[0], dims[2] if y_first else dims[1])
        turns = (dims[1], dims[2]) if y_first else (dims[2], dims[1])
        scratch += [
            pltpu.VMEM((*own, *block), part.dtype),
            pltpu.VMEM((max(turns[0] - 1, 1), *own, *block), part.dtype),
            pltpu.VMEM((max(turns[1] - 1, 1), dims[0], *block), part.dtype),
            pltpu.VMEM((max(dims[0] - 1, 1), *block), part.dtype),
        ]
    copies = dims[0] + 2 * max(dims[1:])
    return pl.pallas_call(
        functools.partial(sum_body, dims, flags),
        out_shape=[jax.ShapeDtypeStruct(part.shape[3:], jnp.float32) for part in parts],
        in_specs=[ANY] * count,
        out_specs=[VMEM] * count,
        scratch_shapes=scratch
        + [
            pltpu.SemaphoreType.DMA((count, copies)),
            pltpu.SemaphoreType.DMA((count, copies)),
            pltpu.SemaphoreType.DMA((count,)),
        ],
        compiler_params=pltpu.CompilerParams(
            collective_id=collective_id, has_side_effects=True, vmem_limit_bytes=VMEM_BYTES
        ),
    )(*parts)


def spread_body(count, wide, swap, data, result, send_sem, recv_sem, local_sem):
    pair = lax.axis_size("mp")
    index = lax.axis_index("dp") * pair + lax.axis_index("mp") if wide else lax.axis_index("dp")

    def target_of(step):
        other = lax.rem(index + step, count)
        if wide:
            return other, (other // pair, lax.rem(other, pair))
        return other, (other, lax.axis_index("mp"))

    barrier = pltpu.get_barrier_semaphore()

    def hello(step, carry):
        pl.semaphore_signal(barrier, inc=1, device_id=target_of(step)[1], device_id_type=MESH)
        return carry

    lax.fori_loop(1, count, hello, 0)
    pl.semaphore_wait(barrier, count - 1)
    own = pltpu.make_async_copy(data.at[index if swap else 0], result.at[index], local_sem)
    own.start()

    def copy_of(step):
        other, target = target_of(step)
        return pltpu.make_async_remote_copy(
            src_ref=data.at[other if swap else 0],
            dst_ref=result.at[index],
            send_sem=send_sem.at[step],
            recv_sem=recv_sem.at[step],
            device_id=target,
            device_id_type=MESH,
        )

    def go(step, carry):
        copy_of(step).start()
        return carry

    def done(step, carry):
        copy_of(step).wait()
        return carry

    lax.fori_loop(1, count, go, 0)
    own.wait()
    lax.fori_loop(1, count, done, 0)


def spread(data, wide, swap, collective_id):
    count = lax.axis_size("dp") * (lax.axis_size("mp") if wide else 1)
    block = data.shape[1:] if swap else data.shape
    return pl.pallas_call(
        functools.partial(spread_body, count, wide, swap),
        out_shape=jax.ShapeDtypeStruct((count, *block), data.dtype),
        in_specs=[VMEM],
        out_specs=VMEM,
        scratch_shapes=[
            pltpu.SemaphoreType.DMA((count,)),
            pltpu.SemaphoreType.DMA((count,)),
            pltpu.SemaphoreType.DMA,
        ],
        compiler_params=pltpu.CompilerParams(
            collective_id=collective_id, has_side_effects=True, vmem_limit_bytes=VMEM_BYTES
        ),
    )(data if swap else data[None])


def layer_norm(values, gain_row, shift_row):
    centered = values - jnp.mean(values, axis=-1, keepdims=True)
    spread = jnp.mean(centered * centered, axis=-1, keepdims=True)
    return centered * lax.rsqrt(spread + norm_eps) * gain_row + shift_row


def gelu_exact(values):
    return jax.nn.gelu(values, approximate=False)


def adam_update(master, first_moment, second_moment, gradient, kind_rate):
    first_new = beta_first * first_moment + (1.0 - beta_first) * gradient
    second_new = beta_second * second_moment + (1.0 - beta_second) * gradient * gradient
    first_hat = first_new / (1.0 - beta_first**STEP)
    second_hat = second_new / (1.0 - beta_second**STEP)
    master_new = master - kind_rate * (
        first_hat / (jnp.sqrt(second_hat) + adam_eps) + weight_decay * master
    )
    return (first_new, second_new, master_new)


def project(fetched_row_values, weight_matrix_entry):
    return jnp.einsum(
        "mvw,wu->mvu", fetched_row_values, weight_matrix_entry, preferred_element_type=jnp.float32
    )


def project_back(row_gradient_block, weight_matrix_entry):
    return jnp.einsum(
        "tic,vc->tiv", row_gradient_block, weight_matrix_entry, preferred_element_type=jnp.float32
    )


def project_turned(rows, turned):
    return jnp.einsum("mvw,uw->mvu", rows, turned, preferred_element_type=jnp.float32)


def project_back_turned(row_gradient_block, turned):
    return jnp.einsum("tic,cv->tiv", row_gradient_block, turned, preferred_element_type=jnp.float32)


def weight_grad(layer_input_list, row_gradient_block):
    return jnp.einsum(
        "hmq,hmw->qw", layer_input_list, row_gradient_block, preferred_element_type=jnp.float32
    ).astype(jnp.bfloat16)


def split_heads(values):
    return values.reshape(values.shape[0], values.shape[1], values.shape[2] // HEAD_DIM, HEAD_DIM)


def pair_sum(partial_sum):
    mine = partial_sum.astype(jnp.bfloat16)
    theirs = lax.ppermute(mine, "mp", [(0, 1), (1, 0)])
    return mine.astype(jnp.float32) + theirs.astype(jnp.float32)


merge_heads = merge_inputs = pair_sum


def seq_scores(query_word, query_entity, key_rows):
    score_word = jnp.einsum(
        "qhd,khd->hqk", query_word, key_rows[:WORDS], preferred_element_type=jnp.float32
    )
    score_entity = jnp.einsum(
        "qhd,khd->hqk", query_entity, key_rows[WORDS:], preferred_element_type=jnp.float32
    )
    return jnp.concatenate([score_word, score_entity], axis=-1) * 0.125


def attend_forward(seq_item):
    query_word, query_entity, key_rows, value_rows = seq_item
    scores = seq_scores(query_word, query_entity, key_rows)
    peak_value = jnp.max(scores, axis=-1, keepdims=True)
    exp_scores = jnp.exp(scores - peak_value)
    exp_total = jnp.sum(exp_scores, axis=-1, keepdims=True)
    prob_low = (exp_scores / exp_total).astype(jnp.bfloat16)
    mixed_heads = jnp.einsum(
        "hqk,khd->qhd", prob_low, value_rows, preferred_element_type=jnp.float32
    )
    return (mixed_heads, (peak_value + jnp.log(exp_total))[..., 0])


def attend_backward(seq_item):
    query_word, query_entity, key_rows, value_rows, log_norm, grad_mixed = seq_item
    scores = seq_scores(query_word, query_entity, key_rows)
    prob_rows = jnp.exp(scores - log_norm[..., None])
    grad_value = jnp.einsum(
        "hqk,qhd->khd",
        prob_rows.astype(jnp.bfloat16),
        grad_mixed,
        preferred_element_type=jnp.float32,
    )
    grad_probs = jnp.einsum(
        "qhd,khd->hqk", grad_mixed, value_rows, preferred_element_type=jnp.float32
    )
    inner_sum = jnp.sum(prob_rows * grad_probs, axis=-1, keepdims=True)
    grad_scores = (prob_rows * (grad_probs - inner_sum) * 0.125).astype(jnp.bfloat16)
    score_word = grad_scores[..., :WORDS]
    score_entity = grad_scores[..., WORDS:]
    grad_qw = jnp.einsum(
        "hqk,khd->qhd", score_word, key_rows[:WORDS], preferred_element_type=jnp.float32
    )
    grad_qe = jnp.einsum(
        "hqk,khd->qhd", score_entity, key_rows[WORDS:], preferred_element_type=jnp.float32
    )
    grad_key = jnp.concatenate(
        [
            jnp.einsum("hqk,qhd->khd", score_word, query_word, preferred_element_type=jnp.float32),
            jnp.einsum(
                "hqk,qhd->khd", score_entity, query_entity, preferred_element_type=jnp.float32
            ),
        ],
        axis=0,
    )
    return (grad_qw, grad_qe, grad_key, grad_value)


def layer_forward(hidden, attn_mats, out_mat, up_mat, down_mat, gain_rows):
    hidden_low = hidden.astype(jnp.bfloat16)
    words_low = hidden_low[:, :WORDS]
    ents_low = hidden_low[:, WORDS:]
    query_word = jnp.concatenate(
        [project(words_low, attn_mats[0]), project(ents_low, attn_mats[2])], axis=1
    ).astype(jnp.bfloat16)
    query_entity = jnp.concatenate(
        [project(words_low, attn_mats[1]), project(ents_low, attn_mats[3])], axis=1
    ).astype(jnp.bfloat16)
    key_rows = project(hidden_low, attn_mats[4]).astype(jnp.bfloat16)
    value_rows = project(hidden_low, attn_mats[5]).astype(jnp.bfloat16)
    mixed_heads, log_norm = lax.map(
        attend_forward,
        (
            split_heads(query_word),
            split_heads(query_entity),
            split_heads(key_rows),
            split_heads(value_rows),
        ),
    )
    mixed_low = mixed_heads.reshape(key_rows.shape).astype(jnp.bfloat16)
    attended = merge_heads(project_turned(mixed_low, out_mat))
    first_out = layer_norm(hidden + attended, gain_rows[0], gain_rows[1])
    first_low = first_out.astype(jnp.bfloat16)
    inner_pre = project(first_low, up_mat)
    inner_low = gelu_exact(inner_pre).astype(jnp.bfloat16)
    outer_out = merge_heads(project_turned(inner_low, down_mat))
    result = layer_norm(first_out + outer_out, gain_rows[2], gain_rows[3])
    saved_acts = (
        hidden,
        hidden_low,
        query_word,
        query_entity,
        key_rows,
        value_rows,
        log_norm,
        mixed_low,
        attended,
        first_out,
        first_low,
        inner_pre,
        inner_low,
        outer_out,
    )
    return (result, saved_acts)


def layer_backward(grad_out, saved_acts, attn_mats, out_mat, up_mat, down_mat, gain_rows):
    (
        hidden,
        hidden_low,
        query_word,
        query_entity,
        key_rows,
        value_rows,
        log_norm,
        mixed_low,
        attended,
        first_out,
        first_low,
        inner_pre,
        inner_low,
        outer_out,
    ) = saved_acts
    second_back = jax.vjp(layer_norm, first_out + outer_out, gain_rows[2], gain_rows[3])[1]
    grad_second, grad_gain_late, grad_shift_late = second_back(grad_out)
    grad_outer = grad_second.astype(jnp.bfloat16)
    grad_down = weight_grad(grad_outer, inner_low)
    grad_inner = project_back_turned(grad_outer, down_mat)
    grad_pre = jax.vjp(gelu_exact, inner_pre)[1](grad_inner)[0].astype(jnp.bfloat16)
    grad_up = weight_grad(first_low, grad_pre)
    grad_first = grad_second + merge_inputs(project_back(grad_pre, up_mat))
    first_back = jax.vjp(layer_norm, hidden + attended, gain_rows[0], gain_rows[1])[1]
    grad_first_in, grad_gain_early, grad_shift_early = first_back(grad_first)
    grad_attended = grad_first_in.astype(jnp.bfloat16)
    grad_out_mat = weight_grad(grad_attended, mixed_low)
    grad_mixed = project_back_turned(grad_attended, out_mat).astype(jnp.bfloat16)
    grad_qw, grad_qe, grad_key, grad_value = lax.map(
        attend_backward,
        (
            split_heads(query_word),
            split_heads(query_entity),
            split_heads(key_rows),
            split_heads(value_rows),
            log_norm,
            split_heads(grad_mixed),
        ),
    )
    flat_shape = key_rows.shape
    grad_qw = grad_qw.reshape(flat_shape).astype(jnp.bfloat16)
    grad_qe = grad_qe.reshape(flat_shape).astype(jnp.bfloat16)
    grad_key = grad_key.reshape(flat_shape).astype(jnp.bfloat16)
    grad_value = grad_value.reshape(flat_shape).astype(jnp.bfloat16)
    words_low = hidden_low[:, :WORDS]
    ents_low = hidden_low[:, WORDS:]
    grad_mats = (
        weight_grad(words_low, jnp.concatenate([grad_qw[:, :WORDS], grad_qe[:, :WORDS]], axis=-1)),
        weight_grad(ents_low, jnp.concatenate([grad_qw[:, WORDS:], grad_qe[:, WORDS:]], axis=-1)),
        weight_grad(hidden_low, jnp.concatenate([grad_key, grad_value], axis=-1)),
    )
    part_words = project_back(grad_qw[:, :WORDS], attn_mats[0]) + project_back(
        grad_qe[:, :WORDS], attn_mats[1]
    )
    part_ents = project_back(grad_qw[:, WORDS:], attn_mats[2]) + project_back(
        grad_qe[:, WORDS:], attn_mats[3]
    )
    part_sum = (
        jnp.concatenate([part_words, part_ents], axis=1)
        + project_back(grad_key, attn_mats[4])
        + project_back(grad_value, attn_mats[5])
    )
    grad_hidden = grad_first_in + merge_inputs(part_sum)
    grad_norms = jnp.stack([grad_gain_early, grad_shift_early, grad_gain_late, grad_shift_late])
    return (grad_hidden, (grad_mats, grad_out_mat, grad_up, grad_down, grad_norms))


LOG2E = 1.4426950408889634
SCORE_STEP = 0.125 * LOG2E
LEN = WORDS + ENT_LEN
BLOCK = 256
BLOCKS = LEN // BLOCK


def mm(left, right):
    return lax.dot_general(
        left, right, (((1,), (0,)), ((), ())), preferred_element_type=jnp.float32
    )


def mm_rt(left, right):
    return lax.dot_general(
        left, right, (((1,), (1,)), ((), ())), preferred_element_type=jnp.float32
    )


def mm_lt(left, right):
    return lax.dot_general(
        left, right, (((0,), (0,)), ((), ())), preferred_element_type=jnp.float32
    )


def flat(ref, *index):
    value = ref[index] if index else ref[...]
    return value.reshape(-1, value.shape[-1])


def lane_mask(rows, which):
    lane = lax.broadcasted_iota(jnp.int32, (rows, 2 * HEAD_DIM), 1)
    return (lane // HEAD_DIM == which).astype(jnp.bfloat16)


def normed(values):
    centered = values - jnp.mean(values, axis=-1, keepdims=True)
    spread_row = jnp.mean(centered * centered, axis=-1, keepdims=True)
    scale = lax.rsqrt(spread_row + norm_eps)
    return centered * scale, scale


def gelu_parts(values):
    cdf = 0.5 * (1.0 + lax.erf(values * 0.7071067811865476))
    bell = jnp.exp2(values * values * (-0.5 * LOG2E)) * 0.3989422804014327
    return values * cdf, cdf + values * bell


LINK_BYTES_US = 45000.0
HOP_US = 1.5
ORDERS = ((0, 1, 2), (0, 2, 1), (2, 0, 1), (1, 0, 2))


def cut_load(size):
    return (size // 2) * (size - size // 2)


def gather_loads(dims, order, shard_bytes):
    loads, held = [0.0, 0.0, 0.0], shard_bytes
    for axis in order:
        loads[axis] += held * cut_load(dims[axis])
        held *= dims[axis]
    return loads


def balanced_orders(dims, sizes):
    total, chosen = [0.0, 0.0, 0.0], []
    for size in sizes:
        options = []
        for rank, order in enumerate(ORDERS):
            loads = gather_loads(dims, order, size)
            after = [a + b for a, b in zip(total, loads)]
            options.append((max(after), sum(after), rank, order, after))
        best = min(options)
        chosen.append(best[3])
        total = best[4]
    return chosen


class Links:
    def __init__(self, dims):
        self.dims = dims
        self.clock, self.free, self.serial = 0.0, [0.0, 0.0, 0.0], 0
        self.active = []

    def issue(self, axis, message_bytes, what):
        if self.dims[axis] > 1:
            begin = max(self.clock, self.free[axis])
            self.free[axis] = begin + message_bytes * cut_load(self.dims[axis]) / LINK_BYTES_US
            finish = self.free[axis] + HOP_US
        else:
            finish = self.clock
        self.serial += 1
        self.active.append((finish, self.serial, what))

    def finish_first(self):
        first = min(self.active, key=lambda item: item[:2])
        self.active.remove(first)
        self.clock = max(self.clock, first[0])
        self.complete(first[2])

    def spend(self, micros):
        self.clock += micros
        while self.active and min(item[0] for item in self.active) <= self.clock:
            self.finish_first()


class Gather(Links):
    def __init__(self, dims, chunks, shards, wholes, kept, sems):
        super().__init__(dims)
        self.chunks, self.shards, self.wholes, self.kept = chunks, shards, wholes, kept
        self.send_sem, self.recv_sem, self.local_sem, self.keep_sem = sems
        self.spot = place(dims)
        self.peers = [axis_peers(dims, axis) for axis in range(3)]
        self.copies, self.done, self.keeping = {}, set(), []
        self.next, self.window = 0, 6

    def slab(self, whole, order, stage):
        held = order[:stage]
        return whole.at[
            (slice(None), *[slice(None) if d in held else self.spot[d] for d in range(3)])
        ]

    def start(self, stage, c):
        which, rows, cols, order = self.chunks[c]
        whole = self.wholes[which].at[rows, :, :, :, :, cols]
        shard = self.shards[which].at[rows, :, cols]
        copies, base = [], sum(self.dims[order[i]] for i in range(stage))
        dst = self.slab(whole, order, stage)
        src = dst
        if stage == 0:
            own = pltpu.make_async_copy(shard, dst, self.local_sem.at[c])
            own.start()
            copies.append(own)
            src = shard
        for slot, (_, target) in enumerate(self.peers[order[stage]]):
            sems = self.send_sem.at[c, base + slot], self.recv_sem.at[c, base + slot]
            copies.append(send(src, dst, *sems, target))
        self.copies[stage, c] = copies
        held = 1
        for axis in order[:stage]:
            held *= self.dims[axis]
        shape = shard.shape
        self.issue(order[stage], held * 2 * shape[0] * shape[1] * shape[2], (stage, c))

    def complete(self, what):
        stage, c = what
        for copy in self.copies.pop(what):
            copy.wait()
        if stage < 2:
            self.start(stage + 1, c)
        else:
            which, rows, cols, _ = self.chunks[c]
            at = (rows, slice(None), slice(None), slice(None), slice(None), cols)
            keep = pltpu.make_async_copy(
                self.wholes[which].at[at], self.kept[which].at[at], self.keep_sem.at[c]
            )
            keep.start()
            self.keeping.append(keep)
            self.done.add(c)
        self.refill()

    def refill(self):
        while self.next < len(self.chunks) and self.next - len(self.done) < self.window:
            self.next += 1
            self.start(0, self.next - 1)

    def need(self, c):
        while c not in self.done:
            self.finish_first()

    def close(self):
        while self.active:
            self.finish_first()
        for keep in self.keeping:
            keep.wait()


class Pair:
    def __init__(self, mine, theirs, sems):
        self.mine, self.theirs = mine, theirs
        self.send_sem, self.recv_sem = sems
        self.phase = 0
        self.other = (lax.axis_index("dp"), 1 - lax.axis_index("mp"))

    def copy(self, phase, c):
        return pltpu.make_async_remote_copy(
            src_ref=self.mine.at[c],
            dst_ref=self.theirs.at[phase % 2, c],
            send_sem=self.send_sem.at[phase, c],
            recv_sem=self.recv_sem.at[phase, c],
            device_id=self.other,
            device_id_type=MESH,
        )

    def run(self, compute, consume, between):
        phase = self.phase
        self.phase += 1

        def take(c):
            self.copy(phase, c).wait()
            total = self.mine[c].astype(jnp.float32) + self.theirs[phase % 2, c].astype(jnp.float32)
            consume(c, pl.ds(c * BLOCK, BLOCK), total)

        for c in range(BLOCKS):
            self.mine[c] = compute(c, pl.ds(c * BLOCK, BLOCK)).astype(jnp.bfloat16)
            self.copy(phase, c).start()
            if c:
                take(c - 1)
            between()
        take(BLOCKS - 1)


SAVED = ("xb", "qw", "qe", "k", "v", "o", "n1", "h1b", "slope", "g", "n2", "stats")


def saved_shapes(half, hidden):
    wide, narrow = (LEN, D), (LEN, half)
    low = jnp.bfloat16
    return {
        "xb": (wide, low),
        "qw": (narrow, low),
        "qe": (narrow, low),
        "k": (narrow, low),
        "v": (narrow, low),
        "o": (narrow, low),
        "n1": (wide, low),
        "h1b": (wide, low),
        "slope": ((LEN, hidden), low),
        "g": ((LEN, hidden), low),
        "n2": (wide, low),
        "stats": ((LEN, 128), jnp.float32),
    }


def attend(act, pair):
    lanes = slice(pair * 2 * HEAD_DIM, (pair + 1) * 2 * HEAD_DIM)

    def block(i, carry):
        rows = pl.ds(i * BLOCK, BLOCK)
        keys, values = act["k"][:, lanes], act["v"][:, lanes]
        total = None
        for which in range(2):
            q_mask, v_mask = lane_mask(BLOCK, which), lane_mask(LEN, which)
            score_w = mm_rt(act["qw"][rows, lanes] * q_mask, keys[:WORDS])
            score_e = mm_rt(act["qe"][rows, lanes] * q_mask, keys[WORDS:])
            peak = jnp.maximum(
                jnp.max(score_w, axis=-1, keepdims=True), jnp.max(score_e, axis=-1, keepdims=True)
            )
            exp_w = jnp.exp2((score_w - peak) * SCORE_STEP)
            exp_e = jnp.exp2((score_e - peak) * SCORE_STEP)
            weight = jnp.sum(exp_w, axis=-1, keepdims=True) + jnp.sum(exp_e, axis=-1, keepdims=True)
            part = values * v_mask
            mixed = mm(exp_w.astype(jnp.bfloat16), part[:WORDS])
            mixed += mm(exp_e.astype(jnp.bfloat16), part[WORDS:])
            mixed = mixed * (1.0 / weight)
            total = mixed if total is None else total + mixed
            head = 2 * pair + which
            act["stats"][rows, head : head + 1] = peak * SCORE_STEP + jnp.log2(weight)
        act["o"][rows, lanes] = total.astype(jnp.bfloat16)
        return carry

    lax.fori_loop(0, BLOCKS, block, 0)


def project_rows(out_ref, x_ref, first, size, step, weights, index):
    def block(i, carry):
        rows = pl.ds(first + i * step, step)
        out_ref[rows, :] = mm(x_ref[rows, :], flat(weights, index)).astype(jnp.bfloat16)
        return carry

    lax.fori_loop(0, size // step, block, 0)


def forward_body(dims, chunks, needs, *refs):
    refs = list(refs)

    def take(count):
        part = refs[:count]
        del refs[:count]
        return part

    words, base, requests, place_mat, table = take(5)
    shards = take(len(needs["kinds"]))
    kept = take(len(needs["kinds"]))
    saved = [dict(zip(SAVED, take(len(SAVED)))) for _ in range(LAYERS)]
    ents_out, gains_out, rows_in, got_out = take(4)
    wholes = take(len(needs["kinds"]))
    act = dict(zip(SAVED, take(len(SAVED))))
    x, h1, gains, mine, theirs = take(5)
    gather_sems = take(4)
    pair_sems = take(2)
    (save_sem,) = take(1)
    got, replies, answers, look_mine, look_theirs = take(5)
    look_send, look_recv, look_pair = take(3)

    gather = Gather(dims, chunks, shards, wholes, kept, gather_sems)
    pair = Pair(mine, theirs, pair_sems)
    count = dims[0] * dims[1] * dims[2]
    greet_line(count, [pair.other])
    asking = Fan(
        count, (look_send.at[0], look_recv.at[0]), lambda me, to: (requests.at[to], got.at[me])
    )
    asking.start()
    gather.refill()
    here = lax.axis_index("dp")
    got[here] = requests[here]
    asking.wait()
    wanted = flat(got)
    got_out[...] = wanted

    def look(j, found):
        lane = lax.broadcasted_iota(jnp.int32, wanted.shape, 1) + j * 128
        hot = jnp.where(wanted == lane, 1.0, 0.0).astype(jnp.bfloat16)
        return found + mm(hot, table[pl.ds(pl.multiple_of(j * 128, 128), 128), :])

    found = jnp.zeros((wanted.shape[0], table.shape[1]), jnp.float32)
    found = lax.fori_loop(0, table.shape[0] // 128, look, found)
    replies[...] = found.reshape(replies.shape)
    answering = Fan(
        count, (look_send.at[1], look_recv.at[1]), lambda me, to: (replies.at[to], answers.at[me])
    )
    answering.start()
    answers[here] = replies[here]
    gather.spend(7.0)
    answering.wait()
    look_mine[...] = mm(place_mat[...], flat(answers).astype(jnp.bfloat16)).astype(jnp.bfloat16)
    swap = send(look_mine, look_theirs, look_pair.at[0], look_pair.at[1], pair.other)
    attn, outs, ups, downs, proj, _, norms = wholes
    saving = {}

    def save(layer, name):
        slot = layer * len(SAVED) + SAVED.index(name)
        copy = pltpu.make_async_copy(act[name], saved[layer][name], save_sem.at[slot])
        copy.start()
        saving[name] = copy

    def free(name):
        if name in saving:
            saving.pop(name).wait()

    x[:WORDS] = words[...].astype(jnp.float32)
    gather.need(needs["norms"])
    width = D // (dims[0] * dims[1] * dims[2])
    gains[...] = jnp.zeros_like(gains)
    for d in range(count):
        z, rest = d // (dims[1] * dims[2]), d % (dims[1] * dims[2])
        pick = lax.broadcasted_iota(jnp.int32, (128, D), 0) + d * width
        lane = lax.broadcasted_iota(jnp.int32, (128, D), 1)
        inside = lax.broadcasted_iota(jnp.int32, (128, D), 0) < width
        hot = jnp.where((pick == lane) & inside, 1.0, 0.0).astype(jnp.bfloat16)
        gains[...] += mm(norms[0, z, rest // dims[2], rest % dims[2]], hot)
    gather.need(needs["proj"])
    swap.wait()
    both = look_mine[...].astype(jnp.float32) + look_theirs[...].astype(jnp.float32)
    rows_in[...] = both.astype(jnp.bfloat16)
    x[WORDS:] = base[...].astype(jnp.float32) + mm(rows_in[...], flat(proj, 0))

    for layer in range(LAYERS):
        gain = [gains[4 * layer + i : 4 * layer + i + 1, :] for i in range(4)]
        free("xb")

        def cast(i, carry):
            rows = pl.ds(i * BLOCK, BLOCK)
            act["xb"][rows, :] = x[rows, :].astype(jnp.bfloat16)
            return carry

        lax.fori_loop(0, BLOCKS, cast, 0)
        save(layer, "xb")
        for name, word_mat, ent_mat in (("k", 4, None), ("v", 5, None), ("qw", 0, 2), ("qe", 1, 3)):
            free(name)
            gather.need(needs["mat", layer, word_mat if ent_mat is None else ent_mat])
            if ent_mat is None:
                project_rows(act[name], act["xb"], 0, LEN, 512, attn, 6 * layer + word_mat)
            else:
                project_rows(act[name], act["xb"], 0, WORDS, 448, attn, 6 * layer + word_mat)
                project_rows(act[name], act["xb"], WORDS, ENT_LEN, ENT_LEN, attn, 6 * layer + ent_mat)
            save(layer, name)
            gather.spend(2.5)
        free("o")
        free("stats")
        for head_pair in range(act["o"].shape[1] // (2 * HEAD_DIM)):
            attend(act, head_pair)
            gather.spend(4.3)
        save(layer, "o")
        gather.need(needs["out", layer])
        for name in ("n1", "h1b"):
            free(name)

        def out_part(c, rows):
            return mm_rt(act["o"][rows, :], flat(outs, layer))

        def first_norm(c, rows, total):
            hat, scale = normed(x[rows, :] + total)
            act["n1"][rows, :] = hat.astype(jnp.bfloat16)
            act["stats"][rows, 8:9] = scale
            value = hat * gain[0] + gain[1]
            h1[rows, :] = value
            act["h1b"][rows, :] = value.astype(jnp.bfloat16)

        pair.run(out_part, first_norm, lambda: gather.spend(1.3))
        save(layer, "n1")
        save(layer, "h1b")
        gather.need(needs["up", layer, 1])
        for name in ("g", "slope", "n2"):
            free(name)
        hidden = act["g"].shape[1]
        tile = 512

        def up_block(c):
            rows = pl.ds(c * BLOCK, BLOCK)
            for first in range(0, hidden, tile):
                cols = slice(first, first + tile)
                weight = ups[layer, :, :, :, :, cols].reshape(D, tile)
                value, slope = gelu_parts(mm(act["h1b"][rows, :], weight))
                act["g"][rows, cols] = value.astype(jnp.bfloat16)
                act["slope"][rows, cols] = slope.astype(jnp.bfloat16)

        for c in range(BLOCKS):
            up_block(c)
            gather.spend(2.6)
        save(layer, "g")
        save(layer, "slope")
        gather.need(needs["down", layer, 1])

        def down_part(c, rows):
            return mm_rt(act["g"][rows, :], flat(downs, layer))

        def second_norm(c, rows, total):
            hat, scale = normed(h1[rows, :] + total)
            act["n2"][rows, :] = hat.astype(jnp.bfloat16)
            act["stats"][rows, 9:10] = scale
            x[rows, :] = hat * gain[2] + gain[3]

        pair.run(down_part, second_norm, lambda: gather.spend(1.8))
        save(layer, "n2")
        save(layer, "stats")
    ents_out[...] = x[WORDS:]
    gains_out[...] = gains[...]
    gather.close()
    for name in list(saving):
        free(name)


KINDS = ("attn", "out", "up", "down", "proj", "head", "norms")


MAT_ORDER = (4, 5, 0, 2, 1, 3)


def gather_plan(dims, shards):
    every = slice(None)
    chunks, needs, sizes = [], {"kinds": KINDS}, []
    hidden = shards[2].shape[-1]

    def add(name, which, row, cols=every, part=1):
        chunks.append((which, pl.ds(row, 1), cols))
        sizes.append(2 * shards[which].shape[1] * shards[which].shape[2] // part)
        needs[name] = len(chunks) - 1

    add("norms", 6, 0)
    add("proj", 4, 0)
    for layer in range(LAYERS):
        for mat in MAT_ORDER:
            add(("mat", layer, mat), 0, 6 * layer + mat)
        add(("out", layer), 1, layer)
        if layer == LAYERS - 1:
            add("head", 5, 0)
        for which, name in ((2, "up"), (3, "down")):
            for part in range(2):
                cols = pl.ds(part * (hidden // 2), hidden // 2)
                add((name, layer, part), which, layer, cols, 2)
    orders = balanced_orders(dims, sizes)
    return [chunk + (order,) for chunk, order in zip(chunks, orders)], needs


def run_forward(dims, words, base, requests, place_mat, table_low, shards, collective_id):
    half, hidden = shards[0].shape[-1], shards[2].shape[-1]
    chunks, needs = gather_plan(dims, shards)
    shapes = saved_shapes(half, hidden)
    low, full = jnp.bfloat16, jnp.float32
    width, slots = table_low.shape[1], requests.shape[0] * requests.shape[1]
    wholes = [(s.shape[0], *dims, *s.shape[1:]) for s in shards]
    copies = sum(dims)
    saved_out = [jax.ShapeDtypeStruct(*shapes[name]) for _ in range(LAYERS) for name in SAVED]
    result = pl.pallas_call(
        functools.partial(forward_body, dims, chunks, needs),
        out_shape=[jax.ShapeDtypeStruct(shape, low) for shape in wholes]
        + saved_out
        + [
            jax.ShapeDtypeStruct((ENT_LEN, D), full),
            jax.ShapeDtypeStruct((16, D), full),
            jax.ShapeDtypeStruct((ENT_LEN, width), low),
            jax.ShapeDtypeStruct((slots, 128), jnp.int32),
        ],
        in_specs=[VMEM] * 5 + [ANY] * len(shards),
        out_specs=[ANY] * (len(wholes) + len(saved_out)) + [VMEM] * 4,
        scratch_shapes=[pltpu.VMEM(shape, low) for shape in wholes]
        + [pltpu.VMEM(*shapes[name]) for name in SAVED]
        + [
            pltpu.VMEM((LEN, D), full),
            pltpu.VMEM((LEN, D), full),
            pltpu.VMEM((16, D), full),
            pltpu.VMEM((BLOCKS, BLOCK, D), low),
            pltpu.VMEM((2, BLOCKS, BLOCK, D), low),
            pltpu.SemaphoreType.DMA((len(chunks), copies)),
            pltpu.SemaphoreType.DMA((len(chunks), copies)),
            pltpu.SemaphoreType.DMA((len(chunks),)),
            pltpu.SemaphoreType.DMA((len(chunks),)),
            pltpu.SemaphoreType.DMA((2 * LAYERS, BLOCKS)),
            pltpu.SemaphoreType.DMA((2 * LAYERS, BLOCKS)),
            pltpu.SemaphoreType.DMA((LAYERS * len(SAVED),)),
            pltpu.VMEM(requests.shape, jnp.int32),
            pltpu.VMEM((*requests.shape[:2], width), full),
            pltpu.VMEM((*requests.shape[:2], width), full),
            pltpu.VMEM((ENT_LEN, width), low),
            pltpu.VMEM((ENT_LEN, width), low),
            pltpu.SemaphoreType.DMA((2, requests.shape[0])),
            pltpu.SemaphoreType.DMA((2, requests.shape[0])),
            pltpu.SemaphoreType.DMA((2,)),
        ],
        compiler_params=pltpu.CompilerParams(
            collective_id=collective_id, has_side_effects=True, vmem_limit_bytes=VMEM_BYTES
        ),
    )(words, base, requests, place_mat, table_low, *shards)
    kept = result[: len(wholes)]
    saved = [
        dict(zip(SAVED, result[len(wholes) + layer * len(SAVED) :][: len(SAVED)]))
        for layer in range(LAYERS)
    ]
    return kept, saved, *result[-4:]


class Fan:
    def __init__(self, count, sems, copy_args):
        self.count, self.sems, self.copy_args = count, sems, copy_args
        self.index = lax.axis_index("dp")

    def copy(self, step):
        other = lax.rem(self.index + step, self.count)
        src, dst = self.copy_args(self.index, other)
        send_sem, recv_sem = self.sems
        return pltpu.make_async_remote_copy(
            src_ref=src,
            dst_ref=dst,
            send_sem=send_sem.at[step],
            recv_sem=recv_sem.at[step],
            device_id=(other, lax.axis_index("mp")),
            device_id_type=MESH,
        )

    def start(self):
        def go(step, carry):
            self.copy(step).start()
            return carry

        lax.fori_loop(1, self.count, go, 0)

    def wait(self):
        def done(step, carry):
            self.copy(step).wait()
            return carry

        lax.fori_loop(1, self.count, done, 0)


def greet_line(count, extra):
    barrier = pltpu.get_barrier_semaphore()
    index, core = lax.axis_index("dp"), lax.axis_index("mp")

    def hello(step, carry):
        other = lax.rem(index + step, count)
        pl.semaphore_signal(barrier, inc=1, device_id=(other, core), device_id_type=MESH)
        return carry

    lax.fori_loop(1, count, hello, 0)
    for target in extra:
        pl.semaphore_signal(barrier, inc=1, device_id=target, device_id_type=MESH)
    pl.semaphore_wait(barrier, count - 1 + len(extra))


TABLE_CUTS = 8


def head_body(count, *refs):
    ents, hits, head, table, local_targets = refs[:5]
    losses, grad_logits, states, grad_head, grad_ents = refs[5:10]
    logits, own_states, all_states, stat_mine, stat_theirs, stat_both, stat_all = refs[10:17]
    grad_part, grad_all, share_mine, share_theirs = refs[17:21]
    send_sem, recv_sem, pair_send, pair_recv = refs[21:]
    index = lax.axis_index("dp")
    other = (index, 1 - lax.axis_index("mp"))
    greet_line(count, [other])
    total_rows = count * MASK_ENT
    span = table.shape[0] // TABLE_CUTS

    masked = mm(hits[...], ents[...].astype(jnp.bfloat16)).astype(jnp.bfloat16)
    head_low = flat(head)
    value, slope = gelu_parts(mm(masked, head_low))
    own_states[...] = value.astype(jnp.bfloat16)
    fan = Fan(count, (send_sem.at[0], recv_sem.at[0]), lambda me, to: (own_states, all_states.at[me]))
    fan.start()
    all_states[index] = own_states[...]
    fan.wait()
    states[...] = flat(all_states)
    target = local_targets[0:1, :]

    def hit_of(c):
        row = lax.broadcasted_iota(jnp.int32, (span, total_rows), 0) + c * span
        return row == target

    def rows_of(c):
        return pl.ds(pl.multiple_of(c * span, 16), span)

    def score(c, carry):
        peak, picked = carry
        part = mm_rt(table[rows_of(c), :], states[...])
        logits[rows_of(c), :] = part
        peak = jnp.maximum(peak, jnp.max(part, axis=0, keepdims=True))
        picked += jnp.sum(jnp.where(hit_of(c), part, 0.0), axis=0, keepdims=True)
        return peak, picked

    empty = jnp.zeros((1, total_rows), jnp.float32)
    peak, picked = lax.fori_loop(0, TABLE_CUTS, score, (empty - 3e38, empty))

    def weigh(c, weight):
        return weight + jnp.sum(jnp.exp(logits[rows_of(c), :] - peak), axis=0, keepdims=True)

    weight = lax.fori_loop(0, TABLE_CUTS, weigh, empty)
    stat_mine[0:1, :] = peak
    stat_mine[1:2, :] = weight
    stat_mine[2:3, :] = picked
    swap = send(stat_mine, stat_theirs, pair_send.at[0], pair_recv.at[0], other)
    swap.wait()
    peak_both = jnp.maximum(stat_mine[0:1, :], stat_theirs[0:1, :])
    stat_both[0:1, :] = peak_both
    stat_both[1:2, :] = stat_mine[1:2, :] * jnp.exp(stat_mine[0:1, :] - peak_both) + stat_theirs[
        1:2, :
    ] * jnp.exp(stat_theirs[0:1, :] - peak_both)
    stat_both[2:3, :] = stat_mine[2:3, :] + stat_theirs[2:3, :]
    fan = Fan(count, (send_sem.at[1], recv_sem.at[1]), lambda me, to: (stat_both, stat_all.at[me]))
    fan.start()
    stat_all[index] = stat_both[...]
    fan.wait()
    peak_all = stat_all[0, 0:1, :]
    for d in range(1, count):
        peak_all = jnp.maximum(peak_all, stat_all[d, 0:1, :])
    weight_all = picked_all = empty
    for d in range(count):
        weight_all += stat_all[d, 1:2, :] * jnp.exp(stat_all[d, 0:1, :] - peak_all)
        picked_all += stat_all[d, 2:3, :]
    log_norm = peak_all + jnp.log(weight_all)
    losses[...] = jnp.broadcast_to(log_norm - picked_all, losses.shape)
    grad_part[...] = jnp.zeros_like(grad_part)

    def grads(c, carry):
        prob = jnp.exp(logits[rows_of(c), :] - log_norm)
        part = (prob - jnp.where(hit_of(c), 1.0, 0.0)) * (1.0 / total_rows)
        low = part.astype(jnp.bfloat16)
        grad_logits[rows_of(c), :] = low
        grad_part[...] += mm_lt(low, table[rows_of(c), :]).reshape(grad_part.shape)
        return carry

    lax.fori_loop(0, TABLE_CUTS, grads, 0)
    fan = Fan(
        count, (send_sem.at[2], recv_sem.at[2]), lambda me, to: (grad_part.at[to], grad_all.at[me])
    )
    fan.start()
    grad_all[index] = grad_part[index]
    fan.wait()
    share_mine[...] = jnp.sum(grad_all[...], axis=0)
    swap = send(share_mine, share_theirs, pair_send.at[1], pair_recv.at[1], other)
    swap.wait()
    grad_pre = ((share_mine[...] + share_theirs[...]) * slope).astype(jnp.bfloat16)
    grad_head[...] = mm_lt(masked, grad_pre).astype(jnp.bfloat16).reshape(grad_head.shape)
    grad_masked = mm_rt(grad_pre, head_low)
    grad_ents[...] = lax.dot_general(
        hits[...].astype(jnp.float32),
        grad_masked,
        (((0,), (0,)), ((), ())),
        precision=lax.Precision.HIGHEST,
        preferred_element_type=jnp.float32,
    )


def run_head(dims, ents, hits, head, table_low, local_targets, collective_id):
    count = dims[0] * dims[1] * dims[2]
    width = table_low.shape[1]
    rows = count * MASK_ENT
    low, full = jnp.bfloat16, jnp.float32
    return pl.pallas_call(
        functools.partial(head_body, count),
        out_shape=[
            jax.ShapeDtypeStruct((8, rows), full),
            jax.ShapeDtypeStruct((table_low.shape[0], rows), low),
            jax.ShapeDtypeStruct((rows, width), low),
            jax.ShapeDtypeStruct(head.shape, low),
            jax.ShapeDtypeStruct((ENT_LEN, D), full),
        ],
        in_specs=[VMEM] * 5,
        out_specs=[VMEM] * 5,
        scratch_shapes=[
            pltpu.VMEM((table_low.shape[0], rows), full),
            pltpu.VMEM((MASK_ENT, width), low),
            pltpu.VMEM((count, MASK_ENT, width), low),
            pltpu.VMEM((8, rows), full),
            pltpu.VMEM((8, rows), full),
            pltpu.VMEM((8, rows), full),
            pltpu.VMEM((count, 8, rows), full),
            pltpu.VMEM((count, MASK_ENT, width), full),
            pltpu.VMEM((count, MASK_ENT, width), full),
            pltpu.VMEM((MASK_ENT, width), full),
            pltpu.VMEM((MASK_ENT, width), full),
            pltpu.SemaphoreType.DMA((3, count)),
            pltpu.SemaphoreType.DMA((3, count)),
            pltpu.SemaphoreType.DMA((2,)),
            pltpu.SemaphoreType.DMA((2,)),
        ],
        compiler_params=pltpu.CompilerParams(
            collective_id=collective_id, has_side_effects=True, vmem_limit_bytes=VMEM_BYTES
        ),
    )(ents, hits, head, table_low, local_targets)


def update_body(names, width, *refs):
    refs = list(refs)

    def take(count):
        part = refs[:count]
        del refs[:count]
        return part

    kinds = len(kind_rates)
    state_in = [take(3) for _ in range(kinds)]
    totals_in = take(len(names))
    incoming, requests, grad_logits, states = take(4)
    state_out = [take(3) for _ in range(kinds)]
    held = [take(3) for _ in range(kinds)]
    totals_held = take(len(names))
    in_sem, total_sem, out_sem = take(3)
    table = kinds - 1
    height = held[table][0].shape[0] // TABLE_CUTS

    def piece(ref, c):
        return ref if c is None else ref.at[pl.ds(c * height, height)]

    def copies(kind, c, inward):
        base = 3 * (kind + (0 if c is None else c))
        pairs = []
        for i in range(3):
            if inward:
                src, dst, sem = state_in[kind][i], held[kind][i], in_sem.at[base + i]
            else:
                src, dst, sem = held[kind][i], state_out[kind][i], out_sem.at[base + i]
            pairs.append(pltpu.make_async_copy(piece(src, c), piece(dst, c), sem))
        return pairs

    leaving = []
    total_copies = [
        pltpu.make_async_copy(src, dst, total_sem.at[i])
        for i, (src, dst) in enumerate(zip(totals_in, totals_held))
    ]
    for c in range(2):
        for copy in copies(table, c, True):
            copy.start()
    for copy in total_copies:
        copy.start()
    for kind in range(table):
        for copy in copies(kind, None, True):
            copy.start()
    for c in range(2, TABLE_CUTS):
        for copy in copies(table, c, True):
            copy.start()
    total_of = dict(zip(names, totals_held))

    def update(kind, at, gradient):
        master, first, second = held[kind]
        first_new = beta_first * first[at] + (1.0 - beta_first) * gradient
        second_new = beta_second * second[at] + (1.0 - beta_second) * gradient * gradient
        first_hat = first_new * (1.0 / (1.0 - beta_first**STEP))
        second_hat = second_new * (1.0 / (1.0 - beta_second**STEP))
        value = master[at]
        value -= kind_rates[kind] * (
            first_hat / (jnp.sqrt(second_hat) + adam_eps) + weight_decay * value
        )
        master[at], first[at], second[at] = value, first_new, second_new

    def finish(kind, c=None):
        for copy in copies(kind, c, False):
            copy.start()
            leaving.append(copy)

    def table_part(c):
        for copy in copies(table, c, True):
            copy.wait()
        rows = slice(c * height, (c + 1) * height)
        gradient = mm(grad_logits[rows, :], states[...])
        row = lax.broadcasted_iota(jnp.int32, (height, requests.shape[1]), 0) + c * height
        hot = jnp.where(row == requests[0:1, :], 1.0, 0.0).astype(jnp.bfloat16)
        gradient += mm(hot, incoming[...].astype(jnp.bfloat16))
        update(table, (rows, slice(None)), gradient)
        finish(table, c)

    table_part(0)
    table_part(1)
    for copy in total_copies:
        copy.wait()
    for kind in range(table):
        for copy in copies(kind, None, True):
            copy.wait()
        for layer in range(LAYERS):
            if kind == 0:
                blocks = []
                for name in ("words", "ents"):
                    total = total_of[layer, name]
                    half = total.shape[1] // 2
                    blocks += [total[:, :half], total[:, half:]]
                blocks += [total_of[layer, "key"][...], total_of[layer, "value"][...]]
                for mat, block in enumerate(blocks):
                    update(kind, (layer, mat), block)
            elif kind == 1:
                update(kind, (layer,), total_of[layer, "out"][...])
            elif kind in (2, 3):
                for i in range(2):
                    total = total_of[layer, ("up%d", "down%d")[kind - 2] % i]
                    half = total.shape[1]
                    cols = slice(i * half, (i + 1) * half)
                    update(kind, (layer, slice(None), cols), total[...])
            elif kind == 4:
                update(kind, (layer,), total_of["norms"][4 * layer : 4 * layer + 4, :width])
        if kind == 5:
            update(kind, (slice(None),), total_of["proj"][...])
        if kind == 6:
            update(kind, (slice(None),), total_of["head"][...])
        finish(kind)
    for c in range(2, TABLE_CUTS):
        table_part(c)
    for copy in leaving:
        copy.wait()


def run_update(states_of, totals, incoming, requests, grad_logits, states):
    names = list(totals)
    full = jnp.float32
    flat_states = [array for group in states_of for array in group]
    width = states_of[4][0].shape[-1]
    kinds = len(kind_rates)
    result = pl.pallas_call(
        functools.partial(update_body, names, width),
        out_shape=[jax.ShapeDtypeStruct(a.shape, full) for a in flat_states],
        in_specs=[ANY] * (len(flat_states) + len(names)) + [VMEM] * 4,
        out_specs=[ANY] * len(flat_states),
        scratch_shapes=[pltpu.VMEM(a.shape, full) for a in flat_states]
        + [pltpu.VMEM(totals[name].shape, full) for name in names]
        + [
            pltpu.SemaphoreType.DMA((3 * (kinds + TABLE_CUTS),)),
            pltpu.SemaphoreType.DMA((len(names),)),
            pltpu.SemaphoreType.DMA((3 * (kinds + TABLE_CUTS),)),
        ],
        compiler_params=pltpu.CompilerParams(vmem_limit_bytes=VMEM_BYTES),
    )(*flat_states, *totals.values(), incoming, requests, grad_logits, states)
    return [result[3 * i : 3 * i + 3] for i in range(kinds)]


def norm_back(grad, hat, scale, gain_row):
    hat = hat.astype(jnp.float32)
    wide = grad * gain_row
    inner = jnp.mean(wide * hat, axis=-1, keepdims=True)
    back = scale * (wide - jnp.mean(wide, axis=-1, keepdims=True) - hat * inner)
    gain_part = jnp.sum(grad * hat, axis=0, keepdims=True)
    return back, gain_part, jnp.sum(grad, axis=0, keepdims=True)


class Sums(Links):
    def __init__(self, dims, units, buffers, totals, sems, free_sem):
        super().__init__(dims)
        self.units, self.totals, self.buffers = units, totals, buffers
        self.send_sem, self.recv_sem = sems
        self.free_sem = free_sem
        self.spot = place(dims)
        self.peers = [axis_peers(dims, axis) for axis in range(3)]
        self.copies, self.done = {}, set()

    def start(self, stage, u):
        slot, order, turn = self.units[u]
        part, arrived = self.buffers[slot][0], self.buffers[slot][1 + stage]
        axis = order[stage]
        group = self.peers[axis]
        if turn and group:
            pl.semaphore_wait(self.free_sem.at[slot, stage], len(group))
        copies, base = [], sum(self.dims[order[i]] for i in range(stage))
        for k, (spot, target) in enumerate(group):
            at = [slice(None)] * 3
            for d in order[:stage]:
                at[d] = self.spot[d]
            at[axis] = spot
            sems = self.send_sem.at[u, base + k], self.recv_sem.at[u, base + k]
            copies.append(send(part.at[tuple(at)], arrived.at[k], *sems, target))
        self.copies[stage, u] = copies
        held = 1
        for d in order[stage + 1 :]:
            held *= self.dims[d]
        self.issue(axis, held * 2 * part.shape[3] * part.shape[4], (stage, u))

    def complete(self, what):
        stage, u = what
        slot, order, turn = self.units[u]
        part, arrived = self.buffers[slot][0], self.buffers[slot][1 + stage]
        for copy in self.copies.pop(what):
            copy.wait()
        axis = order[stage]
        group = self.peers[axis]
        rest = [d for d in range(3) if d not in order[: stage + 1]]

        def total_at(spots):
            at = tuple(spots.get(d, self.spot[d]) for d in range(3))
            value = part[at].astype(jnp.float32)
            for k in range(len(group)):
                value += arrived[(k, *[spots[d] for d in rest])].astype(jnp.float32)
            return at, value

        if stage == 2:
            self.totals[u][...] = total_at({})[1]
            self.done.add(u)
        elif group:
            inner = self.dims[rest[-1]]

            def add(i, carry):
                spots = {rest[-1]: i % inner}
                if len(rest) == 2:
                    spots[rest[0]] = i // inner
                at, value = total_at(spots)
                part[at] = value.astype(part.dtype)
                return carry

            count = inner * (self.dims[rest[0]] if len(rest) == 2 else 1)
            lax.fori_loop(0, count, add, 0)
        if self.reused(u):
            for _, target in group:
                pl.semaphore_signal(
                    self.free_sem.at[slot, stage], inc=1, device_id=target, device_id_type=MESH
                )
        if stage < 2:
            self.start(stage + 1, u)

    def reused(self, u):
        slot, _, turn = self.units[u]
        return not turn and sum(unit[0] == slot for unit in self.units) > 1

    def need(self, u):
        while u not in self.done:
            self.finish_first()

    def close(self):
        while self.active:
            self.finish_first()


UNITS = ("down0", "down1", "up0", "up1", "out", "words", "ents", "key", "value")
EXTRA = ("head", "proj", "norms")


def unit_orders(dims, blocks):
    names = list(blocks)
    sizes = [2 * rows * cols for rows, cols in blocks.values()]
    return {name: order[::-1] for name, order in zip(names, balanced_orders(dims, sizes))}


def sum_plan():
    names = ["head"]
    for layer in reversed(range(LAYERS)):
        names += [(layer, name) for name in UNITS]
    names += ["proj", "norms"]
    return names


def unit_width(name, half, hidden):
    return {
        "down0": hidden // 2, "down1": hidden // 2, "up0": hidden // 2, "up1": hidden // 2,
        "out": half, "words": 2 * half, "ents": 2 * half, "key": half, "value": half,
    }[name]


def backward_body(dims, names, orders, half, hidden, *refs):
    refs = list(refs)

    def take(count):
        part = refs[:count]
        del refs[:count]
        return part

    cotangent, grad_ents, grad_head, gains, entity_rows, place_mat = take(6)
    w_attn, w_out, w_up, w_down, w_proj = take(5)
    saved = [dict(zip(SAVED, take(len(SAVED)))) for _ in range(LAYERS)]
    word_grads, incoming = take(2)
    totals = take(len(names))
    slots = list(UNITS + EXTRA)
    buffers = [take(4) for _ in slots]
    left, right, hat, xh, o, stats, stats_t = take(7)
    mat_wide, mat_out, mat_attn, mat_proj = take(4)
    gacc, glow, gmix, delta, dk_acc, dv_acc, gnorm = take(7)
    mine, theirs = take(2)
    sum_sems = take(2)
    (free_sem,) = take(1)
    pair_sems = take(2)
    (load_sem,) = take(1)
    out_rows, in_rows, row_send, row_recv = take(4)

    units = []
    for name in names:
        kind = name if isinstance(name, str) else name[1]
        turn = not isinstance(name, str) and name[0] < LAYERS - 1
        units.append((slots.index(kind), orders[kind], turn))
    sums = Sums(dims, units, buffers, totals, sum_sems, free_sem)
    pair = Pair(mine, theirs, pair_sems)
    count = dims[0] * dims[1] * dims[2]
    greet_line(count, [pair.other])
    part_of = {slot: buffers[i][0] for i, slot in enumerate(slots)}
    loads, counter = {}, [0]

    def load(key, src, dst):
        copy = pltpu.make_async_copy(src, dst, load_sem.at[counter[0]])
        counter[0] += 1
        copy.start()
        loads.setdefault(key, []).append(copy)

    def ready(key):
        for copy in loads.pop(key, []):
            copy.wait()

    tick = sums.spend

    def begin_layer(layer):
        s = saved[layer]
        load("n2", s["n2"], hat)
        load("stats", s["stats"], stats)
        load("g", s["g"], left)
        load("down", w_down.at[layer], mat_wide)
        load("slope", s["slope"], right)
        load("h1b", s["h1b"], xh)
        load("out", w_out.at[layer], mat_out)
        load("o", s["o"], o)
        load("attn", w_attn.at[pl.ds(6 * layer, 6)], mat_attn)

    begin_layer(LAYERS - 1)
    load("proj", w_proj.at[0], mat_proj)
    slab = 2 if dims[0] % 2 == 0 else 1
    height = slab * D // dims[0]

    def fill(name, lhs, rhs, rhs_cols, row_slice=slice(None)):
        part = part_of[name]
        width = part.shape[-1]

        def block(i, carry):
            cols = pl.ds(pl.multiple_of(i * height, 128), height)
            value = mm_lt(lhs[row_slice, cols], rhs[row_slice, rhs_cols])
            shape = (slab, dims[1], dims[2], part.shape[3], width)
            part[pl.ds(i * slab, slab)] = value.astype(jnp.bfloat16).reshape(shape)
            return carry

        lax.fori_loop(0, dims[0] // slab, block, 0)

    def submit(layer, name):
        sums.start(0, names.index((layer, name)))

    head_part = part_of["head"]
    head_part[...] = grad_head[...]
    sums.start(0, names.index("head"))
    gacc[:WORDS] = cotangent[...].astype(jnp.float32)
    gacc[WORDS:] = grad_ents[...]
    gnorm[...] = jnp.zeros_like(gnorm)

    def add_norm(row, value):
        gnorm[row : row + 1, :] += value

    for layer in reversed(range(LAYERS)):
        last = layer == LAYERS - 1
        gain = [gains[4 * layer + i : 4 * layer + i + 1, :] for i in range(4)]
        ready("n2")
        ready("stats")

        def late_norm(c, carry):
            rows = pl.ds(c * BLOCK, BLOCK)
            back, gain_part, shift_part = norm_back(
                gacc[rows, :], hat[rows, :], stats[rows, 9:10], gain[2]
            )
            gacc[rows, :] = back
            glow[rows, :] = back.astype(jnp.bfloat16)
            add_norm(4 * layer + 2, gain_part)
            add_norm(4 * layer + 3, shift_part)
            return carry

        lax.fori_loop(0, BLOCKS, late_norm, 0)
        tick(3.0)
        load("n1", saved[layer]["n1"], hat)
        ready("g")
        for i in range(2):
            if not last:
                sums.need(names.index((layer + 1, "down%d" % i)))
            cols = slice(i * (hidden // 2), (i + 1) * (hidden // 2))
            fill("down%d" % i, glow, left, cols)
            submit(layer, "down%d" % i)
            tick(2.2)
        ahead = saved[layer]
        for i, name in enumerate(("k", "qw", "qe", "v")):
            load("qkv", ahead[name], left.at[:, pl.ds(i * half, half)])
        ready("down")
        ready("slope")

        def inner(c, carry):
            rows = pl.ds(c * BLOCK, BLOCK)
            for first in range(0, hidden, 512):
                cols = slice(first, first + 512)
                weight = mat_wide[:, :, :, :, cols].reshape(D, 512)
                value = mm(glow[rows, :], weight) * right[rows, cols].astype(jnp.float32)
                right[rows, cols] = value.astype(jnp.bfloat16)
            return carry

        lax.fori_loop(0, BLOCKS, inner, 0)
        tick(3.5)
        load("up", w_up.at[layer], mat_wide)
        ready("h1b")
        for i in range(2):
            if not last:
                sums.need(names.index((layer + 1, "up%d" % i)))
            cols = slice(i * (hidden // 2), (i + 1) * (hidden // 2))
            fill("up%d" % i, xh, right, cols)
            submit(layer, "up%d" % i)
            tick(2.2)
        load("xb", saved[layer]["xb"], xh)
        ready("up")
        ready("n1")

        def up_part(c, rows):
            return mm_rt(right[rows, :], flat(mat_wide))

        def early_norm(c, rows, total):
            back, gain_part, shift_part = norm_back(
                gacc[rows, :] + total, hat[rows, :], stats[rows, 8:9], gain[0]
            )
            gacc[rows, :] = back
            glow[rows, :] = back.astype(jnp.bfloat16)
            add_norm(4 * layer, gain_part)
            add_norm(4 * layer + 1, shift_part)

        pair.run(up_part, early_norm, lambda: tick(2.0))
        ready("o")
        ready("out")
        if not last:
            sums.need(names.index((layer + 1, "out")))
        fill("out", glow, o, slice(None))
        submit(layer, "out")

        def mixed(c, carry):
            rows = pl.ds(c * BLOCK, BLOCK)
            gmix[rows, :] = mm(glow[rows, :], flat(mat_out)).astype(jnp.bfloat16)
            stats_t[:, rows] = stats[rows, :].T
            return carry

        lax.fori_loop(0, BLOCKS, mixed, 0)
        tick(3.7)
        ready("qkv")
        for head_pair in range(half // (2 * HEAD_DIM)):
            lo = head_pair * 2 * HEAD_DIM
            lanes = slice(lo, lo + 2 * HEAD_DIM)
            k_lanes, qw_lanes, qe_lanes, v_lanes = [
                slice(j * half + lo, j * half + lo + 2 * HEAD_DIM) for j in range(4)
            ]

            def products(c, carry):
                rows = pl.ds(c * BLOCK, BLOCK)
                both = gmix[rows, lanes].astype(jnp.float32) * o[rows, lanes].astype(jnp.float32)
                turned = both.T
                delta[0:1, rows] = jnp.sum(turned[:HEAD_DIM], axis=0, keepdims=True)
                delta[1:2, rows] = jnp.sum(turned[HEAD_DIM:], axis=0, keepdims=True)
                return carry

            lax.fori_loop(0, BLOCKS, products, 0)
            dk_acc[...] = jnp.zeros_like(dk_acc)
            dv_acc[...] = jnp.zeros_like(dv_acc)

            def block(i, carry):
                rows = pl.ds(i * BLOCK, BLOCK)
                keys, values = left[:, k_lanes], left[:, v_lanes]
                grad_qw = grad_qe = None
                for which in range(2):
                    head = 2 * head_pair + which
                    q_mask, k_mask = lane_mask(BLOCK, which), lane_mask(LEN, which)
                    query_w = left[rows, qw_lanes] * q_mask
                    query_e = left[rows, qe_lanes] * q_mask
                    grad_o = gmix[rows, lanes] * q_mask
                    log_row = stats_t[head : head + 1, rows]
                    inner_row = delta[which : which + 1, rows]
                    own_keys = keys * k_mask
                    for span, query in ((slice(0, WORDS), query_w), (slice(WORDS, LEN), query_e)):
                        prob = jnp.exp2(mm_rt(keys[span], query) * SCORE_STEP - log_row)
                        grad_prob = mm_rt(values[span], grad_o)
                        dv_acc[span, :] += mm(prob.astype(jnp.bfloat16), grad_o)
                        grad_score = (prob * (grad_prob - inner_row)).astype(jnp.bfloat16)
                        dk_acc[span, :] += mm(grad_score, query)
                        part = mm_lt(grad_score, own_keys[span])
                        if span.start == 0:
                            grad_qw = part if grad_qw is None else grad_qw + part
                        else:
                            grad_qe = part if grad_qe is None else grad_qe + part
                right[rows, lanes] = (grad_qw * 0.125).astype(jnp.bfloat16)
                right[rows, half + lo : half + lo + 2 * HEAD_DIM] = (grad_qe * 0.125).astype(
                    jnp.bfloat16
                )
                return carry

            for first in range(0, BLOCKS, 2):
                lax.fori_loop(first, first + 2, block, 0)
                tick(4.7)
            at = 2 * half + lo
            right[:, at : at + 2 * HEAD_DIM] = (dk_acc[...] * 0.125).astype(jnp.bfloat16)
            at = 3 * half + lo
            right[:, at : at + 2 * HEAD_DIM] = dv_acc[...].astype(jnp.bfloat16)
        ready("xb")
        words, ents = slice(0, WORDS), slice(WORDS, LEN)
        for name, cols, rows in (
            ("words", slice(0, 2 * half), words),
            ("ents", slice(0, 2 * half), ents),
            ("key", slice(2 * half, 3 * half), slice(None)),
            ("value", slice(3 * half, 4 * half), slice(None)),
        ):
            if not last:
                sums.need(names.index((layer + 1, name)))
            fill(name, xh, right, cols, rows)
            submit(layer, name)
            tick(1.4)
        ready("attn")
        mats = [slice(j * half, (j + 1) * half) for j in range(4)]

        def input_part(c, rows):
            total = mm_rt(right[rows, mats[2]], flat(mat_attn, 4))
            total += mm_rt(right[rows, mats[3]], flat(mat_attn, 5))
            start = c * BLOCK
            edge = min(max(WORDS - start, 0), BLOCK)
            pieces = []
            for low, high, pick in ((0, edge, (0, 1)), (edge, BLOCK, (2, 3))):
                if high > low:
                    span = slice(start + low, start + high)
                    piece = mm_rt(right[span, mats[0]], flat(mat_attn, pick[0]))
                    pieces.append(piece + mm_rt(right[span, mats[1]], flat(mat_attn, pick[1])))
            return total + (pieces[0] if len(pieces) == 1 else jnp.concatenate(pieces, axis=0))

        def to_input(c, rows, total):
            gacc[rows, :] += total

        pair.run(input_part, to_input, lambda: tick(2.0))
        if layer:
            begin_layer(layer - 1)
    ready("proj")
    leaving = pltpu.make_async_copy(gacc.at[pl.ds(0, WORDS)], word_grads, load_sem.at[counter[0]])
    leaving.start()
    grad_entity = gacc[WORDS:].astype(jnp.bfloat16)
    row_grads = mm_rt(grad_entity, flat(mat_proj)).astype(jnp.bfloat16)
    out_rows[...] = mm_lt(place_mat[...], row_grads).reshape(out_rows.shape)
    returning = Fan(count, (row_send, row_recv), lambda me, to: (out_rows.at[to], in_rows.at[me]))
    returning.start()
    here = lax.axis_index("dp")
    in_rows[here] = out_rows[here]
    proj_part = part_of["proj"]
    proj_part[...] = mm_lt(entity_rows[...], grad_entity).astype(jnp.bfloat16).reshape(proj_part.shape)
    sums.start(0, names.index("proj"))
    width = D // count
    norm_low = gnorm[...].astype(jnp.bfloat16)
    for d in range(count):
        z, rest = d // (dims[1] * dims[2]), d % (dims[1] * dims[2])
        row = lax.broadcasted_iota(jnp.int32, (128, D), 0)
        lane = lax.broadcasted_iota(jnp.int32, (128, D), 1)
        hot = jnp.where((row + d * width == lane) & (row < width), 1.0, 0.0).astype(jnp.bfloat16)
        block = mm_rt(norm_low, hot).astype(jnp.bfloat16)
        part_of["norms"][z, rest // dims[2], rest % dims[2]] = block
    sums.start(0, names.index("norms"))
    sums.close()
    returning.wait()
    incoming[...] = flat(in_rows)
    leaving.wait()


def run_backward(
    dims, cotangent, grad_ents, grad_head, gains, entity_rows, place_mat, kept, saved, collective_id
):
    names = sum_plan()
    half, hidden = kept[0].shape[-1], kept[2].shape[-1]
    low, full = jnp.bfloat16, jnp.float32
    rows = kept[0].shape[4]
    blocks = {name: (rows, unit_width(name, half, hidden)) for name in UNITS}
    blocks["head"] = (rows, kept[5].shape[-1])
    blocks["proj"] = (kept[4].shape[4], D)
    blocks["norms"] = (16, 128)
    scratch = []
    orders = unit_orders(dims, blocks)
    for name in UNITS + EXTRA:
        order, block = orders[name], blocks[name]
        scratch.append(pltpu.VMEM((*dims, *block), low))
        for stage in range(3):
            rest = [dims[d] for d in range(3) if d not in order[: stage + 1]]
            peers = max(dims[order[stage]] - 1, 1)
            scratch.append(pltpu.VMEM((peers, *rest, *block), low))
    copies = sum(dims)
    kinds = [name if isinstance(name, str) else name[1] for name in names]
    count = dims[0] * dims[1] * dims[2]
    width, slots = kept[5].shape[-1], place_mat.shape[1]
    inputs = [cotangent, grad_ents, grad_head, gains, entity_rows, place_mat, *kept[:5]]
    inputs += [saved[layer][name] for layer in range(LAYERS) for name in SAVED]
    result = pl.pallas_call(
        functools.partial(backward_body, dims, names, orders, half, hidden),
        out_shape=[
            jax.ShapeDtypeStruct((WORDS, D), full),
            jax.ShapeDtypeStruct((slots, width), full),
        ]
        + [jax.ShapeDtypeStruct(blocks[kind], full) for kind in kinds],
        in_specs=[VMEM] * 6 + [ANY] * (len(inputs) - 6),
        out_specs=[ANY] + [VMEM] * (1 + len(names)),
        scratch_shapes=scratch
        + [
            pltpu.VMEM((LEN, hidden), low),
            pltpu.VMEM((LEN, hidden), low),
            pltpu.VMEM((LEN, D), low),
            pltpu.VMEM((LEN, D), low),
            pltpu.VMEM((LEN, half), low),
            pltpu.VMEM((LEN, 128), full),
            pltpu.VMEM((128, LEN), full),
            pltpu.VMEM(kept[2].shape[1:], low),
            pltpu.VMEM(kept[1].shape[1:], low),
            pltpu.VMEM((6, *kept[0].shape[1:]), low),
            pltpu.VMEM(kept[4].shape[1:], low),
            pltpu.VMEM((LEN, D), full),
            pltpu.VMEM((LEN, D), low),
            pltpu.VMEM((LEN, half), low),
            pltpu.VMEM((8, LEN), full),
            pltpu.VMEM((LEN, 2 * HEAD_DIM), full),
            pltpu.VMEM((LEN, 2 * HEAD_DIM), full),
            pltpu.VMEM((16, D), full),
            pltpu.VMEM((BLOCKS, BLOCK, D), low),
            pltpu.VMEM((2, BLOCKS, BLOCK, D), low),
            pltpu.SemaphoreType.DMA((len(names), copies)),
            pltpu.SemaphoreType.DMA((len(names), copies)),
            pltpu.SemaphoreType.REGULAR((len(UNITS + EXTRA), 3)),
            pltpu.SemaphoreType.DMA((2 * LAYERS, BLOCKS)),
            pltpu.SemaphoreType.DMA((2 * LAYERS, BLOCKS)),
            pltpu.SemaphoreType.DMA((64,)),
            pltpu.VMEM((count, slots // count, width), full),
            pltpu.VMEM((count, slots // count, width), full),
            pltpu.SemaphoreType.DMA((count,)),
            pltpu.SemaphoreType.DMA((count,)),
        ],
        compiler_params=pltpu.CompilerParams(
            collective_id=collective_id, has_side_effects=True, vmem_limit_bytes=VMEM_BYTES
        ),
    )(*inputs)
    return result[0], result[1], dict(zip(names, result[2:]))


def padded_rows(values):
    extra = -values.shape[-2] % 16
    return jnp.pad(values, [(0, 0)] * (values.ndim - 2) + [(0, extra), (0, 0)])


def weight_shards(attention_in, attention_out, feed_up, feed_down, norm_params, entity_proj, head_proj):
    def turned(values):
        return jnp.swapaxes(values, 1, 2)

    mats = attention_in.reshape(-1, *attention_in.shape[2:])
    norms = norm_params.reshape(1, -1, norm_params.shape[-1])
    norms = jnp.pad(norms, [(0, 0), (0, 16 - norms.shape[1]), (0, -norms.shape[2] % 128)])
    sources = [mats, turned(attention_out), feed_up, turned(feed_down), entity_proj[None], head_proj[None]]
    heights = [part.shape[1] for part in sources]
    shards = [padded_rows(part.astype(jnp.bfloat16)) for part in sources]
    shards.append(norms.astype(jnp.bfloat16))
    return shards, heights


def unpack_weights(wholes, heights, norm_width):
    kept = []
    for part, height in zip(wholes, heights):
        part = part[..., :height, :]
        kept.append(part.reshape(part.shape[0], -1, part.shape[-1]))
    norm_all = wholes[6][0].reshape(-1, 16, wholes[6].shape[-1])[:, : LAYERS * 4, :norm_width]
    norm_all = jnp.swapaxes(norm_all, 0, 1).reshape(LAYERS, 4, -1)
    return (
        kept[0].reshape(LAYERS, 6, *kept[0].shape[1:]),
        kept[1],
        kept[2],
        kept[3],
        norm_all,
        kept[4][0],
        kept[5][0],
    )


def gather_apart(dims, shards):
    chunks = [(4, 0, 1, True), (5, 0, 1, False), (6, 0, 1, True)]
    for layer in range(LAYERS):
        chunks += [(0, 6 * layer, 3, True), (0, 6 * layer + 3, 3, False)]
        chunks += [(1, layer, 1, layer == 0), (2, layer, 1, True), (3, layer, 1, False)]
    return gather_weights(dims, shards, chunks, 1)


def sum_all(dims, layer_grads, grad_proj, grad_head):
    n_dp = dims[0] * dims[1] * dims[2]

    def blocks(values):
        cut = values.astype(jnp.bfloat16).reshape(*dims, values.shape[0] // n_dp, values.shape[1])
        return padded_rows(cut)

    parts, flags, heights = [], [], []
    for layer in reversed(range(LAYERS)):
        (words_mat, ents_mat, shared_mat), out_mat, up_mat, down_mat, _ = layer_grads[layer]
        late = layer % 2 == 0
        for values, y_first in (
            (up_mat, True),
            (down_mat, False),
            (words_mat, True),
            (ents_mat, False),
            (shared_mat, late),
            (out_mat, not late),
        ):
            parts.append(blocks(values))
            flags.append(y_first)
            heights.append(values.shape[0] // n_dp)
    for values, y_first in ((grad_proj, True), (grad_head, False)):
        parts.append(blocks(values))
        flags.append(y_first)
        heights.append(values.shape[0] // n_dp)
    norms = jnp.concatenate([layer_grads[layer][4] for layer in range(LAYERS)], axis=0)
    width = norms.shape[1] // n_dp
    norms = jnp.swapaxes(norms.reshape(norms.shape[0], n_dp, width), 0, 1)
    norms = jnp.pad(norms, [(0, 0), (0, 16 - norms.shape[1]), (0, -width % 128)])
    parts.append(norms.astype(jnp.bfloat16).reshape(*dims, *norms.shape[1:]))
    flags.append(True)
    totals = sum_gradients(dims, parts, flags, 2)
    norm_sum = totals[-1][: LAYERS * 4, :width].reshape(LAYERS, 4, width)
    totals = [total[:height] for total, height in zip(totals, heights)]
    attn, outs, ups, downs = [], [], [], []
    for layer in range(LAYERS):
        at = 6 * (LAYERS - 1 - layer)
        ups.append(totals[at])
        downs.append(totals[at + 1].T)
        for part in totals[at + 2 : at + 5]:
            half = part.shape[1] // 2
            attn += [part[:, :half], part[:, half:]]
        outs.append(totals[at + 5].T)
    attn = jnp.stack(attn)
    return (
        attn.reshape(LAYERS, 6, *attn.shape[1:]),
        jnp.stack(outs),
        jnp.stack(ups),
        jnp.stack(downs),
        norm_sum,
        totals[-2],
        totals[-1],
    )


def apart_device(
    word_inputs,
    entity_base,
    entity_ids,
    buckets,
    mask_positions,
    targets,
    word_cotangent,
    attention_in,
    attention_in_first,
    attention_in_second,
    attention_out,
    attention_out_first,
    attention_out_second,
    feed_up,
    feed_up_first,
    feed_up_second,
    feed_down,
    feed_down_first,
    feed_down_second,
    norm_params,
    norm_params_first,
    norm_params_second,
    entity_proj,
    entity_proj_first,
    entity_proj_second,
    head_proj,
    head_proj_first,
    head_proj_second,
    entity_table,
    entity_table_first,
    entity_table_second,
):
    dims = chip_grid(lax.axis_size("dp"))
    shards, heights = weight_shards(
        attention_in, attention_out, feed_up, feed_down, norm_params, entity_proj, head_proj
    )
    wholes = gather_apart(dims, shards)
    attn_low, out_low, up_low, down_low, norm_low, proj_low, head_low = unpack_weights(
        wholes, heights, norm_params.shape[-1]
    )
    gain_all = norm_low.astype(jnp.float32)
    slot_total = entity_ids.shape[0]
    shard_rows = entity_table.shape[0]
    bucket_rows = buckets.reshape(buckets.shape[2], buckets.shape[3])
    filled = bucket_rows >= 0
    safe_slot = jnp.maximum(bucket_rows, 0)
    request = jnp.where(filled, entity_ids[safe_slot] % shard_rows, -1)
    received = lax.all_to_all(request, "dp", split_axis=0, concat_axis=0, tiled=True)
    shard_base = lax.axis_index(("dp", "mp")) * shard_rows
    owned_mask = received >= 0
    safe_row = jnp.clip(received, 0, shard_rows - 1)
    table_low = entity_table.astype(jnp.bfloat16)
    replies = jnp.where(owned_mask[:, :, None], table_low[safe_row], jnp.zeros((), jnp.bfloat16))
    replied_rows_result = lax.all_to_all(replies, "dp", split_axis=0, concat_axis=0, tiled=True)
    row_placement_plan = (
        bucket_rows[:, :, None] == jnp.arange(slot_total, dtype=jnp.int32)[None, None, :]
    ).astype(jnp.bfloat16)
    local_shard_rows = jnp.einsum(
        "wvt,wvi->ti", row_placement_plan, replied_rows_result, preferred_element_type=jnp.float32
    )
    paired = pair_sum(local_shard_rows)
    masked_slots = (
        jnp.arange(SEQ_DEV, dtype=jnp.int32)[:, None] * ENT_LEN + mask_positions
    ).reshape(-1)
    keep_weight = 1.0 - jnp.any(
        jnp.arange(slot_total, dtype=jnp.int32)[:, None] == masked_slots[None, :], axis=1
    ).astype(jnp.float32)
    entity_rows = (paired * keep_weight[:, None]).astype(jnp.bfloat16)
    entity_inputs = entity_base.astype(jnp.float32) + jnp.dot(
        entity_rows, proj_low, preferred_element_type=jnp.float32
    )
    hidden = jnp.concatenate(
        [
            word_inputs.astype(jnp.float32).reshape(SEQ_DEV, WORDS, D),
            entity_inputs.reshape(SEQ_DEV, ENT_LEN, D),
        ],
        axis=1,
    )
    saved_layers = []
    for layer_index in range(LAYERS):
        hidden, saved_acts = layer_forward(
            hidden,
            attn_low[layer_index],
            out_low[layer_index],
            up_low[layer_index],
            down_low[layer_index],
            gain_all[layer_index],
        )
        saved_layers.append(saved_acts)
    seq_index = jnp.arange(SEQ_DEV, dtype=jnp.int32)[:, None]
    masked_rows = WORDS + mask_positions
    masked_low = hidden[seq_index, masked_rows].reshape(SEQ_DEV * MASK_ENT, D).astype(jnp.bfloat16)
    head_pre = jnp.dot(masked_low, head_low, preferred_element_type=jnp.float32)
    states_low = gelu_exact(head_pre).astype(jnp.bfloat16)
    all_states = spread(states_low, False, False, 3).reshape(-1, states_low.shape[1])
    logits = lax.dot_general(
        all_states, table_low, (((1,), (1,)), ((), ())), preferred_element_type=jnp.float32
    )
    flat_targets = targets.reshape(-1)
    target_hits = (
        jnp.arange(shard_rows, dtype=jnp.int32)[None, :] == (flat_targets - shard_base)[:, None]
    )
    peak_value = jnp.max(logits, axis=1)
    exp_total = jnp.sum(jnp.exp(logits - peak_value[:, None]), axis=1)
    picked = jnp.sum(jnp.where(target_hits, logits, 0.0), axis=1)
    shares = spread(jnp.stack([peak_value, exp_total, picked]), True, False, 4)
    peak_all = jnp.max(shares[:, 0], axis=0)
    total_all = jnp.sum(shares[:, 1] * jnp.exp(shares[:, 0] - peak_all), axis=0)
    picked_all = jnp.sum(shares[:, 2], axis=0)
    log_norm = peak_all + jnp.log(total_all)
    row_losses = log_norm - picked_all
    prob_rows = jnp.exp(logits - log_norm[:, None])
    grad_logits = ((prob_rows - target_hits.astype(jnp.float32)) / flat_targets.shape[0]).astype(
        jnp.bfloat16
    )
    grad_table = lax.dot_general(
        grad_logits, all_states, (((0,), (0,)), ((), ())), preferred_element_type=jnp.float32
    )
    grad_states = jnp.dot(grad_logits, table_low, preferred_element_type=jnp.float32)
    grad_states = grad_states.reshape(lax.axis_size("dp"), -1, grad_states.shape[1])
    grad_states = jnp.sum(spread(grad_states, False, True, 5), axis=0)
    grad_states = grad_states + lax.ppermute(grad_states, "mp", [(0, 1), (1, 0)])
    grad_head_pre = jax.vjp(gelu_exact, head_pre)[1](grad_states)[0].astype(jnp.bfloat16)
    grad_head = lax.dot_general(
        masked_low, grad_head_pre, (((0,), (0,)), ((), ())), preferred_element_type=jnp.float32
    )
    grad_masked = lax.dot_general(
        grad_head_pre, head_low, (((1,), (1,)), ((), ())), preferred_element_type=jnp.float32
    )
    grad_hidden = jnp.concatenate(
        [
            word_cotangent.astype(jnp.float32).reshape(SEQ_DEV, WORDS, D),
            jnp.zeros((SEQ_DEV, ENT_LEN, D), jnp.float32),
        ],
        axis=1,
    )
    grad_hidden = grad_hidden.at[seq_index, masked_rows].add(
        grad_masked.reshape(SEQ_DEV, MASK_ENT, D)
    )
    kept_grads = []
    for layer_index in reversed(range(LAYERS)):
        grad_hidden, layer_grads = layer_backward(
            grad_hidden,
            saved_layers[layer_index],
            attn_low[layer_index],
            out_low[layer_index],
            up_low[layer_index],
            down_low[layer_index],
            gain_all[layer_index],
        )
        if layer_index == 0:
            word_grads = grad_hidden[:, :WORDS].reshape(SEQ_DEV * WORDS, D)
            grad_entity = grad_hidden[:, WORDS:].reshape(slot_total, D).astype(jnp.bfloat16)
            grad_proj = lax.dot_general(
                entity_rows,
                grad_entity,
                (((0,), (0,)), ((), ())),
                preferred_element_type=jnp.float32,
            )
            row_gradient_block = (
                lax.dot_general(
                    grad_entity,
                    proj_low,
                    (((1,), (1,)), ((), ())),
                    preferred_element_type=jnp.float32,
                )
                * keep_weight[:, None]
            )
            outgoing = jnp.where(filled[:, :, None], row_gradient_block[safe_slot], 0.0)
            incoming = lax.all_to_all(
                outgoing.astype(jnp.bfloat16), "dp", split_axis=0, concat_axis=0, tiled=True
            ).astype(outgoing.dtype)
            grad_table = grad_table.at[safe_row].add(
                jnp.where(owned_mask[:, :, None], incoming, 0.0)
            )
        kept_grads.insert(0, layer_grads)
    reduced = sum_all(dims, kept_grads, grad_proj, grad_head)
    reduced_proj, reduced_head = reduced[5:]
    attn_new = adam_update(
        attention_in, attention_in_first, attention_in_second, reduced[0], kind_rates[0]
    )
    out_new = adam_update(
        attention_out, attention_out_first, attention_out_second, reduced[1], kind_rates[1]
    )
    up_new = adam_update(feed_up, feed_up_first, feed_up_second, reduced[2], kind_rates[2])
    down_new = adam_update(feed_down, feed_down_first, feed_down_second, reduced[3], kind_rates[3])
    norm_new = adam_update(
        norm_params, norm_params_first, norm_params_second, reduced[4], kind_rates[4]
    )
    proj_new = adam_update(
        entity_proj, entity_proj_first, entity_proj_second, reduced_proj, kind_rates[5]
    )
    head_new = adam_update(
        head_proj, head_proj_first, head_proj_second, reduced_head, kind_rates[6]
    )
    table_new = adam_update(
        entity_table, entity_table_first, entity_table_second, grad_table, kind_rates[7]
    )
    return (
        row_losses,
        word_grads,
        attn_new[0],
        attn_new[1],
        attn_new[2],
        out_new[0],
        out_new[1],
        out_new[2],
        up_new[0],
        up_new[1],
        up_new[2],
        down_new[0],
        down_new[1],
        down_new[2],
        norm_new[0],
        norm_new[1],
        norm_new[2],
        proj_new[0],
        proj_new[1],
        proj_new[2],
        head_new[0],
        head_new[1],
        head_new[2],
        table_new[0],
        table_new[1],
        table_new[2],
    )


def turned(*arrays):
    return tuple(jnp.swapaxes(array, 1, 2) for array in arrays)


def fused_device(
    word_inputs,
    entity_base,
    entity_ids,
    buckets,
    mask_positions,
    targets,
    word_cotangent,
    attention_in,
    attention_in_first,
    attention_in_second,
    attention_out,
    attention_out_first,
    attention_out_second,
    feed_up,
    feed_up_first,
    feed_up_second,
    feed_down,
    feed_down_first,
    feed_down_second,
    norm_params,
    norm_params_first,
    norm_params_second,
    entity_proj,
    entity_proj_first,
    entity_proj_second,
    head_proj,
    head_proj_first,
    head_proj_second,
    entity_table,
    entity_table_first,
    entity_table_second,
):
    dims = chip_grid(lax.axis_size("dp"))
    shards, heights = weight_shards(
        attention_in, attention_out, feed_up, feed_down, norm_params, entity_proj, head_proj
    )
    slot_total, shard_rows = entity_ids.shape[0], entity_table.shape[0]
    bucket_rows = buckets.reshape(buckets.shape[2], buckets.shape[3])
    request = jnp.where(
        bucket_rows >= 0, entity_ids[jnp.maximum(bucket_rows, 0)] % shard_rows, -1
    ).astype(jnp.int32)
    requests = jnp.broadcast_to(request[:, :, None], (*request.shape, 128))
    slots = jnp.arange(slot_total, dtype=jnp.int32)
    marks = mask_positions.reshape(-1)[:, None] == slots[None, :]
    keep = jnp.logical_not(jnp.any(marks, axis=0))
    place_mat = (slots[:, None] == bucket_rows.reshape(-1)[None, :]) & keep[:, None]
    place_mat = place_mat.astype(jnp.bfloat16)
    hits = marks.astype(jnp.bfloat16)
    table_low = entity_table.astype(jnp.bfloat16)
    flat_targets = targets.reshape(-1)
    local_targets = flat_targets - lax.axis_index(("dp", "mp")) * shard_rows
    local_targets = jnp.broadcast_to(local_targets[None, :], (8, flat_targets.shape[0]))
    wholes, saved_layers, ents, gain_rows, entity_rows, got = run_forward(
        dims, word_inputs, entity_base, requests, place_mat, table_low, shards, 6
    )
    losses, grad_logits, states, grad_head, grad_ents = run_head(
        dims, ents, hits, wholes[5][0], table_low, local_targets, 7
    )
    word_grads, incoming, totals = run_backward(
        dims,
        word_cotangent,
        grad_ents,
        grad_head,
        gain_rows,
        entity_rows,
        place_mat,
        wholes,
        saved_layers,
        8,
    )
    wanted = jnp.broadcast_to(got[:, 0][None, :], (8, got.shape[0]))
    updated = run_update(
        (
            (attention_in, attention_in_first, attention_in_second),
            turned(attention_out, attention_out_first, attention_out_second),
            (feed_up, feed_up_first, feed_up_second),
            turned(feed_down, feed_down_first, feed_down_second),
            (norm_params, norm_params_first, norm_params_second),
            (entity_proj, entity_proj_first, entity_proj_second),
            (head_proj, head_proj_first, head_proj_second),
            (entity_table, entity_table_first, entity_table_second),
        ),
        totals,
        incoming,
        wanted,
        grad_logits,
        states,
    )
    updated[1], updated[3] = turned(*updated[1]), turned(*updated[3])
    results = [losses[0], word_grads]
    for master, first, second in updated:
        results += [first, second, master]
    return tuple(results)


def on_device(*arrays):
    n_dp = lax.axis_size("dp")
    whole_tiles = D % (16 * n_dp) == 0
    return (fused_device if whole_tiles else apart_device)(*arrays)


def solution(mesh):
    in_specs = (
        P("dp", None),
        P("dp", None),
        P("dp"),
        P("dp", "mp", None, None),
        P("dp", None),
        P(),
        P("dp", None),
        P(None, None, "dp", "mp"),
        P(None, None, "dp", "mp"),
        P(None, None, "dp", "mp"),
        P(None, "mp", "dp"),
        P(None, "mp", "dp"),
        P(None, "mp", "dp"),
        P(None, "dp", "mp"),
        P(None, "dp", "mp"),
        P(None, "dp", "mp"),
        P(None, "mp", "dp"),
        P(None, "mp", "dp"),
        P(None, "mp", "dp"),
        P(None, None, "dp"),
        P(None, None, "dp"),
        P(None, None, "dp"),
        P("dp", None),
        P("dp", None),
        P("dp", None),
        P("dp", None),
        P("dp", None),
        P("dp", None),
        P(("dp", "mp"), None),
        P(("dp", "mp"), None),
        P(("dp", "mp"), None),
    )
    out_specs = (
        P(),
        P("dp", None),
        P(None, None, "dp", "mp"),
        P(None, None, "dp", "mp"),
        P(None, None, "dp", "mp"),
        P(None, "mp", "dp"),
        P(None, "mp", "dp"),
        P(None, "mp", "dp"),
        P(None, "dp", "mp"),
        P(None, "dp", "mp"),
        P(None, "dp", "mp"),
        P(None, "mp", "dp"),
        P(None, "mp", "dp"),
        P(None, "mp", "dp"),
        P(None, None, "dp"),
        P(None, None, "dp"),
        P(None, None, "dp"),
        P("dp", None),
        P("dp", None),
        P("dp", None),
        P("dp", None),
        P("dp", None),
        P("dp", None),
        P(("dp", "mp"), None),
        P(("dp", "mp"), None),
        P(("dp", "mp"), None),
    )
    return jax.shard_map(
        on_device, mesh=mesh, in_specs=in_specs, out_specs=out_specs, check_vma=False
    )
```

```python
import functools

import jax
import jax.numpy as jnp
from jax import lax
from jax.experimental import pallas as pl
from jax.experimental.pallas import tpu as pltpu
from jax.sharding import PartitionSpec as P

D = 768
HEAD_DIM = 64
WORDS = 896
ENT_LEN = 128
MASK_ENT = 16
LAYERS = 2
STEP = 10
SEQ_DEV = 1


norm_eps = 1e-05
beta_first = 0.9
beta_second = 0.999
adam_eps = 1e-12
weight_decay = 0.01
kind_rates = (0.05, 1.0, 0.05, 0.027, 0.75, 0.5, 0.05, 0.2)


MESH = pl.DeviceIdType.MESH
ANY = pl.BlockSpec(memory_space=pl.ANY)
VMEM = pl.BlockSpec(memory_space=pltpu.VMEM)
VMEM_BYTES = 60 * 2**20


def chip_grid(n_dp):
    return {16: (4, 2, 2), 64: (4, 4, 4)}.get(n_dp, (n_dp, 1, 1))


def place(dims):
    index = lax.axis_index("dp")
    return index // (dims[1] * dims[2]), index // dims[2] % dims[1], index % dims[2]


def axis_peers(dims, axis):
    here = place(dims)
    core = lax.axis_index("mp")
    peers = []
    for step in range(1, dims[axis]):
        spot = list(here)
        spot[axis] = lax.rem(here[axis] + step, dims[axis])
        peers.append((spot[axis], (spot[0] * dims[1] * dims[2] + spot[1] * dims[2] + spot[2], core)))
    return peers


def greet(targets):
    barrier = pltpu.get_barrier_semaphore()
    for target in targets:
        pl.semaphore_signal(barrier, inc=1, device_id=target, device_id_type=MESH)
    pl.semaphore_wait(barrier, len(targets))


def send(src, dst, send_sem, recv_sem, target):
    copy = pltpu.make_async_remote_copy(
        src_ref=src,
        dst_ref=dst,
        send_sem=send_sem,
        recv_sem=recv_sem,
        device_id=target,
        device_id_type=MESH,
    )
    copy.start()
    return copy


def gather_body(dims, chunks, count, *refs):
    shards, wholes = refs[:count], refs[count : 2 * count]
    send_sem, recv_sem, local_sem = refs[2 * count :]
    z, y, x = place(dims)
    peers = [axis_peers(dims, axis) for axis in range(3)]
    greet([target for group in peers for _, target in group])
    pending = {}

    def start(stage, c):
        which, first, size, y_first = chunks[c]
        rows = pl.ds(first, size)
        whole = wholes[which]
        copies = []
        if stage == 0:
            src, dst, group = shards[which].at[rows], whole.at[rows, z, y, x], peers[0]
            own = pltpu.make_async_copy(src, dst, local_sem.at[c])
            own.start()
            copies.append(own)
        elif stage == 1:
            src = whole.at[rows, :, y, x]
            dst, group = src, peers[1 if y_first else 2]
        else:
            src = whole.at[rows, :, :, x] if y_first else whole.at[rows, :, y]
            dst, group = src, peers[2 if y_first else 1]
        base = (0, dims[0], dims[0] + max(dims[1:]))[stage]
        for slot, (_, target) in enumerate(group):
            copies.append(
                send(src, dst, send_sem.at[c, base + slot], recv_sem.at[c, base + slot], target)
            )
        pending[stage, c] = copies

    def finish(stage, c):
        for copy in pending.pop((stage, c)):
            copy.wait()

    total = len(chunks)
    start(0, 0)
    for step in range(total + 2):
        if step + 1 < total:
            start(0, step + 1)
        if step < total:
            finish(0, step)
            start(1, step)
        if 0 <= step - 1 < total:
            finish(1, step - 1)
            start(2, step - 1)
        if 0 <= step - 2 < total:
            finish(2, step - 2)


def gather_weights(dims, shards, chunks, collective_id):
    count = len(shards)
    copies = dims[0] + 2 * max(dims[1:])
    return pl.pallas_call(
        functools.partial(gather_body, dims, chunks, count),
        out_shape=[
            jax.ShapeDtypeStruct((s.shape[0], *dims, *s.shape[1:]), s.dtype) for s in shards
        ],
        in_specs=[ANY] * count,
        out_specs=[ANY] * count,
        scratch_shapes=[
            pltpu.SemaphoreType.DMA((len(chunks), copies)),
            pltpu.SemaphoreType.DMA((len(chunks), copies)),
            pltpu.SemaphoreType.DMA((len(chunks),)),
        ],
        compiler_params=pltpu.CompilerParams(
            collective_id=collective_id, has_side_effects=True, vmem_limit_bytes=2**20
        ),
    )(*shards)


def sum_body(dims, flags, *refs):
    count = len(flags)
    parts, totals = refs[:count], refs[count : 2 * count]
    buffers = refs[2 * count : 6 * count]
    send_sem, recv_sem, local_sem = refs[6 * count :]
    z, y, x = place(dims)
    peers = [axis_peers(dims, axis) for axis in range(3)]
    greet([target for group in peers for _, target in group])
    pending = {}

    def start(stage, c):
        y_first = flags[c]
        own, first, second, third = buffers[4 * c : 4 * c + 4]
        copies = []
        base = (0, max(dims[1:]), 2 * max(dims[1:]))[stage]
        if stage == 0:
            mine = parts[c].at[:, y] if y_first else parts[c].at[:, :, x]
            local = pltpu.make_async_copy(mine, own, local_sem.at[c])
            local.start()
            copies.append(local)
        group = peers[((1, 2, 0) if y_first else (2, 1, 0))[stage]]
        for slot, (spot, target) in enumerate(group):
            if stage == 0:
                src = parts[c].at[:, spot] if y_first else parts[c].at[:, :, spot]
                dst = first.at[slot]
            elif stage == 1:
                src, dst = own.at[:, spot], second.at[slot]
            else:
                src, dst = own.at[spot, x if y_first else y], third.at[slot]
            copies.append(
                send(src, dst, send_sem.at[c, base + slot], recv_sem.at[c, base + slot], target)
            )
        pending[stage, c] = copies

    def finish(stage, c):
        y_first = flags[c]
        own, first, second, third = buffers[4 * c : 4 * c + 4]
        for copy in pending.pop((stage, c)):
            copy.wait()
        across = dims[2] if y_first else dims[1]
        line = x if y_first else y
        count_peers = len(peers[((1, 2, 0) if y_first else (2, 1, 0))[stage]])
        if stage == 0 and count_peers:

            def add_first(i, carry):
                value = own[i // across, i % across].astype(jnp.float32)
                for slot in range(count_peers):
                    value += first[slot, i // across, i % across].astype(jnp.float32)
                own[i // across, i % across] = value.astype(own.dtype)
                return carry

            lax.fori_loop(0, dims[0] * across, add_first, 0)
        if stage == 1 and count_peers:

            def add_second(i, carry):
                value = own[i, line].astype(jnp.float32)
                for slot in range(count_peers):
                    value += second[slot, i].astype(jnp.float32)
                own[i, line] = value.astype(own.dtype)
                return carry

            lax.fori_loop(0, dims[0], add_second, 0)
        if stage == 2:
            value = own[z, line].astype(jnp.float32)
            for slot in range(count_peers):
                value += third[slot].astype(jnp.float32)
            totals[c][...] = value

    total = len(flags)
    ahead = 2
    for c in range(min(ahead, total)):
        start(0, c)
    for step in range(total + 2 * ahead):
        if step + ahead < total:
            start(0, step + ahead)
        if step < total:
            finish(0, step)
            start(1, step)
        if 0 <= step - ahead < total:
            finish(1, step - ahead)
            start(2, step - ahead)
        if 0 <= step - 2 * ahead < total:
            finish(2, step - 2 * ahead)


def sum_gradients(dims, parts, flags, collective_id):
    count = len(parts)
    scratch = []
    for part, y_first in zip(parts, flags):
        block = part.shape[3:]
        own = (dims[0], dims[2] if y_first else dims[1])
        turns = (dims[1], dims[2]) if y_first else (dims[2], dims[1])
        scratch += [
            pltpu.VMEM((*own, *block), part.dtype),
            pltpu.VMEM((max(turns[0] - 1, 1), *own, *block), part.dtype),
            pltpu.VMEM((max(turns[1] - 1, 1), dims[0], *block), part.dtype),
            pltpu.VMEM((max(dims[0] - 1, 1), *block), part.dtype),
        ]
    copies = dims[0] + 2 * max(dims[1:])
    return pl.pallas_call(
        functools.partial(sum_body, dims, flags),
        out_shape=[jax.ShapeDtypeStruct(part.shape[3:], jnp.float32) for part in parts],
        in_specs=[ANY] * count,
        out_specs=[VMEM] * count,
        scratch_shapes=scratch
        + [
            pltpu.SemaphoreType.DMA((count, copies)),
            pltpu.SemaphoreType.DMA((count, copies)),
            pltpu.SemaphoreType.DMA((count,)),
        ],
        compiler_params=pltpu.CompilerParams(
            collective_id=collective_id, has_side_effects=True, vmem_limit_bytes=VMEM_BYTES
        ),
    )(*parts)


def spread_body(count, wide, swap, data, result, send_sem, recv_sem, local_sem):
    pair = lax.axis_size("mp")
    index = lax.axis_index("dp") * pair + lax.axis_index("mp") if wide else lax.axis_index("dp")

    def target_of(step):
        other = lax.rem(index + step, count)
        if wide:
            return other, (other // pair, lax.rem(other, pair))
        return other, (other, lax.axis_index("mp"))

    barrier = pltpu.get_barrier_semaphore()

    def hello(step, carry):
        pl.semaphore_signal(barrier, inc=1, device_id=target_of(step)[1], device_id_type=MESH)
        return carry

    lax.fori_loop(1, count, hello, 0)
    pl.semaphore_wait(barrier, count - 1)
    own = pltpu.make_async_copy(data.at[index if swap else 0], result.at[index], local_sem)
    own.start()

    def copy_of(step):
        other, target = target_of(step)
        return pltpu.make_async_remote_copy(
            src_ref=data.at[other if swap else 0],
            dst_ref=result.at[index],
            send_sem=send_sem.at[step],
            recv_sem=recv_sem.at[step],
            device_id=target,
            device_id_type=MESH,
        )

    def go(step, carry):
        copy_of(step).start()
        return carry

    def done(step, carry):
        copy_of(step).wait()
        return carry

    lax.fori_loop(1, count, go, 0)
    own.wait()
    lax.fori_loop(1, count, done, 0)


def spread(data, wide, swap, collective_id):
    count = lax.axis_size("dp") * (lax.axis_size("mp") if wide else 1)
    block = data.shape[1:] if swap else data.shape
    return pl.pallas_call(
        functools.partial(spread_body, count, wide, swap),
        out_shape=jax.ShapeDtypeStruct((count, *block), data.dtype),
        in_specs=[VMEM],
        out_specs=VMEM,
        scratch_shapes=[
            pltpu.SemaphoreType.DMA((count,)),
            pltpu.SemaphoreType.DMA((count,)),
            pltpu.SemaphoreType.DMA,
        ],
        compiler_params=pltpu.CompilerParams(
            collective_id=collective_id, has_side_effects=True, vmem_limit_bytes=VMEM_BYTES
        ),
    )(data if swap else data[None])


def layer_norm(values, gain_row, shift_row):
    centered = values - jnp.mean(values, axis=-1, keepdims=True)
    spread = jnp.mean(centered * centered, axis=-1, keepdims=True)
    return centered * lax.rsqrt(spread + norm_eps) * gain_row + shift_row


def gelu_exact(values):
    return jax.nn.gelu(values, approximate=False)


def adam_update(master, first_moment, second_moment, gradient, kind_rate):
    first_new = beta_first * first_moment + (1.0 - beta_first) * gradient
    second_new = beta_second * second_moment + (1.0 - beta_second) * gradient * gradient
    first_hat = first_new / (1.0 - beta_first**STEP)
    second_hat = second_new / (1.0 - beta_second**STEP)
    master_new = master - kind_rate * (
        first_hat / (jnp.sqrt(second_hat) + adam_eps) + weight_decay * master
    )
    return (first_new, second_new, master_new)


def project(fetched_row_values, weight_matrix_entry):
    return jnp.einsum(
        "mvw,wu->mvu", fetched_row_values, weight_matrix_entry, preferred_element_type=jnp.float32
    )


def project_back(row_gradient_block, weight_matrix_entry):
    return jnp.einsum(
        "tic,vc->tiv", row_gradient_block, weight_matrix_entry, preferred_element_type=jnp.float32
    )


def project_turned(rows, turned):
    return jnp.einsum("mvw,uw->mvu", rows, turned, preferred_element_type=jnp.float32)


def project_back_turned(row_gradient_block, turned):
    return jnp.einsum("tic,cv->tiv", row_gradient_block, turned, preferred_element_type=jnp.float32)


def weight_grad(layer_input_list, row_gradient_block):
    return jnp.einsum(
        "hmq,hmw->qw", layer_input_list, row_gradient_block, preferred_element_type=jnp.float32
    ).astype(jnp.bfloat16)


def split_heads(values):
    return values.reshape(values.shape[0], values.shape[1], values.shape[2] // HEAD_DIM, HEAD_DIM)


def pair_sum(partial_sum):
    mine = partial_sum.astype(jnp.bfloat16)
    theirs = lax.ppermute(mine, "mp", [(0, 1), (1, 0)])
    return mine.astype(jnp.float32) + theirs.astype(jnp.float32)


merge_heads = merge_inputs = pair_sum


def seq_scores(query_word, query_entity, key_rows):
    score_word = jnp.einsum(
        "qhd,khd->hqk", query_word, key_rows[:WORDS], preferred_element_type=jnp.float32
    )
    score_entity = jnp.einsum(
        "qhd,khd->hqk", query_entity, key_rows[WORDS:], preferred_element_type=jnp.float32
    )
    return jnp.concatenate([score_word, score_entity], axis=-1) * 0.125


def attend_forward(seq_item):
    query_word, query_entity, key_rows, value_rows = seq_item
    scores = seq_scores(query_word, query_entity, key_rows)
    peak_value = jnp.max(scores, axis=-1, keepdims=True)
    exp_scores = jnp.exp(scores - peak_value)
    exp_total = jnp.sum(exp_scores, axis=-1, keepdims=True)
    prob_low = (exp_scores / exp_total).astype(jnp.bfloat16)
    mixed_heads = jnp.einsum(
        "hqk,khd->qhd", prob_low, value_rows, preferred_element_type=jnp.float32
    )
    return (mixed_heads, (peak_value + jnp.log(exp_total))[..., 0])


def attend_backward(seq_item):
    query_word, query_entity, key_rows, value_rows, log_norm, grad_mixed = seq_item
    scores = seq_scores(query_word, query_entity, key_rows)
    prob_rows = jnp.exp(scores - log_norm[..., None])
    grad_value = jnp.einsum(
        "hqk,qhd->khd",
        prob_rows.astype(jnp.bfloat16),
        grad_mixed,
        preferred_element_type=jnp.float32,
    )
    grad_probs = jnp.einsum(
        "qhd,khd->hqk", grad_mixed, value_rows, preferred_element_type=jnp.float32
    )
    inner_sum = jnp.sum(prob_rows * grad_probs, axis=-1, keepdims=True)
    grad_scores = (prob_rows * (grad_probs - inner_sum) * 0.125).astype(jnp.bfloat16)
    score_word = grad_scores[..., :WORDS]
    score_entity = grad_scores[..., WORDS:]
    grad_qw = jnp.einsum(
        "hqk,khd->qhd", score_word, key_rows[:WORDS], preferred_element_type=jnp.float32
    )
    grad_qe = jnp.einsum(
        "hqk,khd->qhd", score_entity, key_rows[WORDS:], preferred_element_type=jnp.float32
    )
    grad_key = jnp.concatenate(
        [
            jnp.einsum("hqk,qhd->khd", score_word, query_word, preferred_element_type=jnp.float32),
            jnp.einsum(
                "hqk,qhd->khd", score_entity, query_entity, preferred_element_type=jnp.float32
            ),
        ],
        axis=0,
    )
    return (grad_qw, grad_qe, grad_key, grad_value)


def layer_forward(hidden, attn_mats, out_mat, up_mat, down_mat, gain_rows):
    hidden_low = hidden.astype(jnp.bfloat16)
    words_low = hidden_low[:, :WORDS]
    ents_low = hidden_low[:, WORDS:]
    query_word = jnp.concatenate(
        [project(words_low, attn_mats[0]), project(ents_low, attn_mats[2])], axis=1
    ).astype(jnp.bfloat16)
    query_entity = jnp.concatenate(
        [project(words_low, attn_mats[1]), project(ents_low, attn_mats[3])], axis=1
    ).astype(jnp.bfloat16)
    key_rows = project(hidden_low, attn_mats[4]).astype(jnp.bfloat16)
    value_rows = project(hidden_low, attn_mats[5]).astype(jnp.bfloat16)
    mixed_heads, log_norm = lax.map(
        attend_forward,
        (
            split_heads(query_word),
            split_heads(query_entity),
            split_heads(key_rows),
            split_heads(value_rows),
        ),
    )
    mixed_low = mixed_heads.reshape(key_rows.shape).astype(jnp.bfloat16)
    attended = merge_heads(project_turned(mixed_low, out_mat))
    first_out = layer_norm(hidden + attended, gain_rows[0], gain_rows[1])
    first_low = first_out.astype(jnp.bfloat16)
    inner_pre = project(first_low, up_mat)
    inner_low = gelu_exact(inner_pre).astype(jnp.bfloat16)
    outer_out = merge_heads(project_turned(inner_low, down_mat))
    result = layer_norm(first_out + outer_out, gain_rows[2], gain_rows[3])
    saved_acts = (
        hidden,
        hidden_low,
        query_word,
        query_entity,
        key_rows,
        value_rows,
        log_norm,
        mixed_low,
        attended,
        first_out,
        first_low,
        inner_pre,
        inner_low,
        outer_out,
    )
    return (result, saved_acts)


def layer_backward(grad_out, saved_acts, attn_mats, out_mat, up_mat, down_mat, gain_rows):
    (
        hidden,
        hidden_low,
        query_word,
        query_entity,
        key_rows,
        value_rows,
        log_norm,
        mixed_low,
        attended,
        first_out,
        first_low,
        inner_pre,
        inner_low,
        outer_out,
    ) = saved_acts
    second_back = jax.vjp(layer_norm, first_out + outer_out, gain_rows[2], gain_rows[3])[1]
    grad_second, grad_gain_late, grad_shift_late = second_back(grad_out)
    grad_outer = grad_second.astype(jnp.bfloat16)
    grad_down = weight_grad(grad_outer, inner_low)
    grad_inner = project_back_turned(grad_outer, down_mat)
    grad_pre = jax.vjp(gelu_exact, inner_pre)[1](grad_inner)[0].astype(jnp.bfloat16)
    grad_up = weight_grad(first_low, grad_pre)
    grad_first = grad_second + merge_inputs(project_back(grad_pre, up_mat))
    first_back = jax.vjp(layer_norm, hidden + attended, gain_rows[0], gain_rows[1])[1]
    grad_first_in, grad_gain_early, grad_shift_early = first_back(grad_first)
    grad_attended = grad_first_in.astype(jnp.bfloat16)
    grad_out_mat = weight_grad(grad_attended, mixed_low)
    grad_mixed = project_back_turned(grad_attended, out_mat).astype(jnp.bfloat16)
    grad_qw, grad_qe, grad_key, grad_value = lax.map(
        attend_backward,
        (
            split_heads(query_word),
            split_heads(query_entity),
            split_heads(key_rows),
            split_heads(value_rows),
            log_norm,
            split_heads(grad_mixed),
        ),
    )
    flat_shape = key_rows.shape
    grad_qw = grad_qw.reshape(flat_shape).astype(jnp.bfloat16)
    grad_qe = grad_qe.reshape(flat_shape).astype(jnp.bfloat16)
    grad_key = grad_key.reshape(flat_shape).astype(jnp.bfloat16)
    grad_value = grad_value.reshape(flat_shape).astype(jnp.bfloat16)
    words_low = hidden_low[:, :WORDS]
    ents_low = hidden_low[:, WORDS:]
    grad_mats = (
        weight_grad(words_low, jnp.concatenate([grad_qw[:, :WORDS], grad_qe[:, :WORDS]], axis=-1)),
        weight_grad(ents_low, jnp.concatenate([grad_qw[:, WORDS:], grad_qe[:, WORDS:]], axis=-1)),
        weight_grad(hidden_low, jnp.concatenate([grad_key, grad_value], axis=-1)),
    )
    part_words = project_back(grad_qw[:, :WORDS], attn_mats[0]) + project_back(
        grad_qe[:, :WORDS], attn_mats[1]
    )
    part_ents = project_back(grad_qw[:, WORDS:], attn_mats[2]) + project_back(
        grad_qe[:, WORDS:], attn_mats[3]
    )
    part_sum = (
        jnp.concatenate([part_words, part_ents], axis=1)
        + project_back(grad_key, attn_mats[4])
        + project_back(grad_value, attn_mats[5])
    )
    grad_hidden = grad_first_in + merge_inputs(part_sum)
    grad_norms = jnp.stack([grad_gain_early, grad_shift_early, grad_gain_late, grad_shift_late])
    return (grad_hidden, (grad_mats, grad_out_mat, grad_up, grad_down, grad_norms))


LOG2E = 1.4426950408889634
SCORE_STEP = 0.125 * LOG2E
LEN = WORDS + ENT_LEN
BLOCK = 256
BLOCKS = LEN // BLOCK


def mm(left, right):
    return lax.dot_general(
        left, right, (((1,), (0,)), ((), ())), preferred_element_type=jnp.float32
    )


def mm_rt(left, right):
    return lax.dot_general(
        left, right, (((1,), (1,)), ((), ())), preferred_element_type=jnp.float32
    )


def mm_lt(left, right):
    return lax.dot_general(
        left, right, (((0,), (0,)), ((), ())), preferred_element_type=jnp.float32
    )


def flat(ref, *index):
    value = ref[index] if index else ref[...]
    return value.reshape(-1, value.shape[-1])


def lane_mask(rows, which):
    lane = lax.broadcasted_iota(jnp.int32, (rows, 2 * HEAD_DIM), 1)
    return (lane // HEAD_DIM == which).astype(jnp.bfloat16)


def normed(values):
    centered = values - jnp.mean(values, axis=-1, keepdims=True)
    spread_row = jnp.mean(centered * centered, axis=-1, keepdims=True)
    scale = lax.rsqrt(spread_row + norm_eps)
    return centered * scale, scale


def gelu_parts(values):
    cdf = 0.5 * (1.0 + lax.erf(values * 0.7071067811865476))
    bell = jnp.exp2(values * values * (-0.5 * LOG2E)) * 0.3989422804014327
    return values * cdf, cdf + values * bell


GATHER_RATE = 52000.0
SUM_RATE = 45000.0
HOP_US = 1.5
ORDERS = ((0, 1, 2), (0, 2, 1), (2, 0, 1), (1, 0, 2))


def cut_load(size):
    return (size // 2) * (size - size // 2)


def gather_loads(dims, order, shard_bytes):
    loads, held = [0.0, 0.0, 0.0], shard_bytes
    for axis in order:
        loads[axis] += held * cut_load(dims[axis])
        held *= dims[axis]
    return loads


def balanced_orders(dims, sizes):
    total, chosen = [0.0, 0.0, 0.0], []
    for size in sizes:
        options = []
        for rank, order in enumerate(ORDERS):
            loads = gather_loads(dims, order, size)
            after = [a + b for a, b in zip(total, loads)]
            options.append((max(after), sum(after), rank, order, after))
        best = min(options)
        chosen.append(best[3])
        total = best[4]
    return chosen


class Links:
    def __init__(self, dims, rate):
        self.dims, self.rate = dims, rate
        self.clock, self.free, self.serial = 0.0, [0.0, 0.0, 0.0], 0
        self.active = []

    def issue(self, axis, message_bytes, what):
        if self.dims[axis] > 1:
            begin = max(self.clock, self.free[axis])
            self.free[axis] = begin + message_bytes * cut_load(self.dims[axis]) / self.rate
            finish = self.free[axis] + HOP_US
        else:
            finish = self.clock
        self.serial += 1
        self.active.append((finish, self.serial, what))

    def finish_first(self):
        first = min(self.active, key=lambda item: item[:2])
        self.active.remove(first)
        self.clock = max(self.clock, first[0])
        self.complete(first[2])

    def spend(self, micros):
        self.clock += micros
        while self.active and min(item[0] for item in self.active) <= self.clock:
            self.finish_first()


class Gather(Links):
    def __init__(self, dims, chunks, shards, wholes, kept, sems):
        super().__init__(dims, GATHER_RATE)
        self.chunks, self.shards, self.wholes, self.kept = chunks, shards, wholes, kept
        self.send_sem, self.recv_sem, self.local_sem, self.keep_sem = sems
        self.spot = place(dims)
        self.peers = [axis_peers(dims, axis) for axis in range(3)]
        self.copies, self.done, self.keeping = {}, set(), []
        self.next, self.window = 0, 6

    def slab(self, whole, order, stage):
        held = order[:stage]
        return whole.at[
            (slice(None), *[slice(None) if d in held else self.spot[d] for d in range(3)])
        ]

    def start(self, stage, c):
        which, rows, cols, order = self.chunks[c]
        whole = self.wholes[which].at[rows, :, :, :, :, cols]
        shard = self.shards[which].at[rows, :, cols]
        copies, base = [], sum(self.dims[order[i]] for i in range(stage))
        dst = self.slab(whole, order, stage)
        src = dst
        if stage == 0:
            own = pltpu.make_async_copy(shard, dst, self.local_sem.at[c])
            own.start()
            copies.append(own)
            src = shard
        for slot, (_, target) in enumerate(self.peers[order[stage]]):
            sems = self.send_sem.at[c, base + slot], self.recv_sem.at[c, base + slot]
            copies.append(send(src, dst, *sems, target))
        self.copies[stage, c] = copies
        held = 1
        for axis in order[:stage]:
            held *= self.dims[axis]
        shape = shard.shape
        self.issue(order[stage], held * 2 * shape[0] * shape[1] * shape[2], (stage, c))

    def complete(self, what):
        stage, c = what
        for copy in self.copies.pop(what):
            copy.wait()
        if stage < 2:
            self.start(stage + 1, c)
        else:
            which, rows, cols, _ = self.chunks[c]
            at = (rows, slice(None), slice(None), slice(None), slice(None), cols)
            keep = pltpu.make_async_copy(
                self.wholes[which].at[at], self.kept[which].at[at], self.keep_sem.at[c]
            )
            keep.start()
            self.keeping.append(keep)
            self.done.add(c)
        self.refill()

    def refill(self):
        while self.next < len(self.chunks) and self.next - len(self.done) < self.window:
            self.next += 1
            self.start(0, self.next - 1)

    def need(self, c):
        while c not in self.done:
            self.finish_first()

    def close(self):
        while self.active:
            self.finish_first()
        for keep in self.keeping:
            keep.wait()


class Pair:
    def __init__(self, mine, theirs, sems):
        self.mine, self.theirs = mine, theirs
        self.send_sem, self.recv_sem = sems
        self.phase = 0
        self.other = (lax.axis_index("dp"), 1 - lax.axis_index("mp"))

    def copy(self, phase, c):
        return pltpu.make_async_remote_copy(
            src_ref=self.mine.at[c],
            dst_ref=self.theirs.at[phase % 2, c],
            send_sem=self.send_sem.at[phase, c],
            recv_sem=self.recv_sem.at[phase, c],
            device_id=self.other,
            device_id_type=MESH,
        )

    def run(self, compute, consume, between):
        phase = self.phase
        self.phase += 1

        def take(c):
            self.copy(phase, c).wait()
            total = self.mine[c].astype(jnp.float32) + self.theirs[phase % 2, c].astype(jnp.float32)
            consume(c, pl.ds(c * BLOCK, BLOCK), total)

        for c in range(BLOCKS):
            self.mine[c] = compute(c, pl.ds(c * BLOCK, BLOCK)).astype(jnp.bfloat16)
            self.copy(phase, c).start()
            if c:
                take(c - 1)
            between()
        take(BLOCKS - 1)


SAVED = ("xb", "qw", "qe", "k", "v", "o", "n1", "h1b", "slope", "g", "n2", "stats")


def saved_shapes(half, hidden):
    wide, narrow = (LEN, D), (LEN, half)
    low = jnp.bfloat16
    return {
        "xb": (wide, low),
        "qw": (narrow, low),
        "qe": (narrow, low),
        "k": (narrow, low),
        "v": (narrow, low),
        "o": (narrow, low),
        "n1": (wide, low),
        "h1b": (wide, low),
        "slope": ((LEN, hidden), low),
        "g": ((LEN, hidden), low),
        "n2": (wide, low),
        "stats": ((LEN, 128), jnp.float32),
    }


def attend(act, pair):
    lanes = slice(pair * 2 * HEAD_DIM, (pair + 1) * 2 * HEAD_DIM)

    def block(i, carry):
        rows = pl.ds(i * BLOCK, BLOCK)
        keys, values = act["k"][:, lanes], act["v"][:, lanes]
        total = None
        for which in range(2):
            q_mask, v_mask = lane_mask(BLOCK, which), lane_mask(LEN, which)
            score_w = mm_rt(act["qw"][rows, lanes] * q_mask, keys[:WORDS])
            score_e = mm_rt(act["qe"][rows, lanes] * q_mask, keys[WORDS:])
            peak = jnp.maximum(
                jnp.max(score_w, axis=-1, keepdims=True), jnp.max(score_e, axis=-1, keepdims=True)
            )
            exp_w = jnp.exp2((score_w - peak) * SCORE_STEP)
            exp_e = jnp.exp2((score_e - peak) * SCORE_STEP)
            weight = jnp.sum(exp_w, axis=-1, keepdims=True) + jnp.sum(exp_e, axis=-1, keepdims=True)
            part = values * v_mask
            mixed = mm(exp_w.astype(jnp.bfloat16), part[:WORDS])
            mixed += mm(exp_e.astype(jnp.bfloat16), part[WORDS:])
            mixed = mixed * (1.0 / weight)
            total = mixed if total is None else total + mixed
            head = 2 * pair + which
            act["stats"][rows, head : head + 1] = peak * SCORE_STEP + jnp.log2(weight)
        act["o"][rows, lanes] = total.astype(jnp.bfloat16)
        return carry

    lax.fori_loop(0, BLOCKS, block, 0)


def project_rows(out_ref, x_ref, first, size, step, weights, index):
    def block(i, carry):
        rows = pl.ds(first + i * step, step)
        out_ref[rows, :] = mm(x_ref[rows, :], flat(weights, index)).astype(jnp.bfloat16)
        return carry

    lax.fori_loop(0, size // step, block, 0)


def forward_body(dims, chunks, needs, *refs):
    refs = list(refs)

    def take(count):
        part = refs[:count]
        del refs[:count]
        return part

    words, base, requests, place_mat, table = take(5)
    shards = take(len(needs["kinds"]))
    kept = take(len(needs["kinds"]))
    saved = [dict(zip(SAVED, take(len(SAVED)))) for _ in range(LAYERS)]
    ents_out, gains_out, rows_in, got_out, table_out = take(5)
    wholes = take(len(needs["kinds"]))
    act = dict(zip(SAVED, take(len(SAVED))))
    x, h1, gains, mine, theirs = take(5)
    gather_sems = take(4)
    pair_sems = take(2)
    (save_sem,) = take(1)
    got, replies, answers, look_mine, look_theirs = take(5)
    look_send, look_recv, look_pair, table_full, table_sem = take(5)
    reading = pltpu.make_async_copy(table, table_full, table_sem)
    reading.start()

    gather = Gather(dims, chunks, shards, wholes, kept, gather_sems)
    pair = Pair(mine, theirs, pair_sems)
    count = dims[0] * dims[1] * dims[2]
    greet_line(count, [pair.other])
    asking = Fan(
        count, (look_send.at[0], look_recv.at[0]), lambda me, to: (requests.at[to], got.at[me])
    )
    asking.start()
    gather.refill()
    here = lax.axis_index("dp")
    got[here] = requests[here]
    asking.wait()
    reading.wait()
    wanted = flat(got)
    got_out[...] = wanted

    def look(j, found):
        lane = lax.broadcasted_iota(jnp.int32, wanted.shape, 1) + j * 128
        hot = jnp.where(wanted == lane, 1.0, 0.0).astype(jnp.bfloat16)
        rows = pl.ds(pl.multiple_of(j * 128, 128), 128)
        low = table_full[rows, :].astype(jnp.bfloat16)
        table_out[rows, :] = low
        return found + mm(hot, low)

    found = jnp.zeros((wanted.shape[0], table.shape[1]), jnp.float32)
    found = lax.fori_loop(0, table.shape[0] // 128, look, found)
    replies[...] = found.reshape(replies.shape)
    answering = Fan(
        count, (look_send.at[1], look_recv.at[1]), lambda me, to: (replies.at[to], answers.at[me])
    )
    answering.start()
    answers[here] = replies[here]
    gather.spend(7.0)
    answering.wait()
    look_mine[...] = mm(place_mat[...], flat(answers).astype(jnp.bfloat16)).astype(jnp.bfloat16)
    swap = send(look_mine, look_theirs, look_pair.at[0], look_pair.at[1], pair.other)
    attn, outs, ups, downs, proj, _, norms = wholes
    saving = {}

    def save(layer, name):
        slot = layer * len(SAVED) + SAVED.index(name)
        copy = pltpu.make_async_copy(act[name], saved[layer][name], save_sem.at[slot])
        copy.start()
        saving[name] = copy

    def free(name):
        if name in saving:
            saving.pop(name).wait()

    x[:WORDS] = words[...].astype(jnp.float32)
    gather.need(needs["norms"])
    width = D // (dims[0] * dims[1] * dims[2])
    gains[...] = jnp.zeros_like(gains)
    for d in range(count):
        z, rest = d // (dims[1] * dims[2]), d % (dims[1] * dims[2])
        pick = lax.broadcasted_iota(jnp.int32, (128, D), 0) + d * width
        lane = lax.broadcasted_iota(jnp.int32, (128, D), 1)
        inside = lax.broadcasted_iota(jnp.int32, (128, D), 0) < width
        hot = jnp.where((pick == lane) & inside, 1.0, 0.0).astype(jnp.bfloat16)
        gains[...] += mm(norms[0, z, rest // dims[2], rest % dims[2]], hot)
    gather.need(needs["proj"])
    swap.wait()
    both = look_mine[...].astype(jnp.float32) + look_theirs[...].astype(jnp.float32)
    rows_in[...] = both.astype(jnp.bfloat16)
    x[WORDS:] = base[...].astype(jnp.float32) + mm(rows_in[...], flat(proj, 0))

    for layer in range(LAYERS):
        gain = [gains[4 * layer + i : 4 * layer + i + 1, :] for i in range(4)]
        free("xb")

        def cast(i, carry):
            rows = pl.ds(i * BLOCK, BLOCK)
            act["xb"][rows, :] = x[rows, :].astype(jnp.bfloat16)
            return carry

        lax.fori_loop(0, BLOCKS, cast, 0)
        save(layer, "xb")
        for name, word_mat, ent_mat in (("k", 4, None), ("v", 5, None), ("qw", 0, 2), ("qe", 1, 3)):
            free(name)
            gather.need(needs["mat", layer, word_mat if ent_mat is None else ent_mat])
            if ent_mat is None:
                project_rows(act[name], act["xb"], 0, LEN, 512, attn, 6 * layer + word_mat)
            else:
                project_rows(act[name], act["xb"], 0, WORDS, 448, attn, 6 * layer + word_mat)
                project_rows(act[name], act["xb"], WORDS, ENT_LEN, ENT_LEN, attn, 6 * layer + ent_mat)
            save(layer, name)
            gather.spend(2.5)
        free("o")
        free("stats")
        for head_pair in range(act["o"].shape[1] // (2 * HEAD_DIM)):
            attend(act, head_pair)
            gather.spend(4.3)
        save(layer, "o")
        gather.need(needs["out", layer])
        for name in ("n1", "h1b"):
            free(name)

        def out_part(c, rows):
            return mm_rt(act["o"][rows, :], flat(outs, layer))

        def first_norm(c, rows, total):
            hat, scale = normed(x[rows, :] + total)
            act["n1"][rows, :] = hat.astype(jnp.bfloat16)
            act["stats"][rows, 8:9] = scale
            value = hat * gain[0] + gain[1]
            h1[rows, :] = value
            act["h1b"][rows, :] = value.astype(jnp.bfloat16)

        pair.run(out_part, first_norm, lambda: gather.spend(1.3))
        save(layer, "n1")
        save(layer, "h1b")
        gather.need(needs["up", layer, 1])
        for name in ("g", "slope", "n2"):
            free(name)
        hidden = act["g"].shape[1]
        tile = 512

        def up_block(c):
            rows = pl.ds(c * BLOCK, BLOCK)
            for first in range(0, hidden, tile):
                cols = slice(first, first + tile)
                weight = ups[layer, :, :, :, :, cols].reshape(D, tile)
                value, slope = gelu_parts(mm(act["h1b"][rows, :], weight))
                act["g"][rows, cols] = value.astype(jnp.bfloat16)
                act["slope"][rows, cols] = slope.astype(jnp.bfloat16)

        for c in range(BLOCKS):
            up_block(c)
            gather.spend(2.6)
        save(layer, "g")
        save(layer, "slope")
        gather.need(needs["down", layer, 1])

        def down_part(c, rows):
            return mm_rt(act["g"][rows, :], flat(downs, layer))

        def second_norm(c, rows, total):
            hat, scale = normed(h1[rows, :] + total)
            act["n2"][rows, :] = hat.astype(jnp.bfloat16)
            act["stats"][rows, 9:10] = scale
            x[rows, :] = hat * gain[2] + gain[3]

        pair.run(down_part, second_norm, lambda: gather.spend(1.8))
        save(layer, "n2")
        save(layer, "stats")
    ents_out[...] = x[WORDS:]
    gains_out[...] = gains[...]
    gather.close()
    for name in list(saving):
        free(name)


KINDS = ("attn", "out", "up", "down", "proj", "head", "norms")


MAT_ORDER = (4, 5, 0, 2, 1, 3)


def gather_plan(dims, shards):
    every = slice(None)
    chunks, needs, sizes = [], {"kinds": KINDS}, []
    hidden = shards[2].shape[-1]

    def add(name, which, row, cols=every, part=1):
        chunks.append((which, pl.ds(row, 1), cols))
        sizes.append(2 * shards[which].shape[1] * shards[which].shape[2] // part)
        needs[name] = len(chunks) - 1

    add("norms", 6, 0)
    add("proj", 4, 0)
    for layer in range(LAYERS):
        for mat in MAT_ORDER:
            add(("mat", layer, mat), 0, 6 * layer + mat)
        add(("out", layer), 1, layer)
        if layer == LAYERS - 1:
            add("head", 5, 0)
        for which, name in ((2, "up"), (3, "down")):
            for part in range(2):
                cols = pl.ds(part * (hidden // 2), hidden // 2)
                add((name, layer, part), which, layer, cols, 2)
    orders = balanced_orders(dims, sizes)
    return [chunk + (order,) for chunk, order in zip(chunks, orders)], needs


def run_forward(dims, words, base, requests, place_mat, table, shards, collective_id):
    half, hidden = shards[0].shape[-1], shards[2].shape[-1]
    chunks, needs = gather_plan(dims, shards)
    shapes = saved_shapes(half, hidden)
    low, full = jnp.bfloat16, jnp.float32
    width, slots = table.shape[1], requests.shape[0] * requests.shape[1]
    wholes = [(s.shape[0], *dims, *s.shape[1:]) for s in shards]
    copies = sum(dims)
    saved_out = [jax.ShapeDtypeStruct(*shapes[name]) for _ in range(LAYERS) for name in SAVED]
    result = pl.pallas_call(
        functools.partial(forward_body, dims, chunks, needs),
        out_shape=[jax.ShapeDtypeStruct(shape, low) for shape in wholes]
        + saved_out
        + [
            jax.ShapeDtypeStruct((ENT_LEN, D), full),
            jax.ShapeDtypeStruct((16, D), full),
            jax.ShapeDtypeStruct((ENT_LEN, width), low),
            jax.ShapeDtypeStruct((slots, 128), jnp.int32),
            jax.ShapeDtypeStruct(table.shape, low),
        ],
        in_specs=[VMEM] * 4 + [ANY] * (1 + len(shards)),
        out_specs=[ANY] * (len(wholes) + len(saved_out)) + [VMEM] * 5,
        scratch_shapes=[pltpu.VMEM(shape, low) for shape in wholes]
        + [pltpu.VMEM(*shapes[name]) for name in SAVED]
        + [
            pltpu.VMEM((LEN, D), full),
            pltpu.VMEM((LEN, D), full),
            pltpu.VMEM((16, D), full),
            pltpu.VMEM((BLOCKS, BLOCK, D), low),
            pltpu.VMEM((2, BLOCKS, BLOCK, D), low),
            pltpu.SemaphoreType.DMA((len(chunks), copies)),
            pltpu.SemaphoreType.DMA((len(chunks), copies)),
            pltpu.SemaphoreType.DMA((len(chunks),)),
            pltpu.SemaphoreType.DMA((len(chunks),)),
            pltpu.SemaphoreType.DMA((2 * LAYERS, BLOCKS)),
            pltpu.SemaphoreType.DMA((2 * LAYERS, BLOCKS)),
            pltpu.SemaphoreType.DMA((LAYERS * len(SAVED),)),
            pltpu.VMEM(requests.shape, jnp.int32),
            pltpu.VMEM((*requests.shape[:2], width), full),
            pltpu.VMEM((*requests.shape[:2], width), full),
            pltpu.VMEM((ENT_LEN, width), low),
            pltpu.VMEM((ENT_LEN, width), low),
            pltpu.SemaphoreType.DMA((2, requests.shape[0])),
            pltpu.SemaphoreType.DMA((2, requests.shape[0])),
            pltpu.SemaphoreType.DMA((2,)),
            pltpu.VMEM(table.shape, full),
            pltpu.SemaphoreType.DMA,
        ],
        compiler_params=pltpu.CompilerParams(
            collective_id=collective_id, has_side_effects=True, vmem_limit_bytes=VMEM_BYTES
        ),
    )(words, base, requests, place_mat, table, *shards)
    kept = result[: len(wholes)]
    saved = [
        dict(zip(SAVED, result[len(wholes) + layer * len(SAVED) :][: len(SAVED)]))
        for layer in range(LAYERS)
    ]
    return kept, saved, *result[-5:]


class Fan:
    def __init__(self, count, sems, copy_args):
        self.count, self.sems, self.copy_args = count, sems, copy_args
        self.index = lax.axis_index("dp")

    def copy(self, step):
        other = lax.rem(self.index + step, self.count)
        src, dst = self.copy_args(self.index, other)
        send_sem, recv_sem = self.sems
        return pltpu.make_async_remote_copy(
            src_ref=src,
            dst_ref=dst,
            send_sem=send_sem.at[step],
            recv_sem=recv_sem.at[step],
            device_id=(other, lax.axis_index("mp")),
            device_id_type=MESH,
        )

    def start(self):
        def go(step, carry):
            self.copy(step).start()
            return carry

        lax.fori_loop(1, self.count, go, 0)

    def wait(self):
        def done(step, carry):
            self.copy(step).wait()
            return carry

        lax.fori_loop(1, self.count, done, 0)


def greet_line(count, extra):
    barrier = pltpu.get_barrier_semaphore()
    index, core = lax.axis_index("dp"), lax.axis_index("mp")

    def hello(step, carry):
        other = lax.rem(index + step, count)
        pl.semaphore_signal(barrier, inc=1, device_id=(other, core), device_id_type=MESH)
        return carry

    lax.fori_loop(1, count, hello, 0)
    for target in extra:
        pl.semaphore_signal(barrier, inc=1, device_id=target, device_id_type=MESH)
    pl.semaphore_wait(barrier, count - 1 + len(extra))


TABLE_CUTS = 8


def head_body(count, *refs):
    ents, hits, head, table, local_targets = refs[:5]
    losses, grad_logits, states, grad_head, grad_ents = refs[5:10]
    logits, own_states, all_states, stat_mine, stat_theirs, stat_both, stat_all = refs[10:17]
    grad_part, hit_part, grad_send, grad_all, share_mine, share_theirs = refs[17:23]
    factors, turned_factors, send_sem, recv_sem, pair_send, pair_recv = refs[23:]
    index = lax.axis_index("dp")
    other = (index, 1 - lax.axis_index("mp"))
    greet_line(count, [other])
    total_rows = count * MASK_ENT
    span = table.shape[0] // TABLE_CUTS

    masked = mm(hits[...], ents[...].astype(jnp.bfloat16)).astype(jnp.bfloat16)
    head_low = flat(head)
    value, slope = gelu_parts(mm(masked, head_low))
    own_states[...] = value.astype(jnp.bfloat16)
    fan = Fan(count, (send_sem.at[0], recv_sem.at[0]), lambda me, to: (own_states, all_states.at[me]))
    fan.start()
    all_states[index] = own_states[...]
    fan.wait()
    states[...] = flat(all_states)
    target = local_targets[0:1, :]

    def hit_of(c):
        row = lax.broadcasted_iota(jnp.int32, (span, total_rows), 0) + c * span
        return row == target

    def rows_of(c):
        return pl.ds(pl.multiple_of(c * span, 16), span)

    def score(c, carry):
        peak, picked = carry
        part = mm_rt(table[rows_of(c), :], states[...])
        logits[rows_of(c), :] = part
        peak = jnp.maximum(peak, jnp.max(part, axis=0, keepdims=True))
        picked += jnp.sum(jnp.where(hit_of(c), part, 0.0), axis=0, keepdims=True)
        return peak, picked

    empty = jnp.zeros((1, total_rows), jnp.float32)
    peak, picked = lax.fori_loop(0, TABLE_CUTS, score, (empty - 3e38, empty))

    grad_part[...] = jnp.zeros_like(grad_part)
    hit_part[...] = jnp.zeros_like(hit_part)

    def weigh(c, weight):
        raised = jnp.exp(logits[rows_of(c), :] - peak)
        hot = jnp.where(hit_of(c), 1.0, 0.0).astype(jnp.bfloat16)
        grad_part[...] += mm_lt(raised.astype(jnp.bfloat16), table[rows_of(c), :])
        hit_part[...] += mm_lt(hot, table[rows_of(c), :])
        return weight + jnp.sum(raised, axis=0, keepdims=True)

    weight = lax.fori_loop(0, TABLE_CUTS, weigh, empty)
    stat_mine[0:1, :] = peak
    stat_mine[1:2, :] = weight
    stat_mine[2:3, :] = picked
    block = (count, MASK_ENT, table.shape[1])
    grad_send[:, :MASK_ENT, :] = grad_part[...].astype(jnp.bfloat16).reshape(block)
    grad_send[:, MASK_ENT:, :] = hit_part[...].astype(jnp.bfloat16).reshape(block)
    fan = Fan(count, (send_sem.at[1], recv_sem.at[1]), lambda me, to: (stat_mine, stat_all.at[me]))
    fan.start()
    back = Fan(
        count, (send_sem.at[2], recv_sem.at[2]), lambda me, to: (grad_send.at[to], grad_all.at[me])
    )
    back.start()
    stat_all[index] = stat_mine[...]
    grad_all[index] = grad_send[index]
    fan.wait()
    peak_line = stat_all[0, 0:1, :]
    for d in range(1, count):
        peak_line = jnp.maximum(peak_line, stat_all[d, 0:1, :])
    weight_line = picked_line = empty
    for d in range(count):
        weight_line += stat_all[d, 1:2, :] * jnp.exp(stat_all[d, 0:1, :] - peak_line)
        picked_line += stat_all[d, 2:3, :]
    stat_both[0:1, :] = peak_line
    stat_both[1:2, :] = weight_line
    stat_both[2:3, :] = picked_line
    swap = send(stat_both, stat_theirs, pair_send.at[0], pair_recv.at[0], other)
    swap.wait()
    peak_all = jnp.maximum(peak_line, stat_theirs[0:1, :])
    weight_all = weight_line * jnp.exp(peak_line - peak_all) + stat_theirs[1:2, :] * jnp.exp(
        stat_theirs[0:1, :] - peak_all
    )
    log_norm = peak_all + jnp.log(weight_all)
    losses[...] = jnp.broadcast_to(log_norm - picked_line - stat_theirs[2:3, :], losses.shape)
    factors[...] = jnp.zeros_like(factors)
    for d in range(count):
        factors[d : d + 1, :] = jnp.exp(stat_all[d, 0:1, :] - log_norm)
    turned_factors[...] = factors[...].T
    own = turned_factors[pl.ds(pl.multiple_of(index * MASK_ENT, MASK_ENT), MASK_ENT), :]
    back.wait()
    share = jnp.zeros((MASK_ENT, table.shape[1]), jnp.float32)
    for d in range(count):
        share += grad_all[d, :MASK_ENT, :].astype(jnp.float32) * own[:, d : d + 1]
        share -= grad_all[d, MASK_ENT:, :].astype(jnp.float32)
    share_mine[...] = share * (1.0 / total_rows)
    swap = send(share_mine, share_theirs, pair_send.at[1], pair_recv.at[1], other)

    def grads(c, carry):
        prob = jnp.exp(logits[rows_of(c), :] - log_norm)
        part = (prob - jnp.where(hit_of(c), 1.0, 0.0)) * (1.0 / total_rows)
        grad_logits[rows_of(c), :] = part.astype(jnp.bfloat16)
        return carry

    lax.fori_loop(0, TABLE_CUTS, grads, 0)
    swap.wait()
    grad_pre = ((share_mine[...] + share_theirs[...]) * slope).astype(jnp.bfloat16)
    grad_head[...] = mm_lt(masked, grad_pre).astype(jnp.bfloat16).reshape(grad_head.shape)
    grad_masked = mm_rt(grad_pre, head_low)
    grad_ents[...] = lax.dot_general(
        hits[...].astype(jnp.float32),
        grad_masked,
        (((0,), (0,)), ((), ())),
        precision=lax.Precision.HIGHEST,
        preferred_element_type=jnp.float32,
    )


def run_head(dims, ents, hits, head, table_low, local_targets, collective_id):
    count = dims[0] * dims[1] * dims[2]
    width = table_low.shape[1]
    rows = count * MASK_ENT
    low, full = jnp.bfloat16, jnp.float32
    return pl.pallas_call(
        functools.partial(head_body, count),
        out_shape=[
            jax.ShapeDtypeStruct((8, rows), full),
            jax.ShapeDtypeStruct((table_low.shape[0], rows), low),
            jax.ShapeDtypeStruct((rows, width), low),
            jax.ShapeDtypeStruct(head.shape, low),
            jax.ShapeDtypeStruct((ENT_LEN, D), full),
        ],
        in_specs=[VMEM] * 5,
        out_specs=[VMEM] * 5,
        scratch_shapes=[
            pltpu.VMEM((table_low.shape[0], rows), full),
            pltpu.VMEM((MASK_ENT, width), low),
            pltpu.VMEM((count, MASK_ENT, width), low),
            pltpu.VMEM((8, rows), full),
            pltpu.VMEM((8, rows), full),
            pltpu.VMEM((8, rows), full),
            pltpu.VMEM((count, 8, rows), full),
            pltpu.VMEM((rows, width), full),
            pltpu.VMEM((rows, width), full),
            pltpu.VMEM((count, 2 * MASK_ENT, width), low),
            pltpu.VMEM((count, 2 * MASK_ENT, width), low),
            pltpu.VMEM((MASK_ENT, width), full),
            pltpu.VMEM((MASK_ENT, width), full),
            pltpu.VMEM((128, rows), full),
            pltpu.VMEM((rows, 128), full),
            pltpu.SemaphoreType.DMA((3, count)),
            pltpu.SemaphoreType.DMA((3, count)),
            pltpu.SemaphoreType.DMA((2,)),
            pltpu.SemaphoreType.DMA((2,)),
        ],
        compiler_params=pltpu.CompilerParams(
            collective_id=collective_id, has_side_effects=True, vmem_limit_bytes=VMEM_BYTES
        ),
    )(ents, hits, head, table_low, local_targets)


def update_body(names, width, *refs):
    refs = list(refs)

    def take(count):
        part = refs[:count]
        del refs[:count]
        return part

    kinds = len(kind_rates)
    state_in = [take(3) for _ in range(kinds)]
    totals_in = take(len(names))
    incoming, requests, grad_logits, states = take(4)
    state_out = [take(3) for _ in range(kinds)]
    held = [take(3) for _ in range(kinds)]
    totals_held = take(len(names))
    in_sem, total_sem, out_sem = take(3)
    table = kinds - 1
    height = held[table][0].shape[0] // TABLE_CUTS

    def piece(ref, c):
        return ref if c is None else ref.at[pl.ds(c * height, height)]

    def copies(kind, c, inward):
        base = 3 * (kind + (0 if c is None else c))
        pairs = []
        for i in range(3):
            if inward:
                src, dst, sem = state_in[kind][i], held[kind][i], in_sem.at[base + i]
            else:
                src, dst, sem = held[kind][i], state_out[kind][i], out_sem.at[base + i]
            pairs.append(pltpu.make_async_copy(piece(src, c), piece(dst, c), sem))
        return pairs

    leaving = []
    total_copies = [
        pltpu.make_async_copy(src, dst, total_sem.at[i])
        for i, (src, dst) in enumerate(zip(totals_in, totals_held))
    ]
    for c in range(2):
        for copy in copies(table, c, True):
            copy.start()
    for copy in total_copies:
        copy.start()
    for kind in range(table):
        for copy in copies(kind, None, True):
            copy.start()
    for c in range(2, TABLE_CUTS):
        for copy in copies(table, c, True):
            copy.start()
    total_of = dict(zip(names, totals_held))

    def update(kind, at, gradient):
        master, first, second = held[kind]
        first_new = beta_first * first[at] + (1.0 - beta_first) * gradient
        second_new = beta_second * second[at] + (1.0 - beta_second) * gradient * gradient
        first_hat = first_new * (1.0 / (1.0 - beta_first**STEP))
        second_hat = second_new * (1.0 / (1.0 - beta_second**STEP))
        value = master[at]
        value -= kind_rates[kind] * (
            first_hat / (jnp.sqrt(second_hat) + adam_eps) + weight_decay * value
        )
        master[at], first[at], second[at] = value, first_new, second_new

    def finish(kind, c=None):
        for copy in copies(kind, c, False):
            copy.start()
            leaving.append(copy)

    def table_part(c):
        for copy in copies(table, c, True):
            copy.wait()
        rows = slice(c * height, (c + 1) * height)
        gradient = mm(grad_logits[rows, :], states[...])
        row = lax.broadcasted_iota(jnp.int32, (height, requests.shape[1]), 0) + c * height
        hot = jnp.where(row == requests[0:1, :], 1.0, 0.0).astype(jnp.bfloat16)
        gradient += mm(hot, incoming[...].astype(jnp.bfloat16))
        update(table, (rows, slice(None)), gradient)
        finish(table, c)

    table_part(0)
    table_part(1)
    for copy in total_copies:
        copy.wait()
    for kind in range(table):
        for copy in copies(kind, None, True):
            copy.wait()
        for layer in range(LAYERS):
            if kind == 0:
                blocks = []
                for name in ("words", "ents"):
                    total = total_of[layer, name]
                    half = total.shape[1] // 2
                    blocks += [total[:, :half], total[:, half:]]
                blocks += [total_of[layer, "key"][...], total_of[layer, "value"][...]]
                for mat, block in enumerate(blocks):
                    update(kind, (layer, mat), block)
            elif kind == 1:
                update(kind, (layer,), total_of[layer, "out"][...])
            elif kind in (2, 3):
                for i in range(2):
                    total = total_of[layer, ("up%d", "down%d")[kind - 2] % i]
                    half = total.shape[1]
                    cols = slice(i * half, (i + 1) * half)
                    update(kind, (layer, slice(None), cols), total[...])
            elif kind == 4:
                update(kind, (layer,), total_of["norms"][4 * layer : 4 * layer + 4, :width])
        if kind == 5:
            update(kind, (slice(None),), total_of["proj"][...])
        if kind == 6:
            update(kind, (slice(None),), total_of["head"][...])
        finish(kind)
    for c in range(2, TABLE_CUTS):
        table_part(c)
    for copy in leaving:
        copy.wait()


def run_update(states_of, totals, incoming, requests, grad_logits, states):
    names = list(totals)
    full = jnp.float32
    flat_states = [array for group in states_of for array in group]
    width = states_of[4][0].shape[-1]
    kinds = len(kind_rates)
    result = pl.pallas_call(
        functools.partial(update_body, names, width),
        out_shape=[jax.ShapeDtypeStruct(a.shape, full) for a in flat_states],
        in_specs=[ANY] * (len(flat_states) + len(names)) + [VMEM] * 4,
        out_specs=[ANY] * len(flat_states),
        scratch_shapes=[pltpu.VMEM(a.shape, full) for a in flat_states]
        + [pltpu.VMEM(totals[name].shape, full) for name in names]
        + [
            pltpu.SemaphoreType.DMA((3 * (kinds + TABLE_CUTS),)),
            pltpu.SemaphoreType.DMA((len(names),)),
            pltpu.SemaphoreType.DMA((3 * (kinds + TABLE_CUTS),)),
        ],
        compiler_params=pltpu.CompilerParams(vmem_limit_bytes=VMEM_BYTES),
    )(*flat_states, *totals.values(), incoming, requests, grad_logits, states)
    return [result[3 * i : 3 * i + 3] for i in range(kinds)]


def norm_back(grad, hat, scale, gain_row):
    hat = hat.astype(jnp.float32)
    wide = grad * gain_row
    inner = jnp.mean(wide * hat, axis=-1, keepdims=True)
    back = scale * (wide - jnp.mean(wide, axis=-1, keepdims=True) - hat * inner)
    gain_part = jnp.sum(grad * hat, axis=0, keepdims=True)
    return back, gain_part, jnp.sum(grad, axis=0, keepdims=True)


class Sums(Links):
    def __init__(self, dims, units, buffers, totals, sems, free_sem):
        super().__init__(dims, SUM_RATE)
        self.units, self.totals, self.buffers = units, totals, buffers
        self.send_sem, self.recv_sem = sems
        self.free_sem = free_sem
        self.spot = place(dims)
        self.peers = [axis_peers(dims, axis) for axis in range(3)]
        self.copies, self.done = {}, set()

    def start(self, stage, u):
        slot, order, turn = self.units[u]
        part, arrived = self.buffers[slot][0], self.buffers[slot][1 + stage]
        axis = order[stage]
        group = self.peers[axis]
        if turn and group:
            pl.semaphore_wait(self.free_sem.at[slot, stage], len(group))
        copies, base = [], sum(self.dims[order[i]] for i in range(stage))
        for k, (spot, target) in enumerate(group):
            at = [slice(None)] * 3
            for d in order[:stage]:
                at[d] = self.spot[d]
            at[axis] = spot
            sems = self.send_sem.at[u, base + k], self.recv_sem.at[u, base + k]
            copies.append(send(part.at[tuple(at)], arrived.at[k], *sems, target))
        self.copies[stage, u] = copies
        held = 1
        for d in order[stage + 1 :]:
            held *= self.dims[d]
        self.issue(axis, held * 2 * part.shape[3] * part.shape[4], (stage, u))

    def complete(self, what):
        stage, u = what
        slot, order, turn = self.units[u]
        part, arrived = self.buffers[slot][0], self.buffers[slot][1 + stage]
        for copy in self.copies.pop(what):
            copy.wait()
        axis = order[stage]
        group = self.peers[axis]
        rest = [d for d in range(3) if d not in order[: stage + 1]]

        def total_at(spots):
            at = tuple(spots.get(d, self.spot[d]) for d in range(3))
            value = part[at].astype(jnp.float32)
            for k in range(len(group)):
                value += arrived[(k, *[spots[d] for d in rest])].astype(jnp.float32)
            return at, value

        if stage == 2:
            self.totals[u][...] = total_at({})[1]
            self.done.add(u)
        elif group:
            inner = self.dims[rest[-1]]

            def add(i, carry):
                spots = {rest[-1]: i % inner}
                if len(rest) == 2:
                    spots[rest[0]] = i // inner
                at, value = total_at(spots)
                part[at] = value.astype(part.dtype)
                return carry

            count = inner * (self.dims[rest[0]] if len(rest) == 2 else 1)
            lax.fori_loop(0, count, add, 0)
        if self.reused(u):
            for _, target in group:
                pl.semaphore_signal(
                    self.free_sem.at[slot, stage], inc=1, device_id=target, device_id_type=MESH
                )
        if stage < 2:
            self.start(stage + 1, u)

    def reused(self, u):
        slot, _, turn = self.units[u]
        return not turn and sum(unit[0] == slot for unit in self.units) > 1

    def need(self, u):
        while u not in self.done:
            self.finish_first()

    def close(self):
        while self.active:
            self.finish_first()


UNITS = ("down0", "down1", "up0", "up1", "out", "words", "ents", "key", "value")
EXTRA = ("head", "proj", "norms")


def unit_orders(dims, blocks):
    names = list(blocks)
    sizes = [2 * rows * cols for rows, cols in blocks.values()]
    return {name: order[::-1] for name, order in zip(names, balanced_orders(dims, sizes))}


def sum_plan():
    names = ["head"]
    for layer in reversed(range(LAYERS)):
        names += [(layer, name) for name in UNITS]
    names += ["proj", "norms"]
    return names


def unit_width(name, half, hidden):
    return {
        "down0": hidden // 2, "down1": hidden // 2, "up0": hidden // 2, "up1": hidden // 2,
        "out": half, "words": 2 * half, "ents": 2 * half, "key": half, "value": half,
    }[name]


def backward_body(dims, names, orders, half, hidden, *refs):
    refs = list(refs)

    def take(count):
        part = refs[:count]
        del refs[:count]
        return part

    cotangent, grad_ents, grad_head, gains, entity_rows, place_mat = take(6)
    w_attn, w_out, w_up, w_down, w_proj = take(5)
    saved = [dict(zip(SAVED, take(len(SAVED)))) for _ in range(LAYERS)]
    word_grads, incoming = take(2)
    totals = take(len(names))
    slots = list(UNITS + EXTRA)
    buffers = [take(4) for _ in slots]
    left, right, hat, xh, o, stats, stats_t = take(7)
    mat_wide, mat_out, mat_attn, mat_proj = take(4)
    gacc, glow, gmix, delta, dk_acc, dv_acc, gnorm = take(7)
    mine, theirs = take(2)
    sum_sems = take(2)
    (free_sem,) = take(1)
    pair_sems = take(2)
    (load_sem,) = take(1)
    out_rows, in_rows, row_send, row_recv = take(4)

    units = []
    for name in names:
        kind = name if isinstance(name, str) else name[1]
        turn = not isinstance(name, str) and name[0] < LAYERS - 1
        units.append((slots.index(kind), orders[kind], turn))
    sums = Sums(dims, units, buffers, totals, sum_sems, free_sem)
    pair = Pair(mine, theirs, pair_sems)
    count = dims[0] * dims[1] * dims[2]
    greet_line(count, [pair.other])
    part_of = {slot: buffers[i][0] for i, slot in enumerate(slots)}
    loads, counter = {}, [0]

    def load(key, src, dst):
        copy = pltpu.make_async_copy(src, dst, load_sem.at[counter[0]])
        counter[0] += 1
        copy.start()
        loads.setdefault(key, []).append(copy)

    def ready(key):
        for copy in loads.pop(key, []):
            copy.wait()

    tick = sums.spend

    def begin_layer(layer):
        s = saved[layer]
        load("n2", s["n2"], hat)
        load("stats", s["stats"], stats)
        load("g", s["g"], left)
        load("down", w_down.at[layer], mat_wide)
        load("slope", s["slope"], right)
        load("h1b", s["h1b"], xh)
        load("out", w_out.at[layer], mat_out)
        load("o", s["o"], o)
        load("attn", w_attn.at[pl.ds(6 * layer, 6)], mat_attn)

    begin_layer(LAYERS - 1)
    load("proj", w_proj.at[0], mat_proj)
    slab = 2 if dims[0] % 2 == 0 else 1
    height = slab * D // dims[0]

    def fill(name, lhs, rhs, rhs_cols, row_slice=slice(None)):
        part = part_of[name]
        width = part.shape[-1]

        def block(i, carry):
            cols = pl.ds(pl.multiple_of(i * height, 128), height)
            value = mm_lt(lhs[row_slice, cols], rhs[row_slice, rhs_cols])
            shape = (slab, dims[1], dims[2], part.shape[3], width)
            part[pl.ds(i * slab, slab)] = value.astype(jnp.bfloat16).reshape(shape)
            return carry

        lax.fori_loop(0, dims[0] // slab, block, 0)

    def submit(layer, name):
        sums.start(0, names.index((layer, name)))

    head_part = part_of["head"]
    head_part[...] = grad_head[...]
    sums.start(0, names.index("head"))
    gacc[:WORDS] = cotangent[...].astype(jnp.float32)
    gacc[WORDS:] = grad_ents[...]
    gnorm[...] = jnp.zeros_like(gnorm)

    def add_norm(row, value):
        gnorm[row : row + 1, :] += value

    for layer in reversed(range(LAYERS)):
        last = layer == LAYERS - 1
        gain = [gains[4 * layer + i : 4 * layer + i + 1, :] for i in range(4)]
        ready("n2")
        ready("stats")

        def late_norm(c, carry):
            rows = pl.ds(c * BLOCK, BLOCK)
            back, gain_part, shift_part = norm_back(
                gacc[rows, :], hat[rows, :], stats[rows, 9:10], gain[2]
            )
            gacc[rows, :] = back
            glow[rows, :] = back.astype(jnp.bfloat16)
            add_norm(4 * layer + 2, gain_part)
            add_norm(4 * layer + 3, shift_part)
            return carry

        lax.fori_loop(0, BLOCKS, late_norm, 0)
        tick(3.0)
        load("n1", saved[layer]["n1"], hat)
        ready("g")
        for i in range(2):
            if not last:
                sums.need(names.index((layer + 1, "down%d" % i)))
            cols = slice(i * (hidden // 2), (i + 1) * (hidden // 2))
            fill("down%d" % i, glow, left, cols)
            submit(layer, "down%d" % i)
            tick(2.2)
        ahead = saved[layer]
        for i, name in enumerate(("k", "qw", "qe", "v")):
            load("qkv", ahead[name], left.at[:, pl.ds(i * half, half)])
        ready("down")
        ready("slope")

        def inner(c, carry):
            rows = pl.ds(c * BLOCK, BLOCK)
            for first in range(0, hidden, 512):
                cols = slice(first, first + 512)
                weight = mat_wide[:, :, :, :, cols].reshape(D, 512)
                value = mm(glow[rows, :], weight) * right[rows, cols].astype(jnp.float32)
                right[rows, cols] = value.astype(jnp.bfloat16)
            return carry

        lax.fori_loop(0, BLOCKS, inner, 0)
        tick(3.5)
        load("up", w_up.at[layer], mat_wide)
        ready("h1b")
        for i in range(2):
            if not last:
                sums.need(names.index((layer + 1, "up%d" % i)))
            cols = slice(i * (hidden // 2), (i + 1) * (hidden // 2))
            fill("up%d" % i, xh, right, cols)
            submit(layer, "up%d" % i)
            tick(2.2)
        load("xb", saved[layer]["xb"], xh)
        ready("up")
        ready("n1")

        def up_part(c, rows):
            return mm_rt(right[rows, :], flat(mat_wide))

        def early_norm(c, rows, total):
            back, gain_part, shift_part = norm_back(
                gacc[rows, :] + total, hat[rows, :], stats[rows, 8:9], gain[0]
            )
            gacc[rows, :] = back
            glow[rows, :] = back.astype(jnp.bfloat16)
            add_norm(4 * layer, gain_part)
            add_norm(4 * layer + 1, shift_part)

        pair.run(up_part, early_norm, lambda: tick(2.0))
        ready("o")
        ready("out")
        if not last:
            sums.need(names.index((layer + 1, "out")))
        fill("out", glow, o, slice(None))
        submit(layer, "out")

        def mixed(c, carry):
            rows = pl.ds(c * BLOCK, BLOCK)
            gmix[rows, :] = mm(glow[rows, :], flat(mat_out)).astype(jnp.bfloat16)
            stats_t[:, rows] = stats[rows, :].T
            return carry

        lax.fori_loop(0, BLOCKS, mixed, 0)
        tick(3.7)
        ready("qkv")
        for head_pair in range(half // (2 * HEAD_DIM)):
            lo = head_pair * 2 * HEAD_DIM
            lanes = slice(lo, lo + 2 * HEAD_DIM)
            k_lanes, qw_lanes, qe_lanes, v_lanes = [
                slice(j * half + lo, j * half + lo + 2 * HEAD_DIM) for j in range(4)
            ]

            def products(c, carry):
                rows = pl.ds(c * BLOCK, BLOCK)
                both = gmix[rows, lanes].astype(jnp.float32) * o[rows, lanes].astype(jnp.float32)
                turned = both.T
                delta[0:1, rows] = jnp.sum(turned[:HEAD_DIM], axis=0, keepdims=True)
                delta[1:2, rows] = jnp.sum(turned[HEAD_DIM:], axis=0, keepdims=True)
                return carry

            lax.fori_loop(0, BLOCKS, products, 0)
            dk_acc[...] = jnp.zeros_like(dk_acc)
            dv_acc[...] = jnp.zeros_like(dv_acc)

            def block(i, carry):
                rows = pl.ds(i * BLOCK, BLOCK)
                keys, values = left[:, k_lanes], left[:, v_lanes]
                grad_qw = grad_qe = None
                for which in range(2):
                    head = 2 * head_pair + which
                    q_mask, k_mask = lane_mask(BLOCK, which), lane_mask(LEN, which)
                    query_w = left[rows, qw_lanes] * q_mask
                    query_e = left[rows, qe_lanes] * q_mask
                    grad_o = gmix[rows, lanes] * q_mask
                    log_row = stats_t[head : head + 1, rows]
                    inner_row = delta[which : which + 1, rows]
                    own_keys = keys * k_mask
                    for span, query in ((slice(0, WORDS), query_w), (slice(WORDS, LEN), query_e)):
                        prob = jnp.exp2(mm_rt(keys[span], query) * SCORE_STEP - log_row)
                        grad_prob = mm_rt(values[span], grad_o)
                        dv_acc[span, :] += mm(prob.astype(jnp.bfloat16), grad_o)
                        grad_score = (prob * (grad_prob - inner_row)).astype(jnp.bfloat16)
                        dk_acc[span, :] += mm(grad_score, query)
                        part = mm_lt(grad_score, own_keys[span])
                        if span.start == 0:
                            grad_qw = part if grad_qw is None else grad_qw + part
                        else:
                            grad_qe = part if grad_qe is None else grad_qe + part
                right[rows, lanes] = (grad_qw * 0.125).astype(jnp.bfloat16)
                right[rows, half + lo : half + lo + 2 * HEAD_DIM] = (grad_qe * 0.125).astype(
                    jnp.bfloat16
                )
                return carry

            for first in range(0, BLOCKS, 2):
                lax.fori_loop(first, first + 2, block, 0)
                tick(4.7)
            at = 2 * half + lo
            right[:, at : at + 2 * HEAD_DIM] = (dk_acc[...] * 0.125).astype(jnp.bfloat16)
            at = 3 * half + lo
            right[:, at : at + 2 * HEAD_DIM] = dv_acc[...].astype(jnp.bfloat16)
        ready("xb")
        words, ents = slice(0, WORDS), slice(WORDS, LEN)
        for name, cols, rows in (
            ("words", slice(0, 2 * half), words),
            ("ents", slice(0, 2 * half), ents),
            ("key", slice(2 * half, 3 * half), slice(None)),
            ("value", slice(3 * half, 4 * half), slice(None)),
        ):
            if not last:
                sums.need(names.index((layer + 1, name)))
            fill(name, xh, right, cols, rows)
            submit(layer, name)
            tick(1.4)
        ready("attn")
        mats = [slice(j * half, (j + 1) * half) for j in range(4)]

        def input_part(c, rows):
            total = mm_rt(right[rows, mats[2]], flat(mat_attn, 4))
            total += mm_rt(right[rows, mats[3]], flat(mat_attn, 5))
            start = c * BLOCK
            edge = min(max(WORDS - start, 0), BLOCK)
            pieces = []
            for low, high, pick in ((0, edge, (0, 1)), (edge, BLOCK, (2, 3))):
                if high > low:
                    span = slice(start + low, start + high)
                    piece = mm_rt(right[span, mats[0]], flat(mat_attn, pick[0]))
                    pieces.append(piece + mm_rt(right[span, mats[1]], flat(mat_attn, pick[1])))
            return total + (pieces[0] if len(pieces) == 1 else jnp.concatenate(pieces, axis=0))

        def to_input(c, rows, total):
            gacc[rows, :] += total

        pair.run(input_part, to_input, lambda: tick(2.0))
        if layer:
            begin_layer(layer - 1)
    ready("proj")
    leaving = pltpu.make_async_copy(gacc.at[pl.ds(0, WORDS)], word_grads, load_sem.at[counter[0]])
    leaving.start()
    grad_entity = gacc[WORDS:].astype(jnp.bfloat16)
    row_grads = mm_rt(grad_entity, flat(mat_proj)).astype(jnp.bfloat16)
    out_rows[...] = mm_lt(place_mat[...], row_grads).reshape(out_rows.shape)
    returning = Fan(count, (row_send, row_recv), lambda me, to: (out_rows.at[to], in_rows.at[me]))
    returning.start()
    here = lax.axis_index("dp")
    in_rows[here] = out_rows[here]
    proj_part = part_of["proj"]
    proj_part[...] = mm_lt(entity_rows[...], grad_entity).astype(jnp.bfloat16).reshape(proj_part.shape)
    sums.start(0, names.index("proj"))
    width = D // count
    norm_low = gnorm[...].astype(jnp.bfloat16)
    for d in range(count):
        z, rest = d // (dims[1] * dims[2]), d % (dims[1] * dims[2])
        row = lax.broadcasted_iota(jnp.int32, (128, D), 0)
        lane = lax.broadcasted_iota(jnp.int32, (128, D), 1)
        hot = jnp.where((row + d * width == lane) & (row < width), 1.0, 0.0).astype(jnp.bfloat16)
        block = mm_rt(norm_low, hot).astype(jnp.bfloat16)
        part_of["norms"][z, rest // dims[2], rest % dims[2]] = block
    sums.start(0, names.index("norms"))
    sums.close()
    returning.wait()
    incoming[...] = flat(in_rows)
    leaving.wait()


def run_backward(
    dims, cotangent, grad_ents, grad_head, gains, entity_rows, place_mat, kept, saved, collective_id
):
    names = sum_plan()
    half, hidden = kept[0].shape[-1], kept[2].shape[-1]
    low, full = jnp.bfloat16, jnp.float32
    rows = kept[0].shape[4]
    blocks = {name: (rows, unit_width(name, half, hidden)) for name in UNITS}
    blocks["head"] = (rows, kept[5].shape[-1])
    blocks["proj"] = (kept[4].shape[4], D)
    blocks["norms"] = (16, 128)
    scratch = []
    orders = unit_orders(dims, blocks)
    for name in UNITS + EXTRA:
        order, block = orders[name], blocks[name]
        scratch.append(pltpu.VMEM((*dims, *block), low))
        for stage in range(3):
            rest = [dims[d] for d in range(3) if d not in order[: stage + 1]]
            peers = max(dims[order[stage]] - 1, 1)
            scratch.append(pltpu.VMEM((peers, *rest, *block), low))
    copies = sum(dims)
    kinds = [name if isinstance(name, str) else name[1] for name in names]
    count = dims[0] * dims[1] * dims[2]
    width, slots = kept[5].shape[-1], place_mat.shape[1]
    inputs = [cotangent, grad_ents, grad_head, gains, entity_rows, place_mat, *kept[:5]]
    inputs += [saved[layer][name] for layer in range(LAYERS) for name in SAVED]
    result = pl.pallas_call(
        functools.partial(backward_body, dims, names, orders, half, hidden),
        out_shape=[
            jax.ShapeDtypeStruct((WORDS, D), full),
            jax.ShapeDtypeStruct((slots, width), full),
        ]
        + [jax.ShapeDtypeStruct(blocks[kind], full) for kind in kinds],
        in_specs=[VMEM] * 6 + [ANY] * (len(inputs) - 6),
        out_specs=[ANY] + [VMEM] * (1 + len(names)),
        scratch_shapes=scratch
        + [
            pltpu.VMEM((LEN, hidden), low),
            pltpu.VMEM((LEN, hidden), low),
            pltpu.VMEM((LEN, D), low),
            pltpu.VMEM((LEN, D), low),
            pltpu.VMEM((LEN, half), low),
            pltpu.VMEM((LEN, 128), full),
            pltpu.VMEM((128, LEN), full),
            pltpu.VMEM(kept[2].shape[1:], low),
            pltpu.VMEM(kept[1].shape[1:], low),
            pltpu.VMEM((6, *kept[0].shape[1:]), low),
            pltpu.VMEM(kept[4].shape[1:], low),
            pltpu.VMEM((LEN, D), full),
            pltpu.VMEM((LEN, D), low),
            pltpu.VMEM((LEN, half), low),
            pltpu.VMEM((8, LEN), full),
            pltpu.VMEM((LEN, 2 * HEAD_DIM), full),
            pltpu.VMEM((LEN, 2 * HEAD_DIM), full),
            pltpu.VMEM((16, D), full),
            pltpu.VMEM((BLOCKS, BLOCK, D), low),
            pltpu.VMEM((2, BLOCKS, BLOCK, D), low),
            pltpu.SemaphoreType.DMA((len(names), copies)),
            pltpu.SemaphoreType.DMA((len(names), copies)),
            pltpu.SemaphoreType.REGULAR((len(UNITS + EXTRA), 3)),
            pltpu.SemaphoreType.DMA((2 * LAYERS, BLOCKS)),
            pltpu.SemaphoreType.DMA((2 * LAYERS, BLOCKS)),
            pltpu.SemaphoreType.DMA((64,)),
            pltpu.VMEM((count, slots // count, width), full),
            pltpu.VMEM((count, slots // count, width), full),
            pltpu.SemaphoreType.DMA((count,)),
            pltpu.SemaphoreType.DMA((count,)),
        ],
        compiler_params=pltpu.CompilerParams(
            collective_id=collective_id, has_side_effects=True, vmem_limit_bytes=VMEM_BYTES
        ),
    )(*inputs)
    return result[0], result[1], dict(zip(names, result[2:]))


def padded_rows(values):
    extra = -values.shape[-2] % 16
    return jnp.pad(values, [(0, 0)] * (values.ndim - 2) + [(0, extra), (0, 0)])


def weight_shards(attention_in, attention_out, feed_up, feed_down, norm_params, entity_proj, head_proj):
    def turned(values):
        return jnp.swapaxes(values, 1, 2)

    mats = attention_in.reshape(-1, *attention_in.shape[2:])
    norms = norm_params.reshape(1, -1, norm_params.shape[-1])
    norms = jnp.pad(norms, [(0, 0), (0, 16 - norms.shape[1]), (0, -norms.shape[2] % 128)])
    sources = [mats, turned(attention_out), feed_up, turned(feed_down), entity_proj[None], head_proj[None]]
    heights = [part.shape[1] for part in sources]
    shards = [padded_rows(part.astype(jnp.bfloat16)) for part in sources]
    shards.append(norms.astype(jnp.bfloat16))
    return shards, heights


def unpack_weights(wholes, heights, norm_width):
    kept = []
    for part, height in zip(wholes, heights):
        part = part[..., :height, :]
        kept.append(part.reshape(part.shape[0], -1, part.shape[-1]))
    norm_all = wholes[6][0].reshape(-1, 16, wholes[6].shape[-1])[:, : LAYERS * 4, :norm_width]
    norm_all = jnp.swapaxes(norm_all, 0, 1).reshape(LAYERS, 4, -1)
    return (
        kept[0].reshape(LAYERS, 6, *kept[0].shape[1:]),
        kept[1],
        kept[2],
        kept[3],
        norm_all,
        kept[4][0],
        kept[5][0],
    )


def gather_apart(dims, shards):
    chunks = [(4, 0, 1, True), (5, 0, 1, False), (6, 0, 1, True)]
    for layer in range(LAYERS):
        chunks += [(0, 6 * layer, 3, True), (0, 6 * layer + 3, 3, False)]
        chunks += [(1, layer, 1, layer == 0), (2, layer, 1, True), (3, layer, 1, False)]
    return gather_weights(dims, shards, chunks, 1)


def sum_all(dims, layer_grads, grad_proj, grad_head):
    n_dp = dims[0] * dims[1] * dims[2]

    def blocks(values):
        cut = values.astype(jnp.bfloat16).reshape(*dims, values.shape[0] // n_dp, values.shape[1])
        return padded_rows(cut)

    parts, flags, heights = [], [], []
    for layer in reversed(range(LAYERS)):
        (words_mat, ents_mat, shared_mat), out_mat, up_mat, down_mat, _ = layer_grads[layer]
        late = layer % 2 == 0
        for values, y_first in (
            (up_mat, True),
            (down_mat, False),
            (words_mat, True),
            (ents_mat, False),
            (shared_mat, late),
            (out_mat, not late),
        ):
            parts.append(blocks(values))
            flags.append(y_first)
            heights.append(values.shape[0] // n_dp)
    for values, y_first in ((grad_proj, True), (grad_head, False)):
        parts.append(blocks(values))
        flags.append(y_first)
        heights.append(values.shape[0] // n_dp)
    norms = jnp.concatenate([layer_grads[layer][4] for layer in range(LAYERS)], axis=0)
    width = norms.shape[1] // n_dp
    norms = jnp.swapaxes(norms.reshape(norms.shape[0], n_dp, width), 0, 1)
    norms = jnp.pad(norms, [(0, 0), (0, 16 - norms.shape[1]), (0, -width % 128)])
    parts.append(norms.astype(jnp.bfloat16).reshape(*dims, *norms.shape[1:]))
    flags.append(True)
    totals = sum_gradients(dims, parts, flags, 2)
    norm_sum = totals[-1][: LAYERS * 4, :width].reshape(LAYERS, 4, width)
    totals = [total[:height] for total, height in zip(totals, heights)]
    attn, outs, ups, downs = [], [], [], []
    for layer in range(LAYERS):
        at = 6 * (LAYERS - 1 - layer)
        ups.append(totals[at])
        downs.append(totals[at + 1].T)
        for part in totals[at + 2 : at + 5]:
            half = part.shape[1] // 2
            attn += [part[:, :half], part[:, half:]]
        outs.append(totals[at + 5].T)
    attn = jnp.stack(attn)
    return (
        attn.reshape(LAYERS, 6, *attn.shape[1:]),
        jnp.stack(outs),
        jnp.stack(ups),
        jnp.stack(downs),
        norm_sum,
        totals[-2],
        totals[-1],
    )


def apart_device(
    word_inputs,
    entity_base,
    entity_ids,
    buckets,
    mask_positions,
    targets,
    word_cotangent,
    attention_in,
    attention_in_first,
    attention_in_second,
    attention_out,
    attention_out_first,
    attention_out_second,
    feed_up,
    feed_up_first,
    feed_up_second,
    feed_down,
    feed_down_first,
    feed_down_second,
    norm_params,
    norm_params_first,
    norm_params_second,
    entity_proj,
    entity_proj_first,
    entity_proj_second,
    head_proj,
    head_proj_first,
    head_proj_second,
    entity_table,
    entity_table_first,
    entity_table_second,
):
    dims = chip_grid(lax.axis_size("dp"))
    shards, heights = weight_shards(
        attention_in, attention_out, feed_up, feed_down, norm_params, entity_proj, head_proj
    )
    wholes = gather_apart(dims, shards)
    attn_low, out_low, up_low, down_low, norm_low, proj_low, head_low = unpack_weights(
        wholes, heights, norm_params.shape[-1]
    )
    gain_all = norm_low.astype(jnp.float32)
    slot_total = entity_ids.shape[0]
    shard_rows = entity_table.shape[0]
    bucket_rows = buckets.reshape(buckets.shape[2], buckets.shape[3])
    filled = bucket_rows >= 0
    safe_slot = jnp.maximum(bucket_rows, 0)
    request = jnp.where(filled, entity_ids[safe_slot] % shard_rows, -1)
    received = lax.all_to_all(request, "dp", split_axis=0, concat_axis=0, tiled=True)
    shard_base = lax.axis_index(("dp", "mp")) * shard_rows
    owned_mask = received >= 0
    safe_row = jnp.clip(received, 0, shard_rows - 1)
    table_low = entity_table.astype(jnp.bfloat16)
    replies = jnp.where(owned_mask[:, :, None], table_low[safe_row], jnp.zeros((), jnp.bfloat16))
    replied_rows_result = lax.all_to_all(replies, "dp", split_axis=0, concat_axis=0, tiled=True)
    row_placement_plan = (
        bucket_rows[:, :, None] == jnp.arange(slot_total, dtype=jnp.int32)[None, None, :]
    ).astype(jnp.bfloat16)
    local_shard_rows = jnp.einsum(
        "wvt,wvi->ti", row_placement_plan, replied_rows_result, preferred_element_type=jnp.float32
    )
    paired = pair_sum(local_shard_rows)
    masked_slots = (
        jnp.arange(SEQ_DEV, dtype=jnp.int32)[:, None] * ENT_LEN + mask_positions
    ).reshape(-1)
    keep_weight = 1.0 - jnp.any(
        jnp.arange(slot_total, dtype=jnp.int32)[:, None] == masked_slots[None, :], axis=1
    ).astype(jnp.float32)
    entity_rows = (paired * keep_weight[:, None]).astype(jnp.bfloat16)
    entity_inputs = entity_base.astype(jnp.float32) + jnp.dot(
        entity_rows, proj_low, preferred_element_type=jnp.float32
    )
    hidden = jnp.concatenate(
        [
            word_inputs.astype(jnp.float32).reshape(SEQ_DEV, WORDS, D),
            entity_inputs.reshape(SEQ_DEV, ENT_LEN, D),
        ],
        axis=1,
    )
    saved_layers = []
    for layer_index in range(LAYERS):
        hidden, saved_acts = layer_forward(
            hidden,
            attn_low[layer_index],
            out_low[layer_index],
            up_low[layer_index],
            down_low[layer_index],
            gain_all[layer_index],
        )
        saved_layers.append(saved_acts)
    seq_index = jnp.arange(SEQ_DEV, dtype=jnp.int32)[:, None]
    masked_rows = WORDS + mask_positions
    masked_low = hidden[seq_index, masked_rows].reshape(SEQ_DEV * MASK_ENT, D).astype(jnp.bfloat16)
    head_pre = jnp.dot(masked_low, head_low, preferred_element_type=jnp.float32)
    states_low = gelu_exact(head_pre).astype(jnp.bfloat16)
    all_states = spread(states_low, False, False, 3).reshape(-1, states_low.shape[1])
    logits = lax.dot_general(
        all_states, table_low, (((1,), (1,)), ((), ())), preferred_element_type=jnp.float32
    )
    flat_targets = targets.reshape(-1)
    target_hits = (
        jnp.arange(shard_rows, dtype=jnp.int32)[None, :] == (flat_targets - shard_base)[:, None]
    )
    peak_value = jnp.max(logits, axis=1)
    exp_total = jnp.sum(jnp.exp(logits - peak_value[:, None]), axis=1)
    picked = jnp.sum(jnp.where(target_hits, logits, 0.0), axis=1)
    shares = spread(jnp.stack([peak_value, exp_total, picked]), True, False, 4)
    peak_all = jnp.max(shares[:, 0], axis=0)
    total_all = jnp.sum(shares[:, 1] * jnp.exp(shares[:, 0] - peak_all), axis=0)
    picked_all = jnp.sum(shares[:, 2], axis=0)
    log_norm = peak_all + jnp.log(total_all)
    row_losses = log_norm - picked_all
    prob_rows = jnp.exp(logits - log_norm[:, None])
    grad_logits = ((prob_rows - target_hits.astype(jnp.float32)) / flat_targets.shape[0]).astype(
        jnp.bfloat16
    )
    grad_table = lax.dot_general(
        grad_logits, all_states, (((0,), (0,)), ((), ())), preferred_element_type=jnp.float32
    )
    grad_states = jnp.dot(grad_logits, table_low, preferred_element_type=jnp.float32)
    grad_states = grad_states.reshape(lax.axis_size("dp"), -1, grad_states.shape[1])
    grad_states = jnp.sum(spread(grad_states, False, True, 5), axis=0)
    grad_states = grad_states + lax.ppermute(grad_states, "mp", [(0, 1), (1, 0)])
    grad_head_pre = jax.vjp(gelu_exact, head_pre)[1](grad_states)[0].astype(jnp.bfloat16)
    grad_head = lax.dot_general(
        masked_low, grad_head_pre, (((0,), (0,)), ((), ())), preferred_element_type=jnp.float32
    )
    grad_masked = lax.dot_general(
        grad_head_pre, head_low, (((1,), (1,)), ((), ())), preferred_element_type=jnp.float32
    )
    grad_hidden = jnp.concatenate(
        [
            word_cotangent.astype(jnp.float32).reshape(SEQ_DEV, WORDS, D),
            jnp.zeros((SEQ_DEV, ENT_LEN, D), jnp.float32),
        ],
        axis=1,
    )
    grad_hidden = grad_hidden.at[seq_index, masked_rows].add(
        grad_masked.reshape(SEQ_DEV, MASK_ENT, D)
    )
    kept_grads = []
    for layer_index in reversed(range(LAYERS)):
        grad_hidden, layer_grads = layer_backward(
            grad_hidden,
            saved_layers[layer_index],
            attn_low[layer_index],
            out_low[layer_index],
            up_low[layer_index],
            down_low[layer_index],
            gain_all[layer_index],
        )
        if layer_index == 0:
            word_grads = grad_hidden[:, :WORDS].reshape(SEQ_DEV * WORDS, D)
            grad_entity = grad_hidden[:, WORDS:].reshape(slot_total, D).astype(jnp.bfloat16)
            grad_proj = lax.dot_general(
                entity_rows,
                grad_entity,
                (((0,), (0,)), ((), ())),
                preferred_element_type=jnp.float32,
            )
            row_gradient_block = (
                lax.dot_general(
                    grad_entity,
                    proj_low,
                    (((1,), (1,)), ((), ())),
                    preferred_element_type=jnp.float32,
                )
                * keep_weight[:, None]
            )
            outgoing = jnp.where(filled[:, :, None], row_gradient_block[safe_slot], 0.0)
            incoming = lax.all_to_all(
                outgoing.astype(jnp.bfloat16), "dp", split_axis=0, concat_axis=0, tiled=True
            ).astype(outgoing.dtype)
            grad_table = grad_table.at[safe_row].add(
                jnp.where(owned_mask[:, :, None], incoming, 0.0)
            )
        kept_grads.insert(0, layer_grads)
    reduced = sum_all(dims, kept_grads, grad_proj, grad_head)
    reduced_proj, reduced_head = reduced[5:]
    attn_new = adam_update(
        attention_in, attention_in_first, attention_in_second, reduced[0], kind_rates[0]
    )
    out_new = adam_update(
        attention_out, attention_out_first, attention_out_second, reduced[1], kind_rates[1]
    )
    up_new = adam_update(feed_up, feed_up_first, feed_up_second, reduced[2], kind_rates[2])
    down_new = adam_update(feed_down, feed_down_first, feed_down_second, reduced[3], kind_rates[3])
    norm_new = adam_update(
        norm_params, norm_params_first, norm_params_second, reduced[4], kind_rates[4]
    )
    proj_new = adam_update(
        entity_proj, entity_proj_first, entity_proj_second, reduced_proj, kind_rates[5]
    )
    head_new = adam_update(
        head_proj, head_proj_first, head_proj_second, reduced_head, kind_rates[6]
    )
    table_new = adam_update(
        entity_table, entity_table_first, entity_table_second, grad_table, kind_rates[7]
    )
    return (
        row_losses,
        word_grads,
        attn_new[0],
        attn_new[1],
        attn_new[2],
        out_new[0],
        out_new[1],
        out_new[2],
        up_new[0],
        up_new[1],
        up_new[2],
        down_new[0],
        down_new[1],
        down_new[2],
        norm_new[0],
        norm_new[1],
        norm_new[2],
        proj_new[0],
        proj_new[1],
        proj_new[2],
        head_new[0],
        head_new[1],
        head_new[2],
        table_new[0],
        table_new[1],
        table_new[2],
    )


def turned(*arrays):
    return tuple(jnp.swapaxes(array, 1, 2) for array in arrays)


def fused_device(
    word_inputs,
    entity_base,
    entity_ids,
    buckets,
    mask_positions,
    targets,
    word_cotangent,
    attention_in,
    attention_in_first,
    attention_in_second,
    attention_out,
    attention_out_first,
    attention_out_second,
    feed_up,
    feed_up_first,
    feed_up_second,
    feed_down,
    feed_down_first,
    feed_down_second,
    norm_params,
    norm_params_first,
    norm_params_second,
    entity_proj,
    entity_proj_first,
    entity_proj_second,
    head_proj,
    head_proj_first,
    head_proj_second,
    entity_table,
    entity_table_first,
    entity_table_second,
):
    dims = chip_grid(lax.axis_size("dp"))
    shards, heights = weight_shards(
        attention_in, attention_out, feed_up, feed_down, norm_params, entity_proj, head_proj
    )
    slot_total, shard_rows = entity_ids.shape[0], entity_table.shape[0]
    bucket_rows = buckets.reshape(buckets.shape[2], buckets.shape[3])
    request = jnp.where(
        bucket_rows >= 0, entity_ids[jnp.maximum(bucket_rows, 0)] % shard_rows, -1
    ).astype(jnp.int32)
    requests = jnp.broadcast_to(request[:, :, None], (*request.shape, 128))
    slots = jnp.arange(slot_total, dtype=jnp.int32)
    marks = mask_positions.reshape(-1)[:, None] == slots[None, :]
    keep = jnp.logical_not(jnp.any(marks, axis=0))
    place_mat = (slots[:, None] == bucket_rows.reshape(-1)[None, :]) & keep[:, None]
    place_mat = place_mat.astype(jnp.bfloat16)
    hits = marks.astype(jnp.bfloat16)
    flat_targets = targets.reshape(-1)
    local_targets = flat_targets - lax.axis_index(("dp", "mp")) * shard_rows
    local_targets = jnp.broadcast_to(local_targets[None, :], (8, flat_targets.shape[0]))
    wholes, saved_layers, ents, gain_rows, entity_rows, got, table_low = run_forward(
        dims, word_inputs, entity_base, requests, place_mat, entity_table, shards, 6
    )
    losses, grad_logits, states, grad_head, grad_ents = run_head(
        dims, ents, hits, wholes[5][0], table_low, local_targets, 7
    )
    word_grads, incoming, totals = run_backward(
        dims,
        word_cotangent,
        grad_ents,
        grad_head,
        gain_rows,
        entity_rows,
        place_mat,
        wholes,
        saved_layers,
        8,
    )
    wanted = jnp.broadcast_to(got[:, 0][None, :], (8, got.shape[0]))
    updated = run_update(
        (
            (attention_in, attention_in_first, attention_in_second),
            turned(attention_out, attention_out_first, attention_out_second),
            (feed_up, feed_up_first, feed_up_second),
            turned(feed_down, feed_down_first, feed_down_second),
            (norm_params, norm_params_first, norm_params_second),
            (entity_proj, entity_proj_first, entity_proj_second),
            (head_proj, head_proj_first, head_proj_second),
            (entity_table, entity_table_first, entity_table_second),
        ),
        totals,
        incoming,
        wanted,
        grad_logits,
        states,
    )
    updated[1], updated[3] = turned(*updated[1]), turned(*updated[3])
    results = [losses[0], word_grads]
    for master, first, second in updated:
        results += [first, second, master]
    return tuple(results)


def on_device(*arrays):
    n_dp = lax.axis_size("dp")
    whole_tiles = D % (16 * n_dp) == 0
    return (fused_device if whole_tiles else apart_device)(*arrays)


def solution(mesh):
    in_specs = (
        P("dp", None),
        P("dp", None),
        P("dp"),
        P("dp", "mp", None, None),
        P("dp", None),
        P(),
        P("dp", None),
        P(None, None, "dp", "mp"),
        P(None, None, "dp", "mp"),
        P(None, None, "dp", "mp"),
        P(None, "mp", "dp"),
        P(None, "mp", "dp"),
        P(None, "mp", "dp"),
        P(None, "dp", "mp"),
        P(None, "dp", "mp"),
        P(None, "dp", "mp"),
        P(None, "mp", "dp"),
        P(None, "mp", "dp"),
        P(None, "mp", "dp"),
        P(None, None, "dp"),
        P(None, None, "dp"),
        P(None, None, "dp"),
        P("dp", None),
        P("dp", None),
        P("dp", None),
        P("dp", None),
        P("dp", None),
        P("dp", None),
        P(("dp", "mp"), None),
        P(("dp", "mp"), None),
        P(("dp", "mp"), None),
    )
    out_specs = (
        P(),
        P("dp", None),
        P(None, None, "dp", "mp"),
        P(None, None, "dp", "mp"),
        P(None, None, "dp", "mp"),
        P(None, "mp", "dp"),
        P(None, "mp", "dp"),
        P(None, "mp", "dp"),
        P(None, "dp", "mp"),
        P(None, "dp", "mp"),
        P(None, "dp", "mp"),
        P(None, "mp", "dp"),
        P(None, "mp", "dp"),
        P(None, "mp", "dp"),
        P(None, None, "dp"),
        P(None, None, "dp"),
        P(None, None, "dp"),
        P("dp", None),
        P("dp", None),
        P("dp", None),
        P("dp", None),
        P("dp", None),
        P("dp", None),
        P(("dp", "mp"), None),
        P(("dp", "mp"), None),
        P(("dp", "mp"), None),
    )
    return jax.shard_map(
        on_device, mesh=mesh, in_specs=in_specs, out_specs=out_specs, check_vma=False
    )
```

```python
import functools

import jax
import jax.numpy as jnp
from jax import lax
from jax.experimental import pallas as pl
from jax.experimental.pallas import tpu as pltpu
from jax.sharding import PartitionSpec as P

D = 768
HEAD_DIM = 64
WORDS = 896
ENT_LEN = 128
MASK_ENT = 16
LAYERS = 2
STEP = 10
SEQ_DEV = 1


norm_eps = 1e-05
beta_first = 0.9
beta_second = 0.999
adam_eps = 1e-12
weight_decay = 0.01
kind_rates = (0.05, 1.0, 0.05, 0.027, 0.75, 0.5, 0.05, 0.2)


MESH = pl.DeviceIdType.MESH
ANY = pl.BlockSpec(memory_space=pl.ANY)
VMEM = pl.BlockSpec(memory_space=pltpu.VMEM)
VMEM_BYTES = 60 * 2**20


def chip_grid(n_dp):
    return {16: (4, 2, 2), 64: (4, 4, 4)}.get(n_dp, (n_dp, 1, 1))


def place(dims):
    index = lax.axis_index("dp")
    return index // (dims[1] * dims[2]), index // dims[2] % dims[1], index % dims[2]


def axis_peers(dims, axis):
    here = place(dims)
    core = lax.axis_index("mp")
    peers = []
    for step in range(1, dims[axis]):
        spot = list(here)
        spot[axis] = lax.rem(here[axis] + step, dims[axis])
        peers.append((spot[axis], (spot[0] * dims[1] * dims[2] + spot[1] * dims[2] + spot[2], core)))
    return peers


def greet(targets):
    barrier = pltpu.get_barrier_semaphore()
    for target in targets:
        pl.semaphore_signal(barrier, inc=1, device_id=target, device_id_type=MESH)
    pl.semaphore_wait(barrier, len(targets))


def send(src, dst, send_sem, recv_sem, target):
    copy = pltpu.make_async_remote_copy(
        src_ref=src,
        dst_ref=dst,
        send_sem=send_sem,
        recv_sem=recv_sem,
        device_id=target,
        device_id_type=MESH,
    )
    copy.start()
    return copy


def gather_body(dims, chunks, count, *refs):
    shards, wholes = refs[:count], refs[count : 2 * count]
    send_sem, recv_sem, local_sem = refs[2 * count :]
    z, y, x = place(dims)
    peers = [axis_peers(dims, axis) for axis in range(3)]
    greet([target for group in peers for _, target in group])
    pending = {}

    def start(stage, c):
        which, first, size, y_first = chunks[c]
        rows = pl.ds(first, size)
        whole = wholes[which]
        copies = []
        if stage == 0:
            src, dst, group = shards[which].at[rows], whole.at[rows, z, y, x], peers[0]
            own = pltpu.make_async_copy(src, dst, local_sem.at[c])
            own.start()
            copies.append(own)
        elif stage == 1:
            src = whole.at[rows, :, y, x]
            dst, group = src, peers[1 if y_first else 2]
        else:
            src = whole.at[rows, :, :, x] if y_first else whole.at[rows, :, y]
            dst, group = src, peers[2 if y_first else 1]
        base = (0, dims[0], dims[0] + max(dims[1:]))[stage]
        for slot, (_, target) in enumerate(group):
            copies.append(
                send(src, dst, send_sem.at[c, base + slot], recv_sem.at[c, base + slot], target)
            )
        pending[stage, c] = copies

    def finish(stage, c):
        for copy in pending.pop((stage, c)):
            copy.wait()

    total = len(chunks)
    start(0, 0)
    for step in range(total + 2):
        if step + 1 < total:
            start(0, step + 1)
        if step < total:
            finish(0, step)
            start(1, step)
        if 0 <= step - 1 < total:
            finish(1, step - 1)
            start(2, step - 1)
        if 0 <= step - 2 < total:
            finish(2, step - 2)


def gather_weights(dims, shards, chunks, collective_id):
    count = len(shards)
    copies = dims[0] + 2 * max(dims[1:])
    return pl.pallas_call(
        functools.partial(gather_body, dims, chunks, count),
        out_shape=[
            jax.ShapeDtypeStruct((s.shape[0], *dims, *s.shape[1:]), s.dtype) for s in shards
        ],
        in_specs=[ANY] * count,
        out_specs=[ANY] * count,
        scratch_shapes=[
            pltpu.SemaphoreType.DMA((len(chunks), copies)),
            pltpu.SemaphoreType.DMA((len(chunks), copies)),
            pltpu.SemaphoreType.DMA((len(chunks),)),
        ],
        compiler_params=pltpu.CompilerParams(
            collective_id=collective_id, has_side_effects=True, vmem_limit_bytes=2**20
        ),
    )(*shards)


def sum_body(dims, flags, *refs):
    count = len(flags)
    parts, totals = refs[:count], refs[count : 2 * count]
    buffers = refs[2 * count : 6 * count]
    send_sem, recv_sem, local_sem = refs[6 * count :]
    z, y, x = place(dims)
    peers = [axis_peers(dims, axis) for axis in range(3)]
    greet([target for group in peers for _, target in group])
    pending = {}

    def start(stage, c):
        y_first = flags[c]
        own, first, second, third = buffers[4 * c : 4 * c + 4]
        copies = []
        base = (0, max(dims[1:]), 2 * max(dims[1:]))[stage]
        if stage == 0:
            mine = parts[c].at[:, y] if y_first else parts[c].at[:, :, x]
            local = pltpu.make_async_copy(mine, own, local_sem.at[c])
            local.start()
            copies.append(local)
        group = peers[((1, 2, 0) if y_first else (2, 1, 0))[stage]]
        for slot, (spot, target) in enumerate(group):
            if stage == 0:
                src = parts[c].at[:, spot] if y_first else parts[c].at[:, :, spot]
                dst = first.at[slot]
            elif stage == 1:
                src, dst = own.at[:, spot], second.at[slot]
            else:
                src, dst = own.at[spot, x if y_first else y], third.at[slot]
            copies.append(
                send(src, dst, send_sem.at[c, base + slot], recv_sem.at[c, base + slot], target)
            )
        pending[stage, c] = copies

    def finish(stage, c):
        y_first = flags[c]
        own, first, second, third = buffers[4 * c : 4 * c + 4]
        for copy in pending.pop((stage, c)):
            copy.wait()
        across = dims[2] if y_first else dims[1]
        line = x if y_first else y
        count_peers = len(peers[((1, 2, 0) if y_first else (2, 1, 0))[stage]])
        if stage == 0 and count_peers:

            def add_first(i, carry):
                value = own[i // across, i % across].astype(jnp.float32)
                for slot in range(count_peers):
                    value += first[slot, i // across, i % across].astype(jnp.float32)
                own[i // across, i % across] = value.astype(own.dtype)
                return carry

            lax.fori_loop(0, dims[0] * across, add_first, 0)
        if stage == 1 and count_peers:

            def add_second(i, carry):
                value = own[i, line].astype(jnp.float32)
                for slot in range(count_peers):
                    value += second[slot, i].astype(jnp.float32)
                own[i, line] = value.astype(own.dtype)
                return carry

            lax.fori_loop(0, dims[0], add_second, 0)
        if stage == 2:
            value = own[z, line].astype(jnp.float32)
            for slot in range(count_peers):
                value += third[slot].astype(jnp.float32)
            totals[c][...] = value

    total = len(flags)
    ahead = 2
    for c in range(min(ahead, total)):
        start(0, c)
    for step in range(total + 2 * ahead):
        if step + ahead < total:
            start(0, step + ahead)
        if step < total:
            finish(0, step)
            start(1, step)
        if 0 <= step - ahead < total:
            finish(1, step - ahead)
            start(2, step - ahead)
        if 0 <= step - 2 * ahead < total:
            finish(2, step - 2 * ahead)


def sum_gradients(dims, parts, flags, collective_id):
    count = len(parts)
    scratch = []
    for part, y_first in zip(parts, flags):
        block = part.shape[3:]
        own = (dims[0], dims[2] if y_first else dims[1])
        turns = (dims[1], dims[2]) if y_first else (dims[2], dims[1])
        scratch += [
            pltpu.VMEM((*own, *block), part.dtype),
            pltpu.VMEM((max(turns[0] - 1, 1), *own, *block), part.dtype),
            pltpu.VMEM((max(turns[1] - 1, 1), dims[0], *block), part.dtype),
            pltpu.VMEM((max(dims[0] - 1, 1), *block), part.dtype),
        ]
    copies = dims[0] + 2 * max(dims[1:])
    return pl.pallas_call(
        functools.partial(sum_body, dims, flags),
        out_shape=[jax.ShapeDtypeStruct(part.shape[3:], jnp.float32) for part in parts],
        in_specs=[ANY] * count,
        out_specs=[VMEM] * count,
        scratch_shapes=scratch
        + [
            pltpu.SemaphoreType.DMA((count, copies)),
            pltpu.SemaphoreType.DMA((count, copies)),
            pltpu.SemaphoreType.DMA((count,)),
        ],
        compiler_params=pltpu.CompilerParams(
            collective_id=collective_id, has_side_effects=True, vmem_limit_bytes=VMEM_BYTES
        ),
    )(*parts)


def spread_body(count, wide, swap, data, result, send_sem, recv_sem, local_sem):
    pair = lax.axis_size("mp")
    index = lax.axis_index("dp") * pair + lax.axis_index("mp") if wide else lax.axis_index("dp")

    def target_of(step):
        other = lax.rem(index + step, count)
        if wide:
            return other, (other // pair, lax.rem(other, pair))
        return other, (other, lax.axis_index("mp"))

    barrier = pltpu.get_barrier_semaphore()

    def hello(step, carry):
        pl.semaphore_signal(barrier, inc=1, device_id=target_of(step)[1], device_id_type=MESH)
        return carry

    lax.fori_loop(1, count, hello, 0)
    pl.semaphore_wait(barrier, count - 1)
    own = pltpu.make_async_copy(data.at[index if swap else 0], result.at[index], local_sem)
    own.start()

    def copy_of(step):
        other, target = target_of(step)
        return pltpu.make_async_remote_copy(
            src_ref=data.at[other if swap else 0],
            dst_ref=result.at[index],
            send_sem=send_sem.at[step],
            recv_sem=recv_sem.at[step],
            device_id=target,
            device_id_type=MESH,
        )

    def go(step, carry):
        copy_of(step).start()
        return carry

    def done(step, carry):
        copy_of(step).wait()
        return carry

    lax.fori_loop(1, count, go, 0)
    own.wait()
    lax.fori_loop(1, count, done, 0)


def spread(data, wide, swap, collective_id):
    count = lax.axis_size("dp") * (lax.axis_size("mp") if wide else 1)
    block = data.shape[1:] if swap else data.shape
    return pl.pallas_call(
        functools.partial(spread_body, count, wide, swap),
        out_shape=jax.ShapeDtypeStruct((count, *block), data.dtype),
        in_specs=[VMEM],
        out_specs=VMEM,
        scratch_shapes=[
            pltpu.SemaphoreType.DMA((count,)),
            pltpu.SemaphoreType.DMA((count,)),
            pltpu.SemaphoreType.DMA,
        ],
        compiler_params=pltpu.CompilerParams(
            collective_id=collective_id, has_side_effects=True, vmem_limit_bytes=VMEM_BYTES
        ),
    )(data if swap else data[None])


def layer_norm(values, gain_row, shift_row):
    centered = values - jnp.mean(values, axis=-1, keepdims=True)
    spread = jnp.mean(centered * centered, axis=-1, keepdims=True)
    return centered * lax.rsqrt(spread + norm_eps) * gain_row + shift_row


def gelu_exact(values):
    return jax.nn.gelu(values, approximate=False)


def adam_update(master, first_moment, second_moment, gradient, kind_rate):
    first_new = beta_first * first_moment + (1.0 - beta_first) * gradient
    second_new = beta_second * second_moment + (1.0 - beta_second) * gradient * gradient
    first_hat = first_new / (1.0 - beta_first**STEP)
    second_hat = second_new / (1.0 - beta_second**STEP)
    master_new = master - kind_rate * (
        first_hat / (jnp.sqrt(second_hat) + adam_eps) + weight_decay * master
    )
    return (first_new, second_new, master_new)


def project(fetched_row_values, weight_matrix_entry):
    return jnp.einsum(
        "mvw,wu->mvu", fetched_row_values, weight_matrix_entry, preferred_element_type=jnp.float32
    )


def project_back(row_gradient_block, weight_matrix_entry):
    return jnp.einsum(
        "tic,vc->tiv", row_gradient_block, weight_matrix_entry, preferred_element_type=jnp.float32
    )


def project_turned(rows, turned):
    return jnp.einsum("mvw,uw->mvu", rows, turned, preferred_element_type=jnp.float32)


def project_back_turned(row_gradient_block, turned):
    return jnp.einsum("tic,cv->tiv", row_gradient_block, turned, preferred_element_type=jnp.float32)


def weight_grad(layer_input_list, row_gradient_block):
    return jnp.einsum(
        "hmq,hmw->qw", layer_input_list, row_gradient_block, preferred_element_type=jnp.float32
    ).astype(jnp.bfloat16)


def split_heads(values):
    return values.reshape(values.shape[0], values.shape[1], values.shape[2] // HEAD_DIM, HEAD_DIM)


def pair_sum(partial_sum):
    mine = partial_sum.astype(jnp.bfloat16)
    theirs = lax.ppermute(mine, "mp", [(0, 1), (1, 0)])
    return mine.astype(jnp.float32) + theirs.astype(jnp.float32)


merge_heads = merge_inputs = pair_sum


def seq_scores(query_word, query_entity, key_rows):
    score_word = jnp.einsum(
        "qhd,khd->hqk", query_word, key_rows[:WORDS], preferred_element_type=jnp.float32
    )
    score_entity = jnp.einsum(
        "qhd,khd->hqk", query_entity, key_rows[WORDS:], preferred_element_type=jnp.float32
    )
    return jnp.concatenate([score_word, score_entity], axis=-1) * 0.125


def attend_forward(seq_item):
    query_word, query_entity, key_rows, value_rows = seq_item
    scores = seq_scores(query_word, query_entity, key_rows)
    peak_value = jnp.max(scores, axis=-1, keepdims=True)
    exp_scores = jnp.exp(scores - peak_value)
    exp_total = jnp.sum(exp_scores, axis=-1, keepdims=True)
    prob_low = (exp_scores / exp_total).astype(jnp.bfloat16)
    mixed_heads = jnp.einsum(
        "hqk,khd->qhd", prob_low, value_rows, preferred_element_type=jnp.float32
    )
    return (mixed_heads, (peak_value + jnp.log(exp_total))[..., 0])


def attend_backward(seq_item):
    query_word, query_entity, key_rows, value_rows, log_norm, grad_mixed = seq_item
    scores = seq_scores(query_word, query_entity, key_rows)
    prob_rows = jnp.exp(scores - log_norm[..., None])
    grad_value = jnp.einsum(
        "hqk,qhd->khd",
        prob_rows.astype(jnp.bfloat16),
        grad_mixed,
        preferred_element_type=jnp.float32,
    )
    grad_probs = jnp.einsum(
        "qhd,khd->hqk", grad_mixed, value_rows, preferred_element_type=jnp.float32
    )
    inner_sum = jnp.sum(prob_rows * grad_probs, axis=-1, keepdims=True)
    grad_scores = (prob_rows * (grad_probs - inner_sum) * 0.125).astype(jnp.bfloat16)
    score_word = grad_scores[..., :WORDS]
    score_entity = grad_scores[..., WORDS:]
    grad_qw = jnp.einsum(
        "hqk,khd->qhd", score_word, key_rows[:WORDS], preferred_element_type=jnp.float32
    )
    grad_qe = jnp.einsum(
        "hqk,khd->qhd", score_entity, key_rows[WORDS:], preferred_element_type=jnp.float32
    )
    grad_key = jnp.concatenate(
        [
            jnp.einsum("hqk,qhd->khd", score_word, query_word, preferred_element_type=jnp.float32),
            jnp.einsum(
                "hqk,qhd->khd", score_entity, query_entity, preferred_element_type=jnp.float32
            ),
        ],
        axis=0,
    )
    return (grad_qw, grad_qe, grad_key, grad_value)


def layer_forward(hidden, attn_mats, out_mat, up_mat, down_mat, gain_rows):
    hidden_low = hidden.astype(jnp.bfloat16)
    words_low = hidden_low[:, :WORDS]
    ents_low = hidden_low[:, WORDS:]
    query_word = jnp.concatenate(
        [project(words_low, attn_mats[0]), project(ents_low, attn_mats[2])], axis=1
    ).astype(jnp.bfloat16)
    query_entity = jnp.concatenate(
        [project(words_low, attn_mats[1]), project(ents_low, attn_mats[3])], axis=1
    ).astype(jnp.bfloat16)
    key_rows = project(hidden_low, attn_mats[4]).astype(jnp.bfloat16)
    value_rows = project(hidden_low, attn_mats[5]).astype(jnp.bfloat16)
    mixed_heads, log_norm = lax.map(
        attend_forward,
        (
            split_heads(query_word),
            split_heads(query_entity),
            split_heads(key_rows),
            split_heads(value_rows),
        ),
    )
    mixed_low = mixed_heads.reshape(key_rows.shape).astype(jnp.bfloat16)
    attended = merge_heads(project_turned(mixed_low, out_mat))
    first_out = layer_norm(hidden + attended, gain_rows[0], gain_rows[1])
    first_low = first_out.astype(jnp.bfloat16)
    inner_pre = project(first_low, up_mat)
    inner_low = gelu_exact(inner_pre).astype(jnp.bfloat16)
    outer_out = merge_heads(project_turned(inner_low, down_mat))
    result = layer_norm(first_out + outer_out, gain_rows[2], gain_rows[3])
    saved_acts = (
        hidden,
        hidden_low,
        query_word,
        query_entity,
        key_rows,
        value_rows,
        log_norm,
        mixed_low,
        attended,
        first_out,
        first_low,
        inner_pre,
        inner_low,
        outer_out,
    )
    return (result, saved_acts)


def layer_backward(grad_out, saved_acts, attn_mats, out_mat, up_mat, down_mat, gain_rows):
    (
        hidden,
        hidden_low,
        query_word,
        query_entity,
        key_rows,
        value_rows,
        log_norm,
        mixed_low,
        attended,
        first_out,
        first_low,
        inner_pre,
        inner_low,
        outer_out,
    ) = saved_acts
    second_back = jax.vjp(layer_norm, first_out + outer_out, gain_rows[2], gain_rows[3])[1]
    grad_second, grad_gain_late, grad_shift_late = second_back(grad_out)
    grad_outer = grad_second.astype(jnp.bfloat16)
    grad_down = weight_grad(grad_outer, inner_low)
    grad_inner = project_back_turned(grad_outer, down_mat)
    grad_pre = jax.vjp(gelu_exact, inner_pre)[1](grad_inner)[0].astype(jnp.bfloat16)
    grad_up = weight_grad(first_low, grad_pre)
    grad_first = grad_second + merge_inputs(project_back(grad_pre, up_mat))
    first_back = jax.vjp(layer_norm, hidden + attended, gain_rows[0], gain_rows[1])[1]
    grad_first_in, grad_gain_early, grad_shift_early = first_back(grad_first)
    grad_attended = grad_first_in.astype(jnp.bfloat16)
    grad_out_mat = weight_grad(grad_attended, mixed_low)
    grad_mixed = project_back_turned(grad_attended, out_mat).astype(jnp.bfloat16)
    grad_qw, grad_qe, grad_key, grad_value = lax.map(
        attend_backward,
        (
            split_heads(query_word),
            split_heads(query_entity),
            split_heads(key_rows),
            split_heads(value_rows),
            log_norm,
            split_heads(grad_mixed),
        ),
    )
    flat_shape = key_rows.shape
    grad_qw = grad_qw.reshape(flat_shape).astype(jnp.bfloat16)
    grad_qe = grad_qe.reshape(flat_shape).astype(jnp.bfloat16)
    grad_key = grad_key.reshape(flat_shape).astype(jnp.bfloat16)
    grad_value = grad_value.reshape(flat_shape).astype(jnp.bfloat16)
    words_low = hidden_low[:, :WORDS]
    ents_low = hidden_low[:, WORDS:]
    grad_mats = (
        weight_grad(words_low, jnp.concatenate([grad_qw[:, :WORDS], grad_qe[:, :WORDS]], axis=-1)),
        weight_grad(ents_low, jnp.concatenate([grad_qw[:, WORDS:], grad_qe[:, WORDS:]], axis=-1)),
        weight_grad(hidden_low, jnp.concatenate([grad_key, grad_value], axis=-1)),
    )
    part_words = project_back(grad_qw[:, :WORDS], attn_mats[0]) + project_back(
        grad_qe[:, :WORDS], attn_mats[1]
    )
    part_ents = project_back(grad_qw[:, WORDS:], attn_mats[2]) + project_back(
        grad_qe[:, WORDS:], attn_mats[3]
    )
    part_sum = (
        jnp.concatenate([part_words, part_ents], axis=1)
        + project_back(grad_key, attn_mats[4])
        + project_back(grad_value, attn_mats[5])
    )
    grad_hidden = grad_first_in + merge_inputs(part_sum)
    grad_norms = jnp.stack([grad_gain_early, grad_shift_early, grad_gain_late, grad_shift_late])
    return (grad_hidden, (grad_mats, grad_out_mat, grad_up, grad_down, grad_norms))


LOG2E = 1.4426950408889634
SCORE_STEP = 0.125 * LOG2E
LEN = WORDS + ENT_LEN
BLOCK = 256
BLOCKS = LEN // BLOCK


def mm(left, right):
    return lax.dot_general(
        left, right, (((1,), (0,)), ((), ())), preferred_element_type=jnp.float32
    )


def mm_rt(left, right):
    return lax.dot_general(
        left, right, (((1,), (1,)), ((), ())), preferred_element_type=jnp.float32
    )


def mm_lt(left, right):
    return lax.dot_general(
        left, right, (((0,), (0,)), ((), ())), preferred_element_type=jnp.float32
    )


def flat(ref, *index):
    value = ref[index] if index else ref[...]
    return value.reshape(-1, value.shape[-1])


def lane_mask(rows, which):
    lane = lax.broadcasted_iota(jnp.int32, (rows, 2 * HEAD_DIM), 1)
    return (lane // HEAD_DIM == which).astype(jnp.bfloat16)


def normed(values):
    centered = values - jnp.mean(values, axis=-1, keepdims=True)
    spread_row = jnp.mean(centered * centered, axis=-1, keepdims=True)
    scale = lax.rsqrt(spread_row + norm_eps)
    return centered * scale, scale


def gelu_parts(values):
    cdf = 0.5 * (1.0 + lax.erf(values * 0.7071067811865476))
    bell = jnp.exp2(values * values * (-0.5 * LOG2E)) * 0.3989422804014327
    return values * cdf, cdf + values * bell


GATHER_RATE = 52000.0
SUM_RATE = 40000.0
HOP_US = 1.5
ORDERS = ((0, 1, 2), (0, 2, 1), (2, 0, 1), (1, 0, 2))


def cut_load(size):
    return (size // 2) * (size - size // 2)


def gather_loads(dims, order, shard_bytes):
    loads, held = [0.0, 0.0, 0.0], shard_bytes
    for axis in order:
        loads[axis] += held * cut_load(dims[axis])
        held *= dims[axis]
    return loads


def balanced_orders(dims, sizes):
    total, chosen = [0.0, 0.0, 0.0], []
    for size in sizes:
        options = []
        for rank, order in enumerate(ORDERS):
            loads = gather_loads(dims, order, size)
            after = [a + b for a, b in zip(total, loads)]
            options.append((max(after), sum(after), rank, order, after))
        best = min(options)
        chosen.append(best[3])
        total = best[4]
    return chosen


class Links:
    def __init__(self, dims, rate):
        self.dims, self.rate = dims, rate
        self.clock, self.free, self.serial = 0.0, [0.0, 0.0, 0.0], 0
        self.active = []

    def issue(self, axis, message_bytes, what):
        if self.dims[axis] > 1:
            begin = max(self.clock, self.free[axis])
            self.free[axis] = begin + message_bytes * cut_load(self.dims[axis]) / self.rate
            finish = self.free[axis] + HOP_US
        else:
            finish = self.clock
        self.serial += 1
        self.active.append((finish, self.serial, what))

    def finish_first(self):
        first = min(self.active, key=lambda item: item[:2])
        self.active.remove(first)
        self.clock = max(self.clock, first[0])
        self.complete(first[2])

    def spend(self, micros):
        self.clock += micros
        while self.active and min(item[0] for item in self.active) <= self.clock:
            self.finish_first()


class Gather(Links):
    def __init__(self, dims, chunks, shards, wholes, kept, sems):
        super().__init__(dims, GATHER_RATE)
        self.chunks, self.shards, self.wholes, self.kept = chunks, shards, wholes, kept
        self.send_sem, self.recv_sem, self.local_sem, self.keep_sem = sems
        self.spot = place(dims)
        self.peers = [axis_peers(dims, axis) for axis in range(3)]
        self.copies, self.done, self.keeping = {}, set(), []
        self.next, self.window = 0, 6

    def slab(self, whole, order, stage):
        held = order[:stage]
        return whole.at[
            (slice(None), *[slice(None) if d in held else self.spot[d] for d in range(3)])
        ]

    def start(self, stage, c):
        which, rows, cols, order = self.chunks[c]
        whole = self.wholes[which].at[rows, :, :, :, :, cols]
        shard = self.shards[which].at[rows, :, cols]
        copies, base = [], sum(self.dims[order[i]] for i in range(stage))
        dst = self.slab(whole, order, stage)
        src = dst
        if stage == 0:
            own = pltpu.make_async_copy(shard, dst, self.local_sem.at[c])
            own.start()
            copies.append(own)
            src = shard
        for slot, (_, target) in enumerate(self.peers[order[stage]]):
            sems = self.send_sem.at[c, base + slot], self.recv_sem.at[c, base + slot]
            copies.append(send(src, dst, *sems, target))
        self.copies[stage, c] = copies
        held = 1
        for axis in order[:stage]:
            held *= self.dims[axis]
        shape = shard.shape
        self.issue(order[stage], held * 2 * shape[0] * shape[1] * shape[2], (stage, c))

    def complete(self, what):
        stage, c = what
        for copy in self.copies.pop(what):
            copy.wait()
        if stage < 2:
            self.start(stage + 1, c)
        else:
            which, rows, cols, _ = self.chunks[c]
            at = (rows, slice(None), slice(None), slice(None), slice(None), cols)
            keep = pltpu.make_async_copy(
                self.wholes[which].at[at], self.kept[which].at[at], self.keep_sem.at[c]
            )
            keep.start()
            self.keeping.append(keep)
            self.done.add(c)
        self.refill()

    def refill(self):
        while self.next < len(self.chunks) and self.next - len(self.done) < self.window:
            self.next += 1
            self.start(0, self.next - 1)

    def need(self, c):
        while c not in self.done:
            self.finish_first()

    def close(self):
        while self.active:
            self.finish_first()
        for keep in self.keeping:
            keep.wait()


class Pair:
    def __init__(self, mine, theirs, sems):
        self.mine, self.theirs = mine, theirs
        self.send_sem, self.recv_sem = sems
        self.phase = 0
        self.other = (lax.axis_index("dp"), 1 - lax.axis_index("mp"))

    def copy(self, phase, c):
        return pltpu.make_async_remote_copy(
            src_ref=self.mine.at[c],
            dst_ref=self.theirs.at[phase % 2, c],
            send_sem=self.send_sem.at[phase, c],
            recv_sem=self.recv_sem.at[phase, c],
            device_id=self.other,
            device_id_type=MESH,
        )

    def run(self, compute, consume, between):
        phase = self.phase
        self.phase += 1

        def take(c):
            self.copy(phase, c).wait()
            total = self.mine[c].astype(jnp.float32) + self.theirs[phase % 2, c].astype(jnp.float32)
            consume(c, pl.ds(c * BLOCK, BLOCK), total)

        for c in range(BLOCKS):
            self.mine[c] = compute(c, pl.ds(c * BLOCK, BLOCK)).astype(jnp.bfloat16)
            self.copy(phase, c).start()
            if c:
                take(c - 1)
            between()
        take(BLOCKS - 1)


SAVED = ("xb", "qw", "qe", "k", "v", "o", "n1", "h1b", "slope", "g", "n2", "stats")


def saved_shapes(half, hidden):
    wide, narrow = (LEN, D), (LEN, half)
    low = jnp.bfloat16
    return {
        "xb": (wide, low),
        "qw": (narrow, low),
        "qe": (narrow, low),
        "k": (narrow, low),
        "v": (narrow, low),
        "o": (narrow, low),
        "n1": (wide, low),
        "h1b": (wide, low),
        "slope": ((LEN, hidden), low),
        "g": ((LEN, hidden), low),
        "n2": (wide, low),
        "stats": ((LEN, 128), jnp.float32),
    }


def attend(act, pair):
    lanes = slice(pair * 2 * HEAD_DIM, (pair + 1) * 2 * HEAD_DIM)

    def block(i, carry):
        rows = pl.ds(i * BLOCK, BLOCK)
        keys, values = act["k"][:, lanes], act["v"][:, lanes]
        total = None
        for which in range(2):
            q_mask, v_mask = lane_mask(BLOCK, which), lane_mask(LEN, which)
            score_w = mm_rt(act["qw"][rows, lanes] * q_mask, keys[:WORDS])
            score_e = mm_rt(act["qe"][rows, lanes] * q_mask, keys[WORDS:])
            peak = jnp.maximum(
                jnp.max(score_w, axis=-1, keepdims=True), jnp.max(score_e, axis=-1, keepdims=True)
            )
            exp_w = jnp.exp2((score_w - peak) * SCORE_STEP)
            exp_e = jnp.exp2((score_e - peak) * SCORE_STEP)
            weight = jnp.sum(exp_w, axis=-1, keepdims=True) + jnp.sum(exp_e, axis=-1, keepdims=True)
            part = values * v_mask
            mixed = mm(exp_w.astype(jnp.bfloat16), part[:WORDS])
            mixed += mm(exp_e.astype(jnp.bfloat16), part[WORDS:])
            mixed = mixed * (1.0 / weight)
            total = mixed if total is None else total + mixed
            head = 2 * pair + which
            act["stats"][rows, head : head + 1] = peak * SCORE_STEP + jnp.log2(weight)
        act["o"][rows, lanes] = total.astype(jnp.bfloat16)
        return carry

    lax.fori_loop(0, BLOCKS, block, 0)


def project_rows(out_ref, x_ref, first, size, step, weights, index):
    def block(i, carry):
        rows = pl.ds(first + i * step, step)
        out_ref[rows, :] = mm(x_ref[rows, :], flat(weights, index)).astype(jnp.bfloat16)
        return carry

    lax.fori_loop(0, size // step, block, 0)


def forward_body(dims, chunks, needs, *refs):
    refs = list(refs)

    def take(count):
        part = refs[:count]
        del refs[:count]
        return part

    words, base, requests, place_mat, table = take(5)
    shards = take(len(needs["kinds"]))
    kept = take(len(needs["kinds"]))
    saved = [dict(zip(SAVED, take(len(SAVED)))) for _ in range(LAYERS)]
    ents_out, gains_out, rows_in, got_out, table_out = take(5)
    wholes = take(len(needs["kinds"]))
    act = dict(zip(SAVED, take(len(SAVED))))
    x, h1, gains, mine, theirs = take(5)
    gather_sems = take(4)
    pair_sems = take(2)
    (save_sem,) = take(1)
    got, replies, answers, look_mine, look_theirs = take(5)
    look_send, look_recv, look_pair, table_full, table_sem = take(5)
    reading = pltpu.make_async_copy(table, table_full, table_sem)
    reading.start()

    gather = Gather(dims, chunks, shards, wholes, kept, gather_sems)
    pair = Pair(mine, theirs, pair_sems)
    count = dims[0] * dims[1] * dims[2]
    greet_line(count, [pair.other])
    asking = Fan(
        count, (look_send.at[0], look_recv.at[0]), lambda me, to: (requests.at[to], got.at[me])
    )
    asking.start()
    gather.refill()
    here = lax.axis_index("dp")
    got[here] = requests[here]
    asking.wait()
    reading.wait()
    wanted = flat(got)
    got_out[...] = wanted

    def look(j, found):
        lane = lax.broadcasted_iota(jnp.int32, wanted.shape, 1) + j * 128
        hot = jnp.where(wanted == lane, 1.0, 0.0).astype(jnp.bfloat16)
        rows = pl.ds(pl.multiple_of(j * 128, 128), 128)
        low = table_full[rows, :].astype(jnp.bfloat16)
        table_out[rows, :] = low
        return found + mm(hot, low)

    found = jnp.zeros((wanted.shape[0], table.shape[1]), jnp.float32)
    found = lax.fori_loop(0, table.shape[0] // 128, look, found)
    replies[...] = found.reshape(replies.shape)
    answering = Fan(
        count, (look_send.at[1], look_recv.at[1]), lambda me, to: (replies.at[to], answers.at[me])
    )
    answering.start()
    answers[here] = replies[here]
    gather.spend(7.0)
    answering.wait()
    look_mine[...] = mm(place_mat[...], flat(answers).astype(jnp.bfloat16)).astype(jnp.bfloat16)
    swap = send(look_mine, look_theirs, look_pair.at[0], look_pair.at[1], pair.other)
    attn, outs, ups, downs, proj, _, norms = wholes
    saving = {}

    def save(layer, name):
        slot = layer * len(SAVED) + SAVED.index(name)
        copy = pltpu.make_async_copy(act[name], saved[layer][name], save_sem.at[slot])
        copy.start()
        saving[name] = copy

    def free(name):
        if name in saving:
            saving.pop(name).wait()

    x[:WORDS] = words[...].astype(jnp.float32)
    gather.need(needs["norms"])
    width = D // (dims[0] * dims[1] * dims[2])
    gains[...] = jnp.zeros_like(gains)
    for d in range(count):
        z, rest = d // (dims[1] * dims[2]), d % (dims[1] * dims[2])
        pick = lax.broadcasted_iota(jnp.int32, (128, D), 0) + d * width
        lane = lax.broadcasted_iota(jnp.int32, (128, D), 1)
        inside = lax.broadcasted_iota(jnp.int32, (128, D), 0) < width
        hot = jnp.where((pick == lane) & inside, 1.0, 0.0).astype(jnp.bfloat16)
        gains[...] += mm(norms[0, z, rest // dims[2], rest % dims[2]], hot)
    gather.need(needs["proj"])
    swap.wait()
    both = look_mine[...].astype(jnp.float32) + look_theirs[...].astype(jnp.float32)
    rows_in[...] = both.astype(jnp.bfloat16)
    x[WORDS:] = base[...].astype(jnp.float32) + mm(rows_in[...], flat(proj, 0))

    for layer in range(LAYERS):
        gain = [gains[4 * layer + i : 4 * layer + i + 1, :] for i in range(4)]
        free("xb")

        def cast(i, carry):
            rows = pl.ds(i * BLOCK, BLOCK)
            act["xb"][rows, :] = x[rows, :].astype(jnp.bfloat16)
            return carry

        lax.fori_loop(0, BLOCKS, cast, 0)
        save(layer, "xb")
        for name, word_mat, ent_mat in (("k", 4, None), ("v", 5, None), ("qw", 0, 2), ("qe", 1, 3)):
            free(name)
            gather.need(needs["mat", layer, word_mat if ent_mat is None else ent_mat])
            if ent_mat is None:
                project_rows(act[name], act["xb"], 0, LEN, 512, attn, 6 * layer + word_mat)
            else:
                project_rows(act[name], act["xb"], 0, WORDS, 448, attn, 6 * layer + word_mat)
                project_rows(act[name], act["xb"], WORDS, ENT_LEN, ENT_LEN, attn, 6 * layer + ent_mat)
            save(layer, name)
            gather.spend(2.5)
        free("o")
        free("stats")
        for head_pair in range(act["o"].shape[1] // (2 * HEAD_DIM)):
            attend(act, head_pair)
            gather.spend(4.3)
        save(layer, "o")
        gather.need(needs["out", layer])
        for name in ("n1", "h1b"):
            free(name)

        def out_part(c, rows):
            return mm_rt(act["o"][rows, :], flat(outs, layer))

        def first_norm(c, rows, total):
            hat, scale = normed(x[rows, :] + total)
            act["n1"][rows, :] = hat.astype(jnp.bfloat16)
            act["stats"][rows, 8:9] = scale
            value = hat * gain[0] + gain[1]
            h1[rows, :] = value
            act["h1b"][rows, :] = value.astype(jnp.bfloat16)

        pair.run(out_part, first_norm, lambda: gather.spend(1.3))
        save(layer, "n1")
        save(layer, "h1b")
        gather.need(needs["up", layer, 1])
        for name in ("g", "slope", "n2"):
            free(name)
        hidden = act["g"].shape[1]
        tile = 512

        def up_block(c):
            rows = pl.ds(c * BLOCK, BLOCK)
            for first in range(0, hidden, tile):
                cols = slice(first, first + tile)
                weight = ups[layer, :, :, :, :, cols].reshape(D, tile)
                value, slope = gelu_parts(mm(act["h1b"][rows, :], weight))
                act["g"][rows, cols] = value.astype(jnp.bfloat16)
                act["slope"][rows, cols] = slope.astype(jnp.bfloat16)

        for c in range(BLOCKS):
            up_block(c)
            gather.spend(2.6)
        save(layer, "g")
        save(layer, "slope")
        gather.need(needs["down", layer, 1])

        def down_part(c, rows):
            return mm_rt(act["g"][rows, :], flat(downs, layer))

        def second_norm(c, rows, total):
            hat, scale = normed(h1[rows, :] + total)
            act["n2"][rows, :] = hat.astype(jnp.bfloat16)
            act["stats"][rows, 9:10] = scale
            x[rows, :] = hat * gain[2] + gain[3]

        pair.run(down_part, second_norm, lambda: gather.spend(1.8))
        save(layer, "n2")
        save(layer, "stats")
    ents_out[...] = x[WORDS:]
    gains_out[...] = gains[...]
    gather.close()
    for name in list(saving):
        free(name)


KINDS = ("attn", "out", "up", "down", "proj", "head", "norms")


MAT_ORDER = (4, 5, 0, 2, 1, 3)


def gather_plan(dims, shards):
    every = slice(None)
    chunks, needs, sizes = [], {"kinds": KINDS}, []
    hidden = shards[2].shape[-1]

    def add(name, which, row, cols=every, part=1):
        chunks.append((which, pl.ds(row, 1), cols))
        sizes.append(2 * shards[which].shape[1] * shards[which].shape[2] // part)
        needs[name] = len(chunks) - 1

    add("norms", 6, 0)
    add("proj", 4, 0)
    for layer in range(LAYERS):
        for mat in MAT_ORDER:
            add(("mat", layer, mat), 0, 6 * layer + mat)
        add(("out", layer), 1, layer)
        if layer == LAYERS - 1:
            add("head", 5, 0)
        for which, name in ((2, "up"), (3, "down")):
            for part in range(2):
                cols = pl.ds(part * (hidden // 2), hidden // 2)
                add((name, layer, part), which, layer, cols, 2)
    orders = balanced_orders(dims, sizes)
    return [chunk + (order,) for chunk, order in zip(chunks, orders)], needs


def run_forward(dims, words, base, requests, place_mat, table, shards, collective_id):
    half, hidden = shards[0].shape[-1], shards[2].shape[-1]
    chunks, needs = gather_plan(dims, shards)
    shapes = saved_shapes(half, hidden)
    low, full = jnp.bfloat16, jnp.float32
    width, slots = table.shape[1], requests.shape[0] * requests.shape[1]
    wholes = [(s.shape[0], *dims, *s.shape[1:]) for s in shards]
    copies = sum(dims)
    saved_out = [jax.ShapeDtypeStruct(*shapes[name]) for _ in range(LAYERS) for name in SAVED]
    result = pl.pallas_call(
        functools.partial(forward_body, dims, chunks, needs),
        out_shape=[jax.ShapeDtypeStruct(shape, low) for shape in wholes]
        + saved_out
        + [
            jax.ShapeDtypeStruct((ENT_LEN, D), full),
            jax.ShapeDtypeStruct((16, D), full),
            jax.ShapeDtypeStruct((ENT_LEN, width), low),
            jax.ShapeDtypeStruct((slots, 128), jnp.int32),
            jax.ShapeDtypeStruct(table.shape, low),
        ],
        in_specs=[VMEM] * 4 + [ANY] * (1 + len(shards)),
        out_specs=[ANY] * (len(wholes) + len(saved_out)) + [VMEM] * 5,
        scratch_shapes=[pltpu.VMEM(shape, low) for shape in wholes]
        + [pltpu.VMEM(*shapes[name]) for name in SAVED]
        + [
            pltpu.VMEM((LEN, D), full),
            pltpu.VMEM((LEN, D), full),
            pltpu.VMEM((16, D), full),
            pltpu.VMEM((BLOCKS, BLOCK, D), low),
            pltpu.VMEM((2, BLOCKS, BLOCK, D), low),
            pltpu.SemaphoreType.DMA((len(chunks), copies)),
            pltpu.SemaphoreType.DMA((len(chunks), copies)),
            pltpu.SemaphoreType.DMA((len(chunks),)),
            pltpu.SemaphoreType.DMA((len(chunks),)),
            pltpu.SemaphoreType.DMA((2 * LAYERS, BLOCKS)),
            pltpu.SemaphoreType.DMA((2 * LAYERS, BLOCKS)),
            pltpu.SemaphoreType.DMA((LAYERS * len(SAVED),)),
            pltpu.VMEM(requests.shape, jnp.int32),
            pltpu.VMEM((*requests.shape[:2], width), full),
            pltpu.VMEM((*requests.shape[:2], width), full),
            pltpu.VMEM((ENT_LEN, width), low),
            pltpu.VMEM((ENT_LEN, width), low),
            pltpu.SemaphoreType.DMA((2, requests.shape[0])),
            pltpu.SemaphoreType.DMA((2, requests.shape[0])),
            pltpu.SemaphoreType.DMA((2,)),
            pltpu.VMEM(table.shape, full),
            pltpu.SemaphoreType.DMA,
        ],
        compiler_params=pltpu.CompilerParams(
            collective_id=collective_id, has_side_effects=True, vmem_limit_bytes=VMEM_BYTES
        ),
    )(words, base, requests, place_mat, table, *shards)
    kept = result[: len(wholes)]
    saved = [
        dict(zip(SAVED, result[len(wholes) + layer * len(SAVED) :][: len(SAVED)]))
        for layer in range(LAYERS)
    ]
    return kept, saved, *result[-5:]


class Fan:
    def __init__(self, count, sems, copy_args):
        self.count, self.sems, self.copy_args = count, sems, copy_args
        self.index = lax.axis_index("dp")

    def copy(self, step):
        other = lax.rem(self.index + step, self.count)
        src, dst = self.copy_args(self.index, other)
        send_sem, recv_sem = self.sems
        return pltpu.make_async_remote_copy(
            src_ref=src,
            dst_ref=dst,
            send_sem=send_sem.at[step],
            recv_sem=recv_sem.at[step],
            device_id=(other, lax.axis_index("mp")),
            device_id_type=MESH,
        )

    def start(self):
        def go(step, carry):
            self.copy(step).start()
            return carry

        lax.fori_loop(1, self.count, go, 0)

    def wait(self):
        def done(step, carry):
            self.copy(step).wait()
            return carry

        lax.fori_loop(1, self.count, done, 0)


def greet_line(count, extra):
    barrier = pltpu.get_barrier_semaphore()
    index, core = lax.axis_index("dp"), lax.axis_index("mp")

    def hello(step, carry):
        other = lax.rem(index + step, count)
        pl.semaphore_signal(barrier, inc=1, device_id=(other, core), device_id_type=MESH)
        return carry

    lax.fori_loop(1, count, hello, 0)
    for target in extra:
        pl.semaphore_signal(barrier, inc=1, device_id=target, device_id_type=MESH)
    pl.semaphore_wait(barrier, count - 1 + len(extra))


TABLE_CUTS = 8


def head_body(count, *refs):
    ents, hits, head, table, local_targets = refs[:5]
    losses, grad_logits, states, grad_head, grad_ents = refs[5:10]
    logits, own_states, all_states, stat_mine, stat_theirs, stat_both, stat_all = refs[10:17]
    grad_part, hit_part, grad_send, grad_all, share_mine, share_theirs = refs[17:23]
    factors, turned_factors, send_sem, recv_sem, pair_send, pair_recv = refs[23:]
    index = lax.axis_index("dp")
    other = (index, 1 - lax.axis_index("mp"))
    greet_line(count, [other])
    total_rows = count * MASK_ENT
    span = table.shape[0] // TABLE_CUTS

    masked = mm(hits[...], ents[...].astype(jnp.bfloat16)).astype(jnp.bfloat16)
    head_low = flat(head)
    value, slope = gelu_parts(mm(masked, head_low))
    own_states[...] = value.astype(jnp.bfloat16)
    fan = Fan(count, (send_sem.at[0], recv_sem.at[0]), lambda me, to: (own_states, all_states.at[me]))
    fan.start()
    all_states[index] = own_states[...]
    fan.wait()
    states[...] = flat(all_states)
    target = local_targets[0:1, :]

    def hit_of(c):
        row = lax.broadcasted_iota(jnp.int32, (span, total_rows), 0) + c * span
        return row == target

    def rows_of(c):
        return pl.ds(pl.multiple_of(c * span, 16), span)

    def score(c, carry):
        peak, picked = carry
        part = mm_rt(table[rows_of(c), :], states[...])
        logits[rows_of(c), :] = part
        peak = jnp.maximum(peak, jnp.max(part, axis=0, keepdims=True))
        picked += jnp.sum(jnp.where(hit_of(c), part, 0.0), axis=0, keepdims=True)
        return peak, picked

    empty = jnp.zeros((1, total_rows), jnp.float32)
    peak, picked = lax.fori_loop(0, TABLE_CUTS, score, (empty - 3e38, empty))

    grad_part[...] = jnp.zeros_like(grad_part)
    hit_part[...] = jnp.zeros_like(hit_part)

    def weigh(c, weight):
        raised = jnp.exp(logits[rows_of(c), :] - peak)
        hot = jnp.where(hit_of(c), 1.0, 0.0).astype(jnp.bfloat16)
        grad_part[...] += mm_lt(raised.astype(jnp.bfloat16), table[rows_of(c), :])
        hit_part[...] += mm_lt(hot, table[rows_of(c), :])
        return weight + jnp.sum(raised, axis=0, keepdims=True)

    weight = lax.fori_loop(0, TABLE_CUTS, weigh, empty)
    stat_mine[0:1, :] = peak
    stat_mine[1:2, :] = weight
    stat_mine[2:3, :] = picked
    block = (count, MASK_ENT, table.shape[1])
    grad_send[:, :MASK_ENT, :] = grad_part[...].astype(jnp.bfloat16).reshape(block)
    grad_send[:, MASK_ENT:, :] = hit_part[...].astype(jnp.bfloat16).reshape(block)
    fan = Fan(count, (send_sem.at[1], recv_sem.at[1]), lambda me, to: (stat_mine, stat_all.at[me]))
    fan.start()
    back = Fan(
        count, (send_sem.at[2], recv_sem.at[2]), lambda me, to: (grad_send.at[to], grad_all.at[me])
    )
    back.start()
    stat_all[index] = stat_mine[...]
    grad_all[index] = grad_send[index]
    fan.wait()
    peak_line = stat_all[0, 0:1, :]
    for d in range(1, count):
        peak_line = jnp.maximum(peak_line, stat_all[d, 0:1, :])
    weight_line = picked_line = empty
    for d in range(count):
        weight_line += stat_all[d, 1:2, :] * jnp.exp(stat_all[d, 0:1, :] - peak_line)
        picked_line += stat_all[d, 2:3, :]
    stat_both[0:1, :] = peak_line
    stat_both[1:2, :] = weight_line
    stat_both[2:3, :] = picked_line
    swap = send(stat_both, stat_theirs, pair_send.at[0], pair_recv.at[0], other)
    swap.wait()
    peak_all = jnp.maximum(peak_line, stat_theirs[0:1, :])
    weight_all = weight_line * jnp.exp(peak_line - peak_all) + stat_theirs[1:2, :] * jnp.exp(
        stat_theirs[0:1, :] - peak_all
    )
    log_norm = peak_all + jnp.log(weight_all)
    losses[...] = jnp.broadcast_to(log_norm - picked_line - stat_theirs[2:3, :], losses.shape)
    factors[...] = jnp.zeros_like(factors)
    for d in range(count):
        factors[d : d + 1, :] = jnp.exp(stat_all[d, 0:1, :] - log_norm)
    turned_factors[...] = factors[...].T
    own = turned_factors[pl.ds(pl.multiple_of(index * MASK_ENT, MASK_ENT), MASK_ENT), :]
    back.wait()
    share = jnp.zeros((MASK_ENT, table.shape[1]), jnp.float32)
    for d in range(count):
        share += grad_all[d, :MASK_ENT, :].astype(jnp.float32) * own[:, d : d + 1]
        share -= grad_all[d, MASK_ENT:, :].astype(jnp.float32)
    share_mine[...] = share * (1.0 / total_rows)
    swap = send(share_mine, share_theirs, pair_send.at[1], pair_recv.at[1], other)

    def grads(c, carry):
        prob = jnp.exp(logits[rows_of(c), :] - log_norm)
        part = (prob - jnp.where(hit_of(c), 1.0, 0.0)) * (1.0 / total_rows)
        grad_logits[rows_of(c), :] = part.astype(jnp.bfloat16)
        return carry

    lax.fori_loop(0, TABLE_CUTS, grads, 0)
    swap.wait()
    grad_pre = ((share_mine[...] + share_theirs[...]) * slope).astype(jnp.bfloat16)
    grad_head[...] = mm_lt(masked, grad_pre).astype(jnp.bfloat16).reshape(grad_head.shape)
    grad_masked = mm_rt(grad_pre, head_low)
    grad_ents[...] = lax.dot_general(
        hits[...].astype(jnp.float32),
        grad_masked,
        (((0,), (0,)), ((), ())),
        precision=lax.Precision.HIGHEST,
        preferred_element_type=jnp.float32,
    )


def run_head(dims, ents, hits, head, table_low, local_targets, collective_id):
    count = dims[0] * dims[1] * dims[2]
    width = table_low.shape[1]
    rows = count * MASK_ENT
    low, full = jnp.bfloat16, jnp.float32
    return pl.pallas_call(
        functools.partial(head_body, count),
        out_shape=[
            jax.ShapeDtypeStruct((8, rows), full),
            jax.ShapeDtypeStruct((table_low.shape[0], rows), low),
            jax.ShapeDtypeStruct((rows, width), low),
            jax.ShapeDtypeStruct(head.shape, low),
            jax.ShapeDtypeStruct((ENT_LEN, D), full),
        ],
        in_specs=[VMEM] * 5,
        out_specs=[VMEM] * 5,
        scratch_shapes=[
            pltpu.VMEM((table_low.shape[0], rows), full),
            pltpu.VMEM((MASK_ENT, width), low),
            pltpu.VMEM((count, MASK_ENT, width), low),
            pltpu.VMEM((8, rows), full),
            pltpu.VMEM((8, rows), full),
            pltpu.VMEM((8, rows), full),
            pltpu.VMEM((count, 8, rows), full),
            pltpu.VMEM((rows, width), full),
            pltpu.VMEM((rows, width), full),
            pltpu.VMEM((count, 2 * MASK_ENT, width), low),
            pltpu.VMEM((count, 2 * MASK_ENT, width), low),
            pltpu.VMEM((MASK_ENT, width), full),
            pltpu.VMEM((MASK_ENT, width), full),
            pltpu.VMEM((128, rows), full),
            pltpu.VMEM((rows, 128), full),
            pltpu.SemaphoreType.DMA((3, count)),
            pltpu.SemaphoreType.DMA((3, count)),
            pltpu.SemaphoreType.DMA((2,)),
            pltpu.SemaphoreType.DMA((2,)),
        ],
        compiler_params=pltpu.CompilerParams(
            collective_id=collective_id, has_side_effects=True, vmem_limit_bytes=VMEM_BYTES
        ),
    )(ents, hits, head, table_low, local_targets)


def update_body(names, width, *refs):
    refs = list(refs)

    def take(count):
        part = refs[:count]
        del refs[:count]
        return part

    kinds = len(kind_rates)
    state_in = [take(3) for _ in range(kinds)]
    totals_in = take(len(names))
    incoming, requests, grad_logits, states = take(4)
    state_out = [take(3) for _ in range(kinds)]
    held = [take(3) for _ in range(kinds)]
    totals_held = take(len(names))
    in_sem, total_sem, out_sem = take(3)
    table = kinds - 1
    height = held[table][0].shape[0] // TABLE_CUTS

    def piece(ref, c):
        return ref if c is None else ref.at[pl.ds(c * height, height)]

    def copies(kind, c, inward):
        base = 3 * (kind + (0 if c is None else c))
        pairs = []
        for i in range(3):
            if inward:
                src, dst, sem = state_in[kind][i], held[kind][i], in_sem.at[base + i]
            else:
                src, dst, sem = held[kind][i], state_out[kind][i], out_sem.at[base + i]
            pairs.append(pltpu.make_async_copy(piece(src, c), piece(dst, c), sem))
        return pairs

    leaving = []
    total_copies = [
        pltpu.make_async_copy(src, dst, total_sem.at[i])
        for i, (src, dst) in enumerate(zip(totals_in, totals_held))
    ]
    for c in range(2):
        for copy in copies(table, c, True):
            copy.start()
    for copy in total_copies:
        copy.start()
    for kind in range(table):
        for copy in copies(kind, None, True):
            copy.start()
    for c in range(2, TABLE_CUTS):
        for copy in copies(table, c, True):
            copy.start()
    total_of = dict(zip(names, totals_held))

    def update(kind, at, gradient):
        master, first, second = held[kind]
        first_new = beta_first * first[at] + (1.0 - beta_first) * gradient
        second_new = beta_second * second[at] + (1.0 - beta_second) * gradient * gradient
        first_hat = first_new * (1.0 / (1.0 - beta_first**STEP))
        second_hat = second_new * (1.0 / (1.0 - beta_second**STEP))
        value = master[at]
        value -= kind_rates[kind] * (
            first_hat / (jnp.sqrt(second_hat) + adam_eps) + weight_decay * value
        )
        master[at], first[at], second[at] = value, first_new, second_new

    def finish(kind, c=None):
        for copy in copies(kind, c, False):
            copy.start()
            leaving.append(copy)

    def table_part(c):
        for copy in copies(table, c, True):
            copy.wait()
        rows = slice(c * height, (c + 1) * height)
        gradient = mm(grad_logits[rows, :], states[...])
        row = lax.broadcasted_iota(jnp.int32, (height, requests.shape[1]), 0) + c * height
        hot = jnp.where(row == requests[0:1, :], 1.0, 0.0).astype(jnp.bfloat16)
        gradient += mm(hot, incoming[...].astype(jnp.bfloat16))
        update(table, (rows, slice(None)), gradient)
        finish(table, c)

    table_part(0)
    table_part(1)
    for copy in total_copies:
        copy.wait()
    for kind in range(table):
        for copy in copies(kind, None, True):
            copy.wait()
        for layer in range(LAYERS):
            if kind == 0:
                blocks = []
                for name in ("words", "ents"):
                    total = total_of[layer, name]
                    half = total.shape[1] // 2
                    blocks += [total[:, :half], total[:, half:]]
                blocks += [total_of[layer, "key"][...], total_of[layer, "value"][...]]
                for mat, block in enumerate(blocks):
                    update(kind, (layer, mat), block)
            elif kind == 1:
                update(kind, (layer,), total_of[layer, "out"][...])
            elif kind in (2, 3):
                for i in range(2):
                    total = total_of[layer, ("up%d", "down%d")[kind - 2] % i]
                    half = total.shape[1]
                    cols = slice(i * half, (i + 1) * half)
                    update(kind, (layer, slice(None), cols), total[...])
            elif kind == 4:
                update(kind, (layer,), total_of["norms"][4 * layer : 4 * layer + 4, :width])
        if kind == 5:
            update(kind, (slice(None),), total_of["proj"][...])
        if kind == 6:
            update(kind, (slice(None),), total_of["head"][...])
        finish(kind)
    for c in range(2, TABLE_CUTS):
        table_part(c)
    for copy in leaving:
        copy.wait()


def run_update(states_of, totals, incoming, requests, grad_logits, states):
    names = list(totals)
    full = jnp.float32
    flat_states = [array for group in states_of for array in group]
    width = states_of[4][0].shape[-1]
    kinds = len(kind_rates)
    result = pl.pallas_call(
        functools.partial(update_body, names, width),
        out_shape=[jax.ShapeDtypeStruct(a.shape, full) for a in flat_states],
        in_specs=[ANY] * (len(flat_states) + len(names)) + [VMEM] * 4,
        out_specs=[ANY] * len(flat_states),
        scratch_shapes=[pltpu.VMEM(a.shape, full) for a in flat_states]
        + [pltpu.VMEM(totals[name].shape, full) for name in names]
        + [
            pltpu.SemaphoreType.DMA((3 * (kinds + TABLE_CUTS),)),
            pltpu.SemaphoreType.DMA((len(names),)),
            pltpu.SemaphoreType.DMA((3 * (kinds + TABLE_CUTS),)),
        ],
        compiler_params=pltpu.CompilerParams(vmem_limit_bytes=VMEM_BYTES),
    )(*flat_states, *totals.values(), incoming, requests, grad_logits, states)
    return [result[3 * i : 3 * i + 3] for i in range(kinds)]


def norm_back(grad, hat, scale, gain_row):
    hat = hat.astype(jnp.float32)
    wide = grad * gain_row
    inner = jnp.mean(wide * hat, axis=-1, keepdims=True)
    back = scale * (wide - jnp.mean(wide, axis=-1, keepdims=True) - hat * inner)
    gain_part = jnp.sum(grad * hat, axis=0, keepdims=True)
    return back, gain_part, jnp.sum(grad, axis=0, keepdims=True)


class Sums(Links):
    def __init__(self, dims, units, buffers, totals, sems, free_sem):
        super().__init__(dims, SUM_RATE)
        self.units, self.totals, self.buffers = units, totals, buffers
        self.send_sem, self.recv_sem = sems
        self.free_sem = free_sem
        self.spot = place(dims)
        self.peers = [axis_peers(dims, axis) for axis in range(3)]
        self.copies, self.done = {}, set()

    def start(self, stage, u):
        slot, order, turn = self.units[u]
        part, arrived = self.buffers[slot][0], self.buffers[slot][1 + stage]
        axis = order[stage]
        group = self.peers[axis]
        if turn and group:
            pl.semaphore_wait(self.free_sem.at[slot, stage], len(group))
        copies, base = [], sum(self.dims[order[i]] for i in range(stage))
        for k, (spot, target) in enumerate(group):
            at = [slice(None)] * 3
            for d in order[:stage]:
                at[d] = self.spot[d]
            at[axis] = spot
            sems = self.send_sem.at[u, base + k], self.recv_sem.at[u, base + k]
            copies.append(send(part.at[tuple(at)], arrived.at[k], *sems, target))
        self.copies[stage, u] = copies
        held = 1
        for d in order[stage + 1 :]:
            held *= self.dims[d]
        self.issue(axis, held * 2 * part.shape[3] * part.shape[4], (stage, u))

    def complete(self, what):
        stage, u = what
        slot, order, turn = self.units[u]
        part, arrived = self.buffers[slot][0], self.buffers[slot][1 + stage]
        for copy in self.copies.pop(what):
            copy.wait()
        axis = order[stage]
        group = self.peers[axis]
        rest = [d for d in range(3) if d not in order[: stage + 1]]

        def total_at(spots):
            at = tuple(spots.get(d, self.spot[d]) for d in range(3))
            value = part[at].astype(jnp.float32)
            for k in range(len(group)):
                value += arrived[(k, *[spots[d] for d in rest])].astype(jnp.float32)
            return at, value

        if stage == 2:
            self.totals[u][...] = total_at({})[1]
            self.done.add(u)
        elif group:
            inner = self.dims[rest[-1]]

            def add(i, carry):
                spots = {rest[-1]: i % inner}
                if len(rest) == 2:
                    spots[rest[0]] = i // inner
                at, value = total_at(spots)
                part[at] = value.astype(part.dtype)
                return carry

            count = inner * (self.dims[rest[0]] if len(rest) == 2 else 1)
            lax.fori_loop(0, count, add, 0)
        if self.reused(u):
            for _, target in group:
                pl.semaphore_signal(
                    self.free_sem.at[slot, stage], inc=1, device_id=target, device_id_type=MESH
                )
        if stage < 2:
            self.start(stage + 1, u)

    def reused(self, u):
        slot, _, turn = self.units[u]
        return not turn and sum(unit[0] == slot for unit in self.units) > 1

    def need(self, u):
        while u not in self.done:
            self.finish_first()

    def close(self):
        while self.active:
            self.finish_first()


UNITS = ("down0", "down1", "up0", "up1", "out", "words", "ents", "key", "value")
EXTRA = ("head", "proj", "norms")


def unit_orders(dims, blocks):
    names = list(blocks)
    sizes = [2 * rows * cols for rows, cols in blocks.values()]
    return {name: order[::-1] for name, order in zip(names, balanced_orders(dims, sizes))}


def sum_plan():
    names = ["head"]
    for layer in reversed(range(LAYERS)):
        names += [(layer, name) for name in UNITS]
    names += ["proj", "norms"]
    return names


def unit_width(name, half, hidden):
    return {
        "down0": hidden // 2, "down1": hidden // 2, "up0": hidden // 2, "up1": hidden // 2,
        "out": half, "words": 2 * half, "ents": 2 * half, "key": half, "value": half,
    }[name]


def backward_body(dims, names, orders, half, hidden, *refs):
    refs = list(refs)

    def take(count):
        part = refs[:count]
        del refs[:count]
        return part

    cotangent, grad_ents, grad_head, gains, entity_rows, place_mat = take(6)
    w_attn, w_out, w_up, w_down, w_proj = take(5)
    saved = [dict(zip(SAVED, take(len(SAVED)))) for _ in range(LAYERS)]
    word_grads, incoming = take(2)
    totals = take(len(names))
    slots = list(UNITS + EXTRA)
    buffers = [take(4) for _ in slots]
    left, right, hat, xh, o, stats, stats_t = take(7)
    mat_wide, mat_out, mat_attn, mat_proj = take(4)
    gacc, glow, gmix, delta, dk_acc, dv_acc, gnorm = take(7)
    mine, theirs = take(2)
    sum_sems = take(2)
    (free_sem,) = take(1)
    pair_sems = take(2)
    (load_sem,) = take(1)
    out_rows, in_rows, row_send, row_recv = take(4)

    units = []
    for name in names:
        kind = name if isinstance(name, str) else name[1]
        turn = not isinstance(name, str) and name[0] < LAYERS - 1
        units.append((slots.index(kind), orders[kind], turn))
    sums = Sums(dims, units, buffers, totals, sum_sems, free_sem)
    pair = Pair(mine, theirs, pair_sems)
    count = dims[0] * dims[1] * dims[2]
    greet_line(count, [pair.other])
    part_of = {slot: buffers[i][0] for i, slot in enumerate(slots)}
    loads, counter = {}, [0]

    def load(key, src, dst):
        copy = pltpu.make_async_copy(src, dst, load_sem.at[counter[0]])
        counter[0] += 1
        copy.start()
        loads.setdefault(key, []).append(copy)

    def ready(key):
        for copy in loads.pop(key, []):
            copy.wait()

    tick = sums.spend

    def begin_layer(layer):
        s = saved[layer]
        load("n2", s["n2"], hat)
        load("stats", s["stats"], stats)
        load("g", s["g"], left)
        load("down", w_down.at[layer], mat_wide)
        load("slope", s["slope"], right)
        load("h1b", s["h1b"], xh)
        load("out", w_out.at[layer], mat_out)
        load("o", s["o"], o)
        load("attn", w_attn.at[pl.ds(6 * layer, 6)], mat_attn)

    begin_layer(LAYERS - 1)
    load("proj", w_proj.at[0], mat_proj)
    slab = 2 if dims[0] % 2 == 0 else 1
    height = slab * D // dims[0]

    def fill(name, lhs, rhs, rhs_cols, row_slice=slice(None)):
        part = part_of[name]
        width = part.shape[-1]

        def block(i, carry):
            cols = pl.ds(pl.multiple_of(i * height, 128), height)
            value = mm_lt(lhs[row_slice, cols], rhs[row_slice, rhs_cols])
            shape = (slab, dims[1], dims[2], part.shape[3], width)
            part[pl.ds(i * slab, slab)] = value.astype(jnp.bfloat16).reshape(shape)
            return carry

        lax.fori_loop(0, dims[0] // slab, block, 0)

    def submit(layer, name):
        sums.start(0, names.index((layer, name)))

    head_part = part_of["head"]
    head_part[...] = grad_head[...]
    sums.start(0, names.index("head"))
    gacc[:WORDS] = cotangent[...].astype(jnp.float32)
    gacc[WORDS:] = grad_ents[...]
    gnorm[...] = jnp.zeros_like(gnorm)

    def add_norm(row, value):
        gnorm[row : row + 1, :] += value

    for layer in reversed(range(LAYERS)):
        last = layer == LAYERS - 1
        gain = [gains[4 * layer + i : 4 * layer + i + 1, :] for i in range(4)]
        ready("n2")
        ready("stats")

        def late_norm(c, carry):
            rows = pl.ds(c * BLOCK, BLOCK)
            back, gain_part, shift_part = norm_back(
                gacc[rows, :], hat[rows, :], stats[rows, 9:10], gain[2]
            )
            gacc[rows, :] = back
            glow[rows, :] = back.astype(jnp.bfloat16)
            add_norm(4 * layer + 2, gain_part)
            add_norm(4 * layer + 3, shift_part)
            return carry

        lax.fori_loop(0, BLOCKS, late_norm, 0)
        tick(3.0)
        load("n1", saved[layer]["n1"], hat)
        ready("g")
        for i in range(2):
            if not last:
                sums.need(names.index((layer + 1, "down%d" % i)))
            cols = slice(i * (hidden // 2), (i + 1) * (hidden // 2))
            fill("down%d" % i, glow, left, cols)
            submit(layer, "down%d" % i)
            tick(2.2)
        ahead = saved[layer]
        for i, name in enumerate(("k", "qw", "qe", "v")):
            load("qkv", ahead[name], left.at[:, pl.ds(i * half, half)])
        ready("down")
        ready("slope")

        def inner(c, carry):
            rows = pl.ds(c * BLOCK, BLOCK)
            for first in range(0, hidden, 512):
                cols = slice(first, first + 512)
                weight = mat_wide[:, :, :, :, cols].reshape(D, 512)
                value = mm(glow[rows, :], weight) * right[rows, cols].astype(jnp.float32)
                right[rows, cols] = value.astype(jnp.bfloat16)
            return carry

        lax.fori_loop(0, BLOCKS, inner, 0)
        tick(3.5)
        load("up", w_up.at[layer], mat_wide)
        ready("h1b")
        for i in range(2):
            if not last:
                sums.need(names.index((layer + 1, "up%d" % i)))
            cols = slice(i * (hidden // 2), (i + 1) * (hidden // 2))
            fill("up%d" % i, xh, right, cols)
            submit(layer, "up%d" % i)
            tick(2.2)
        load("xb", saved[layer]["xb"], xh)
        ready("up")
        ready("n1")

        def up_part(c, rows):
            return mm_rt(right[rows, :], flat(mat_wide))

        def early_norm(c, rows, total):
            back, gain_part, shift_part = norm_back(
                gacc[rows, :] + total, hat[rows, :], stats[rows, 8:9], gain[0]
            )
            gacc[rows, :] = back
            glow[rows, :] = back.astype(jnp.bfloat16)
            add_norm(4 * layer, gain_part)
            add_norm(4 * layer + 1, shift_part)

        pair.run(up_part, early_norm, lambda: tick(2.0))
        ready("o")
        ready("out")
        if not last:
            sums.need(names.index((layer + 1, "out")))
        fill("out", glow, o, slice(None))
        submit(layer, "out")

        def mixed(c, carry):
            rows = pl.ds(c * BLOCK, BLOCK)
            gmix[rows, :] = mm(glow[rows, :], flat(mat_out)).astype(jnp.bfloat16)
            stats_t[:, rows] = stats[rows, :].T
            return carry

        lax.fori_loop(0, BLOCKS, mixed, 0)
        tick(3.7)
        ready("qkv")
        for head_pair in range(half // (2 * HEAD_DIM)):
            lo = head_pair * 2 * HEAD_DIM
            lanes = slice(lo, lo + 2 * HEAD_DIM)
            k_lanes, qw_lanes, qe_lanes, v_lanes = [
                slice(j * half + lo, j * half + lo + 2 * HEAD_DIM) for j in range(4)
            ]

            def products(c, carry):
                rows = pl.ds(c * BLOCK, BLOCK)
                both = gmix[rows, lanes].astype(jnp.float32) * o[rows, lanes].astype(jnp.float32)
                turned = both.T
                delta[0:1, rows] = jnp.sum(turned[:HEAD_DIM], axis=0, keepdims=True)
                delta[1:2, rows] = jnp.sum(turned[HEAD_DIM:], axis=0, keepdims=True)
                return carry

            lax.fori_loop(0, BLOCKS, products, 0)
            dk_acc[...] = jnp.zeros_like(dk_acc)
            dv_acc[...] = jnp.zeros_like(dv_acc)

            def block(i, carry):
                rows = pl.ds(i * BLOCK, BLOCK)
                keys, values = left[:, k_lanes], left[:, v_lanes]
                grad_qw = grad_qe = None
                for which in range(2):
                    head = 2 * head_pair + which
                    q_mask, k_mask = lane_mask(BLOCK, which), lane_mask(LEN, which)
                    query_w = left[rows, qw_lanes] * q_mask
                    query_e = left[rows, qe_lanes] * q_mask
                    grad_o = gmix[rows, lanes] * q_mask
                    log_row = stats_t[head : head + 1, rows]
                    inner_row = delta[which : which + 1, rows]
                    own_keys = keys * k_mask
                    for span, query in ((slice(0, WORDS), query_w), (slice(WORDS, LEN), query_e)):
                        prob = jnp.exp2(mm_rt(keys[span], query) * SCORE_STEP - log_row)
                        grad_prob = mm_rt(values[span], grad_o)
                        dv_acc[span, :] += mm(prob.astype(jnp.bfloat16), grad_o)
                        grad_score = (prob * (grad_prob - inner_row)).astype(jnp.bfloat16)
                        dk_acc[span, :] += mm(grad_score, query)
                        part = mm_lt(grad_score, own_keys[span])
                        if span.start == 0:
                            grad_qw = part if grad_qw is None else grad_qw + part
                        else:
                            grad_qe = part if grad_qe is None else grad_qe + part
                right[rows, lanes] = (grad_qw * 0.125).astype(jnp.bfloat16)
                right[rows, half + lo : half + lo + 2 * HEAD_DIM] = (grad_qe * 0.125).astype(
                    jnp.bfloat16
                )
                return carry

            for first in range(0, BLOCKS, 2):
                lax.fori_loop(first, first + 2, block, 0)
                tick(4.7)
            at = 2 * half + lo
            right[:, at : at + 2 * HEAD_DIM] = (dk_acc[...] * 0.125).astype(jnp.bfloat16)
            at = 3 * half + lo
            right[:, at : at + 2 * HEAD_DIM] = dv_acc[...].astype(jnp.bfloat16)
        ready("xb")
        words, ents = slice(0, WORDS), slice(WORDS, LEN)
        for name, cols, rows in (
            ("words", slice(0, 2 * half), words),
            ("ents", slice(0, 2 * half), ents),
            ("key", slice(2 * half, 3 * half), slice(None)),
            ("value", slice(3 * half, 4 * half), slice(None)),
        ):
            if not last:
                sums.need(names.index((layer + 1, name)))
            fill(name, xh, right, cols, rows)
            submit(layer, name)
            tick(1.4)
        ready("attn")
        mats = [slice(j * half, (j + 1) * half) for j in range(4)]

        def input_part(c, rows):
            total = mm_rt(right[rows, mats[2]], flat(mat_attn, 4))
            total += mm_rt(right[rows, mats[3]], flat(mat_attn, 5))
            start = c * BLOCK
            edge = min(max(WORDS - start, 0), BLOCK)
            pieces = []
            for low, high, pick in ((0, edge, (0, 1)), (edge, BLOCK, (2, 3))):
                if high > low:
                    span = slice(start + low, start + high)
                    piece = mm_rt(right[span, mats[0]], flat(mat_attn, pick[0]))
                    pieces.append(piece + mm_rt(right[span, mats[1]], flat(mat_attn, pick[1])))
            return total + (pieces[0] if len(pieces) == 1 else jnp.concatenate(pieces, axis=0))

        def to_input(c, rows, total):
            gacc[rows, :] += total

        pair.run(input_part, to_input, lambda: tick(2.0))
        if layer:
            begin_layer(layer - 1)
    ready("proj")
    leaving = pltpu.make_async_copy(gacc.at[pl.ds(0, WORDS)], word_grads, load_sem.at[counter[0]])
    leaving.start()
    grad_entity = gacc[WORDS:].astype(jnp.bfloat16)
    row_grads = mm_rt(grad_entity, flat(mat_proj)).astype(jnp.bfloat16)
    out_rows[...] = mm_lt(place_mat[...], row_grads).reshape(out_rows.shape)
    returning = Fan(count, (row_send, row_recv), lambda me, to: (out_rows.at[to], in_rows.at[me]))
    returning.start()
    here = lax.axis_index("dp")
    in_rows[here] = out_rows[here]
    proj_part = part_of["proj"]
    proj_part[...] = mm_lt(entity_rows[...], grad_entity).astype(jnp.bfloat16).reshape(proj_part.shape)
    sums.start(0, names.index("proj"))
    width = D // count
    norm_low = gnorm[...].astype(jnp.bfloat16)
    for d in range(count):
        z, rest = d // (dims[1] * dims[2]), d % (dims[1] * dims[2])
        row = lax.broadcasted_iota(jnp.int32, (128, D), 0)
        lane = lax.broadcasted_iota(jnp.int32, (128, D), 1)
        hot = jnp.where((row + d * width == lane) & (row < width), 1.0, 0.0).astype(jnp.bfloat16)
        block = mm_rt(norm_low, hot).astype(jnp.bfloat16)
        part_of["norms"][z, rest // dims[2], rest % dims[2]] = block
    sums.start(0, names.index("norms"))
    sums.close()
    returning.wait()
    incoming[...] = flat(in_rows)
    leaving.wait()


def run_backward(
    dims, cotangent, grad_ents, grad_head, gains, entity_rows, place_mat, kept, saved, collective_id
):
    names = sum_plan()
    half, hidden = kept[0].shape[-1], kept[2].shape[-1]
    low, full = jnp.bfloat16, jnp.float32
    rows = kept[0].shape[4]
    blocks = {name: (rows, unit_width(name, half, hidden)) for name in UNITS}
    blocks["head"] = (rows, kept[5].shape[-1])
    blocks["proj"] = (kept[4].shape[4], D)
    blocks["norms"] = (16, 128)
    scratch = []
    orders = unit_orders(dims, blocks)
    for name in UNITS + EXTRA:
        order, block = orders[name], blocks[name]
        scratch.append(pltpu.VMEM((*dims, *block), low))
        for stage in range(3):
            rest = [dims[d] for d in range(3) if d not in order[: stage + 1]]
            peers = max(dims[order[stage]] - 1, 1)
            scratch.append(pltpu.VMEM((peers, *rest, *block), low))
    copies = sum(dims)
    kinds = [name if isinstance(name, str) else name[1] for name in names]
    count = dims[0] * dims[1] * dims[2]
    width, slots = kept[5].shape[-1], place_mat.shape[1]
    inputs = [cotangent, grad_ents, grad_head, gains, entity_rows, place_mat, *kept[:5]]
    inputs += [saved[layer][name] for layer in range(LAYERS) for name in SAVED]
    result = pl.pallas_call(
        functools.partial(backward_body, dims, names, orders, half, hidden),
        out_shape=[
            jax.ShapeDtypeStruct((WORDS, D), full),
            jax.ShapeDtypeStruct((slots, width), full),
        ]
        + [jax.ShapeDtypeStruct(blocks[kind], full) for kind in kinds],
        in_specs=[VMEM] * 6 + [ANY] * (len(inputs) - 6),
        out_specs=[ANY] + [VMEM] * (1 + len(names)),
        scratch_shapes=scratch
        + [
            pltpu.VMEM((LEN, hidden), low),
            pltpu.VMEM((LEN, hidden), low),
            pltpu.VMEM((LEN, D), low),
            pltpu.VMEM((LEN, D), low),
            pltpu.VMEM((LEN, half), low),
            pltpu.VMEM((LEN, 128), full),
            pltpu.VMEM((128, LEN), full),
            pltpu.VMEM(kept[2].shape[1:], low),
            pltpu.VMEM(kept[1].shape[1:], low),
            pltpu.VMEM((6, *kept[0].shape[1:]), low),
            pltpu.VMEM(kept[4].shape[1:], low),
            pltpu.VMEM((LEN, D), full),
            pltpu.VMEM((LEN, D), low),
            pltpu.VMEM((LEN, half), low),
            pltpu.VMEM((8, LEN), full),
            pltpu.VMEM((LEN, 2 * HEAD_DIM), full),
            pltpu.VMEM((LEN, 2 * HEAD_DIM), full),
            pltpu.VMEM((16, D), full),
            pltpu.VMEM((BLOCKS, BLOCK, D), low),
            pltpu.VMEM((2, BLOCKS, BLOCK, D), low),
            pltpu.SemaphoreType.DMA((len(names), copies)),
            pltpu.SemaphoreType.DMA((len(names), copies)),
            pltpu.SemaphoreType.REGULAR((len(UNITS + EXTRA), 3)),
            pltpu.SemaphoreType.DMA((2 * LAYERS, BLOCKS)),
            pltpu.SemaphoreType.DMA((2 * LAYERS, BLOCKS)),
            pltpu.SemaphoreType.DMA((64,)),
            pltpu.VMEM((count, slots // count, width), full),
            pltpu.VMEM((count, slots // count, width), full),
            pltpu.SemaphoreType.DMA((count,)),
            pltpu.SemaphoreType.DMA((count,)),
        ],
        compiler_params=pltpu.CompilerParams(
            collective_id=collective_id, has_side_effects=True, vmem_limit_bytes=VMEM_BYTES
        ),
    )(*inputs)
    return result[0], result[1], dict(zip(names, result[2:]))


def padded_rows(values):
    extra = -values.shape[-2] % 16
    return jnp.pad(values, [(0, 0)] * (values.ndim - 2) + [(0, extra), (0, 0)])


def weight_shards(attention_in, attention_out, feed_up, feed_down, norm_params, entity_proj, head_proj):
    def turned(values):
        return jnp.swapaxes(values, 1, 2)

    mats = attention_in.reshape(-1, *attention_in.shape[2:])
    norms = norm_params.reshape(1, -1, norm_params.shape[-1])
    norms = jnp.pad(norms, [(0, 0), (0, 16 - norms.shape[1]), (0, -norms.shape[2] % 128)])
    sources = [mats, turned(attention_out), feed_up, turned(feed_down), entity_proj[None], head_proj[None]]
    heights = [part.shape[1] for part in sources]
    shards = [padded_rows(part.astype(jnp.bfloat16)) for part in sources]
    shards.append(norms.astype(jnp.bfloat16))
    return shards, heights


def unpack_weights(wholes, heights, norm_width):
    kept = []
    for part, height in zip(wholes, heights):
        part = part[..., :height, :]
        kept.append(part.reshape(part.shape[0], -1, part.shape[-1]))
    norm_all = wholes[6][0].reshape(-1, 16, wholes[6].shape[-1])[:, : LAYERS * 4, :norm_width]
    norm_all = jnp.swapaxes(norm_all, 0, 1).reshape(LAYERS, 4, -1)
    return (
        kept[0].reshape(LAYERS, 6, *kept[0].shape[1:]),
        kept[1],
        kept[2],
        kept[3],
        norm_all,
        kept[4][0],
        kept[5][0],
    )


def gather_apart(dims, shards):
    chunks = [(4, 0, 1, True), (5, 0, 1, False), (6, 0, 1, True)]
    for layer in range(LAYERS):
        chunks += [(0, 6 * layer, 3, True), (0, 6 * layer + 3, 3, False)]
        chunks += [(1, layer, 1, layer == 0), (2, layer, 1, True), (3, layer, 1, False)]
    return gather_weights(dims, shards, chunks, 1)


def sum_all(dims, layer_grads, grad_proj, grad_head):
    n_dp = dims[0] * dims[1] * dims[2]

    def blocks(values):
        cut = values.astype(jnp.bfloat16).reshape(*dims, values.shape[0] // n_dp, values.shape[1])
        return padded_rows(cut)

    parts, flags, heights = [], [], []
    for layer in reversed(range(LAYERS)):
        (words_mat, ents_mat, shared_mat), out_mat, up_mat, down_mat, _ = layer_grads[layer]
        late = layer % 2 == 0
        for values, y_first in (
            (up_mat, True),
            (down_mat, False),
            (words_mat, True),
            (ents_mat, False),
            (shared_mat, late),
            (out_mat, not late),
        ):
            parts.append(blocks(values))
            flags.append(y_first)
            heights.append(values.shape[0] // n_dp)
    for values, y_first in ((grad_proj, True), (grad_head, False)):
        parts.append(blocks(values))
        flags.append(y_first)
        heights.append(values.shape[0] // n_dp)
    norms = jnp.concatenate([layer_grads[layer][4] for layer in range(LAYERS)], axis=0)
    width = norms.shape[1] // n_dp
    norms = jnp.swapaxes(norms.reshape(norms.shape[0], n_dp, width), 0, 1)
    norms = jnp.pad(norms, [(0, 0), (0, 16 - norms.shape[1]), (0, -width % 128)])
    parts.append(norms.astype(jnp.bfloat16).reshape(*dims, *norms.shape[1:]))
    flags.append(True)
    totals = sum_gradients(dims, parts, flags, 2)
    norm_sum = totals[-1][: LAYERS * 4, :width].reshape(LAYERS, 4, width)
    totals = [total[:height] for total, height in zip(totals, heights)]
    attn, outs, ups, downs = [], [], [], []
    for layer in range(LAYERS):
        at = 6 * (LAYERS - 1 - layer)
        ups.append(totals[at])
        downs.append(totals[at + 1].T)
        for part in totals[at + 2 : at + 5]:
            half = part.shape[1] // 2
            attn += [part[:, :half], part[:, half:]]
        outs.append(totals[at + 5].T)
    attn = jnp.stack(attn)
    return (
        attn.reshape(LAYERS, 6, *attn.shape[1:]),
        jnp.stack(outs),
        jnp.stack(ups),
        jnp.stack(downs),
        norm_sum,
        totals[-2],
        totals[-1],
    )


def apart_device(
    word_inputs,
    entity_base,
    entity_ids,
    buckets,
    mask_positions,
    targets,
    word_cotangent,
    attention_in,
    attention_in_first,
    attention_in_second,
    attention_out,
    attention_out_first,
    attention_out_second,
    feed_up,
    feed_up_first,
    feed_up_second,
    feed_down,
    feed_down_first,
    feed_down_second,
    norm_params,
    norm_params_first,
    norm_params_second,
    entity_proj,
    entity_proj_first,
    entity_proj_second,
    head_proj,
    head_proj_first,
    head_proj_second,
    entity_table,
    entity_table_first,
    entity_table_second,
):
    dims = chip_grid(lax.axis_size("dp"))
    shards, heights = weight_shards(
        attention_in, attention_out, feed_up, feed_down, norm_params, entity_proj, head_proj
    )
    wholes = gather_apart(dims, shards)
    attn_low, out_low, up_low, down_low, norm_low, proj_low, head_low = unpack_weights(
        wholes, heights, norm_params.shape[-1]
    )
    gain_all = norm_low.astype(jnp.float32)
    slot_total = entity_ids.shape[0]
    shard_rows = entity_table.shape[0]
    bucket_rows = buckets.reshape(buckets.shape[2], buckets.shape[3])
    filled = bucket_rows >= 0
    safe_slot = jnp.maximum(bucket_rows, 0)
    request = jnp.where(filled, entity_ids[safe_slot] % shard_rows, -1)
    received = lax.all_to_all(request, "dp", split_axis=0, concat_axis=0, tiled=True)
    shard_base = lax.axis_index(("dp", "mp")) * shard_rows
    owned_mask = received >= 0
    safe_row = jnp.clip(received, 0, shard_rows - 1)
    table_low = entity_table.astype(jnp.bfloat16)
    replies = jnp.where(owned_mask[:, :, None], table_low[safe_row], jnp.zeros((), jnp.bfloat16))
    replied_rows_result = lax.all_to_all(replies, "dp", split_axis=0, concat_axis=0, tiled=True)
    row_placement_plan = (
        bucket_rows[:, :, None] == jnp.arange(slot_total, dtype=jnp.int32)[None, None, :]
    ).astype(jnp.bfloat16)
    local_shard_rows = jnp.einsum(
        "wvt,wvi->ti", row_placement_plan, replied_rows_result, preferred_element_type=jnp.float32
    )
    paired = pair_sum(local_shard_rows)
    masked_slots = (
        jnp.arange(SEQ_DEV, dtype=jnp.int32)[:, None] * ENT_LEN + mask_positions
    ).reshape(-1)
    keep_weight = 1.0 - jnp.any(
        jnp.arange(slot_total, dtype=jnp.int32)[:, None] == masked_slots[None, :], axis=1
    ).astype(jnp.float32)
    entity_rows = (paired * keep_weight[:, None]).astype(jnp.bfloat16)
    entity_inputs = entity_base.astype(jnp.float32) + jnp.dot(
        entity_rows, proj_low, preferred_element_type=jnp.float32
    )
    hidden = jnp.concatenate(
        [
            word_inputs.astype(jnp.float32).reshape(SEQ_DEV, WORDS, D),
            entity_inputs.reshape(SEQ_DEV, ENT_LEN, D),
        ],
        axis=1,
    )
    saved_layers = []
    for layer_index in range(LAYERS):
        hidden, saved_acts = layer_forward(
            hidden,
            attn_low[layer_index],
            out_low[layer_index],
            up_low[layer_index],
            down_low[layer_index],
            gain_all[layer_index],
        )
        saved_layers.append(saved_acts)
    seq_index = jnp.arange(SEQ_DEV, dtype=jnp.int32)[:, None]
    masked_rows = WORDS + mask_positions
    masked_low = hidden[seq_index, masked_rows].reshape(SEQ_DEV * MASK_ENT, D).astype(jnp.bfloat16)
    head_pre = jnp.dot(masked_low, head_low, preferred_element_type=jnp.float32)
    states_low = gelu_exact(head_pre).astype(jnp.bfloat16)
    all_states = spread(states_low, False, False, 3).reshape(-1, states_low.shape[1])
    logits = lax.dot_general(
        all_states, table_low, (((1,), (1,)), ((), ())), preferred_element_type=jnp.float32
    )
    flat_targets = targets.reshape(-1)
    target_hits = (
        jnp.arange(shard_rows, dtype=jnp.int32)[None, :] == (flat_targets - shard_base)[:, None]
    )
    peak_value = jnp.max(logits, axis=1)
    exp_total = jnp.sum(jnp.exp(logits - peak_value[:, None]), axis=1)
    picked = jnp.sum(jnp.where(target_hits, logits, 0.0), axis=1)
    shares = spread(jnp.stack([peak_value, exp_total, picked]), True, False, 4)
    peak_all = jnp.max(shares[:, 0], axis=0)
    total_all = jnp.sum(shares[:, 1] * jnp.exp(shares[:, 0] - peak_all), axis=0)
    picked_all = jnp.sum(shares[:, 2], axis=0)
    log_norm = peak_all + jnp.log(total_all)
    row_losses = log_norm - picked_all
    prob_rows = jnp.exp(logits - log_norm[:, None])
    grad_logits = ((prob_rows - target_hits.astype(jnp.float32)) / flat_targets.shape[0]).astype(
        jnp.bfloat16
    )
    grad_table = lax.dot_general(
        grad_logits, all_states, (((0,), (0,)), ((), ())), preferred_element_type=jnp.float32
    )
    grad_states = jnp.dot(grad_logits, table_low, preferred_element_type=jnp.float32)
    grad_states = grad_states.reshape(lax.axis_size("dp"), -1, grad_states.shape[1])
    grad_states = jnp.sum(spread(grad_states, False, True, 5), axis=0)
    grad_states = grad_states + lax.ppermute(grad_states, "mp", [(0, 1), (1, 0)])
    grad_head_pre = jax.vjp(gelu_exact, head_pre)[1](grad_states)[0].astype(jnp.bfloat16)
    grad_head = lax.dot_general(
        masked_low, grad_head_pre, (((0,), (0,)), ((), ())), preferred_element_type=jnp.float32
    )
    grad_masked = lax.dot_general(
        grad_head_pre, head_low, (((1,), (1,)), ((), ())), preferred_element_type=jnp.float32
    )
    grad_hidden = jnp.concatenate(
        [
            word_cotangent.astype(jnp.float32).reshape(SEQ_DEV, WORDS, D),
            jnp.zeros((SEQ_DEV, ENT_LEN, D), jnp.float32),
        ],
        axis=1,
    )
    grad_hidden = grad_hidden.at[seq_index, masked_rows].add(
        grad_masked.reshape(SEQ_DEV, MASK_ENT, D)
    )
    kept_grads = []
    for layer_index in reversed(range(LAYERS)):
        grad_hidden, layer_grads = layer_backward(
            grad_hidden,
            saved_layers[layer_index],
            attn_low[layer_index],
            out_low[layer_index],
            up_low[layer_index],
            down_low[layer_index],
            gain_all[layer_index],
        )
        if layer_index == 0:
            word_grads = grad_hidden[:, :WORDS].reshape(SEQ_DEV * WORDS, D)
            grad_entity = grad_hidden[:, WORDS:].reshape(slot_total, D).astype(jnp.bfloat16)
            grad_proj = lax.dot_general(
                entity_rows,
                grad_entity,
                (((0,), (0,)), ((), ())),
                preferred_element_type=jnp.float32,
            )
            row_gradient_block = (
                lax.dot_general(
                    grad_entity,
                    proj_low,
                    (((1,), (1,)), ((), ())),
                    preferred_element_type=jnp.float32,
                )
                * keep_weight[:, None]
            )
            outgoing = jnp.where(filled[:, :, None], row_gradient_block[safe_slot], 0.0)
            incoming = lax.all_to_all(
                outgoing.astype(jnp.bfloat16), "dp", split_axis=0, concat_axis=0, tiled=True
            ).astype(outgoing.dtype)
            grad_table = grad_table.at[safe_row].add(
                jnp.where(owned_mask[:, :, None], incoming, 0.0)
            )
        kept_grads.insert(0, layer_grads)
    reduced = sum_all(dims, kept_grads, grad_proj, grad_head)
    reduced_proj, reduced_head = reduced[5:]
    attn_new = adam_update(
        attention_in, attention_in_first, attention_in_second, reduced[0], kind_rates[0]
    )
    out_new = adam_update(
        attention_out, attention_out_first, attention_out_second, reduced[1], kind_rates[1]
    )
    up_new = adam_update(feed_up, feed_up_first, feed_up_second, reduced[2], kind_rates[2])
    down_new = adam_update(feed_down, feed_down_first, feed_down_second, reduced[3], kind_rates[3])
    norm_new = adam_update(
        norm_params, norm_params_first, norm_params_second, reduced[4], kind_rates[4]
    )
    proj_new = adam_update(
        entity_proj, entity_proj_first, entity_proj_second, reduced_proj, kind_rates[5]
    )
    head_new = adam_update(
        head_proj, head_proj_first, head_proj_second, reduced_head, kind_rates[6]
    )
    table_new = adam_update(
        entity_table, entity_table_first, entity_table_second, grad_table, kind_rates[7]
    )
    return (
        row_losses,
        word_grads,
        attn_new[0],
        attn_new[1],
        attn_new[2],
        out_new[0],
        out_new[1],
        out_new[2],
        up_new[0],
        up_new[1],
        up_new[2],
        down_new[0],
        down_new[1],
        down_new[2],
        norm_new[0],
        norm_new[1],
        norm_new[2],
        proj_new[0],
        proj_new[1],
        proj_new[2],
        head_new[0],
        head_new[1],
        head_new[2],
        table_new[0],
        table_new[1],
        table_new[2],
    )


def turned(*arrays):
    return tuple(jnp.swapaxes(array, 1, 2) for array in arrays)


def fused_device(
    word_inputs,
    entity_base,
    entity_ids,
    buckets,
    mask_positions,
    targets,
    word_cotangent,
    attention_in,
    attention_in_first,
    attention_in_second,
    attention_out,
    attention_out_first,
    attention_out_second,
    feed_up,
    feed_up_first,
    feed_up_second,
    feed_down,
    feed_down_first,
    feed_down_second,
    norm_params,
    norm_params_first,
    norm_params_second,
    entity_proj,
    entity_proj_first,
    entity_proj_second,
    head_proj,
    head_proj_first,
    head_proj_second,
    entity_table,
    entity_table_first,
    entity_table_second,
):
    dims = chip_grid(lax.axis_size("dp"))
    shards, heights = weight_shards(
        attention_in, attention_out, feed_up, feed_down, norm_params, entity_proj, head_proj
    )
    slot_total, shard_rows = entity_ids.shape[0], entity_table.shape[0]
    bucket_rows = buckets.reshape(buckets.shape[2], buckets.shape[3])
    request = jnp.where(
        bucket_rows >= 0, entity_ids[jnp.maximum(bucket_rows, 0)] % shard_rows, -1
    ).astype(jnp.int32)
    requests = jnp.broadcast_to(request[:, :, None], (*request.shape, 128))
    slots = jnp.arange(slot_total, dtype=jnp.int32)
    marks = mask_positions.reshape(-1)[:, None] == slots[None, :]
    keep = jnp.logical_not(jnp.any(marks, axis=0))
    place_mat = (slots[:, None] == bucket_rows.reshape(-1)[None, :]) & keep[:, None]
    place_mat = place_mat.astype(jnp.bfloat16)
    hits = marks.astype(jnp.bfloat16)
    flat_targets = targets.reshape(-1)
    local_targets = flat_targets - lax.axis_index(("dp", "mp")) * shard_rows
    local_targets = jnp.broadcast_to(local_targets[None, :], (8, flat_targets.shape[0]))
    wholes, saved_layers, ents, gain_rows, entity_rows, got, table_low = run_forward(
        dims, word_inputs, entity_base, requests, place_mat, entity_table, shards, 6
    )
    losses, grad_logits, states, grad_head, grad_ents = run_head(
        dims, ents, hits, wholes[5][0], table_low, local_targets, 7
    )
    word_grads, incoming, totals = run_backward(
        dims,
        word_cotangent,
        grad_ents,
        grad_head,
        gain_rows,
        entity_rows,
        place_mat,
        wholes,
        saved_layers,
        8,
    )
    wanted = jnp.broadcast_to(got[:, 0][None, :], (8, got.shape[0]))
    updated = run_update(
        (
            (attention_in, attention_in_first, attention_in_second),
            turned(attention_out, attention_out_first, attention_out_second),
            (feed_up, feed_up_first, feed_up_second),
            turned(feed_down, feed_down_first, feed_down_second),
            (norm_params, norm_params_first, norm_params_second),
            (entity_proj, entity_proj_first, entity_proj_second),
            (head_proj, head_proj_first, head_proj_second),
            (entity_table, entity_table_first, entity_table_second),
        ),
        totals,
        incoming,
        wanted,
        grad_logits,
        states,
    )
    updated[1], updated[3] = turned(*updated[1]), turned(*updated[3])
    results = [losses[0], word_grads]
    for master, first, second in updated:
        results += [first, second, master]
    return tuple(results)


def on_device(*arrays):
    n_dp = lax.axis_size("dp")
    whole_tiles = D % (16 * n_dp) == 0
    return (fused_device if whole_tiles else apart_device)(*arrays)


def solution(mesh):
    in_specs = (
        P("dp", None),
        P("dp", None),
        P("dp"),
        P("dp", "mp", None, None),
        P("dp", None),
        P(),
        P("dp", None),
        P(None, None, "dp", "mp"),
        P(None, None, "dp", "mp"),
        P(None, None, "dp", "mp"),
        P(None, "mp", "dp"),
        P(None, "mp", "dp"),
        P(None, "mp", "dp"),
        P(None, "dp", "mp"),
        P(None, "dp", "mp"),
        P(None, "dp", "mp"),
        P(None, "mp", "dp"),
        P(None, "mp", "dp"),
        P(None, "mp", "dp"),
        P(None, None, "dp"),
        P(None, None, "dp"),
        P(None, None, "dp"),
        P("dp", None),
        P("dp", None),
        P("dp", None),
        P("dp", None),
        P("dp", None),
        P("dp", None),
        P(("dp", "mp"), None),
        P(("dp", "mp"), None),
        P(("dp", "mp"), None),
    )
    out_specs = (
        P(),
        P("dp", None),
        P(None, None, "dp", "mp"),
        P(None, None, "dp", "mp"),
        P(None, None, "dp", "mp"),
        P(None, "mp", "dp"),
        P(None, "mp", "dp"),
        P(None, "mp", "dp"),
        P(None, "dp", "mp"),
        P(None, "dp", "mp"),
        P(None, "dp", "mp"),
        P(None, "mp", "dp"),
        P(None, "mp", "dp"),
        P(None, "mp", "dp"),
        P(None, None, "dp"),
        P(None, None, "dp"),
        P(None, None, "dp"),
        P("dp", None),
        P("dp", None),
        P("dp", None),
        P("dp", None),
        P("dp", None),
        P("dp", None),
        P(("dp", "mp"), None),
        P(("dp", "mp"), None),
        P(("dp", "mp"), None),
    )
    return jax.shard_map(
        on_device, mesh=mesh, in_specs=in_specs, out_specs=out_specs, check_vma=False
    )
```
